32 devices in a mesh: wa: 4 (over y, x), ta: 8 (over z, core).
Axes of the slice: x: 2, y: 2, z: 4, core: 2. Of those that a mesh axis runs over, the one named last changes fastest.
Arguments:
- tokens: bfloat16 [768, 16384], P('wa', 'ta'), may hold values from -6 to 6
- seq_lengths: int32 [8], P('ta'), may hold values from 128 to 2048, as said below
- norm1_gain: float32 [768], P('wa'), may hold values from 0.5 to 1.5
- norm1_bias: float32 [768], P('wa'), may hold values from -4 to 4
- value_weight: bfloat16 [768, 768], P('ta', 'wa'), may hold values from -0.21875 to 0.21875
- value_bias: float32 [768], P('wa'), may hold values from -1.5 to 1.5
- synth_logits: bfloat16 [2048, 12, 2048], P('ta', 'wa'), may hold values from -8 to 8
- out_weight: bfloat16 [768, 768], P('wa', 'ta'), may hold values from -1.25 to 1.25
- out_bias: float32 [768], P('wa'), may hold values from -4 to 4
- norm2_gain: float32 [768], P('wa'), may hold values from 0.5 to 1.5
- norm2_bias: float32 [768], P('wa'), may hold values from -4 to 4
- up_weight: bfloat16 [768, 3072], P('wa', 'ta'), may hold values from -0.21875 to 0.21875
- up_bias: float32 [3072], P('wa'), may hold values from -4 to 4
- down_weight: bfloat16 [3072, 768], P('ta', 'wa'), may hold values from -0.109375 to 0.109375
- down_bias: float32 [768], P('wa'), may hold values from -4 to 4
- cotangent: bfloat16 [768, 16384], P('wa', 'ta'), may hold values from -6 to 6
Outputs:
- output: bfloat16 [768, 16384], P('wa', 'ta')
- tokens_grad: float32 [768, 16384], P('wa', 'ta')
- norm1_gain_grad: float32 [768], P('wa')
- norm1_bias_grad: float32 [768], P('wa')
- value_weight_grad: float32 [768, 768], P('ta', 'wa')
- value_bias_grad: float32 [768], P('wa')
- logits_grad: float32 [2048, 12, 2048], P('ta', 'wa')
- out_weight_grad: float32 [768, 768], P('wa', 'ta')
- out_bias_grad: float32 [768], P('wa')
- norm2_gain_grad: float32 [768], P('wa')
- norm2_bias_grad: float32 [768], P('wa')
- up_weight_grad: float32 [768, 3072], P('wa', 'ta')
- up_bias_grad: float32 [3072], P('wa')
- down_weight_grad: float32 [3072, 768], P('ta', 'wa')
- down_bias_grad: float32 [768], P('wa')
The draws below stay inside these ranges and needn't reach their ends.
Inputs may be any that keep to these rules, and one draw needn't show every extreme that they name: `seq_lengths`: in every draw at least one packed row has the full length 2048.
All inputs are finite; a program needn't handle non-finite values.
Results may differ from the reference program's by a relative error of at most 0.007.
Values may be sent and summed in bfloat16 or wider, within the bound.
A program may use at most 256 MiB of HBM per device.

```python
import jax
import jax.numpy as jnp
from jax import lax

D = 768
HEADS = 12
HEAD_DIM = 64
FF = 3072
SEQ_LEN = 2048
SEQS = 8
TOKENS = 16384


def draw_seq_lengths(key, part):
    key = jax.random.fold_in(key, 7)
    key_first, key_second, key_third = jax.random.split(key, 3)
    factor_one = jax.random.randint(key_first, (SEQS,), 1, SEQ_LEN + 1)
    factor_two = jax.random.randint(key_second, (SEQS,), 1, SEQ_LEN + 1)
    lengths = jnp.maximum(SEQ_LEN // 16, factor_one * factor_two // SEQ_LEN)
    chosen = jax.random.randint(key_third, (), 0, SEQS)
    return jnp.where(jnp.arange(SEQS) == chosen, SEQ_LEN, lengths).astype(jnp.int32)


def level_of(stream_key, dims, cuts, smallest, top_value):
    level = 1.0
    for axis_at, parts in cuts:
        draws = jax.random.uniform(jax.random.fold_in(jax.random.fold_in(stream_key, 6), axis_at), (parts,), jnp.float32, smallest / len(cuts), top_value / len(cuts))
        level = level * jnp.repeat(jnp.exp(draws), dims[axis_at] // parts).reshape((-1,) + (1,) * (len(dims) - 1 - axis_at))
    return level


def scatter_about(own_key, shape, scale, reach, pieces=(), held_as=jnp.bfloat16):
    entries = scale * jax.random.normal(own_key, shape, jnp.float32)
    if pieces:
        entries = entries * level_of(own_key, shape, pieces, -0.22, 0.18)
    return jnp.clip(entries, -reach, reach).astype(held_as)


def setup_inputs(seed: int = 0) -> dict:
    splits = jax.random.split(jax.random.key(seed), 17)
    return {
        "tokens": scatter_about(splits[0], (D, TOKENS), 1.0, 6.0, ((0, 4), (1, 8))),
        "seq_lengths": draw_seq_lengths(jax.random.fold_in(splits[16], 71), 0),
        "norm1_gain": jnp.clip(1.0 + 0.1 * jax.random.normal(splits[2], (D,), jnp.float32), 0.5, 1.5),
        "norm1_bias": scatter_about(splits[3], (D,), 0.3, 4.0, ((0, 4),), jnp.float32),
        "value_weight": scatter_about(splits[4], (D, D), D ** -0.5, 0.21875, ((0, 8), (1, 4))),
        "value_bias": scatter_about(splits[5], (D,), 0.1, 1.5, ((0, 4),), jnp.float32),
        "synth_logits": scatter_about(splits[6], (SEQ_LEN, HEADS, SEQ_LEN), 2.0, 8.0, ((0, 8), (1, 4))),
        "out_weight": scatter_about(splits[7], (D, D), (D // 32) ** -0.5, 1.25, ((0, 4), (1, 8))),
        "out_bias": scatter_about(splits[8], (D,), 0.3, 4.0, ((0, 4),), jnp.float32),
        "norm2_gain": jnp.clip(1.0 + 0.1 * jax.random.normal(splits[9], (D,), jnp.float32), 0.5, 1.5),
        "norm2_bias": scatter_about(splits[10], (D,), 0.3, 4.0, ((0, 4),), jnp.float32),
        "up_weight": scatter_about(splits[11], (D, FF), D ** -0.5, 0.21875, ((0, 4), (1, 8))),
        "up_bias": scatter_about(splits[12], (FF,), 0.3, 4.0, ((0, 4),), jnp.float32),
        "down_weight": scatter_about(splits[13], (FF, D), FF ** -0.5, 0.109375, ((0, 8), (1, 4))),
        "down_bias": scatter_about(splits[14], (D,), 0.3, 4.0, ((0, 4),), jnp.float32),
        "cotangent": scatter_about(splits[15], (D, TOKENS), 1.0, 6.0, ((0, 4), (1, 8))),
    }


EPSILON = 1e-05
NEGATIVE = -1e+30
HIGHEST = lax.Precision.HIGHEST

@jax.custom_vjp
def low(v):
    return lax.optimization_barrier(v.astype(jnp.bfloat16)).astype(jnp.float32)

@jax.custom_vjp
def low_back(v):
    return v

def low_keep(v):
    return (low(v), None)

def low_pass(kept, grad):
    return (grad,)

def back_keep(v):
    return (v, None)

def back_low(kept, grad):
    return (low(grad),)
low.defvjp(low_keep, low_pass)
low_back.defvjp(back_keep, back_low)

def layer_norm(inputs, norm_gain, norm_bias):
    row_mean = lax.optimization_barrier(jnp.mean(inputs, axis=-1, keepdims=True))
    centred = inputs - row_mean
    variance = lax.optimization_barrier(jnp.mean(centred * centred, axis=-1, keepdims=True))
    return centred * lax.rsqrt(variance + EPSILON) * norm_gain + norm_bias

def mix_sequence(logits, seq_values, length):
    positions = jnp.arange(SEQ_LEN)
    key_valid = positions[None, None, :] < length
    scores = jnp.where(key_valid, logits, NEGATIVE)
    probs_low = low(jax.nn.softmax(scores, axis=-1))
    head_values = seq_values.reshape(SEQ_LEN, HEADS, HEAD_DIM)
    mixed_rows = jnp.einsum('qhk,khd->qhd', probs_low, head_values, precision=HIGHEST)
    query_valid = (positions < length).astype(mixed_rows.dtype)
    return (mixed_rows * query_valid[:, None, None]).reshape(SEQ_LEN, D)

def reference(tokens, seq_lengths, norm1_gain, norm1_bias, value_weight, value_bias, synth_logits, out_weight, out_bias, norm2_gain, norm2_bias, up_weight, up_bias, down_weight, down_bias, cotangent):
    mixer = jax.checkpoint(mix_sequence)

    def forward(inputs, gain_one, bias_one, weight_value, bias_value, logits, weight_out, bias_out, gain_two, bias_two, weight_up, bias_up, weight_down, bias_down):
        layer_one = low(layer_norm(inputs, gain_one, bias_one))
        values = low(low_back(jnp.dot(layer_one, weight_value, precision=HIGHEST) + bias_value))
        mixed = lax.map(lambda operands: mixer(logits, operands[0], operands[1]), (values.reshape(SEQS, SEQ_LEN, D), seq_lengths))
        attended = low(low_back(mixed.reshape(TOKENS, D)))
        branch = low_back(jnp.dot(attended, weight_out, precision=HIGHEST) + bias_out)
        resid = inputs + branch
        layer_two = low(layer_norm(resid, gain_two, bias_two))
        upper = low_back(jnp.dot(layer_two, weight_up, precision=HIGHEST) + bias_up)
        hidden = low(jax.nn.gelu(upper))
        feed = low_back(jnp.dot(hidden, weight_down, precision=HIGHEST) + bias_down)
        return resid + feed
    params = (tokens.astype(jnp.float32).T, norm1_gain, norm1_bias, value_weight.astype(jnp.float32), value_bias, synth_logits.astype(jnp.float32), out_weight.astype(jnp.float32), out_bias, norm2_gain, norm2_bias, up_weight.astype(jnp.float32), up_bias, down_weight.astype(jnp.float32), down_bias)
    output, pullback = jax.vjp(forward, *params)
    grads = pullback(cotangent.astype(jnp.float32).T)
    return (output.T.astype(jnp.bfloat16), grads[0].T, grads[1], grads[2], grads[3], grads[4], grads[5], grads[6], grads[7], grads[8], grads[9], grads[10], grads[11], grads[12], grads[13])
```

```python
import jax
import jax.numpy as jnp
from jax import lax
from jax.sharding import PartitionSpec as P

D = 768


EPSILON = 1e-05
ALONG_FEATURES = (((1,), (1,)), ((), ()))
ALONG_ROWS = (((0,), (0,)), ((), ()))


def row_statistics(first_term, second_term):
    return lax.psum((jnp.sum(first_term, axis=1), jnp.sum(second_term, axis=1)), "wa")


def all_features(features_part):
    return lax.all_gather(features_part, "wa", axis=1, tiled=True)


def feature_share(partial_sum):
    return lax.psum_scatter(partial_sum, "wa", scatter_dimension=1, tiled=True)


def norm_forward(inputs, norm_gain, norm_bias):
    row_total, row_squares = row_statistics(inputs, inputs * inputs)
    row_mean = row_total / D
    variance = row_squares / D - row_mean * row_mean
    inverse = lax.rsqrt(variance + EPSILON)
    normed = (inputs - row_mean[:, None]) * inverse[:, None]
    return (normed * norm_gain + norm_bias, normed, inverse)


def norm_backward(incoming, normed, inverse, norm_gain):
    scaled = incoming * norm_gain
    row_total, row_along = row_statistics(scaled, scaled * normed)
    return inverse[:, None] * (scaled - row_total[:, None] / D - normed * row_along[:, None] / D)


def weights_of(logit_rows, length_all):
    seq_len = logit_rows.shape[2]
    key_valid = (jnp.arange(seq_len)[None, :] < length_all[:, None]).astype(jnp.bfloat16)
    terms = jnp.exp(logit_rows.astype(jnp.float32)).astype(jnp.bfloat16)
    sums = jnp.einsum("phk,sk->sph", terms, key_valid, preferred_element_type=jnp.float32)
    return (terms, sums, key_valid)


def attend(terms, sums, value_all, query_rows):
    mixed = jnp.einsum("phk,skhd->sphd", terms, value_all, preferred_element_type=jnp.float32)
    mixed = mixed / sums[..., None]
    return (mixed, (mixed * query_rows[:, :, None, None]).astype(jnp.bfloat16))


def attend_back(terms, sums, key_valid, value_all, mixed, grad_rows):
    along = jnp.sum(grad_rows.astype(jnp.float32) * mixed, axis=-1) / sums
    scaled = (grad_rows.astype(jnp.float32) / sums[..., None]).astype(jnp.bfloat16)
    dvalue_part = jnp.einsum("phk,sphd->skhd", terms, scaled, preferred_element_type=jnp.float32)
    dlogits = jnp.einsum("sphd,skhd->phk", scaled, value_all, preferred_element_type=jnp.float32)
    high = along.astype(jnp.bfloat16)
    rest = (along - high.astype(jnp.float32)).astype(jnp.bfloat16)
    shift = sum(
        jnp.einsum("sph,sk->phk", part, key_valid, preferred_element_type=jnp.float32)
        for part in (high, rest)
    )
    return (dvalue_part, terms.astype(jnp.float32) * (dlogits - shift))


def on_device(
    tokens,
    seq_lengths,
    norm1_gain,
    norm1_bias,
    value_weight,
    value_bias,
    synth_logits,
    out_weight,
    out_bias,
    norm2_gain,
    norm2_bias,
    up_weight,
    up_bias,
    down_weight,
    down_bias,
    cotangent,
):
    rows_dev = tokens.shape[1]
    local_width = tokens.shape[0]
    seq_count = seq_lengths.shape[0]
    seq_len = synth_logits.shape[2]
    head_count = synth_logits.shape[1]
    head_dim = local_width // head_count
    value_cols, out_rows, up_rows, down_cols = (
        lax.all_gather(value_weight, "ta", axis=0, tiled=True),
        lax.all_gather(out_weight, "ta", axis=1, tiled=True),
        lax.all_gather(up_weight, "ta", axis=1, tiled=True),
        lax.all_gather(down_weight, "ta", axis=0, tiled=True),
    )
    up_block, down_block = (
        lax.all_to_all(up_rows.T, "wa", split_axis=0, concat_axis=1, tiled=True),
        lax.all_to_all(down_cols, "wa", split_axis=0, concat_axis=1, tiled=True),
    )
    inputs = tokens.T.astype(jnp.float32)
    pre_one, normed_one, inverse_one = norm_forward(inputs, norm1_gain, norm1_bias)
    layer_one = all_features(pre_one.astype(jnp.bfloat16))
    values = (
        jnp.dot(layer_one, value_cols, preferred_element_type=jnp.float32) + value_bias
    ).astype(jnp.bfloat16)
    value_heads = values.reshape(seq_count, seq_len, head_count, head_dim)
    positions = jnp.arange(seq_len)
    key_valid = positions[None, :] < seq_lengths[:, None]
    query_valid = key_valid.astype(jnp.float32)
    length_all = lax.all_gather(seq_lengths, "ta", axis=0, tiled=True)
    block_rows = synth_logits.shape[0]
    value_all = lax.all_gather(
        value_heads * key_valid[:, :, None, None].astype(jnp.bfloat16), "ta", axis=0, tiled=True
    )
    terms, sums, key_valid_all = weights_of(synth_logits, length_all)
    block_positions = lax.axis_index("ta") * block_rows + jnp.arange(block_rows)
    query_rows = (block_positions[None, :] < length_all[:, None]).astype(jnp.float32)
    mixed_rows, mixed_low = attend(terms, sums, value_all, query_rows)
    attended = lax.all_to_all(mixed_low, "ta", split_axis=0, concat_axis=1, tiled=True)
    attended = attended.reshape(rows_dev, local_width)
    branch = (
        feature_share(jnp.dot(attended, out_rows, preferred_element_type=jnp.float32)) + out_bias
    )
    resid = inputs + branch
    pre_two, normed_two, inverse_two = norm_forward(resid, norm2_gain, norm2_bias)
    layer_two = all_features(pre_two.astype(jnp.bfloat16))
    upper = (
        lax.dot_general(layer_two, up_block, ALONG_FEATURES, preferred_element_type=jnp.float32)
        + up_bias
    )
    hidden, gelu_back = jax.vjp(jax.nn.gelu, upper)
    hidden_low = hidden.astype(jnp.bfloat16)
    feed = (
        feature_share(jnp.dot(hidden_low, down_block, preferred_element_type=jnp.float32))
        + down_bias
    )
    output = (resid + feed).astype(jnp.bfloat16)
    cotangent_rows = cotangent.T
    grad_in = cotangent_rows.astype(jnp.float32)
    grad_full = all_features(cotangent_rows)
    dhidden = lax.dot_general(
        grad_full, down_block, ALONG_FEATURES, preferred_element_type=jnp.float32
    )
    dupper = gelu_back(dhidden)[0].astype(jnp.bfloat16)
    down_part = lax.dot_general(
        hidden_low, grad_full, ALONG_ROWS, preferred_element_type=jnp.float32
    )
    up_part = lax.dot_general(dupper, layer_two, ALONG_ROWS, preferred_element_type=jnp.float32)
    up_bias_part = jnp.sum(dupper.astype(jnp.float32), axis=0)
    down_bias_part = jnp.sum(grad_in, axis=0)
    dlayer_two = feature_share(jnp.dot(dupper, up_block, preferred_element_type=jnp.float32))
    gain_two_part = jnp.sum(dlayer_two * normed_two, axis=0)
    bias_two_part = jnp.sum(dlayer_two, axis=0)
    dresid = grad_in + norm_backward(dlayer_two, normed_two, inverse_two, norm2_gain)
    dbranch = dresid.astype(jnp.bfloat16)
    dbranch_full = all_features(dbranch)
    dattended = lax.dot_general(
        dbranch_full, out_rows, ALONG_FEATURES, preferred_element_type=jnp.float32
    ).astype(jnp.bfloat16)
    out_part = lax.dot_general(
        attended, dbranch_full, ALONG_ROWS, preferred_element_type=jnp.float32
    )
    out_bias_part = jnp.sum(dbranch.astype(jnp.float32), axis=0)
    grad_heads = dattended.reshape(seq_count, seq_len, head_count, head_dim)
    grad_heads = grad_heads * query_valid[:, :, None, None].astype(jnp.bfloat16)
    grad_block = lax.all_to_all(grad_heads, "ta", split_axis=1, concat_axis=0, tiled=True)
    dvalue_part, logits_grad = attend_back(
        terms, sums, key_valid_all, value_all, mixed_rows, grad_block
    )
    dvalue_rows = dvalue_part.astype(jnp.bfloat16).reshape(-1, local_width)
    dvalue_rows = lax.psum_scatter(dvalue_rows, "ta", scatter_dimension=0, tiled=True)
    dvalues = dvalue_rows * query_valid.reshape(rows_dev, 1).astype(jnp.bfloat16)
    value_part = lax.dot_general(layer_one, dvalues, ALONG_ROWS, preferred_element_type=jnp.float32)
    value_bias_part = jnp.sum(dvalues.astype(jnp.float32), axis=0)
    dlayer_one = feature_share(
        lax.dot_general(dvalues, value_cols, ALONG_FEATURES, preferred_element_type=jnp.float32)
    )
    gain_one_part = jnp.sum(dlayer_one * normed_one, axis=0)
    bias_one_part = jnp.sum(dlayer_one, axis=0)
    tokens_grad = dresid + norm_backward(dlayer_one, normed_one, inverse_one, norm1_gain)
    up_back, down_back = (
        lax.all_to_all(up_part, "wa", split_axis=1, concat_axis=0, tiled=True),
        lax.all_to_all(down_part, "wa", split_axis=1, concat_axis=0, tiled=True),
    )
    value_grad, out_grad, up_grad, down_grad = (
        lax.psum_scatter(value_part, "ta", scatter_dimension=0, tiled=True),
        lax.psum_scatter(out_part, "ta", scatter_dimension=1, tiled=True),
        lax.psum_scatter(up_back, "ta", scatter_dimension=0, tiled=True),
        lax.psum_scatter(down_back, "ta", scatter_dimension=0, tiled=True),
    )
    vector_grads = lax.psum(
        (
            gain_one_part,
            bias_one_part,
            value_bias_part,
            out_bias_part,
            gain_two_part,
            bias_two_part,
            up_bias_part,
            down_bias_part,
        ),
        "ta",
    )
    return (
        output.T,
        tokens_grad.T,
        vector_grads[0],
        vector_grads[1],
        value_grad,
        vector_grads[2],
        logits_grad,
        out_grad,
        vector_grads[3],
        vector_grads[4],
        vector_grads[5],
        up_grad.T,
        vector_grads[6],
        down_grad,
        vector_grads[7],
    )


def solution(mesh):
    placed = (
        P("wa", "ta"),
        P("ta"),
        P("wa"),
        P("wa"),
        P("ta", "wa"),
        P("wa"),
        P("ta", "wa", None),
        P("wa", "ta"),
        P("wa"),
        P("wa"),
        P("wa"),
        P("wa", "ta"),
        P("wa"),
        P("ta", "wa"),
        P("wa"),
        P("wa", "ta"),
    )
    return jax.shard_map(
        on_device,
        mesh=mesh,
        in_specs=placed,
        out_specs=(
            P("wa", "ta"),
            P("wa", "ta"),
            P("wa"),
            P("wa"),
            P("ta", "wa"),
            P("wa"),
            P("ta", "wa", None),
            P("wa", "ta"),
            P("wa"),
            P("wa"),
            P("wa"),
            P("wa", "ta"),
            P("wa"),
            P("ta", "wa"),
            P("wa"),
        ),
        check_vma=False,
    )
```

```python
import functools

import jax
import jax.numpy as jnp
from jax import lax
from jax.experimental import pallas as pl
from jax.experimental.pallas import tpu as pltpu
from jax.sharding import PartitionSpec as P

D = 768


EPSILON = 1e-05
ALONG_FEATURES = (((1,), (1,)), ((), ()))
ALONG_ROWS = (((0,), (0,)), ((), ()))


def row_statistics(first_term, second_term):
    return lax.psum((jnp.sum(first_term, axis=1), jnp.sum(second_term, axis=1)), "wa")


def all_features(features_part):
    return lax.all_gather(features_part, "wa", axis=1, tiled=True)


def feature_share(partial_sum):
    return lax.psum_scatter(partial_sum, "wa", scatter_dimension=1, tiled=True)


def norm_forward(inputs, norm_gain, norm_bias):
    row_total, row_squares = row_statistics(inputs, inputs * inputs)
    row_mean = row_total / D
    variance = row_squares / D - row_mean * row_mean
    inverse = lax.rsqrt(variance + EPSILON)
    normed = (inputs - row_mean[:, None]) * inverse[:, None]
    return (normed * norm_gain + norm_bias, normed, inverse)


def norm_backward(incoming, normed, inverse, norm_gain):
    scaled = incoming * norm_gain
    row_total, row_along = row_statistics(scaled, scaled * normed)
    return inverse[:, None] * (scaled - row_total[:, None] / D - normed * row_along[:, None] / D)


def weights_of(logit_rows, length_all):
    seq_len = logit_rows.shape[2]
    key_valid = (jnp.arange(seq_len)[None, :] < length_all[:, None]).astype(jnp.bfloat16)
    terms = jnp.exp(logit_rows.astype(jnp.float32)).astype(jnp.bfloat16)
    sums = jnp.einsum("phk,sk->sph", terms, key_valid, preferred_element_type=jnp.float32)
    return (terms, sums, key_valid)


def attend(terms, sums, value_all, query_rows):
    mixed = jnp.einsum("phk,skhd->sphd", terms, value_all, preferred_element_type=jnp.float32)
    mixed = mixed / sums[..., None]
    return (mixed, (mixed * query_rows[:, :, None, None]).astype(jnp.bfloat16))


def attend_back(terms, sums, key_valid, value_all, mixed, grad_rows):
    along = jnp.sum(grad_rows.astype(jnp.float32) * mixed, axis=-1) / sums
    scaled = (grad_rows.astype(jnp.float32) / sums[..., None]).astype(jnp.bfloat16)
    dvalue_part = jnp.einsum("phk,sphd->skhd", terms, scaled, preferred_element_type=jnp.float32)
    dlogits = jnp.einsum("sphd,skhd->phk", scaled, value_all, preferred_element_type=jnp.float32)
    high = along.astype(jnp.bfloat16)
    rest = (along - high.astype(jnp.float32)).astype(jnp.bfloat16)
    shift = sum(
        jnp.einsum("sph,sk->phk", part, key_valid, preferred_element_type=jnp.float32)
        for part in (high, rest)
    )
    return (dvalue_part, terms.astype(jnp.float32) * (dlogits - shift))


def on_device(
    tokens,
    seq_lengths,
    norm1_gain,
    norm1_bias,
    value_weight,
    value_bias,
    synth_logits,
    out_weight,
    out_bias,
    norm2_gain,
    norm2_bias,
    up_weight,
    up_bias,
    down_weight,
    down_bias,
    cotangent,
):
    rows_dev = tokens.shape[1]
    local_width = tokens.shape[0]
    seq_count = seq_lengths.shape[0]
    seq_len = synth_logits.shape[2]
    head_count = synth_logits.shape[1]
    head_dim = local_width // head_count
    value_cols, out_rows, up_rows, down_cols = (
        lax.all_gather(value_weight, "ta", axis=0, tiled=True),
        lax.all_gather(out_weight, "ta", axis=1, tiled=True),
        lax.all_gather(up_weight, "ta", axis=1, tiled=True),
        lax.all_gather(down_weight, "ta", axis=0, tiled=True),
    )
    up_block, down_block = (
        lax.all_to_all(up_rows.T, "wa", split_axis=0, concat_axis=1, tiled=True),
        lax.all_to_all(down_cols, "wa", split_axis=0, concat_axis=1, tiled=True),
    )
    inputs = tokens.T.astype(jnp.float32)
    pre_one, normed_one, inverse_one = norm_forward(inputs, norm1_gain, norm1_bias)
    layer_one = all_features(pre_one.astype(jnp.bfloat16))
    values = (
        jnp.dot(layer_one, value_cols, preferred_element_type=jnp.float32) + value_bias
    ).astype(jnp.bfloat16)
    value_heads = values.reshape(seq_count, seq_len, head_count, head_dim)
    positions = jnp.arange(seq_len)
    key_valid = positions[None, :] < seq_lengths[:, None]
    query_valid = key_valid.astype(jnp.float32)
    length_all = lax.all_gather(seq_lengths, "ta", axis=0, tiled=True)
    block_rows = synth_logits.shape[0]
    value_all = lax.all_gather(
        value_heads * key_valid[:, :, None, None].astype(jnp.bfloat16), "ta", axis=0, tiled=True
    )
    terms, sums, key_valid_all = weights_of(synth_logits, length_all)
    block_positions = lax.axis_index("ta") * block_rows + jnp.arange(block_rows)
    query_rows = (block_positions[None, :] < length_all[:, None]).astype(jnp.float32)
    mixed_rows, mixed_low = attend(terms, sums, value_all, query_rows)
    attended = lax.all_to_all(mixed_low, "ta", split_axis=0, concat_axis=1, tiled=True)
    attended = attended.reshape(rows_dev, local_width)
    branch = (
        feature_share(jnp.dot(attended, out_rows, preferred_element_type=jnp.float32)) + out_bias
    )
    resid = inputs + branch
    pre_two, normed_two, inverse_two = norm_forward(resid, norm2_gain, norm2_bias)
    layer_two = all_features(pre_two.astype(jnp.bfloat16))
    upper = (
        lax.dot_general(layer_two, up_block, ALONG_FEATURES, preferred_element_type=jnp.float32)
        + up_bias
    )
    hidden, gelu_back = jax.vjp(jax.nn.gelu, upper)
    hidden_low = hidden.astype(jnp.bfloat16)
    feed = (
        feature_share(jnp.dot(hidden_low, down_block, preferred_element_type=jnp.float32))
        + down_bias
    )
    output = (resid + feed).astype(jnp.bfloat16)
    cotangent_rows = cotangent.T
    grad_in = cotangent_rows.astype(jnp.float32)
    grad_full = all_features(cotangent_rows)
    dhidden = lax.dot_general(
        grad_full, down_block, ALONG_FEATURES, preferred_element_type=jnp.float32
    )
    dupper = gelu_back(dhidden)[0].astype(jnp.bfloat16)
    down_part = lax.dot_general(
        hidden_low, grad_full, ALONG_ROWS, preferred_element_type=jnp.float32
    )
    up_part = lax.dot_general(dupper, layer_two, ALONG_ROWS, preferred_element_type=jnp.float32)
    up_bias_part = jnp.sum(dupper.astype(jnp.float32), axis=0)
    down_bias_part = jnp.sum(grad_in, axis=0)
    dlayer_two = feature_share(jnp.dot(dupper, up_block, preferred_element_type=jnp.float32))
    gain_two_part = jnp.sum(dlayer_two * normed_two, axis=0)
    bias_two_part = jnp.sum(dlayer_two, axis=0)
    dresid = grad_in + norm_backward(dlayer_two, normed_two, inverse_two, norm2_gain)
    dbranch = dresid.astype(jnp.bfloat16)
    dbranch_full = all_features(dbranch)
    dattended = lax.dot_general(
        dbranch_full, out_rows, ALONG_FEATURES, preferred_element_type=jnp.float32
    ).astype(jnp.bfloat16)
    out_part = lax.dot_general(
        attended, dbranch_full, ALONG_ROWS, preferred_element_type=jnp.float32
    )
    out_bias_part = jnp.sum(dbranch.astype(jnp.float32), axis=0)
    grad_heads = dattended.reshape(seq_count, seq_len, head_count, head_dim)
    grad_heads = grad_heads * query_valid[:, :, None, None].astype(jnp.bfloat16)
    grad_block = lax.all_to_all(grad_heads, "ta", split_axis=1, concat_axis=0, tiled=True)
    dvalue_part, logits_grad = attend_back(
        terms, sums, key_valid_all, value_all, mixed_rows, grad_block
    )
    dvalue_rows = dvalue_part.astype(jnp.bfloat16).reshape(-1, local_width)
    dvalue_rows = lax.psum_scatter(dvalue_rows, "ta", scatter_dimension=0, tiled=True)
    dvalues = dvalue_rows * query_valid.reshape(rows_dev, 1).astype(jnp.bfloat16)
    value_part = lax.dot_general(layer_one, dvalues, ALONG_ROWS, preferred_element_type=jnp.float32)
    value_bias_part = jnp.sum(dvalues.astype(jnp.float32), axis=0)
    dlayer_one = feature_share(
        lax.dot_general(dvalues, value_cols, ALONG_FEATURES, preferred_element_type=jnp.float32)
    )
    gain_one_part = jnp.sum(dlayer_one * normed_one, axis=0)
    bias_one_part = jnp.sum(dlayer_one, axis=0)
    tokens_grad = dresid + norm_backward(dlayer_one, normed_one, inverse_one, norm1_gain)
    up_back, down_back = (
        lax.all_to_all(up_part, "wa", split_axis=1, concat_axis=0, tiled=True),
        lax.all_to_all(down_part, "wa", split_axis=1, concat_axis=0, tiled=True),
    )
    value_grad, out_grad, up_grad, down_grad = (
        lax.psum_scatter(value_part, "ta", scatter_dimension=0, tiled=True),
        lax.psum_scatter(out_part, "ta", scatter_dimension=1, tiled=True),
        lax.psum_scatter(up_back, "ta", scatter_dimension=0, tiled=True),
        lax.psum_scatter(down_back, "ta", scatter_dimension=0, tiled=True),
    )
    vector_grads = lax.psum(
        (
            gain_one_part,
            bias_one_part,
            value_bias_part,
            out_bias_part,
            gain_two_part,
            bias_two_part,
            up_bias_part,
            down_bias_part,
        ),
        "ta",
    )
    return (
        output.T,
        tokens_grad.T,
        vector_grads[0],
        vector_grads[1],
        value_grad,
        vector_grads[2],
        logits_grad,
        out_grad,
        vector_grads[3],
        vector_grads[4],
        vector_grads[5],
        up_grad.T,
        vector_grads[6],
        down_grad,
        vector_grads[7],
    )


MESH = pl.DeviceIdType.MESH
ROWS_NT = (((1,), (1,)), ((), ()))
ROWS_TN = (((0,), (0,)), ((), ()))
F32 = jnp.float32
BF16 = jnp.bfloat16
VMEM_BYTES = 60 * 2**20
CHUNK = 128
PAD = 128


def whole(count):
    return [pl.BlockSpec(memory_space=pltpu.VMEM)] * count


def anywhere(count):
    return [pl.BlockSpec(memory_space=pl.ANY)] * count


def shape_of(shape, dtype):
    return jax.ShapeDtypeStruct(shape, dtype)


def lanes(start, size=CHUNK):
    return pl.ds(pl.multiple_of(start, CHUNK), size)


def rows_at(start, size, unit):
    return pl.ds(pl.multiple_of(start, unit), size)


class Place:
    def __init__(self, nwa, nta):
        self.nwa, self.nta, self.nz = nwa, nta, nta // 2
        self.wa = lax.axis_index("wa")
        self.ta = lax.axis_index("ta")
        self.z = self.ta // 2
        self.c = self.ta % 2
        self.peer = self.ta + 1 - 2 * self.c
        self.wx = self.wa + 1 - 2 * (self.wa % 2)
        self.wy = (self.wa + 2) % 4
        self.wd = 3 - self.wa

    def enter(self):
        barrier = pltpu.get_barrier_semaphore()
        total = self.nwa * self.nta

        def greet(step, carry):
            w = (self.wa + step // self.nta) % self.nwa
            t = (self.ta + step % self.nta) % self.nta
            pl.semaphore_signal(barrier, inc=1, device_id=(w, t), device_id_type=MESH)
            return carry

        lax.fori_loop(1, total, greet, 0)
        pl.semaphore_wait(barrier, total - 1)


def send(src, dst, ssem, rsem, device):
    return pltpu.make_async_remote_copy(
        src_ref=src,
        dst_ref=dst,
        send_sem=ssem,
        recv_sem=rsem,
        device_id=device,
        device_id_type=MESH,
    )


def when(condition):
    return pl.when(condition)


def norm_stats(block):
    width = block.shape[0]
    mean = jnp.sum(block, axis=0, keepdims=True) / width
    centred = block - mean
    variance = jnp.sum(centred * centred, axis=0, keepdims=True) / width
    inverse = lax.rsqrt(variance + EPSILON)
    return (centred * inverse, inverse)


def forward_kernel(
    dims,
    tok,
    cot,
    wp,
    pcol,
    prow,
    ln,
    logits,
    xown,
    cown,
    attended,
    weights,
    layer_out,
    value_out,
    term_out,
    mixed,
    zinv,
    lens,
    pfull,
    rfull,
    x,
    wvc,
    layer_pad,
    layer,
    value,
    terms,
    attsend,
    sem_tok,
    sem_par,
    sem_ta,
    sem_val,
    sem_w,
    sem_cot,
    sem_att,
    sem_local,
):
    nwa, nta = dims
    me = Place(nwa, nta)
    wa, ta, z, c = me.wa, me.ta, me.z, me.c
    nz = me.nz
    width = tok.shape[0]
    half = width // 2
    seq = tok.shape[1]
    part = seq // nz
    query = seq // nta
    slot = wvc.shape[1] // nta
    wdepth = wvc.shape[0] * nwa // nta
    heads = logits.shape[0]
    hdim = width // heads
    split = wp.shape[1] - PAD
    me.enter()
    done = []

    def block_rows(w, off=0, size=width):
        return rows_at(w * width + off, size, 32)

    def tok_copy(k, q):
        device = (me.wx if k == 0 else me.wy, ta)
        return send(
            tok.at[:, pl.ds(q * part, part)],
            x.at[block_rows(wa), pl.ds(q * part, part)],
            sem_tok.at[0, k, q],
            sem_tok.at[1, k, q],
            device,
        )

    def tok_fwd(k, q):
        source = me.wx if k == 0 else me.wy
        device = (me.wy if k == 0 else me.wx, ta)
        where = x.at[block_rows(source, k * half, half), pl.ds(q * part, part)]
        return send(where, where, sem_tok.at[0, 2 + k, q], sem_tok.at[1, 2 + k, q], device)

    own_x = pltpu.make_async_copy(tok, x.at[block_rows(wa)], sem_local.at[0])
    own_x.start()
    for q in range(nz):
        for k in range(2):
            tok_copy(k, q).start()

    def par_copy(step, what):
        w = (wa + step) % nwa
        if what == 0:
            src, dst = pcol, pfull.at[block_rows(wa)]
        else:
            src, dst = prow, rfull.at[:, lanes(wa * prow.shape[1], prow.shape[1])]
        return send(src, dst, sem_par.at[0, what, step], sem_par.at[1, what, step], (w, ta))

    def ta_copy(step, what):
        t = (ta + step) % nta
        if what == 0:
            src, dst = wp.at[:, pl.ds(split, PAD)], wvc.at[:, lanes(ta * slot)]
        else:
            src, dst = ln, lens.at[rows_at(ta * 8, 8, 8)]
        return send(src, dst, sem_ta.at[0, what, step], sem_ta.at[1, what, step], (wa, t))

    for step in range(1, nta):
        ta_copy(step, 0).start()
        ta_copy(step, 1).start()
    for step in range(1, nwa):
        par_copy(step, 0).start()
        par_copy(step, 1).start()
    own_wv = pltpu.make_async_copy(
        wp.at[:, pl.ds(split, PAD)], wvc.at[:, lanes(ta * slot)], sem_local.at[1]
    )
    own_wv.start()
    pfull[block_rows(wa), :] = pcol[...]
    rfull[:, lanes(wa * prow.shape[1], prow.shape[1])] = prow[...]
    lens[rows_at(ta * 8, 8, 8), :] = ln[...]

    own_w = pltpu.make_async_copy(wp, weights.at[wa, ta], sem_local.at[2])
    own_w.start()

    def w_line(up, b, own):
        t = 2 * b + c
        where = weights.at[wa, t]
        k = 0 if up else 1
        return send(
            wp if own else where,
            where,
            sem_w.at[0, k, b],
            sem_w.at[1, k, b],
            (wa, ta + 2 if up else ta - 2),
        )

    @pl.when(z < nz - 1)
    def _():
        w_line(True, z, True).start()

    @pl.when(z > 0)
    def _():
        w_line(False, z, True).start()

    layer_pad[...] = jnp.zeros_like(layer_pad)
    for h in range(heads):
        terms[h] = jnp.exp(logits[h].astype(F32)).astype(BF16)
    out_terms = pltpu.make_async_copy(terms, term_out, sem_local.at[3])
    out_terms.start()

    own_wv.wait()
    for step in range(1, nta):
        ta_copy(step, 0).wait_recv()
        ta_copy(step, 1).wait_recv()
    for step in range(1, nwa):
        par_copy(step, 0).wait_recv()
        par_copy(step, 1).wait_recv()
    own_x.wait()

    positions = lax.broadcasted_iota(jnp.int32, (nta * 8, seq), 1).astype(F32)
    key_valid = jnp.where(positions < lens[:, 0:1], 1.0, 0.0).astype(BF16)
    for h in range(heads):
        sums = lax.dot_general(key_valid, terms[h], ROWS_NT, preferred_element_type=F32)
        zinv[h] = 1.0 / sums

    def value_copy(kind, b, q, core):
        where = value.at[2 * b + core, :, pl.ds(q * part, part)]
        t = (ta + 2, ta - 2, me.peer)[kind]
        return send(where, where, sem_val.at[0, kind, b, q], sem_val.at[1, kind, b, q], (wa, t))

    def w_hop(h):
        @pl.when(z - 1 - h >= 0)
        def _():
            w_line(True, z - 1 - h, False).wait_recv()

            @pl.when(z < nz - 1)
            def _():
                w_line(True, z - 1 - h, False).start()

        @pl.when(z + 1 + h < nz)
        def _():
            w_line(False, z + 1 + h, False).wait_recv()

            @pl.when(z > 0)
            def _():
                w_line(False, z + 1 + h, False).start()

    for q in range(nz):
        cols = pl.ds(q * part, part)
        for k in range(2):
            tok_copy(k, q).wait_recv()
            tok_fwd(k, q).start()
        for k in range(2):
            where = x.at[block_rows(me.wd, k * half, half), cols]
            send(
                where,
                where,
                sem_tok.at[0, 2 + k, q],
                sem_tok.at[1, 2 + k, q],
                (me.wy if k == 0 else me.wx, ta),
            ).wait_recv()
        normed, _ = norm_stats(x[:, cols].astype(F32))
        low = (normed * pfull[:, 0:1] + pfull[:, 1:2]).astype(BF16)
        layer[:, cols] = low
        for t in range(nta):
            layer_pad[t * slot : t * slot + wdepth, :] = low[t * wdepth : (t + 1) * wdepth]
        made = jnp.dot(wvc[...], layer_pad[...], preferred_element_type=F32) + pcol[:, 2:3]
        place = lax.broadcasted_iota(jnp.int32, (width, part), 1) + q * part
        made = jnp.where(place.astype(F32) < ln[0:1, 0:1], made, 0.0)
        value[ta, :, cols] = made.astype(BF16)
        xown[:, pl.ds(q * CHUNK, CHUNK)] = x[:, lanes(q * part + wa * CHUNK)]

        @pl.when(z < nz - 1)
        def _():
            value_copy(0, z, q, c).start()

        @pl.when(z > 0)
        def _():
            value_copy(1, z, q, c).start()

        value_copy(2, z, q, c).start()
        if q >= 1 and q - 1 < nz - 1:
            w_hop(q - 1)
    out_layer = pltpu.make_async_copy(layer, layer_out, sem_local.at[4])
    out_layer.start()

    def cot_copy(step, q):
        w = (wa + step) % nwa
        return send(
            cot.at[:, lanes(q * part + w * CHUNK)],
            cown.at[block_rows(wa), pl.ds(q * CHUNK, CHUNK)],
            sem_cot.at[0, step, q],
            sem_cot.at[1, step, q],
            (w, ta),
        )

    def cot_own(q):
        return pltpu.make_async_copy(
            cot.at[:, lanes(q * part + wa * CHUNK)],
            cown.at[block_rows(wa), pl.ds(q * CHUNK, CHUNK)],
            sem_cot.at[0, 0, q],
        )

    own_w.wait()

    def w_plane(k, b):
        device = (me.wx if k == 0 else me.wy, ta)
        where = weights.at[wa, 2 * b + c]
        return send(where, where, sem_w.at[0, 2 + k, b], sem_w.at[1, 2 + k, b], device)

    def w_diag(k, b, source):
        device = (me.wy if k == 0 else me.wx, ta)
        where = weights.at[source, 2 * b + c, pl.ds(k * half, half)]
        return send(where, where, sem_w.at[0, 4 + k, b], sem_w.at[1, 4 + k, b], device)

    def w_core(r, b, core):
        source = (wa, me.wx, me.wy, me.wd)[r]
        where = weights.at[source, 2 * b + core]
        return send(where, where, sem_w.at[0, 6 + r, b], sem_w.at[1, 6 + r, b], (wa, me.peer))

    for b in range(nz):
        w_plane(0, b).start()
        w_plane(1, b).start()
        w_core(0, b, c).start()
    for q in range(nz):
        cot_own(q).start()
        for step in range(1, nwa):
            cot_copy(step, q).start()

    def w_forward(b):
        w_plane(0, b).wait_recv()
        w_diag(0, b, me.wx).start()
        w_core(1, b, c).start()
        w_plane(1, b).wait_recv()
        w_diag(1, b, me.wy).start()
        w_core(2, b, c).start()

    def w_finish(b):
        for k in range(2):
            w_diag(k, b, me.wd).wait_recv()
        w_core(3, b, c).start()

    def att_copy(s, j):
        return send(
            attsend.at[s, :, pl.ds(j * CHUNK, CHUNK)],
            attended.at[block_rows(wa), lanes(z * CHUNK)],
            sem_att.at[0, s, j],
            sem_att.at[1, wa, z],
            (2 * c + j, s),
        )

    def att_local(s, j):
        return pltpu.make_async_copy(
            attsend.at[s, :, pl.ds(j * CHUNK, CHUNK)],
            attended.at[block_rows(wa), lanes(z * CHUNK)],
            sem_att.at[0, s, j],
        )

    def is_self(s, j):
        return jnp.logical_and(s == ta, 2 * c + j == wa)

    def mix(b):
        for core in range(2):
            s = 2 * b + core
            out_value = pltpu.make_async_copy(value.at[s], value_out.at[s], sem_local.at[6 + core])
            out_value.start()
        length = [lens[rows_at((2 * b + core) * 8, 8, 8), :][0:1, 0:1] for core in range(2)]
        place = lax.broadcasted_iota(jnp.int32, (hdim, query), 1) + ta * query
        place = place.astype(F32)
        for h in range(heads):
            group = slice(h * hdim, (h + 1) * hdim)
            pair = jnp.concatenate([value[2 * b, group, :], value[2 * b + 1, group, :]], axis=0)
            both = lax.dot_general(pair, terms[h], ROWS_NT, preferred_element_type=F32)
            for core in range(2):
                s = 2 * b + core
                inverse = zinv[h, rows_at(s * 8, 8, 8), :][0:1]
                one = both[core * hdim : (core + 1) * hdim] * inverse
                mixed[s, group, :] = one
                one = jnp.where(place < length[core], one, 0.0)
                attsend[s, group, :] = one.astype(BF16)
        for core in range(2):
            s = 2 * b + core
            for j in range(2):

                @pl.when(is_self(s, j))
                def _():
                    att_local(s, j).start()

                @pl.when(jnp.logical_not(is_self(s, j)))
                def _():
                    att_copy(s, j).start()

            pltpu.make_async_copy(value.at[s], value_out.at[s], sem_local.at[6 + core]).wait()

    def core_ready(b):
        for q in range(nz):
            value_copy(2, b, q, 1 - c).wait_recv()

    for h in range(nz - 1):
        below, above = z - 1 - h, z + 1 + h
        for q in range(nz):

            @pl.when(below >= 0)
            def _():
                value_copy(0, below, q, c).wait_recv()

                @pl.when(z < nz - 1)
                def _():
                    value_copy(0, below, q, c).start()

                value_copy(2, below, q, c).start()

            @pl.when(above < nz)
            def _():
                value_copy(1, above, q, c).wait_recv()

                @pl.when(z > 0)
                def _():
                    value_copy(1, above, q, c).start()

                value_copy(2, above, q, c).start()

        if h == 0:
            core_ready(z)
            mix(z)

        @pl.when(below >= 0)
        def _():
            core_ready(below)
            mix(below)

        @pl.when(above < nz)
        def _():
            core_ready(above)
            mix(above)

        w_forward(h)
    for b in range(nz - 1, nz):
        w_forward(b)
    for b in range(nz):
        w_finish(b)

    for step in range(1, nta):
        ta_copy(step, 0).wait_send()
        ta_copy(step, 1).wait_send()
    for step in range(1, nwa):
        par_copy(step, 0).wait_send()
        par_copy(step, 1).wait_send()
        for q in range(nz):
            cot_copy(step, q).wait_send()
    for q in range(nz):
        cot_own(q).wait()
        for k in range(2):
            tok_copy(k, q).wait_send()
            tok_fwd(k, q).wait_send()
    for step in range(1, nwa):
        for q in range(nz):
            cot_copy(step, q).wait_recv()

    def line_sends(b, carry):
        reach_up = jnp.logical_and(b <= z, z < nz - 1)
        reach_down = jnp.logical_and(b >= z, z > 0)

        @pl.when(reach_up)
        def _():
            w_line(True, b, False).wait_send()
            for q in range(nz):
                value_copy(0, b, q, c).wait_send()

        @pl.when(reach_down)
        def _():
            w_line(False, b, False).wait_send()
            for q in range(nz):
                value_copy(1, b, q, c).wait_send()

        for q in range(nz):
            value_copy(2, b, q, c).wait_send()
        for k in range(2):
            w_plane(k, b).wait_send()
        w_diag(0, b, me.wx).wait_send()
        w_diag(1, b, me.wy).wait_send()
        for r in range(4):
            w_core(r, b, c).wait_send()
            w_core(r, b, 1 - c).wait_recv()
        return carry

    lax.fori_loop(0, nz, line_sends, 0)

    def att_sends(s, carry):
        for j in range(2):

            @pl.when(is_self(s, j))
            def _():
                att_local(s, j).wait()

            @pl.when(jnp.logical_not(is_self(s, j)))
            def _():
                att_copy(s, j).wait_send()

        return carry

    lax.fori_loop(0, nta, att_sends, 0)
    mine = wa // 2

    def att_arrivals(k, carry):
        w, b = k // nz, k % nz

        @pl.when(jnp.logical_not(jnp.logical_and(w == wa, 2 * b + mine == ta)))
        def _():
            where = attended.at[block_rows(w), lanes(b * CHUNK)]
            send(where, where, sem_att.at[0, 0, 0], sem_att.at[1, w, b], (w, 2 * b + mine)).wait_recv()

        return carry

    lax.fori_loop(0, nwa * nz, att_arrivals, 0)
    out_terms.wait()
    out_layer.wait()


def run_forward(dims, tok, cot, wp, pcol, prow, ln, logits):
    nwa, nta = dims
    nz = nta // 2
    width, seq = tok.shape
    depth = width * nwa
    own = seq // nwa
    heads, query, _ = logits.shape
    slot = PAD
    dma = pltpu.SemaphoreType.DMA
    return pl.pallas_call(
        functools.partial(forward_kernel, dims),
        out_shape=(
            shape_of((depth, own), BF16),
            shape_of((depth, own), BF16),
            shape_of((depth, own), BF16),
            shape_of((nwa, nta) + wp.shape, BF16),
            shape_of((depth, seq), BF16),
            shape_of((nta, width, seq), BF16),
            shape_of((heads, query, seq), BF16),
            shape_of((nta, width, query), F32),
            shape_of((heads, nta * 8, query), F32),
            shape_of((nta * 8, CHUNK), F32),
            shape_of((depth, pcol.shape[1]), F32),
            shape_of((8, prow.shape[1] * nwa), F32),
        ),
        in_specs=anywhere(3) + whole(4),
        out_specs=tuple(whole(3) + anywhere(4) + whole(5)),
        scratch_shapes=[
            pltpu.VMEM((depth, seq), BF16),
            pltpu.VMEM((width, nta * slot), BF16),
            pltpu.VMEM((nta * slot, seq // nz), BF16),
            pltpu.VMEM((depth, seq), BF16),
            pltpu.VMEM((nta, width, seq), BF16),
            pltpu.VMEM((heads, query, seq), BF16),
            pltpu.VMEM((nta, width, query), BF16),
            dma((2, 4, nz)),
            dma((2, 2, nwa)),
            dma((2, 2, nta)),
            dma((2, 3, nz, nz)),
            dma((2, 10, nz)),
            dma((2, nwa, nz)),
            dma((2, nta, max(nz, 2))),
            dma((8,)),
        ],
        compiler_params=pltpu.CompilerParams(
            collective_id=1, has_side_effects=True, vmem_limit_bytes=VMEM_BYTES
        ),
        cost_estimate=pl.CostEstimate(
            flops=4 * 10**9, bytes_accessed=60 * 10**6, transcendentals=2 * 10**6
        ),
    )(tok, cot, wp, pcol, prow, ln, logits)


def gelu_pair(u):
    root = 0.7978845608028654
    square = u * u
    bent = jnp.tanh(root * u * (1.0 + 0.044715 * square))
    low_half = 0.5 * (1.0 + bent)
    slope = low_half + 0.5 * u * (1.0 - bent * bent) * root * (1.0 + 3.0 * 0.044715 * square)
    return (u * low_half, slope)


def middle_kernel(
    dims,
    attended,
    xown,
    cown,
    pfull,
    rfull,
    ln,
    block,
    wo,
    out,
    dattended,
    dresid,
    gblock,
    gwo,
    vcol,
    vrow,
    resid,
    normed,
    inverse,
    layer,
    layer_t,
    grad_t,
    feed,
    dlayer,
    wide,
):
    nwa, nta = dims
    step = pl.program_id(0)
    wa = lax.axis_index("wa")
    depth, own = xown.shape
    width = depth // nwa
    cols = block.shape[3] // 2
    wdepth = depth // nta
    up = block[:, 0, :, :cols].reshape(depth, cols)
    down_t = block[:, 0, :, cols:].reshape(depth, cols)

    def wide_wo():
        joined = [
            jnp.concatenate([wo[w, t] for t in range(nta)], axis=1) for w in range(nwa)
        ]
        return jnp.concatenate(joined, axis=0)

    @pl.when(step == 0)
    def _():
        branch = lax.dot_general(wide_wo(), attended[...], ROWS_TN, preferred_element_type=F32)
        branch = jnp.concatenate(
            [branch[t * PAD : t * PAD + wdepth] for t in range(nta)], axis=0
        )
        res = xown[...].astype(F32) + branch + pfull[:, 3:4]
        resid[...] = res
        norm, inv = norm_stats(res)
        normed[...] = norm
        inverse[...] = jnp.broadcast_to(inv, inverse.shape)
        low = (norm * pfull[:, 4:5] + pfull[:, 5:6]).astype(BF16)
        layer[...] = low
        layer_t[...] = low.T
        grad_t[...] = cown[...].T
        feed[...] = jnp.zeros_like(feed)
        dlayer[...] = jnp.zeros_like(dlayer)

    at = lanes(step * cols, cols)
    upper = jnp.dot(layer_t[...], up, preferred_element_type=F32) + rfull[0:1, at]
    hidden, slope = gelu_pair(upper)
    hidden = hidden.astype(BF16)
    dhidden = jnp.dot(grad_t[...], down_t, preferred_element_type=F32)
    dupper = (dhidden * slope).astype(BF16)
    vrow[:, at] = jnp.broadcast_to(
        jnp.sum(dupper.astype(F32), axis=0, keepdims=True), (vrow.shape[0], cols)
    )
    feed[...] += lax.dot_general(down_t, hidden, ROWS_NT, preferred_element_type=F32)
    dlayer[...] += lax.dot_general(up, dupper, ROWS_NT, preferred_element_type=F32)
    gup = jnp.dot(layer[...], dupper, preferred_element_type=F32)
    gdown = jnp.dot(cown[...], hidden, preferred_element_type=F32)
    gblock[:, 0, :, :cols] = gup.reshape(nwa, width, cols).astype(BF16)
    gblock[:, 0, :, cols:] = gdown.reshape(nwa, width, cols).astype(BF16)

    @pl.when(step == pl.num_programs(0) - 1)
    def _():
        grad = cown[...].astype(F32)
        out[...] = (resid[...] + feed[...] + pfull[:, 6:7]).astype(BF16)
        dl = dlayer[...]
        norm = normed[...]
        e = dl * pfull[:, 4:5]
        mean_e = jnp.sum(e, axis=0, keepdims=True) / depth
        mean_n = jnp.sum(e * norm, axis=0, keepdims=True) / depth
        dres = grad + inverse[0:1, :] * (e - mean_e - norm * mean_n)
        dresid[...] = dres
        low = dres.astype(BF16)
        vcol[...] = jnp.zeros_like(vcol)
        vcol[:, 3:4] = jnp.sum(low.astype(F32), axis=1, keepdims=True)
        vcol[:, 4:5] = jnp.sum(dl * norm, axis=1, keepdims=True)
        vcol[:, 5:6] = jnp.sum(dl, axis=1, keepdims=True)
        vcol[:, 6:7] = jnp.sum(grad, axis=1, keepdims=True)
        wide[...] = jnp.zeros_like(wide)
        for t in range(nta):
            wide[t * PAD : t * PAD + wdepth, :] = low[t * wdepth : (t + 1) * wdepth]
        da = jnp.dot(wide_wo(), wide[...], preferred_element_type=F32)
        lane = lax.broadcasted_iota(jnp.int32, (depth, own), 1)
        place = (lane // CHUNK) * (CHUNK * nwa) + lane % CHUNK + wa * CHUNK
        da = jnp.where(place.astype(F32) < ln[0:1, 0:1], da, 0.0)
        dattended[...] = da.astype(BF16)
        made = lax.dot_general(attended[...], wide[...], ROWS_NT, preferred_element_type=F32)
        for t in range(nta):
            gwo[:, t] = made[:, t * PAD : (t + 1) * PAD].reshape(nwa, width, PAD).astype(BF16)


def run_middle(dims, attended, xown, cown, pfull, rfull, ln, weights):
    nwa, nta = dims
    depth, own = xown.shape
    width = weights.shape[2]
    both = weights.shape[3] - 2 * PAD
    hidden = both // 2 * nta

    def full(shape):
        return pl.BlockSpec(shape, lambda i: (0,) * len(shape))

    block = pl.BlockSpec((nwa, 1, width, both), lambda i: (0, i, 0, 0))
    wo = pl.BlockSpec((nwa, nta, width, PAD), lambda i: (0, 0, 0, both // PAD))
    return pl.pallas_call(
        functools.partial(middle_kernel, dims),
        grid=(nta,),
        out_shape=(
            shape_of((depth, own), BF16),
            shape_of((depth, own), BF16),
            shape_of((depth, own), F32),
            shape_of((nwa, nta, width, both), BF16),
            shape_of((nwa, nta, width, PAD), BF16),
            shape_of((depth, PAD), F32),
            shape_of((8, hidden), F32),
        ),
        in_specs=[
            full((depth, own)),
            full((depth, own)),
            full((depth, own)),
            full(pfull.shape),
            full(rfull.shape),
            full(ln.shape),
            block,
            wo,
        ],
        out_specs=(
            full((depth, own)),
            full((depth, own)),
            full((depth, own)),
            block,
            full((nwa, nta, width, PAD)),
            full((depth, PAD)),
            full((8, hidden)),
        ),
        scratch_shapes=[
            pltpu.VMEM((depth, own), F32),
            pltpu.VMEM((depth, own), F32),
            pltpu.VMEM((8, own), F32),
            pltpu.VMEM((depth, own), BF16),
            pltpu.VMEM((own, depth), BF16),
            pltpu.VMEM((own, depth), BF16),
            pltpu.VMEM((depth, own), F32),
            pltpu.VMEM((depth, own), F32),
            pltpu.VMEM((nta * PAD, own), BF16),
        ],
        compiler_params=pltpu.CompilerParams(vmem_limit_bytes=VMEM_BYTES),
        cost_estimate=pl.CostEstimate(
            flops=17 * 10**9, bytes_accessed=40 * 10**6, transcendentals=2 * 10**6
        ),
    )(attended, xown, cown, pfull, rfull, ln, weights, weights)


def backward_kernel(
    dims,
    dattended,
    outown,
    dresid,
    xown,
    terms,
    mixed,
    zinv,
    lens,
    ln,
    pfull,
    layer,
    weights,
    vcol,
    vrow,
    scaled,
    shift,
    output,
    tgrad,
    vgrad,
    vectors,
    da,
    partial,
    paired,
    up_in,
    up_out,
    down_in,
    down_out,
    dvalue,
    dvown,
    wv,
    vsend,
    vrecv,
    tsend,
    csend,
    crecv,
    csum,
    crecv2,
    sem_da,
    sem_out,
    sem_core,
    sem_line,
    sem_dv,
    sem_tg,
    sem_v,
    sem_c,
    sem_c2,
    sem_local,
):
    nwa, nta = dims
    me = Place(nwa, nta)
    wa, ta, z, c = me.wa, me.ta, me.z, me.c
    nz = me.nz
    depth, own = dresid.shape
    width = depth // nwa
    wdepth = depth // nta
    heads, query, seq = terms.shape
    hdim = width // heads
    part = seq // nz
    me.enter()

    def block_rows(w):
        return rows_at(w * width, width, 32)

    def da_copy(w, b, local):
        core = wa // 2
        src = dattended.at[block_rows(w), lanes(b * CHUNK)]
        dst = da.at[ta, :, lanes((wa % 2) * CHUNK)]
        if local:
            return pltpu.make_async_copy(src, dst, sem_da.at[0, w, b])
        return send(src, dst, sem_da.at[0, w, b], sem_da.at[1, ta, wa % 2], (w, 2 * b + core))

    def da_self(w, b):
        return jnp.logical_and(w == wa, 2 * b + wa // 2 == ta)

    def da_start(k, carry):
        w, b = (wa + k // nz) % nwa, k % nz

        @pl.when(da_self(w, b))
        def _():
            da_copy(w, b, True).start()

        @pl.when(jnp.logical_not(da_self(w, b)))
        def _():
            da_copy(w, b, False).start()

        return carry

    lax.fori_loop(0, nwa * nz, da_start, 0)

    def back_copy(src, dst, sems, step, q):
        w = (wa + step) % nwa
        return send(
            src.at[block_rows(w), pl.ds(q * CHUNK, CHUNK)],
            dst.at[:, lanes(q * part + wa * CHUNK)],
            sems.at[0, step, q],
            sems.at[1, step, q],
            (w, ta),
        )

    def back_own(src, dst, sems, q):
        return pltpu.make_async_copy(
            src.at[block_rows(wa), pl.ds(q * CHUNK, CHUNK)],
            dst.at[:, lanes(q * part + wa * CHUNK)],
            sems.at[0, 0, q],
        )

    for q in range(nz):
        back_own(outown, output, sem_out, q).start()
        for step in range(1, nwa):
            back_copy(outown, output, sem_out, step, q).start()
    get_wv = pltpu.make_async_copy(
        weights.at[:, :, :, pl.ds(weights.shape[3] - PAD, PAD)], wv, sem_local.at[0]
    )
    get_wv.start()

    def da_arrive(k, carry):
        s, j = k // 2, k % 2
        own_piece = jnp.logical_and(s == ta, 2 * c + j == wa)
        where = da.at[s, :, lanes(j * CHUNK)]

        @pl.when(jnp.logical_not(own_piece))
        def _():
            send(where, where, sem_da.at[0, 0, 0], sem_da.at[1, s, j], (2 * c + j, s)).wait_recv()

        return carry

    def da_sent(k, carry):
        w, b = (wa + k // nz) % nwa, k % nz

        @pl.when(da_self(w, b))
        def _():
            da_copy(w, b, True).wait()

        @pl.when(jnp.logical_not(da_self(w, b)))
        def _():
            da_copy(w, b, False).wait_send()

        return carry

    lax.fori_loop(0, nwa * nz, da_sent, 0)
    lax.fori_loop(0, 2 * nta, da_arrive, 0)

    for h in range(heads):
        group = slice(h * hdim, (h + 1) * hdim)
        for s in range(nta):
            one = da[s, group, :].astype(F32)
            inv = zinv[h, s * 8 : s * 8 + 1, :]
            along = jnp.sum(one * mixed[s, group, :], axis=0, keepdims=True)
            shift[h, s * 8 : (s + 1) * 8, :] = jnp.broadcast_to(along * inv, (8, query))
            scaled[s, group, :] = (one * inv).astype(BF16)
    for h in range(heads):
        group = slice(h * hdim, (h + 1) * hdim)
        stacked = jnp.concatenate([scaled[s, group, :] for s in range(nta)], axis=0)
        made = jnp.dot(stacked, terms[h], preferred_element_type=F32).astype(BF16)
        for s in range(nta):
            partial[s, group, :] = made[s * hdim : (s + 1) * hdim]

    def core_copy(b, core):
        return send(
            partial.at[2 * b + core],
            paired.at[b],
            sem_core.at[0, b],
            sem_core.at[1, b],
            (wa, me.peer),
        )

    order = []
    for j in range(nz):
        for b in (nz - 1 - j, j):
            if b not in order:
                order.append(b)
    for b in order:
        core_copy(b, 1 - c).start()

    def line_copy(up, j):
        k = 0 if up else 1
        return send(
            (up_out if up else down_out).at[j],
            (up_in if up else down_in).at[j],
            sem_line.at[0, k, j],
            sem_line.at[1, k, j],
            (wa, ta + 2 if up else ta - 2),
        )

    ready = set()

    def core_ready(b):
        if b not in ready:
            ready.add(b)
            core_copy(b, c).wait_recv()

    def chip_sum(b):
        return partial[2 * b + c].astype(F32) + paired[b].astype(F32)

    for j in range(nz - 1):
        target = nz - 1 - j
        core_ready(target)

        @pl.when(z < target)
        def _():
            @pl.when(z > 0)
            def _():
                line_copy(True, j).wait_recv()
                up_out[j] = (chip_sum(target) + up_in[j].astype(F32)).astype(BF16)

            @pl.when(z == 0)
            def _():
                up_out[j] = chip_sum(target).astype(BF16)

            line_copy(True, j).start()

        core_ready(j)

        @pl.when(z > j)
        def _():
            @pl.when(z < nz - 1)
            def _():
                line_copy(False, j).wait_recv()
                down_out[j] = (chip_sum(j) + down_in[j].astype(F32)).astype(BF16)

            @pl.when(z == nz - 1)
            def _():
                down_out[j] = chip_sum(j).astype(BF16)

            line_copy(False, j).start()

    for b in range(nz):
        core_ready(b)
    place = lax.broadcasted_iota(jnp.int32, (width, seq), 1).astype(F32)
    key_valid = place < ln[0:1, 0:1]

    @pl.when(z == 0)
    def _():
        line_copy(False, 0).wait_recv()
        total = chip_sum(0) + down_in[0].astype(F32)
        dvalue[...] = jnp.where(key_valid, total, 0.0).astype(BF16)

    @pl.when(z == nz - 1)
    def _():
        line_copy(True, 0).wait_recv()
        total = chip_sum(nz - 1) + up_in[0].astype(F32)
        dvalue[...] = jnp.where(key_valid, total, 0.0).astype(BF16)

    for b in range(1, nz - 1):

        @pl.when(z == b)
        def _():
            line_copy(True, nz - 1 - b).wait_recv()
            line_copy(False, b).wait_recv()
            total = chip_sum(b) + up_in[nz - 1 - b].astype(F32) + down_in[b].astype(F32)
            dvalue[...] = jnp.where(key_valid, total, 0.0).astype(BF16)

    def dv_copy(step, q):
        w = (wa + step) % nwa
        return send(
            dvalue.at[:, lanes(q * part + w * CHUNK)],
            dvown.at[block_rows(wa), pl.ds(q * CHUNK, CHUNK)],
            sem_dv.at[0, step, q],
            sem_dv.at[1, step, q],
            (w, ta),
        )

    for q in range(nz):
        for step in range(1, nwa):
            dv_copy(step, q).start()
        dvown[block_rows(wa), q * CHUNK : (q + 1) * CHUNK] = dvalue[
            :, lanes(q * part + wa * CHUNK)
        ]

    vmade = lax.dot_general(layer[...], dvalue[...], ROWS_NT, preferred_element_type=F32)
    vsend[...] = vmade.astype(BF16).reshape(nta, wdepth, width)
    vbias = jnp.sum(dvalue[...].astype(F32), axis=1, keepdims=True)

    def v_copy(step):
        t = (ta + step) % nta
        return send(
            vsend.at[t], vrecv.at[step], sem_v.at[0, step], sem_v.at[1, step], (wa, t)
        )

    for step in range(1, nta):
        v_copy(step).start()

    get_wv.wait()
    for step in range(1, nwa):
        for q in range(nz):
            dv_copy(step, q).wait_recv()
    dl_parts = []
    for t in range(nta):
        turned = jnp.concatenate([wv[w, t] for w in range(nwa)], axis=0)
        dl_parts.append(
            lax.dot_general(turned, dvown[...], ROWS_TN, preferred_element_type=F32)[:wdepth]
        )
    dl = jnp.concatenate(dl_parts, axis=0)
    norm, inv = norm_stats(xown[...].astype(F32))
    e = dl * pfull[:, 0:1]
    mean_e = jnp.sum(e, axis=0, keepdims=True) / depth
    mean_n = jnp.sum(e * norm, axis=0, keepdims=True) / depth
    tsend[...] = (dresid[...] + inv * (e - mean_e - norm * mean_n)).astype(BF16)
    for q in range(nz):
        back_own(tsend, tgrad, sem_tg, q).start()
        for step in range(1, nwa):
            back_copy(tsend, tgrad, sem_tg, step, q).start()

    gain = jnp.sum(dl * norm, axis=1, keepdims=True)
    bias = jnp.sum(dl, axis=1, keepdims=True)
    column = lax.broadcasted_iota(jnp.int32, (depth, PAD), 1)
    cols = jnp.where(column == 0, gain, jnp.where(column == 1, bias, vcol[...]))
    wide = vrow.shape[1] // nwa
    gap = csend.shape[2] - wide
    for w in range(nwa):
        piece = cols[w * width : (w + 1) * width]
        piece = jnp.concatenate([piece, jnp.zeros((gap - width, PAD), F32)], axis=0)
        csend[w, :, :gap] = piece.T[:8]
        csend[w, :, gap:] = vrow[:, w * wide : (w + 1) * wide]

    def c_copy(step):
        w = (wa + step) % nwa
        return send(csend.at[w], crecv.at[step], sem_c.at[0, step], sem_c.at[1, step], (w, ta))

    for step in range(1, nwa):
        c_copy(step).start()
    crecv[0] = csend[wa]
    piece = jnp.concatenate(
        [jnp.broadcast_to(vbias, (width, PAD)), jnp.zeros((gap - width, PAD), F32)], axis=0
    )
    vb_row = jnp.concatenate([piece.T[:8], jnp.zeros((8, wide), F32)], axis=1)
    row = lax.broadcasted_iota(jnp.int32, vb_row.shape, 0)
    total = jnp.where(row == 2, vb_row, 0.0) + crecv[0]
    for step in range(1, nwa):
        c_copy(step).wait_recv()
        total = total + crecv[step]
    csum[...] = total

    def c2_copy(step):
        t = (ta + step) % nta
        return send(csum, crecv2.at[step], sem_c2.at[0, step], sem_c2.at[1, step], (wa, t))

    for step in range(1, nta):
        c2_copy(step).start()
    value_total = vsend[ta].astype(F32)
    for step in range(1, nta):
        v_copy(step).wait_recv()
        value_total = value_total + vrecv[step].astype(F32)
    vgrad[...] = value_total
    crecv2[0] = csum[...]
    for step in range(1, nta):
        c2_copy(step).wait_recv()
    full = jnp.zeros(csum.shape, F32)
    for t in range(nta):
        full = full + crecv2[(ta - t + nta) % nta]
    vectors[...] = full

    for step in range(1, nwa):
        for q in range(nz):
            back_copy(tsend, tgrad, sem_tg, step, q).wait()
            back_copy(outown, output, sem_out, step, q).wait()
            dv_copy(step, q).wait_send()
        c_copy(step).wait_send()
    for q in range(nz):
        back_own(outown, output, sem_out, q).wait()
        back_own(tsend, tgrad, sem_tg, q).wait()
    for step in range(1, nta):
        v_copy(step).wait_send()
        c2_copy(step).wait_send()
    for b in range(nz):
        core_copy(b, 1 - c).wait_send()
    for j in range(nz - 1):

        @pl.when(z < nz - 1 - j)
        def _():
            line_copy(True, j).wait_send()

        @pl.when(z > j)
        def _():
            line_copy(False, j).wait_send()


def run_backward(
    dims, dattended, outown, dresid, xown, terms, mixed, zinv, lens, ln, pfull, layer, weights, vcol, vrow
):
    nwa, nta = dims
    nz = nta // 2
    depth, own = dresid.shape
    width = depth // nwa
    heads, query, seq = terms.shape
    wdepth = depth // nta
    wide = 256 + vrow.shape[1] // nwa
    dma = pltpu.SemaphoreType.DMA
    return pl.pallas_call(
        functools.partial(backward_kernel, dims),
        out_shape=(
            shape_of((nta, width, query), BF16),
            shape_of((heads, nta * 8, query), F32),
            shape_of((width, seq), BF16),
            shape_of((width, seq), BF16),
            shape_of((wdepth, width), F32),
            shape_of((8, wide), F32),
        ),
        in_specs=whole(11) + anywhere(1) + whole(2),
        out_specs=tuple(whole(6)),
        scratch_shapes=[
            pltpu.VMEM((nta, width, query), BF16),
            pltpu.VMEM((nta, width, seq), BF16),
            pltpu.VMEM((nz, width, seq), BF16),
            pltpu.VMEM((nz - 1, width, seq), BF16),
            pltpu.VMEM((nz - 1, width, seq), BF16),
            pltpu.VMEM((nz - 1, width, seq), BF16),
            pltpu.VMEM((nz - 1, width, seq), BF16),
            pltpu.VMEM((width, seq), BF16),
            pltpu.VMEM((depth, own), BF16),
            pltpu.VMEM((nwa, nta, width, PAD), BF16),
            pltpu.VMEM((nta, wdepth, width), BF16),
            pltpu.VMEM((nta, wdepth, width), BF16),
            pltpu.VMEM((depth, own), BF16),
            pltpu.VMEM((nwa, 8, wide), F32),
            pltpu.VMEM((nwa, 8, wide), F32),
            pltpu.VMEM((8, wide), F32),
            pltpu.VMEM((nta, 8, wide), F32),
            dma((2, nta, max(nz, 2))),
            dma((2, nwa, nz)),
            dma((2, nz)),
            dma((2, 2, nz)),
            dma((2, nwa, nz)),
            dma((2, nwa, nz)),
            dma((2, nta)),
            dma((2, nwa)),
            dma((2, nta)),
            dma((2,)),
        ],
        compiler_params=pltpu.CompilerParams(
            collective_id=2, has_side_effects=True, vmem_limit_bytes=VMEM_BYTES
        ),
        cost_estimate=pl.CostEstimate(
            flops=4 * 10**9, bytes_accessed=80 * 10**6, transcendentals=0
        ),
    )(dattended, outown, dresid, xown, terms, mixed, zinv, lens, ln, pfull, layer, weights, vcol, vrow)


def logits_kernel(terms, scaled, value, shift, lens, out):
    nta = scaled.shape[0]
    cols = terms.shape[2]
    stacked = jnp.concatenate([scaled[s] for s in range(nta)], axis=0)
    values = jnp.concatenate([value[s] for s in range(nta)], axis=0)
    made = lax.dot_general(stacked, values, ROWS_TN, preferred_element_type=F32)
    where = (nta * 8, cols)
    place = lax.broadcasted_iota(jnp.int32, where, 1) + pl.program_id(1) * cols
    first = lax.broadcasted_iota(jnp.int32, where, 0) % 8 == 0
    valid = jnp.logical_and(place.astype(F32) < lens[:, 0:1], first)
    valid = jnp.where(valid, 1.0, 0.0).astype(BF16)
    high = shift[0].astype(BF16)
    rest = (shift[0] - high.astype(F32)).astype(BF16)
    made = made - lax.dot_general(high, valid, ROWS_TN, preferred_element_type=F32)
    made = made - lax.dot_general(rest, valid, ROWS_TN, preferred_element_type=F32)
    out[0] = terms[0].astype(F32) * made


def run_logits(terms, scaled, value, shift, lens):
    heads, query, seq = terms.shape
    nta, width, _ = scaled.shape
    hdim = width // heads
    cols = min(1024, seq)
    return pl.pallas_call(
        logits_kernel,
        grid=(heads, seq // cols),
        out_shape=shape_of((heads, query, seq), F32),
        in_specs=[
            pl.BlockSpec((1, query, cols), lambda h, k: (h, 0, k)),
            pl.BlockSpec((nta, hdim, query), lambda h, k: (0, h, 0)),
            pl.BlockSpec((nta, hdim, cols), lambda h, k: (0, h, k)),
            pl.BlockSpec((1, nta * 8, query), lambda h, k: (h, 0, 0)),
            pl.BlockSpec(lens.shape, lambda h, k: (0, 0)),
        ],
        out_specs=pl.BlockSpec((1, query, cols), lambda h, k: (h, 0, k)),
        compiler_params=pltpu.CompilerParams(vmem_limit_bytes=VMEM_BYTES),
        cost_estimate=pl.CostEstimate(
            flops=2 * 10**9, bytes_accessed=16 * 10**6, transcendentals=0
        ),
    )(terms, scaled, value, shift, lens)


def on_device_fast(
    dims,
    tokens,
    seq_lengths,
    norm1_gain,
    norm1_bias,
    value_weight,
    value_bias,
    synth_logits,
    out_weight,
    out_bias,
    norm2_gain,
    norm2_bias,
    up_weight,
    up_bias,
    down_weight,
    down_bias,
    cotangent,
):
    nwa, nta = dims
    width = tokens.shape[0]
    slim = ((0, 0), (0, PAD - out_weight.shape[1]))
    packed = jnp.concatenate(
        [up_weight, down_weight.T, jnp.pad(out_weight, slim), jnp.pad(value_weight.T, slim)], axis=1
    )
    per_feature = (
        norm1_gain,
        norm1_bias,
        value_bias,
        out_bias,
        norm2_gain,
        norm2_bias,
        down_bias,
    )
    pcol = jnp.pad(jnp.stack(per_feature, axis=1), ((0, 0), (0, PAD - len(per_feature))))
    prow = jnp.broadcast_to(up_bias[None, :], (8, up_bias.shape[0]))
    ln = jnp.broadcast_to(seq_lengths.astype(F32)[:, None], (8, CHUNK))
    logits = synth_logits.transpose(1, 0, 2)
    (
        xown,
        cown,
        attended,
        weights,
        layer,
        value,
        terms,
        mixed,
        zinv,
        lens,
        pfull,
        rfull,
    ) = run_forward(dims, tokens, cotangent, packed, pcol, prow, ln, logits)
    outown, dattended, dresid, gblock, gwo, vcol, vrow = run_middle(
        dims, attended, xown, cown, pfull, rfull, ln, weights
    )
    both = gblock.shape[3]
    gblock = lax.psum_scatter(
        gblock.reshape(-1, both), ("wa", "ta"), scatter_dimension=0, tiled=True
    )
    gwo = lax.psum_scatter(gwo.reshape(-1, PAD), ("wa", "ta"), scatter_dimension=0, tiled=True)
    scaled, shift, output, tgrad, vgrad, vectors = run_backward(
        dims,
        dattended,
        outown,
        dresid,
        xown,
        terms,
        mixed,
        zinv,
        lens,
        ln,
        pfull,
        layer,
        weights,
        vcol,
        vrow,
    )
    logits_grad = run_logits(terms, scaled, value, shift, lens)
    cols = both // 2
    gap = vectors.shape[1] - up_bias.shape[0]
    return (
        output,
        tgrad.astype(F32),
        vectors[0, :width],
        vectors[1, :width],
        vgrad,
        vectors[2, :width],
        logits_grad.transpose(1, 0, 2),
        gwo[:, : out_weight.shape[1]].astype(F32),
        vectors[3, :width],
        vectors[4, :width],
        vectors[5, :width],
        gblock[:, :cols].astype(F32),
        vectors[0, gap:],
        gblock[:, cols:].T.astype(F32),
        vectors[6, :width],
    )


def fits(mesh):
    return mesh.shape["wa"] == 4 and mesh.shape["ta"] == 8


def solution(mesh):
    placed = (
        P("wa", "ta"),
        P("ta"),
        P("wa"),
        P("wa"),
        P("ta", "wa"),
        P("wa"),
        P("ta", "wa", None),
        P("wa", "ta"),
        P("wa"),
        P("wa"),
        P("wa"),
        P("wa", "ta"),
        P("wa"),
        P("ta", "wa"),
        P("wa"),
        P("wa", "ta"),
    )
    sizes = (mesh.shape["wa"], mesh.shape["ta"])
    body = functools.partial(on_device_fast, sizes) if fits(mesh) else on_device
    return jax.shard_map(
        body,
        mesh=mesh,
        in_specs=placed,
        out_specs=(
            P("wa", "ta"),
            P("wa", "ta"),
            P("wa"),
            P("wa"),
            P("ta", "wa"),
            P("wa"),
            P("ta", "wa", None),
            P("wa", "ta"),
            P("wa"),
            P("wa"),
            P("wa"),
            P("wa", "ta"),
            P("wa"),
            P("ta", "wa"),
            P("wa"),
        ),
        check_vma=False,
    )
```

```python
import functools

import jax
import jax.numpy as jnp
from jax import lax
from jax.experimental import pallas as pl
from jax.experimental.pallas import tpu as pltpu
from jax.sharding import PartitionSpec as P

D = 768


EPSILON = 1e-05
ALONG_FEATURES = (((1,), (1,)), ((), ()))
ALONG_ROWS = (((0,), (0,)), ((), ()))


def row_statistics(first_term, second_term):
    return lax.psum((jnp.sum(first_term, axis=1), jnp.sum(second_term, axis=1)), "wa")


def all_features(features_part):
    return lax.all_gather(features_part, "wa", axis=1, tiled=True)


def feature_share(partial_sum):
    return lax.psum_scatter(partial_sum, "wa", scatter_dimension=1, tiled=True)


def norm_forward(inputs, norm_gain, norm_bias):
    row_total, row_squares = row_statistics(inputs, inputs * inputs)
    row_mean = row_total / D
    variance = row_squares / D - row_mean * row_mean
    inverse = lax.rsqrt(variance + EPSILON)
    normed = (inputs - row_mean[:, None]) * inverse[:, None]
    return (normed * norm_gain + norm_bias, normed, inverse)


def norm_backward(incoming, normed, inverse, norm_gain):
    scaled = incoming * norm_gain
    row_total, row_along = row_statistics(scaled, scaled * normed)
    return inverse[:, None] * (scaled - row_total[:, None] / D - normed * row_along[:, None] / D)


def weights_of(logit_rows, length_all):
    seq_len = logit_rows.shape[2]
    key_valid = (jnp.arange(seq_len)[None, :] < length_all[:, None]).astype(jnp.bfloat16)
    terms = jnp.exp(logit_rows.astype(jnp.float32)).astype(jnp.bfloat16)
    sums = jnp.einsum("phk,sk->sph", terms, key_valid, preferred_element_type=jnp.float32)
    return (terms, sums, key_valid)


def attend(terms, sums, value_all, query_rows):
    mixed = jnp.einsum("phk,skhd->sphd", terms, value_all, preferred_element_type=jnp.float32)
    mixed = mixed / sums[..., None]
    return (mixed, (mixed * query_rows[:, :, None, None]).astype(jnp.bfloat16))


def attend_back(terms, sums, key_valid, value_all, mixed, grad_rows):
    along = jnp.sum(grad_rows.astype(jnp.float32) * mixed, axis=-1) / sums
    scaled = (grad_rows.astype(jnp.float32) / sums[..., None]).astype(jnp.bfloat16)
    dvalue_part = jnp.einsum("phk,sphd->skhd", terms, scaled, preferred_element_type=jnp.float32)
    dlogits = jnp.einsum("sphd,skhd->phk", scaled, value_all, preferred_element_type=jnp.float32)
    high = along.astype(jnp.bfloat16)
    rest = (along - high.astype(jnp.float32)).astype(jnp.bfloat16)
    shift = sum(
        jnp.einsum("sph,sk->phk", part, key_valid, preferred_element_type=jnp.float32)
        for part in (high, rest)
    )
    return (dvalue_part, terms.astype(jnp.float32) * (dlogits - shift))


def on_device(
    tokens,
    seq_lengths,
    norm1_gain,
    norm1_bias,
    value_weight,
    value_bias,
    synth_logits,
    out_weight,
    out_bias,
    norm2_gain,
    norm2_bias,
    up_weight,
    up_bias,
    down_weight,
    down_bias,
    cotangent,
):
    rows_dev = tokens.shape[1]
    local_width = tokens.shape[0]
    seq_count = seq_lengths.shape[0]
    seq_len = synth_logits.shape[2]
    head_count = synth_logits.shape[1]
    head_dim = local_width // head_count
    value_cols, out_rows, up_rows, down_cols = (
        lax.all_gather(value_weight, "ta", axis=0, tiled=True),
        lax.all_gather(out_weight, "ta", axis=1, tiled=True),
        lax.all_gather(up_weight, "ta", axis=1, tiled=True),
        lax.all_gather(down_weight, "ta", axis=0, tiled=True),
    )
    up_block, down_block = (
        lax.all_to_all(up_rows.T, "wa", split_axis=0, concat_axis=1, tiled=True),
        lax.all_to_all(down_cols, "wa", split_axis=0, concat_axis=1, tiled=True),
    )
    inputs = tokens.T.astype(jnp.float32)
    pre_one, normed_one, inverse_one = norm_forward(inputs, norm1_gain, norm1_bias)
    layer_one = all_features(pre_one.astype(jnp.bfloat16))
    values = (
        jnp.dot(layer_one, value_cols, preferred_element_type=jnp.float32) + value_bias
    ).astype(jnp.bfloat16)
    value_heads = values.reshape(seq_count, seq_len, head_count, head_dim)
    positions = jnp.arange(seq_len)
    key_valid = positions[None, :] < seq_lengths[:, None]
    query_valid = key_valid.astype(jnp.float32)
    length_all = lax.all_gather(seq_lengths, "ta", axis=0, tiled=True)
    block_rows = synth_logits.shape[0]
    value_all = lax.all_gather(
        value_heads * key_valid[:, :, None, None].astype(jnp.bfloat16), "ta", axis=0, tiled=True
    )
    terms, sums, key_valid_all = weights_of(synth_logits, length_all)
    block_positions = lax.axis_index("ta") * block_rows + jnp.arange(block_rows)
    query_rows = (block_positions[None, :] < length_all[:, None]).astype(jnp.float32)
    mixed_rows, mixed_low = attend(terms, sums, value_all, query_rows)
    attended = lax.all_to_all(mixed_low, "ta", split_axis=0, concat_axis=1, tiled=True)
    attended = attended.reshape(rows_dev, local_width)
    branch = (
        feature_share(jnp.dot(attended, out_rows, preferred_element_type=jnp.float32)) + out_bias
    )
    resid = inputs + branch
    pre_two, normed_two, inverse_two = norm_forward(resid, norm2_gain, norm2_bias)
    layer_two = all_features(pre_two.astype(jnp.bfloat16))
    upper = (
        lax.dot_general(layer_two, up_block, ALONG_FEATURES, preferred_element_type=jnp.float32)
        + up_bias
    )
    hidden, gelu_back = jax.vjp(jax.nn.gelu, upper)
    hidden_low = hidden.astype(jnp.bfloat16)
    feed = (
        feature_share(jnp.dot(hidden_low, down_block, preferred_element_type=jnp.float32))
        + down_bias
    )
    output = (resid + feed).astype(jnp.bfloat16)
    cotangent_rows = cotangent.T
    grad_in = cotangent_rows.astype(jnp.float32)
    grad_full = all_features(cotangent_rows)
    dhidden = lax.dot_general(
        grad_full, down_block, ALONG_FEATURES, preferred_element_type=jnp.float32
    )
    dupper = gelu_back(dhidden)[0].astype(jnp.bfloat16)
    down_part = lax.dot_general(
        hidden_low, grad_full, ALONG_ROWS, preferred_element_type=jnp.float32
    )
    up_part = lax.dot_general(dupper, layer_two, ALONG_ROWS, preferred_element_type=jnp.float32)
    up_bias_part = jnp.sum(dupper.astype(jnp.float32), axis=0)
    down_bias_part = jnp.sum(grad_in, axis=0)
    dlayer_two = feature_share(jnp.dot(dupper, up_block, preferred_element_type=jnp.float32))
    gain_two_part = jnp.sum(dlayer_two * normed_two, axis=0)
    bias_two_part = jnp.sum(dlayer_two, axis=0)
    dresid = grad_in + norm_backward(dlayer_two, normed_two, inverse_two, norm2_gain)
    dbranch = dresid.astype(jnp.bfloat16)
    dbranch_full = all_features(dbranch)
    dattended = lax.dot_general(
        dbranch_full, out_rows, ALONG_FEATURES, preferred_element_type=jnp.float32
    ).astype(jnp.bfloat16)
    out_part = lax.dot_general(
        attended, dbranch_full, ALONG_ROWS, preferred_element_type=jnp.float32
    )
    out_bias_part = jnp.sum(dbranch.astype(jnp.float32), axis=0)
    grad_heads = dattended.reshape(seq_count, seq_len, head_count, head_dim)
    grad_heads = grad_heads * query_valid[:, :, None, None].astype(jnp.bfloat16)
    grad_block = lax.all_to_all(grad_heads, "ta", split_axis=1, concat_axis=0, tiled=True)
    dvalue_part, logits_grad = attend_back(
        terms, sums, key_valid_all, value_all, mixed_rows, grad_block
    )
    dvalue_rows = dvalue_part.astype(jnp.bfloat16).reshape(-1, local_width)
    dvalue_rows = lax.psum_scatter(dvalue_rows, "ta", scatter_dimension=0, tiled=True)
    dvalues = dvalue_rows * query_valid.reshape(rows_dev, 1).astype(jnp.bfloat16)
    value_part = lax.dot_general(layer_one, dvalues, ALONG_ROWS, preferred_element_type=jnp.float32)
    value_bias_part = jnp.sum(dvalues.astype(jnp.float32), axis=0)
    dlayer_one = feature_share(
        lax.dot_general(dvalues, value_cols, ALONG_FEATURES, preferred_element_type=jnp.float32)
    )
    gain_one_part = jnp.sum(dlayer_one * normed_one, axis=0)
    bias_one_part = jnp.sum(dlayer_one, axis=0)
    tokens_grad = dresid + norm_backward(dlayer_one, normed_one, inverse_one, norm1_gain)
    up_back, down_back = (
        lax.all_to_all(up_part, "wa", split_axis=1, concat_axis=0, tiled=True),
        lax.all_to_all(down_part, "wa", split_axis=1, concat_axis=0, tiled=True),
    )
    value_grad, out_grad, up_grad, down_grad = (
        lax.psum_scatter(value_part, "ta", scatter_dimension=0, tiled=True),
        lax.psum_scatter(out_part, "ta", scatter_dimension=1, tiled=True),
        lax.psum_scatter(up_back, "ta", scatter_dimension=0, tiled=True),
        lax.psum_scatter(down_back, "ta", scatter_dimension=0, tiled=True),
    )
    vector_grads = lax.psum(
        (
            gain_one_part,
            bias_one_part,
            value_bias_part,
            out_bias_part,
            gain_two_part,
            bias_two_part,
            up_bias_part,
            down_bias_part,
        ),
        "ta",
    )
    return (
        output.T,
        tokens_grad.T,
        vector_grads[0],
        vector_grads[1],
        value_grad,
        vector_grads[2],
        logits_grad,
        out_grad,
        vector_grads[3],
        vector_grads[4],
        vector_grads[5],
        up_grad.T,
        vector_grads[6],
        down_grad,
        vector_grads[7],
    )


MESH = pl.DeviceIdType.MESH
ROWS_NT = (((1,), (1,)), ((), ()))
ROWS_TN = (((0,), (0,)), ((), ()))
F32 = jnp.float32
BF16 = jnp.bfloat16
VMEM_BYTES = 60 * 2**20
CHUNK = 128
PAD = 128


def whole(count):
    return [pl.BlockSpec(memory_space=pltpu.VMEM)] * count


def anywhere(count):
    return [pl.BlockSpec(memory_space=pl.ANY)] * count


def shape_of(shape, dtype):
    return jax.ShapeDtypeStruct(shape, dtype)


def lanes(start, size=CHUNK):
    return pl.ds(pl.multiple_of(start, CHUNK), size)


def rows_at(start, size, unit):
    return pl.ds(pl.multiple_of(start, unit), size)


class Place:
    def __init__(self, nwa, nta):
        self.nwa, self.nta, self.nz = nwa, nta, nta // 2
        self.wa = lax.axis_index("wa")
        self.ta = lax.axis_index("ta")
        self.z = self.ta // 2
        self.c = self.ta % 2
        self.peer = self.ta + 1 - 2 * self.c
        self.wx = self.wa + 1 - 2 * (self.wa % 2)
        self.wy = (self.wa + 2) % 4
        self.wd = 3 - self.wa

    def enter(self):
        barrier = pltpu.get_barrier_semaphore()
        total = self.nwa * self.nta

        def greet(step, carry):
            w = (self.wa + step // self.nta) % self.nwa
            t = (self.ta + step % self.nta) % self.nta
            pl.semaphore_signal(barrier, inc=1, device_id=(w, t), device_id_type=MESH)
            return carry

        lax.fori_loop(1, total, greet, 0)
        pl.semaphore_wait(barrier, total - 1)


def send(src, dst, ssem, rsem, device):
    return pltpu.make_async_remote_copy(
        src_ref=src,
        dst_ref=dst,
        send_sem=ssem,
        recv_sem=rsem,
        device_id=device,
        device_id_type=MESH,
    )


def when(condition):
    return pl.when(condition)


def norm_stats(block):
    width = block.shape[0]
    mean = jnp.sum(block, axis=0, keepdims=True) / width
    centred = block - mean
    variance = jnp.sum(centred * centred, axis=0, keepdims=True) / width
    inverse = lax.rsqrt(variance + EPSILON)
    return (centred * inverse, inverse)


def forward_kernel(
    dims,
    tok,
    cot,
    wp,
    pcol,
    prow,
    ln,
    logits,
    xown,
    cown,
    attended,
    weights,
    layer_out,
    value_out,
    term_out,
    mixed,
    zinv,
    lens,
    pfull,
    rfull,
    x,
    wvc,
    layer_pad,
    layer,
    value,
    terms,
    attsend,
    sem_tok,
    sem_par,
    sem_ta,
    sem_val,
    sem_w,
    sem_cot,
    sem_att,
    sem_local,
):
    nwa, nta = dims
    me = Place(nwa, nta)
    wa, ta, z, c = me.wa, me.ta, me.z, me.c
    nz = me.nz
    width = tok.shape[0]
    half = width // 2
    seq = tok.shape[1]
    part = seq // nz
    query = seq // nta
    slot = wvc.shape[1] // nta
    wdepth = wvc.shape[0] * nwa // nta
    heads = logits.shape[0]
    hdim = width // heads
    split = wp.shape[1] - PAD
    me.enter()
    done = []

    def block_rows(w, off=0, size=width):
        return rows_at(w * width + off, size, 32)

    def tok_copy(k, q):
        device = (me.wx if k == 0 else me.wy, ta)
        return send(
            tok.at[:, pl.ds(q * part, part)],
            x.at[block_rows(wa), pl.ds(q * part, part)],
            sem_tok.at[0, k, q],
            sem_tok.at[1, k, q],
            device,
        )

    def tok_fwd(k, q):
        source = me.wx if k == 0 else me.wy
        device = (me.wy if k == 0 else me.wx, ta)
        where = x.at[block_rows(source, k * half, half), pl.ds(q * part, part)]
        return send(where, where, sem_tok.at[0, 2 + k, q], sem_tok.at[1, 2 + k, q], device)

    own_x = pltpu.make_async_copy(tok, x.at[block_rows(wa)], sem_local.at[0])
    own_x.start()
    for q in range(nz):
        for k in range(2):
            tok_copy(k, q).start()

    def par_copy(step, what):
        w = (wa + step) % nwa
        if what == 0:
            src, dst = pcol, pfull.at[block_rows(wa)]
        else:
            src, dst = prow, rfull.at[:, lanes(wa * prow.shape[1], prow.shape[1])]
        return send(src, dst, sem_par.at[0, what, step], sem_par.at[1, what, step], (w, ta))

    def ta_copy(step, what):
        t = (ta + step) % nta
        if what == 0:
            src, dst = wp.at[:, pl.ds(split, PAD)], wvc.at[:, lanes(ta * slot)]
        else:
            src, dst = ln, lens.at[rows_at(ta * 8, 8, 8)]
        return send(src, dst, sem_ta.at[0, what, step], sem_ta.at[1, what, step], (wa, t))

    for step in range(1, nta):
        ta_copy(step, 0).start()
        ta_copy(step, 1).start()
    for step in range(1, nwa):
        par_copy(step, 0).start()
        par_copy(step, 1).start()
    own_wv = pltpu.make_async_copy(
        wp.at[:, pl.ds(split, PAD)], wvc.at[:, lanes(ta * slot)], sem_local.at[1]
    )
    own_wv.start()
    pfull[block_rows(wa), :] = pcol[...]
    rfull[:, lanes(wa * prow.shape[1], prow.shape[1])] = prow[...]
    lens[rows_at(ta * 8, 8, 8), :] = ln[...]

    own_w = pltpu.make_async_copy(wp, weights.at[wa, ta], sem_local.at[2])
    own_w.start()

    def w_line(up, b, own):
        t = 2 * b + c
        where = weights.at[wa, t]
        k = 0 if up else 1
        return send(
            wp if own else where,
            where,
            sem_w.at[0, k, b],
            sem_w.at[1, k, b],
            (wa, ta + 2 if up else ta - 2),
        )

    @pl.when(z < nz - 1)
    def _():
        w_line(True, z, True).start()

    @pl.when(z > 0)
    def _():
        w_line(False, z, True).start()

    layer_pad[...] = jnp.zeros_like(layer_pad)
    for h in range(heads):
        terms[h] = jnp.exp(logits[h].astype(F32)).astype(BF16)
    out_terms = pltpu.make_async_copy(terms, term_out, sem_local.at[3])
    out_terms.start()

    own_wv.wait()
    for step in range(1, nta):
        ta_copy(step, 0).wait_recv()
        ta_copy(step, 1).wait_recv()
    for step in range(1, nwa):
        par_copy(step, 0).wait_recv()
        par_copy(step, 1).wait_recv()
    own_x.wait()

    positions = lax.broadcasted_iota(jnp.int32, (nta * 8, seq), 1).astype(F32)
    key_valid = jnp.where(positions < lens[:, 0:1], 1.0, 0.0).astype(BF16)
    for h in range(heads):
        sums = lax.dot_general(key_valid, terms[h], ROWS_NT, preferred_element_type=F32)
        zinv[h] = 1.0 / sums

    def value_copy(kind, b, q, core):
        where = value.at[2 * b + core, :, pl.ds(q * part, part)]
        t = (ta + 2, ta - 2, me.peer)[kind]
        return send(where, where, sem_val.at[0, kind, b, q], sem_val.at[1, kind, b, q], (wa, t))

    def w_hop(h):
        @pl.when(z - 1 - h >= 0)
        def _():
            w_line(True, z - 1 - h, False).wait_recv()

            @pl.when(z < nz - 1)
            def _():
                w_line(True, z - 1 - h, False).start()

        @pl.when(z + 1 + h < nz)
        def _():
            w_line(False, z + 1 + h, False).wait_recv()

            @pl.when(z > 0)
            def _():
                w_line(False, z + 1 + h, False).start()

    for q in range(nz):
        cols = pl.ds(q * part, part)
        for k in range(2):
            tok_copy(k, q).wait_recv()
            tok_fwd(k, q).start()
        for k in range(2):
            where = x.at[block_rows(me.wd, k * half, half), cols]
            send(
                where,
                where,
                sem_tok.at[0, 2 + k, q],
                sem_tok.at[1, 2 + k, q],
                (me.wy if k == 0 else me.wx, ta),
            ).wait_recv()
        normed, _ = norm_stats(x[:, cols].astype(F32))
        low = (normed * pfull[:, 0:1] + pfull[:, 1:2]).astype(BF16)
        layer[:, cols] = low
        for t in range(nta):
            layer_pad[t * slot : t * slot + wdepth, :] = low[t * wdepth : (t + 1) * wdepth]
        made = jnp.dot(wvc[...], layer_pad[...], preferred_element_type=F32) + pcol[:, 2:3]
        place = lax.broadcasted_iota(jnp.int32, (width, part), 1) + q * part
        made = jnp.where(place.astype(F32) < ln[0:1, 0:1], made, 0.0)
        value[ta, :, cols] = made.astype(BF16)
        xown[:, pl.ds(q * CHUNK, CHUNK)] = x[:, lanes(q * part + wa * CHUNK)]

        @pl.when(z < nz - 1)
        def _():
            value_copy(0, z, q, c).start()

        @pl.when(z > 0)
        def _():
            value_copy(1, z, q, c).start()

        value_copy(2, z, q, c).start()
        if q >= 1 and q - 1 < nz - 1:
            w_hop(q - 1)
    out_layer = pltpu.make_async_copy(layer, layer_out, sem_local.at[4])
    out_layer.start()

    def cot_copy(step, q):
        w = (wa + step) % nwa
        return send(
            cot.at[:, lanes(q * part + w * CHUNK)],
            cown.at[block_rows(wa), pl.ds(q * CHUNK, CHUNK)],
            sem_cot.at[0, step, q],
            sem_cot.at[1, step, q],
            (w, ta),
        )

    def cot_own(q):
        return pltpu.make_async_copy(
            cot.at[:, lanes(q * part + wa * CHUNK)],
            cown.at[block_rows(wa), pl.ds(q * CHUNK, CHUNK)],
            sem_cot.at[0, 0, q],
        )

    own_w.wait()

    def w_plane(k, b):
        device = (me.wx if k == 0 else me.wy, ta)
        where = weights.at[wa, 2 * b + c]
        return send(where, where, sem_w.at[0, 2 + k, b], sem_w.at[1, 2 + k, b], device)

    def w_diag(k, b, source):
        device = (me.wy if k == 0 else me.wx, ta)
        where = weights.at[source, 2 * b + c, pl.ds(k * half, half)]
        return send(where, where, sem_w.at[0, 4 + k, b], sem_w.at[1, 4 + k, b], device)

    def w_core(r, b, core):
        source = (wa, me.wx, me.wy, me.wd)[r]
        where = weights.at[source, 2 * b + core]
        return send(where, where, sem_w.at[0, 6 + r, b], sem_w.at[1, 6 + r, b], (wa, me.peer))

    for b in range(nz):
        w_plane(0, b).start()
        w_plane(1, b).start()
        w_core(0, b, c).start()
    for q in range(nz):
        cot_own(q).start()
        for step in range(1, nwa):
            cot_copy(step, q).start()

    def w_forward(b):
        w_plane(0, b).wait_recv()
        w_diag(0, b, me.wx).start()
        w_core(1, b, c).start()
        w_plane(1, b).wait_recv()
        w_diag(1, b, me.wy).start()
        w_core(2, b, c).start()

    def w_finish(b):
        for k in range(2):
            w_diag(k, b, me.wd).wait_recv()
        w_core(3, b, c).start()

    def att_copy(s, j):
        return send(
            attsend.at[s, :, pl.ds(j * CHUNK, CHUNK)],
            attended.at[block_rows(wa), lanes(z * CHUNK)],
            sem_att.at[0, s, j],
            sem_att.at[1, wa, z],
            (2 * c + j, s),
        )

    def att_local(s, j):
        return pltpu.make_async_copy(
            attsend.at[s, :, pl.ds(j * CHUNK, CHUNK)],
            attended.at[block_rows(wa), lanes(z * CHUNK)],
            sem_att.at[0, s, j],
        )

    def is_self(s, j):
        return jnp.logical_and(s == ta, 2 * c + j == wa)

    def mix(b):
        for core in range(2):
            s = 2 * b + core
            out_value = pltpu.make_async_copy(value.at[s], value_out.at[s], sem_local.at[6 + core])
            out_value.start()
        length = [lens[rows_at((2 * b + core) * 8, 8, 8), :][0:1, 0:1] for core in range(2)]
        place = lax.broadcasted_iota(jnp.int32, (hdim, query), 1) + ta * query
        place = place.astype(F32)
        for h in range(heads):
            group = slice(h * hdim, (h + 1) * hdim)
            pair = jnp.concatenate([value[2 * b, group, :], value[2 * b + 1, group, :]], axis=0)
            both = lax.dot_general(pair, terms[h], ROWS_NT, preferred_element_type=F32)
            for core in range(2):
                s = 2 * b + core
                inverse = zinv[h, rows_at(s * 8, 8, 8), :][0:1]
                one = both[core * hdim : (core + 1) * hdim] * inverse
                mixed[s, group, :] = one
                one = jnp.where(place < length[core], one, 0.0)
                attsend[s, group, :] = one.astype(BF16)
        for core in range(2):
            s = 2 * b + core
            for j in range(2):

                @pl.when(is_self(s, j))
                def _():
                    att_local(s, j).start()

                @pl.when(jnp.logical_not(is_self(s, j)))
                def _():
                    att_copy(s, j).start()

            pltpu.make_async_copy(value.at[s], value_out.at[s], sem_local.at[6 + core]).wait()

    def core_ready(b):
        for q in range(nz):
            value_copy(2, b, q, 1 - c).wait_recv()

    for h in range(nz - 1):
        below, above = z - 1 - h, z + 1 + h
        for q in range(nz):

            @pl.when(below >= 0)
            def _():
                value_copy(0, below, q, c).wait_recv()

                @pl.when(z < nz - 1)
                def _():
                    value_copy(0, below, q, c).start()

                value_copy(2, below, q, c).start()

            @pl.when(above < nz)
            def _():
                value_copy(1, above, q, c).wait_recv()

                @pl.when(z > 0)
                def _():
                    value_copy(1, above, q, c).start()

                value_copy(2, above, q, c).start()

        if h == 0:
            core_ready(z)
            mix(z)

        @pl.when(below >= 0)
        def _():
            core_ready(below)
            mix(below)

        @pl.when(above < nz)
        def _():
            core_ready(above)
            mix(above)

        w_forward(h)
    for b in range(nz - 1, nz):
        w_forward(b)
    for b in range(nz):
        w_finish(b)

    for step in range(1, nta):
        ta_copy(step, 0).wait_send()
        ta_copy(step, 1).wait_send()
    for step in range(1, nwa):
        par_copy(step, 0).wait_send()
        par_copy(step, 1).wait_send()
        for q in range(nz):
            cot_copy(step, q).wait_send()
    for q in range(nz):
        cot_own(q).wait()
        for k in range(2):
            tok_copy(k, q).wait_send()
            tok_fwd(k, q).wait_send()
    for step in range(1, nwa):
        for q in range(nz):
            cot_copy(step, q).wait_recv()

    def line_sends(b, carry):
        reach_up = jnp.logical_and(b <= z, z < nz - 1)
        reach_down = jnp.logical_and(b >= z, z > 0)

        @pl.when(reach_up)
        def _():
            w_line(True, b, False).wait_send()
            for q in range(nz):
                value_copy(0, b, q, c).wait_send()

        @pl.when(reach_down)
        def _():
            w_line(False, b, False).wait_send()
            for q in range(nz):
                value_copy(1, b, q, c).wait_send()

        for q in range(nz):
            value_copy(2, b, q, c).wait_send()
        for k in range(2):
            w_plane(k, b).wait_send()
        w_diag(0, b, me.wx).wait_send()
        w_diag(1, b, me.wy).wait_send()
        for r in range(4):
            w_core(r, b, c).wait_send()
            w_core(r, b, 1 - c).wait_recv()
        return carry

    lax.fori_loop(0, nz, line_sends, 0)

    def att_sends(s, carry):
        for j in range(2):

            @pl.when(is_self(s, j))
            def _():
                att_local(s, j).wait()

            @pl.when(jnp.logical_not(is_self(s, j)))
            def _():
                att_copy(s, j).wait_send()

        return carry

    lax.fori_loop(0, nta, att_sends, 0)
    mine = wa // 2

    def att_arrivals(k, carry):
        w, b = k // nz, k % nz

        @pl.when(jnp.logical_not(jnp.logical_and(w == wa, 2 * b + mine == ta)))
        def _():
            where = attended.at[block_rows(w), lanes(b * CHUNK)]
            send(where, where, sem_att.at[0, 0, 0], sem_att.at[1, w, b], (w, 2 * b + mine)).wait_recv()

        return carry

    lax.fori_loop(0, nwa * nz, att_arrivals, 0)
    out_terms.wait()
    out_layer.wait()


def run_forward(dims, tok, cot, wp, pcol, prow, ln, logits):
    nwa, nta = dims
    nz = nta // 2
    width, seq = tok.shape
    depth = width * nwa
    own = seq // nwa
    heads, query, _ = logits.shape
    slot = PAD
    dma = pltpu.SemaphoreType.DMA
    return pl.pallas_call(
        functools.partial(forward_kernel, dims),
        out_shape=(
            shape_of((depth, own), BF16),
            shape_of((depth, own), BF16),
            shape_of((depth, own), BF16),
            shape_of((nwa, nta) + wp.shape, BF16),
            shape_of((depth, seq), BF16),
            shape_of((nta, width, seq), BF16),
            shape_of((heads, query, seq), BF16),
            shape_of((nta, width, query), F32),
            shape_of((heads, nta * 8, query), F32),
            shape_of((nta * 8, CHUNK), F32),
            shape_of((depth, pcol.shape[1]), F32),
            shape_of((8, prow.shape[1] * nwa), F32),
        ),
        in_specs=anywhere(3) + whole(4),
        out_specs=tuple(whole(3) + anywhere(4) + whole(5)),
        scratch_shapes=[
            pltpu.VMEM((depth, seq), BF16),
            pltpu.VMEM((width, nta * slot), BF16),
            pltpu.VMEM((nta * slot, seq // nz), BF16),
            pltpu.VMEM((depth, seq), BF16),
            pltpu.VMEM((nta, width, seq), BF16),
            pltpu.VMEM((heads, query, seq), BF16),
            pltpu.VMEM((nta, width, query), BF16),
            dma((2, 4, nz)),
            dma((2, 2, nwa)),
            dma((2, 2, nta)),
            dma((2, 3, nz, nz)),
            dma((2, 10, nz)),
            dma((2, nwa, nz)),
            dma((2, nta, max(nz, 2))),
            dma((8,)),
        ],
        compiler_params=pltpu.CompilerParams(
            collective_id=1, has_side_effects=True, vmem_limit_bytes=VMEM_BYTES
        ),
        cost_estimate=pl.CostEstimate(
            flops=4 * 10**9, bytes_accessed=60 * 10**6, transcendentals=2 * 10**6
        ),
    )(tok, cot, wp, pcol, prow, ln, logits)


def gelu_pair(u):
    root = 0.7978845608028654
    square = u * u
    bent = jnp.tanh(root * u * (1.0 + 0.044715 * square))
    low_half = 0.5 * (1.0 + bent)
    slope = low_half + 0.5 * u * (1.0 - bent * bent) * root * (1.0 + 3.0 * 0.044715 * square)
    return (u * low_half, slope)


def middle_kernel(
    dims,
    attended,
    xown,
    cown,
    pfull,
    rfull,
    ln,
    block,
    wo,
    out,
    dattended,
    dresid,
    wgrad,
    vcol,
    vrow,
    resid,
    normed,
    inverse,
    layer,
    layer_t,
    grad_t,
    feed,
    dlayer,
    wide,
    gblock,
    gwo,
    sem_g,
):
    nwa, nta = dims
    step = pl.program_id(0)
    last = pl.num_programs(0) - 1
    wa = lax.axis_index("wa")
    depth, own = xown.shape
    width = depth // nwa
    cols = block.shape[3] // 2
    wdepth = depth // nta
    up = block[:, 0, :, :cols].reshape(depth, cols)
    down_t = block[:, 0, :, cols:].reshape(depth, cols)

    def wide_wo():
        joined = [
            jnp.concatenate([wo[w, t] for t in range(nta)], axis=1) for w in range(nwa)
        ]
        return jnp.concatenate(joined, axis=0)

    @pl.when(step == 0)
    def _():
        branch = lax.dot_general(wide_wo(), attended[...], ROWS_TN, preferred_element_type=F32)
        branch = jnp.concatenate(
            [branch[t * PAD : t * PAD + wdepth] for t in range(nta)], axis=0
        )
        res = xown[...].astype(F32) + branch + pfull[:, 3:4]
        resid[...] = res
        norm, inv = norm_stats(res)
        normed[...] = norm
        inverse[...] = jnp.broadcast_to(inv, inverse.shape)
        low = (norm * pfull[:, 4:5] + pfull[:, 5:6]).astype(BF16)
        layer[...] = low
        layer_t[...] = low.T
        grad_t[...] = cown[...].T
        feed[...] = jnp.zeros_like(feed)
        dlayer[...] = jnp.zeros_like(dlayer)

    at = lanes(step * cols, cols)
    upper = jnp.dot(layer_t[...], up, preferred_element_type=F32) + rfull[0:1, at]
    hidden, slope = gelu_pair(upper)
    hidden = hidden.astype(BF16)
    dhidden = jnp.dot(grad_t[...], down_t, preferred_element_type=F32)
    dupper = (dhidden * slope).astype(BF16)
    vrow[:, at] = jnp.broadcast_to(
        jnp.sum(dupper.astype(F32), axis=0, keepdims=True), (vrow.shape[0], cols)
    )
    feed[...] += lax.dot_general(down_t, hidden, ROWS_NT, preferred_element_type=F32)
    dlayer[...] += lax.dot_general(up, dupper, ROWS_NT, preferred_element_type=F32)
    gup = jnp.dot(layer[...], dupper, preferred_element_type=F32)
    gdown = jnp.dot(cown[...], hidden, preferred_element_type=F32)

    def put(at_step, slot):
        return pltpu.make_async_copy(
            gblock.at[slot],
            wgrad.at[:, at_step // 2, at_step % 2, :, pl.ds(0, 2 * cols)],
            sem_g.at[slot],
        )

    for slot in range(2):

        @pl.when(step % 2 == slot)
        def _():
            @pl.when(step >= 2)
            def _():
                put(step - 2, slot).wait()

            gblock[slot, :, :, :cols] = gup.reshape(nwa, width, cols).astype(BF16)
            gblock[slot, :, :, cols:] = gdown.reshape(nwa, width, cols).astype(BF16)
            put(step, slot).start()

    @pl.when(step == last)
    def _():
        grad = cown[...].astype(F32)
        out[...] = (resid[...] + feed[...] + pfull[:, 6:7]).astype(BF16)
        dl = dlayer[...]
        norm = normed[...]
        e = dl * pfull[:, 4:5]
        mean_e = jnp.sum(e, axis=0, keepdims=True) / depth
        mean_n = jnp.sum(e * norm, axis=0, keepdims=True) / depth
        dres = grad + inverse[0:1, :] * (e - mean_e - norm * mean_n)
        dresid[...] = dres
        low = dres.astype(BF16)
        vcol[...] = jnp.zeros_like(vcol)
        vcol[:, 3:4] = jnp.sum(low.astype(F32), axis=1, keepdims=True)
        vcol[:, 4:5] = jnp.sum(dl * norm, axis=1, keepdims=True)
        vcol[:, 5:6] = jnp.sum(dl, axis=1, keepdims=True)
        vcol[:, 6:7] = jnp.sum(grad, axis=1, keepdims=True)
        wide[...] = jnp.zeros_like(wide)
        for t in range(nta):
            wide[t * PAD : t * PAD + wdepth, :] = low[t * wdepth : (t + 1) * wdepth]
        da = jnp.dot(wide_wo(), wide[...], preferred_element_type=F32)
        lane = lax.broadcasted_iota(jnp.int32, (depth, own), 1)
        place = (lane // CHUNK) * (CHUNK * nwa) + lane % CHUNK + wa * CHUNK
        da = jnp.where(place.astype(F32) < ln[0:1, 0:1], da, 0.0)
        dattended[...] = da.astype(BF16)
        made = lax.dot_general(attended[...], wide[...], ROWS_NT, preferred_element_type=F32)
        for t in range(nta):
            piece = made[:, t * PAD : (t + 1) * PAD].reshape(nwa, width, PAD)
            gwo[:, t // 2, t % 2] = piece.astype(BF16)
        rest = pltpu.make_async_copy(
            gwo, wgrad.at[:, :, :, :, pl.ds(2 * cols, PAD)], sem_g.at[2]
        )
        rest.start()
        put(last - 1, (nta - 2) % 2).wait()
        put(last, (nta - 1) % 2).wait()
        rest.wait()


def run_middle(dims, attended, xown, cown, pfull, rfull, ln, weights):
    nwa, nta = dims
    depth, own = xown.shape
    width = weights.shape[2]
    both = weights.shape[3] - 2 * PAD
    hidden = both // 2 * nta

    def full(shape):
        return pl.BlockSpec(shape, lambda i: (0,) * len(shape))

    block = pl.BlockSpec((nwa, 1, width, both), lambda i: (0, i, 0, 0))
    wo = pl.BlockSpec((nwa, nta, width, PAD), lambda i: (0, 0, 0, both // PAD))
    return pl.pallas_call(
        functools.partial(middle_kernel, dims),
        grid=(nta,),
        out_shape=(
            shape_of((depth, own), BF16),
            shape_of((depth, own), BF16),
            shape_of((depth, own), F32),
            shape_of((nwa, nta // 2, 2, width, both + PAD), BF16),
            shape_of((depth, PAD), F32),
            shape_of((8, hidden), F32),
        ),
        in_specs=[
            full((depth, own)),
            full((depth, own)),
            full((depth, own)),
            full(pfull.shape),
            full(rfull.shape),
            full(ln.shape),
            block,
            wo,
        ],
        out_specs=(
            full((depth, own)),
            full((depth, own)),
            full((depth, own)),
            pl.BlockSpec(memory_space=pl.ANY),
            full((depth, PAD)),
            full((8, hidden)),
        ),
        scratch_shapes=[
            pltpu.VMEM((depth, own), F32),
            pltpu.VMEM((depth, own), F32),
            pltpu.VMEM((8, own), F32),
            pltpu.VMEM((depth, own), BF16),
            pltpu.VMEM((own, depth), BF16),
            pltpu.VMEM((own, depth), BF16),
            pltpu.VMEM((depth, own), F32),
            pltpu.VMEM((depth, own), F32),
            pltpu.VMEM((nta * PAD, own), BF16),
            pltpu.VMEM((2, nwa, width, both), BF16),
            pltpu.VMEM((nwa, nta // 2, 2, width, PAD), BF16),
            pltpu.SemaphoreType.DMA((3,)),
        ],
        compiler_params=pltpu.CompilerParams(vmem_limit_bytes=VMEM_BYTES),
        cost_estimate=pl.CostEstimate(
            flops=17 * 10**9, bytes_accessed=40 * 10**6, transcendentals=2 * 10**6
        ),
    )(attended, xown, cown, pfull, rfull, ln, weights, weights)


def backward_kernel(
    dims,
    dattended,
    outown,
    dresid,
    xown,
    terms,
    mixed,
    zinv,
    lens,
    ln,
    pfull,
    layer,
    weights,
    wgrad,
    vcol,
    vrow,
    scaled,
    shift,
    output,
    tgrad,
    vgrad,
    vectors,
    wsum,
    da,
    partial,
    paired,
    up_in,
    down_in,
    gown,
    gpeer,
    first_x,
    first_y,
    second_x,
    second_y,
    gup_in,
    gdown_in,
    dvalue,
    dvown,
    wv,
    vsend,
    vrecv,
    tsend,
    csend,
    crecv,
    csum,
    crecv2,
    sem_da,
    sem_out,
    sem_core,
    sem_line,
    sem_dv,
    sem_tg,
    sem_v,
    sem_c,
    sem_c2,
    sem_local,
    sem_g,
    sem_gline,
):
    nwa, nta = dims
    me = Place(nwa, nta)
    wa, ta, z, c = me.wa, me.ta, me.z, me.c
    nz = me.nz
    depth, own = dresid.shape
    width = depth // nwa
    wdepth = depth // nta
    heads, query, seq = terms.shape
    hdim = width // heads
    part = seq // nz
    me.enter()

    def block_rows(w):
        return rows_at(w * width, width, 32)

    def da_copy(w, b, local):
        core = wa // 2
        src = dattended.at[block_rows(w), lanes(b * CHUNK)]
        dst = da.at[ta, :, lanes((wa % 2) * CHUNK)]
        if local:
            return pltpu.make_async_copy(src, dst, sem_da.at[0, w, b])
        return send(src, dst, sem_da.at[0, w, b], sem_da.at[1, ta, wa % 2], (w, 2 * b + core))

    def da_self(w, b):
        return jnp.logical_and(w == wa, 2 * b + wa // 2 == ta)

    def da_start(k, carry):
        w, b = (wa + k // nz) % nwa, k % nz

        @pl.when(da_self(w, b))
        def _():
            da_copy(w, b, True).start()

        @pl.when(jnp.logical_not(da_self(w, b)))
        def _():
            da_copy(w, b, False).start()

        return carry

    lax.fori_loop(0, nwa * nz, da_start, 0)

    def back_copy(src, dst, sems, step, q):
        w = (wa + step) % nwa
        return send(
            src.at[block_rows(w), pl.ds(q * CHUNK, CHUNK)],
            dst.at[:, lanes(q * part + wa * CHUNK)],
            sems.at[0, step, q],
            sems.at[1, step, q],
            (w, ta),
        )

    def back_own(src, dst, sems, q):
        return pltpu.make_async_copy(
            src.at[block_rows(wa), pl.ds(q * CHUNK, CHUNK)],
            dst.at[:, lanes(q * part + wa * CHUNK)],
            sems.at[0, 0, q],
        )

    for q in range(nz):
        back_own(outown, output, sem_out, q).start()
        for step in range(1, nwa):
            back_copy(outown, output, sem_out, step, q).start()
    get_wv = pltpu.make_async_copy(
        weights.at[:, :, :, pl.ds(weights.shape[3] - PAD, PAD)], wv, sem_local.at[0]
    )
    get_wv.start()

    half = width // 2
    order = []
    for j in range(nz):
        for b in (nz - 1 - j, j):
            if b not in order:
                order.append(b)

    def g_core(b, core):
        return send(
            wgrad.at[:, b, core],
            gpeer.at[b],
            sem_g.at[0, 0, b],
            sem_g.at[1, 0, b],
            (wa, me.peer),
        )

    def g_load(b):
        return pltpu.make_async_copy(wgrad.at[:, b, c], gown.at[b], sem_g.at[0, 7, b])

    def g_first(k, r, b):
        near = me.wx if k == 0 else me.wy
        which = near if r == 0 else me.wd
        return send(
            gown.at[b, which, pl.ds(k * half, half)],
            (first_x if k == 0 else first_y).at[b, r],
            sem_g.at[0, 1 + 2 * k + r, b],
            sem_g.at[1, 1 + 2 * k + r, b],
            (near, ta),
        )

    def g_second(k, b):
        near = me.wy if k == 0 else me.wx
        return send(
            gown.at[b, near, pl.ds(k * half, half)],
            (second_x if k == 0 else second_y).at[b],
            sem_g.at[0, 5 + k, b],
            sem_g.at[1, 5 + k, b],
            (near, ta),
        )

    def g_add(b, which, k, extra):
        rows = pl.ds(k * half, half)
        gown[b, which, rows, :] = (
            gown[b, which, rows, :].astype(F32) + extra.astype(F32)
        ).astype(BF16)

    def g_cores(b):
        g_load(b).wait()
        g_core(b, c).wait_recv()
        for w in range(nwa):
            gown[b, w] = (gown[b, w].astype(F32) + gpeer[b, w].astype(F32)).astype(BF16)
        for k in range(2):
            for r in range(2):
                g_first(k, r, b).start()

    def g_plane(b):
        for k in range(2):
            for r in range(2):
                g_first(k, r, b).wait_recv()
            landed = first_x if k == 0 else first_y
            g_add(b, me.wy if k == 0 else me.wx, k, landed[b, 1])
            g_second(k, b).start()
            g_add(b, wa, k, landed[b, 0])

    def g_end(b):
        for k in range(2):
            g_second(k, b).wait_recv()
            g_add(b, wa, k, (second_x if k == 0 else second_y)[b])

    def g_line(up, j):
        k = 0 if up else 1
        target = nz - 1 - j if up else j
        return send(
            gown.at[target, wa],
            (gup_in if up else gdown_in).at[j],
            sem_gline.at[0, k, j],
            sem_gline.at[1, k, j],
            (wa, ta + 2 if up else ta - 2),
        )

    def g_hop(j):
        target = nz - 1 - j

        @pl.when(z < target)
        def _():
            @pl.when(z > 0)
            def _():
                g_line(True, j).wait_recv()
                gown[target, wa] = (
                    gown[target, wa].astype(F32) + gup_in[j].astype(F32)
                ).astype(BF16)

            g_line(True, j).start()

        @pl.when(z > j)
        def _():
            @pl.when(z < nz - 1)
            def _():
                g_line(False, j).wait_recv()
                gown[j, wa] = (gown[j, wa].astype(F32) + gdown_in[j].astype(F32)).astype(BF16)

            g_line(False, j).start()

    def g_final():
        @pl.when(z == 0)
        def _():
            g_line(False, 0).wait_recv()
            wsum[...] = gown[0, wa].astype(F32) + gdown_in[0].astype(F32)

        @pl.when(z == nz - 1)
        def _():
            g_line(True, 0).wait_recv()
            wsum[...] = gown[nz - 1, wa].astype(F32) + gup_in[0].astype(F32)

        for b in range(1, nz - 1):

            @pl.when(z == b)
            def _():
                g_line(True, nz - 1 - b).wait_recv()
                g_line(False, b).wait_recv()
                both = gup_in[nz - 1 - b].astype(F32) + gdown_in[b].astype(F32)
                wsum[...] = gown[b, wa].astype(F32) + both

    for b in order:
        g_core(b, 1 - c).start()
        g_load(b).start()

    for b in order:
        g_cores(b)

    def da_arrive(k, carry):
        s, j = k // 2, k % 2
        own_piece = jnp.logical_and(s == ta, 2 * c + j == wa)
        where = da.at[s, :, lanes(j * CHUNK)]

        @pl.when(jnp.logical_not(own_piece))
        def _():
            send(where, where, sem_da.at[0, 0, 0], sem_da.at[1, s, j], (2 * c + j, s)).wait_recv()

        return carry

    def da_sent(k, carry):
        w, b = (wa + k // nz) % nwa, k % nz

        @pl.when(da_self(w, b))
        def _():
            da_copy(w, b, True).wait()

        @pl.when(jnp.logical_not(da_self(w, b)))
        def _():
            da_copy(w, b, False).wait_send()

        return carry

    lax.fori_loop(0, nwa * nz, da_sent, 0)
    lax.fori_loop(0, 2 * nta, da_arrive, 0)

    for h in range(heads):
        group = slice(h * hdim, (h + 1) * hdim)
        for s in range(nta):
            one = da[s, group, :].astype(F32)
            inv = zinv[h, s * 8 : s * 8 + 1, :]
            along = jnp.sum(one * mixed[s, group, :], axis=0, keepdims=True)
            shift[h, s * 8 : (s + 1) * 8, :] = jnp.broadcast_to(along * inv, (8, query))
            scaled[s, group, :] = (one * inv).astype(BF16)
    for h in range(heads):
        group = slice(h * hdim, (h + 1) * hdim)
        stacked = jnp.concatenate([scaled[s, group, :] for s in range(nta)], axis=0)
        made = jnp.dot(stacked, terms[h], preferred_element_type=F32).astype(BF16)
        for s in range(nta):
            partial[s, group, :] = made[s * hdim : (s + 1) * hdim]

    def core_copy(b, core):
        return send(
            partial.at[2 * b + core],
            paired.at[b],
            sem_core.at[0, b],
            sem_core.at[1, b],
            (wa, me.peer),
        )

    for b in order:
        core_copy(b, 1 - c).start()

    def line_copy(up, j):
        k = 0 if up else 1
        return send(
            partial.at[2 * (nz - 1 - j if up else j) + c],
            (up_in if up else down_in).at[j],
            sem_line.at[0, k, j],
            sem_line.at[1, k, j],
            (wa, ta + 2 if up else ta - 2),
        )

    ready = set()

    def core_ready(b):
        if b not in ready:
            ready.add(b)
            core_copy(b, c).wait_recv()

    def chip_sum(b):
        return partial[2 * b + c].astype(F32) + paired[b].astype(F32)

    for j in range(nz - 1):
        target = nz - 1 - j
        core_ready(target)

        @pl.when(z < target)
        def _():
            @pl.when(z > 0)
            def _():
                line_copy(True, j).wait_recv()
                partial[2 * target + c] = (chip_sum(target) + up_in[j].astype(F32)).astype(BF16)

            @pl.when(z == 0)
            def _():
                partial[2 * target + c] = chip_sum(target).astype(BF16)

            line_copy(True, j).start()

        core_ready(j)

        @pl.when(z > j)
        def _():
            @pl.when(z < nz - 1)
            def _():
                line_copy(False, j).wait_recv()
                partial[2 * j + c] = (chip_sum(j) + down_in[j].astype(F32)).astype(BF16)

            @pl.when(z == nz - 1)
            def _():
                partial[2 * j + c] = chip_sum(j).astype(BF16)

            line_copy(False, j).start()

        if j == 0:
            g_plane(order[0])
            g_plane(order[1])
        if j == 1:
            for b in order[2:]:
                g_plane(b)
            g_end(order[0])
            g_end(order[1])
            g_hop(0)

    for b in order[2:]:
        g_end(b)
    for b in range(nz):
        core_ready(b)
    place = lax.broadcasted_iota(jnp.int32, (width, seq), 1).astype(F32)
    key_valid = place < ln[0:1, 0:1]

    @pl.when(z == 0)
    def _():
        line_copy(False, 0).wait_recv()
        total = chip_sum(0) + down_in[0].astype(F32)
        dvalue[...] = jnp.where(key_valid, total, 0.0).astype(BF16)

    @pl.when(z == nz - 1)
    def _():
        line_copy(True, 0).wait_recv()
        total = chip_sum(nz - 1) + up_in[0].astype(F32)
        dvalue[...] = jnp.where(key_valid, total, 0.0).astype(BF16)

    for b in range(1, nz - 1):

        @pl.when(z == b)
        def _():
            line_copy(True, nz - 1 - b).wait_recv()
            line_copy(False, b).wait_recv()
            total = chip_sum(b) + up_in[nz - 1 - b].astype(F32) + down_in[b].astype(F32)
            dvalue[...] = jnp.where(key_valid, total, 0.0).astype(BF16)

    def dv_copy(step, q):
        w = (wa + step) % nwa
        return send(
            dvalue.at[:, lanes(q * part + w * CHUNK)],
            dvown.at[block_rows(wa), pl.ds(q * CHUNK, CHUNK)],
            sem_dv.at[0, step, q],
            sem_dv.at[1, step, q],
            (w, ta),
        )

    for q in range(nz):
        for step in range(1, nwa):
            dv_copy(step, q).start()
        dvown[block_rows(wa), q * CHUNK : (q + 1) * CHUNK] = dvalue[
            :, lanes(q * part + wa * CHUNK)
        ]

    vmade = lax.dot_general(layer[...], dvalue[...], ROWS_NT, preferred_element_type=F32)
    vsend[...] = vmade.astype(BF16).reshape(nta, wdepth, width)
    vbias = jnp.sum(dvalue[...].astype(F32), axis=1, keepdims=True)

    def v_copy(step):
        t = (ta + step) % nta
        return send(
            vsend.at[t], vrecv.at[step], sem_v.at[0, step], sem_v.at[1, step], (wa, t)
        )

    for step in range(1, nta):
        v_copy(step).start()

    for j in range(1, nz - 1):
        g_hop(j)
    get_wv.wait()
    for step in range(1, nwa):
        for q in range(nz):
            dv_copy(step, q).wait_recv()
    dl_parts = []
    for t in range(nta):
        turned = jnp.concatenate([wv[w, t] for w in range(nwa)], axis=0)
        dl_parts.append(
            lax.dot_general(turned, dvown[...], ROWS_TN, preferred_element_type=F32)[:wdepth]
        )
    dl = jnp.concatenate(dl_parts, axis=0)
    norm, inv = norm_stats(xown[...].astype(F32))
    e = dl * pfull[:, 0:1]
    mean_e = jnp.sum(e, axis=0, keepdims=True) / depth
    mean_n = jnp.sum(e * norm, axis=0, keepdims=True) / depth
    tsend[...] = (dresid[...] + inv * (e - mean_e - norm * mean_n)).astype(BF16)
    for q in range(nz):
        back_own(tsend, tgrad, sem_tg, q).start()
        for step in range(1, nwa):
            back_copy(tsend, tgrad, sem_tg, step, q).start()

    gain = jnp.sum(dl * norm, axis=1, keepdims=True)
    bias = jnp.sum(dl, axis=1, keepdims=True)
    column = lax.broadcasted_iota(jnp.int32, (depth, PAD), 1)
    cols = jnp.where(column == 0, gain, jnp.where(column == 1, bias, vcol[...]))
    wide = vrow.shape[1] // nwa
    gap = csend.shape[2] - wide
    for w in range(nwa):
        piece = cols[w * width : (w + 1) * width]
        piece = jnp.concatenate([piece, jnp.zeros((gap - width, PAD), F32)], axis=0)
        csend[w, :, :gap] = piece.T[:8]
        csend[w, :, gap:] = vrow[:, w * wide : (w + 1) * wide]

    def c_copy(step):
        w = (wa + step) % nwa
        return send(csend.at[w], crecv.at[step], sem_c.at[0, step], sem_c.at[1, step], (w, ta))

    for step in range(1, nwa):
        c_copy(step).start()
    crecv[0] = csend[wa]
    piece = jnp.concatenate(
        [jnp.broadcast_to(vbias, (width, PAD)), jnp.zeros((gap - width, PAD), F32)], axis=0
    )
    vb_row = jnp.concatenate([piece.T[:8], jnp.zeros((8, wide), F32)], axis=1)
    row = lax.broadcasted_iota(jnp.int32, vb_row.shape, 0)
    total = jnp.where(row == 2, vb_row, 0.0) + crecv[0]
    for step in range(1, nwa):
        c_copy(step).wait_recv()
        total = total + crecv[step]
    csum[...] = total

    def c2_copy(step):
        t = (ta + step) % nta
        return send(csum, crecv2.at[step], sem_c2.at[0, step], sem_c2.at[1, step], (wa, t))

    for step in range(1, nta):
        c2_copy(step).start()
    g_final()
    value_total = vsend[ta].astype(F32)
    for step in range(1, nta):
        v_copy(step).wait_recv()
        value_total = value_total + vrecv[step].astype(F32)
    vgrad[...] = value_total
    crecv2[0] = csum[...]
    for step in range(1, nta):
        c2_copy(step).wait_recv()
    full = jnp.zeros(csum.shape, F32)
    for t in range(nta):
        full = full + crecv2[(ta - t + nta) % nta]
    vectors[...] = full

    for step in range(1, nwa):
        for q in range(nz):
            back_copy(tsend, tgrad, sem_tg, step, q).wait()
            back_copy(outown, output, sem_out, step, q).wait()
            dv_copy(step, q).wait_send()
        c_copy(step).wait_send()
    for q in range(nz):
        back_own(outown, output, sem_out, q).wait()
        back_own(tsend, tgrad, sem_tg, q).wait()
    for step in range(1, nta):
        v_copy(step).wait_send()
        c2_copy(step).wait_send()
    for b in range(nz):
        core_copy(b, 1 - c).wait_send()
        g_core(b, 1 - c).wait_send()
        for k in range(2):
            g_first(k, 0, b).wait_send()
            g_first(k, 1, b).wait_send()
            g_second(k, b).wait_send()
    for j in range(nz - 1):

        @pl.when(z < nz - 1 - j)
        def _():
            line_copy(True, j).wait_send()
            g_line(True, j).wait_send()

        @pl.when(z > j)
        def _():
            line_copy(False, j).wait_send()
            g_line(False, j).wait_send()


def run_backward(
    dims, dattended, outown, dresid, xown, terms, mixed, zinv, lens, ln, pfull, layer, weights, wgrad, vcol, vrow
):
    nwa, nta = dims
    nz = nta // 2
    half, both = weights.shape[2] // 2, wgrad.shape[4]
    depth, own = dresid.shape
    width = depth // nwa
    heads, query, seq = terms.shape
    wdepth = depth // nta
    wide = 256 + vrow.shape[1] // nwa
    dma = pltpu.SemaphoreType.DMA
    return pl.pallas_call(
        functools.partial(backward_kernel, dims),
        out_shape=(
            shape_of((nta, width, query), BF16),
            shape_of((heads, nta * 8, query), F32),
            shape_of((width, seq), BF16),
            shape_of((width, seq), BF16),
            shape_of((wdepth, width), F32),
            shape_of((8, wide), F32),
            shape_of((width, both), F32),
        ),
        in_specs=whole(11) + anywhere(2) + whole(2),
        out_specs=tuple(whole(7)),
        scratch_shapes=[
            pltpu.VMEM((nta, width, query), BF16),
            pltpu.VMEM((nta, width, seq), BF16),
            pltpu.VMEM((nz, width, seq), BF16),
            pltpu.VMEM((nz - 1, width, seq), BF16),
            pltpu.VMEM((nz - 1, width, seq), BF16),
            pltpu.VMEM((nz, nwa, width, both), BF16),
            pltpu.VMEM((nz, nwa, width, both), BF16),
            pltpu.VMEM((nz, 2, half, both), BF16),
            pltpu.VMEM((nz, 2, half, both), BF16),
            pltpu.VMEM((nz, half, both), BF16),
            pltpu.VMEM((nz, half, both), BF16),
            pltpu.VMEM((nz - 1, width, both), BF16),
            pltpu.VMEM((nz - 1, width, both), BF16),
            pltpu.VMEM((width, seq), BF16),
            pltpu.VMEM((depth, own), BF16),
            pltpu.VMEM((nwa, nta, width, PAD), BF16),
            pltpu.VMEM((nta, wdepth, width), BF16),
            pltpu.VMEM((nta, wdepth, width), BF16),
            pltpu.VMEM((depth, own), BF16),
            pltpu.VMEM((nwa, 8, wide), F32),
            pltpu.VMEM((nwa, 8, wide), F32),
            pltpu.VMEM((8, wide), F32),
            pltpu.VMEM((nta, 8, wide), F32),
            dma((2, nta, max(nz, 2))),
            dma((2, nwa, nz)),
            dma((2, nz)),
            dma((2, 2, nz)),
            dma((2, nwa, nz)),
            dma((2, nwa, nz)),
            dma((2, nta)),
            dma((2, nwa)),
            dma((2, nta)),
            dma((2,)),
            dma((2, 8, nz)),
            dma((2, 2, nz)),
        ],
        compiler_params=pltpu.CompilerParams(
            collective_id=2, has_side_effects=True, vmem_limit_bytes=VMEM_BYTES
        ),
        cost_estimate=pl.CostEstimate(
            flops=4 * 10**9, bytes_accessed=80 * 10**6, transcendentals=0
        ),
    )(
        dattended, outown, dresid, xown, terms, mixed, zinv, lens, ln, pfull, layer, weights, wgrad,
        vcol, vrow,
    )


def logits_kernel(terms, scaled, value, shift, lens, out):
    nta = scaled.shape[0]
    cols = terms.shape[2]
    stacked = jnp.concatenate([scaled[s] for s in range(nta)], axis=0)
    values = jnp.concatenate([value[s] for s in range(nta)], axis=0)
    made = lax.dot_general(stacked, values, ROWS_TN, preferred_element_type=F32)
    where = (nta * 8, cols)
    place = lax.broadcasted_iota(jnp.int32, where, 1) + pl.program_id(1) * cols
    first = lax.broadcasted_iota(jnp.int32, where, 0) % 8 == 0
    valid = jnp.logical_and(place.astype(F32) < lens[:, 0:1], first)
    valid = jnp.where(valid, 1.0, 0.0).astype(BF16)
    high = shift[0].astype(BF16)
    rest = (shift[0] - high.astype(F32)).astype(BF16)
    made = made - lax.dot_general(high, valid, ROWS_TN, preferred_element_type=F32)
    made = made - lax.dot_general(rest, valid, ROWS_TN, preferred_element_type=F32)
    out[0] = terms[0].astype(F32) * made


def run_logits(terms, scaled, value, shift, lens):
    heads, query, seq = terms.shape
    nta, width, _ = scaled.shape
    hdim = width // heads
    cols = min(1024, seq)
    return pl.pallas_call(
        logits_kernel,
        grid=(heads, seq // cols),
        out_shape=shape_of((heads, query, seq), F32),
        in_specs=[
            pl.BlockSpec((1, query, cols), lambda h, k: (h, 0, k)),
            pl.BlockSpec((nta, hdim, query), lambda h, k: (0, h, 0)),
            pl.BlockSpec((nta, hdim, cols), lambda h, k: (0, h, k)),
            pl.BlockSpec((1, nta * 8, query), lambda h, k: (h, 0, 0)),
            pl.BlockSpec(lens.shape, lambda h, k: (0, 0)),
        ],
        out_specs=pl.BlockSpec((1, query, cols), lambda h, k: (h, 0, k)),
        compiler_params=pltpu.CompilerParams(vmem_limit_bytes=VMEM_BYTES),
        cost_estimate=pl.CostEstimate(
            flops=2 * 10**9, bytes_accessed=16 * 10**6, transcendentals=0
        ),
    )(terms, scaled, value, shift, lens)


def on_device_fast(
    dims,
    tokens,
    seq_lengths,
    norm1_gain,
    norm1_bias,
    value_weight,
    value_bias,
    synth_logits,
    out_weight,
    out_bias,
    norm2_gain,
    norm2_bias,
    up_weight,
    up_bias,
    down_weight,
    down_bias,
    cotangent,
):
    nwa, nta = dims
    width = tokens.shape[0]
    slim = ((0, 0), (0, PAD - out_weight.shape[1]))
    packed = jnp.concatenate(
        [up_weight, down_weight.T, jnp.pad(out_weight, slim), jnp.pad(value_weight.T, slim)], axis=1
    )
    per_feature = (
        norm1_gain,
        norm1_bias,
        value_bias,
        out_bias,
        norm2_gain,
        norm2_bias,
        down_bias,
    )
    pcol = jnp.pad(jnp.stack(per_feature, axis=1), ((0, 0), (0, PAD - len(per_feature))))
    prow = jnp.broadcast_to(up_bias[None, :], (8, up_bias.shape[0]))
    ln = jnp.broadcast_to(seq_lengths.astype(F32)[:, None], (8, CHUNK))
    logits = synth_logits.transpose(1, 0, 2)
    (
        xown,
        cown,
        attended,
        weights,
        layer,
        value,
        terms,
        mixed,
        zinv,
        lens,
        pfull,
        rfull,
    ) = run_forward(dims, tokens, cotangent, packed, pcol, prow, ln, logits)
    outown, dattended, dresid, wgrad, vcol, vrow = run_middle(
        dims, attended, xown, cown, pfull, rfull, ln, weights
    )
    scaled, shift, output, tgrad, vgrad, vectors, wsum = run_backward(
        dims,
        dattended,
        outown,
        dresid,
        xown,
        terms,
        mixed,
        zinv,
        lens,
        ln,
        pfull,
        layer,
        weights,
        wgrad,
        vcol,
        vrow,
    )
    logits_grad = run_logits(terms, scaled, value, shift, lens)
    cols = up_weight.shape[1]
    gap = vectors.shape[1] - up_bias.shape[0]
    return (
        output,
        tgrad.astype(F32),
        vectors[0, :width],
        vectors[1, :width],
        vgrad,
        vectors[2, :width],
        logits_grad.transpose(1, 0, 2),
        wsum[:, 2 * cols : 2 * cols + out_weight.shape[1]],
        vectors[3, :width],
        vectors[4, :width],
        vectors[5, :width],
        wsum[:, :cols],
        vectors[0, gap:],
        wsum[:, cols : 2 * cols].T,
        vectors[6, :width],
    )


def fits(mesh):
    return mesh.shape["wa"] == 4 and mesh.shape["ta"] == 8


def solution(mesh):
    placed = (
        P("wa", "ta"),
        P("ta"),
        P("wa"),
        P("wa"),
        P("ta", "wa"),
        P("wa"),
        P("ta", "wa", None),
        P("wa", "ta"),
        P("wa"),
        P("wa"),
        P("wa"),
        P("wa", "ta"),
        P("wa"),
        P("ta", "wa"),
        P("wa"),
        P("wa", "ta"),
    )
    sizes = (mesh.shape["wa"], mesh.shape["ta"])
    body = functools.partial(on_device_fast, sizes) if fits(mesh) else on_device
    return jax.shard_map(
        body,
        mesh=mesh,
        in_specs=placed,
        out_specs=(
            P("wa", "ta"),
            P("wa", "ta"),
            P("wa"),
            P("wa"),
            P("ta", "wa"),
            P("wa"),
            P("ta", "wa", None),
            P("wa", "ta"),
            P("wa"),
            P("wa"),
            P("wa"),
            P("wa", "ta"),
            P("wa"),
            P("ta", "wa"),
            P("wa"),
        ),
        check_vma=False,
    )
```

```python
import functools

import jax
import jax.numpy as jnp
from jax import lax
from jax.experimental import pallas as pl
from jax.experimental.pallas import tpu as pltpu
from jax.sharding import PartitionSpec as P

D = 768


EPSILON = 1e-05
ALONG_FEATURES = (((1,), (1,)), ((), ()))
ALONG_ROWS = (((0,), (0,)), ((), ()))


def row_statistics(first_term, second_term):
    return lax.psum((jnp.sum(first_term, axis=1), jnp.sum(second_term, axis=1)), "wa")


def all_features(features_part):
    return lax.all_gather(features_part, "wa", axis=1, tiled=True)


def feature_share(partial_sum):
    return lax.psum_scatter(partial_sum, "wa", scatter_dimension=1, tiled=True)


def norm_forward(inputs, norm_gain, norm_bias):
    row_total, row_squares = row_statistics(inputs, inputs * inputs)
    row_mean = row_total / D
    variance = row_squares / D - row_mean * row_mean
    inverse = lax.rsqrt(variance + EPSILON)
    normed = (inputs - row_mean[:, None]) * inverse[:, None]
    return (normed * norm_gain + norm_bias, normed, inverse)


def norm_backward(incoming, normed, inverse, norm_gain):
    scaled = incoming * norm_gain
    row_total, row_along = row_statistics(scaled, scaled * normed)
    return inverse[:, None] * (scaled - row_total[:, None] / D - normed * row_along[:, None] / D)


def weights_of(logit_rows, length_all):
    seq_len = logit_rows.shape[2]
    key_valid = (jnp.arange(seq_len)[None, :] < length_all[:, None]).astype(jnp.bfloat16)
    terms = jnp.exp(logit_rows.astype(jnp.float32)).astype(jnp.bfloat16)
    sums = jnp.einsum("phk,sk->sph", terms, key_valid, preferred_element_type=jnp.float32)
    return (terms, sums, key_valid)


def attend(terms, sums, value_all, query_rows):
    mixed = jnp.einsum("phk,skhd->sphd", terms, value_all, preferred_element_type=jnp.float32)
    mixed = mixed / sums[..., None]
    return (mixed, (mixed * query_rows[:, :, None, None]).astype(jnp.bfloat16))


def attend_back(terms, sums, key_valid, value_all, mixed, grad_rows):
    along = jnp.sum(grad_rows.astype(jnp.float32) * mixed, axis=-1) / sums
    scaled = (grad_rows.astype(jnp.float32) / sums[..., None]).astype(jnp.bfloat16)
    dvalue_part = jnp.einsum("phk,sphd->skhd", terms, scaled, preferred_element_type=jnp.float32)
    dlogits = jnp.einsum("sphd,skhd->phk", scaled, value_all, preferred_element_type=jnp.float32)
    high = along.astype(jnp.bfloat16)
    rest = (along - high.astype(jnp.float32)).astype(jnp.bfloat16)
    shift = sum(
        jnp.einsum("sph,sk->phk", part, key_valid, preferred_element_type=jnp.float32)
        for part in (high, rest)
    )
    return (dvalue_part, terms.astype(jnp.float32) * (dlogits - shift))


def on_device(
    tokens,
    seq_lengths,
    norm1_gain,
    norm1_bias,
    value_weight,
    value_bias,
    synth_logits,
    out_weight,
    out_bias,
    norm2_gain,
    norm2_bias,
    up_weight,
    up_bias,
    down_weight,
    down_bias,
    cotangent,
):
    rows_dev = tokens.shape[1]
    local_width = tokens.shape[0]
    seq_count = seq_lengths.shape[0]
    seq_len = synth_logits.shape[2]
    head_count = synth_logits.shape[1]
    head_dim = local_width // head_count
    value_cols, out_rows, up_rows, down_cols = (
        lax.all_gather(value_weight, "ta", axis=0, tiled=True),
        lax.all_gather(out_weight, "ta", axis=1, tiled=True),
        lax.all_gather(up_weight, "ta", axis=1, tiled=True),
        lax.all_gather(down_weight, "ta", axis=0, tiled=True),
    )
    up_block, down_block = (
        lax.all_to_all(up_rows.T, "wa", split_axis=0, concat_axis=1, tiled=True),
        lax.all_to_all(down_cols, "wa", split_axis=0, concat_axis=1, tiled=True),
    )
    inputs = tokens.T.astype(jnp.float32)
    pre_one, normed_one, inverse_one = norm_forward(inputs, norm1_gain, norm1_bias)
    layer_one = all_features(pre_one.astype(jnp.bfloat16))
    values = (
        jnp.dot(layer_one, value_cols, preferred_element_type=jnp.float32) + value_bias
    ).astype(jnp.bfloat16)
    value_heads = values.reshape(seq_count, seq_len, head_count, head_dim)
    positions = jnp.arange(seq_len)
    key_valid = positions[None, :] < seq_lengths[:, None]
    query_valid = key_valid.astype(jnp.float32)
    length_all = lax.all_gather(seq_lengths, "ta", axis=0, tiled=True)
    block_rows = synth_logits.shape[0]
    value_all = lax.all_gather(
        value_heads * key_valid[:, :, None, None].astype(jnp.bfloat16), "ta", axis=0, tiled=True
    )
    terms, sums, key_valid_all = weights_of(synth_logits, length_all)
    block_positions = lax.axis_index("ta") * block_rows + jnp.arange(block_rows)
    query_rows = (block_positions[None, :] < length_all[:, None]).astype(jnp.float32)
    mixed_rows, mixed_low = attend(terms, sums, value_all, query_rows)
    attended = lax.all_to_all(mixed_low, "ta", split_axis=0, concat_axis=1, tiled=True)
    attended = attended.reshape(rows_dev, local_width)
    branch = (
        feature_share(jnp.dot(attended, out_rows, preferred_element_type=jnp.float32)) + out_bias
    )
    resid = inputs + branch
    pre_two, normed_two, inverse_two = norm_forward(resid, norm2_gain, norm2_bias)
    layer_two = all_features(pre_two.astype(jnp.bfloat16))
    upper = (
        lax.dot_general(layer_two, up_block, ALONG_FEATURES, preferred_element_type=jnp.float32)
        + up_bias
    )
    hidden, gelu_back = jax.vjp(jax.nn.gelu, upper)
    hidden_low = hidden.astype(jnp.bfloat16)
    feed = (
        feature_share(jnp.dot(hidden_low, down_block, preferred_element_type=jnp.float32))
        + down_bias
    )
    output = (resid + feed).astype(jnp.bfloat16)
    cotangent_rows = cotangent.T
    grad_in = cotangent_rows.astype(jnp.float32)
    grad_full = all_features(cotangent_rows)
    dhidden = lax.dot_general(
        grad_full, down_block, ALONG_FEATURES, preferred_element_type=jnp.float32
    )
    dupper = gelu_back(dhidden)[0].astype(jnp.bfloat16)
    down_part = lax.dot_general(
        hidden_low, grad_full, ALONG_ROWS, preferred_element_type=jnp.float32
    )
    up_part = lax.dot_general(dupper, layer_two, ALONG_ROWS, preferred_element_type=jnp.float32)
    up_bias_part = jnp.sum(dupper.astype(jnp.float32), axis=0)
    down_bias_part = jnp.sum(grad_in, axis=0)
    dlayer_two = feature_share(jnp.dot(dupper, up_block, preferred_element_type=jnp.float32))
    gain_two_part = jnp.sum(dlayer_two * normed_two, axis=0)
    bias_two_part = jnp.sum(dlayer_two, axis=0)
    dresid = grad_in + norm_backward(dlayer_two, normed_two, inverse_two, norm2_gain)
    dbranch = dresid.astype(jnp.bfloat16)
    dbranch_full = all_features(dbranch)
    dattended = lax.dot_general(
        dbranch_full, out_rows, ALONG_FEATURES, preferred_element_type=jnp.float32
    ).astype(jnp.bfloat16)
    out_part = lax.dot_general(
        attended, dbranch_full, ALONG_ROWS, preferred_element_type=jnp.float32
    )
    out_bias_part = jnp.sum(dbranch.astype(jnp.float32), axis=0)
    grad_heads = dattended.reshape(seq_count, seq_len, head_count, head_dim)
    grad_heads = grad_heads * query_valid[:, :, None, None].astype(jnp.bfloat16)
    grad_block = lax.all_to_all(grad_heads, "ta", split_axis=1, concat_axis=0, tiled=True)
    dvalue_part, logits_grad = attend_back(
        terms, sums, key_valid_all, value_all, mixed_rows, grad_block
    )
    dvalue_rows = dvalue_part.astype(jnp.bfloat16).reshape(-1, local_width)
    dvalue_rows = lax.psum_scatter(dvalue_rows, "ta", scatter_dimension=0, tiled=True)
    dvalues = dvalue_rows * query_valid.reshape(rows_dev, 1).astype(jnp.bfloat16)
    value_part = lax.dot_general(layer_one, dvalues, ALONG_ROWS, preferred_element_type=jnp.float32)
    value_bias_part = jnp.sum(dvalues.astype(jnp.float32), axis=0)
    dlayer_one = feature_share(
        lax.dot_general(dvalues, value_cols, ALONG_FEATURES, preferred_element_type=jnp.float32)
    )
    gain_one_part = jnp.sum(dlayer_one * normed_one, axis=0)
    bias_one_part = jnp.sum(dlayer_one, axis=0)
    tokens_grad = dresid + norm_backward(dlayer_one, normed_one, inverse_one, norm1_gain)
    up_back, down_back = (
        lax.all_to_all(up_part, "wa", split_axis=1, concat_axis=0, tiled=True),
        lax.all_to_all(down_part, "wa", split_axis=1, concat_axis=0, tiled=True),
    )
    value_grad, out_grad, up_grad, down_grad = (
        lax.psum_scatter(value_part, "ta", scatter_dimension=0, tiled=True),
        lax.psum_scatter(out_part, "ta", scatter_dimension=1, tiled=True),
        lax.psum_scatter(up_back, "ta", scatter_dimension=0, tiled=True),
        lax.psum_scatter(down_back, "ta", scatter_dimension=0, tiled=True),
    )
    vector_grads = lax.psum(
        (
            gain_one_part,
            bias_one_part,
            value_bias_part,
            out_bias_part,
            gain_two_part,
            bias_two_part,
            up_bias_part,
            down_bias_part,
        ),
        "ta",
    )
    return (
        output.T,
        tokens_grad.T,
        vector_grads[0],
        vector_grads[1],
        value_grad,
        vector_grads[2],
        logits_grad,
        out_grad,
        vector_grads[3],
        vector_grads[4],
        vector_grads[5],
        up_grad.T,
        vector_grads[6],
        down_grad,
        vector_grads[7],
    )


MESH = pl.DeviceIdType.MESH
ROWS_NT = (((1,), (1,)), ((), ()))
ROWS_TN = (((0,), (0,)), ((), ()))
F32 = jnp.float32
BF16 = jnp.bfloat16
VMEM_BYTES = 60 * 2**20
CHUNK = 128
PAD = 128
AHEAD = 1


def whole(count):
    return [pl.BlockSpec(memory_space=pltpu.VMEM)] * count


def anywhere(count):
    return [pl.BlockSpec(memory_space=pl.ANY)] * count


def shape_of(shape, dtype):
    return jax.ShapeDtypeStruct(shape, dtype)


def lanes(start, size=CHUNK):
    return pl.ds(pl.multiple_of(start, CHUNK), size)


def rows_at(start, size, unit):
    return pl.ds(pl.multiple_of(start, unit), size)


class Place:
    def __init__(self, nwa, nta):
        self.nwa, self.nta, self.nz = nwa, nta, nta // 2
        self.wa = lax.axis_index("wa")
        self.ta = lax.axis_index("ta")
        self.z = self.ta // 2
        self.c = self.ta % 2
        self.peer = self.ta + 1 - 2 * self.c
        self.wx = self.wa + 1 - 2 * (self.wa % 2)
        self.wy = (self.wa + 2) % 4
        self.wd = 3 - self.wa

    def enter(self):
        barrier = pltpu.get_barrier_semaphore()
        total = self.nwa * self.nta

        def greet(step, carry):
            w = (self.wa + step // self.nta) % self.nwa
            t = (self.ta + step % self.nta) % self.nta
            pl.semaphore_signal(barrier, inc=1, device_id=(w, t), device_id_type=MESH)
            return carry

        lax.fori_loop(1, total, greet, 0)
        pl.semaphore_wait(barrier, total - 1)


def send(src, dst, ssem, rsem, device):
    return pltpu.make_async_remote_copy(
        src_ref=src,
        dst_ref=dst,
        send_sem=ssem,
        recv_sem=rsem,
        device_id=device,
        device_id_type=MESH,
    )


def when(condition):
    return pl.when(condition)


def norm_stats(block):
    width = block.shape[0]
    mean = jnp.sum(block, axis=0, keepdims=True) / width
    centred = block - mean
    variance = jnp.sum(centred * centred, axis=0, keepdims=True) / width
    inverse = lax.rsqrt(variance + EPSILON)
    return (centred * inverse, inverse)


def forward_kernel(
    dims,
    tok,
    cot,
    wp,
    prow,
    ln,
    logits,
    xown,
    cown,
    attended,
    weights,
    layer_out,
    value_out,
    term_out,
    mixed,
    zinv,
    lens,
    pfull,
    rfull,
    x,
    wvc,
    layer_pad,
    layer,
    value,
    terms,
    attsend,
    rows,
    sem_tok,
    sem_par,
    sem_ta,
    sem_val,
    sem_w,
    sem_cot,
    sem_att,
    sem_local,
    sem_out,
    sem_wv,
):
    nwa, nta = dims
    me = Place(nwa, nta)
    wa, ta, z, c = me.wa, me.ta, me.z, me.c
    nz = me.nz
    width = tok.shape[0]
    half = width // 2
    seq = tok.shape[1]
    part = seq // nz
    query = seq // nta
    slot = wvc.shape[1] // nta
    wdepth = wvc.shape[0] * nwa // nta
    heads = logits.shape[0]
    hdim = width // heads
    split = wp.shape[1] - PAD
    me.enter()
    done = []

    def block_rows(w, off=0, size=width):
        return rows_at(w * width + off, size, 32)

    def tok_copy(k, q):
        device = (me.wx if k == 0 else me.wy, ta)
        return send(
            tok.at[:, pl.ds(q * part, part)],
            x.at[block_rows(wa), pl.ds(q * part, part)],
            sem_tok.at[0, k, q],
            sem_tok.at[1, k, q],
            device,
        )

    def tok_fwd(k, q):
        source = me.wx if k == 0 else me.wy
        device = (me.wy if k == 0 else me.wx, ta)
        where = x.at[block_rows(source, k * half, half), pl.ds(q * part, part)]
        return send(where, where, sem_tok.at[0, 2 + k, q], sem_tok.at[1, 2 + k, q], device)

    own_x = pltpu.make_async_copy(tok, x.at[block_rows(wa)], sem_local.at[0])
    own_x.start()

    def tok_start(q):
        for k in range(2):
            tok_copy(k, q).start()

    def tok_turn(q):
        for k in range(2):
            tok_copy(k, q).wait_recv()
            tok_fwd(k, q).start()
        if q + AHEAD < nz:
            tok_start(q + AHEAD)

    for q in range(AHEAD):
        tok_start(q)

    def par_copy(step):
        w = (wa + step) % nwa
        return send(prow, rows.at[wa], sem_par.at[0, step], sem_par.at[1, step], (w, ta))

    def ta_copy(step):
        t = (ta + step) % nta
        return send(
            ln, lens.at[rows_at(ta * 8, 8, 8)], sem_ta.at[0, step], sem_ta.at[1, step], (wa, t)
        )

    def wv_column(b, core):
        return wvc.at[:, lanes((2 * b + core) * slot)]

    def wv_z(step):
        b = (z + step) % nz
        src = wp.at[:, pl.ds(split, PAD)]
        return send(
            src, wv_column(z, c), sem_wv.at[0, 0, step], sem_wv.at[1, 0, step], (wa, 2 * b + c)
        )

    def wv_core(step, core):
        where = wv_column((z - step + nz) % nz, core)
        return send(where, where, sem_wv.at[0, 1, step], sem_wv.at[1, 1, step], (wa, me.peer))

    own_wv = pltpu.make_async_copy(wp.at[:, pl.ds(split, PAD)], wv_column(z, c), sem_local.at[1])
    own_wv.start()
    for step in range(nz - 1, 0, -1):
        wv_z(step).start()
    for step in range(1, nwa):
        par_copy(step).start()
    for step in range(1, nta):
        ta_copy(step).start()
    rows[wa] = prow[...]
    lens[rows_at(ta * 8, 8, 8), :] = ln[...]
    own_wv.wait()
    wv_core(0, c).start()

    own_w = pltpu.make_async_copy(wp, weights.at[wa, ta], sem_local.at[2])
    own_w.start()

    def w_line(up, b, own):
        t = 2 * b + c
        where = weights.at[wa, t]
        k = 0 if up else 1
        return send(
            wp if own else where,
            where,
            sem_w.at[0, k, b],
            sem_w.at[1, k, b],
            (wa, ta + 2 if up else ta - 2),
        )

    layer_pad[...] = jnp.zeros_like(layer_pad)
    for h in range(heads):
        terms[h] = jnp.exp(logits[h].astype(F32)).astype(BF16)
    out_terms = pltpu.make_async_copy(terms, term_out, sem_local.at[3])
    out_terms.start()

    for step in range(1, nz):
        wv_z(step).wait_recv()
        wv_core(step, c).start()
    @pl.when(z < nz - 1)
    def _():
        w_line(True, z, True).start()

    @pl.when(z > 0)
    def _():
        w_line(False, z, True).start()

    tok_turn(0)
    for step in range(1, nwa):
        par_copy(step).wait_recv()
    gap = 2 * CHUNK
    for w in range(nwa):
        piece = jnp.concatenate([rows[w, :, :gap], jnp.zeros((PAD - 8, gap), F32)], axis=0)
        pfull[w * width : (w + 1) * width, :] = piece.T[:width]
        wide = rows.shape[2] - gap
        rfull[:, w * wide : (w + 1) * wide] = rows[w, :, gap:]
    for step in range(1, nta):
        ta_copy(step).wait_recv()
    for step in range(nz):
        wv_core(step, 1 - c).wait_recv()
    own_x.wait()

    positions = lax.broadcasted_iota(jnp.int32, (nta * 8, seq), 1).astype(F32)
    key_valid = jnp.where(positions < lens[:, 0:1], 1.0, 0.0).astype(BF16)
    for h in range(heads):
        sums = lax.dot_general(key_valid, terms[h], ROWS_NT, preferred_element_type=F32)
        zinv[h] = 1.0 / sums

    def value_copy(kind, b, q, core):
        where = value.at[2 * b + core, :, pl.ds(q * part, part)]
        t = (ta + 2, ta - 2, me.peer)[kind]
        return send(where, where, sem_val.at[0, kind, b, q], sem_val.at[1, kind, b, q], (wa, t))

    def w_plane(k, b):
        device = (me.wx if k == 0 else me.wy, ta)
        where = weights.at[wa, 2 * b + c]
        return send(where, where, sem_w.at[0, 2 + k, b], sem_w.at[1, 2 + k, b], device)

    def w_diag(k, b, source):
        device = (me.wy if k == 0 else me.wx, ta)
        where = weights.at[source, 2 * b + c, pl.ds(k * half, half)]
        return send(where, where, sem_w.at[0, 4 + k, b], sem_w.at[1, 4 + k, b], device)

    def w_core(r, b, core):
        source = (wa, me.wx, me.wy, me.wd)[r]
        where = weights.at[source, 2 * b + core]
        return send(where, where, sem_w.at[0, 6 + r, b], sem_w.at[1, 6 + r, b], (wa, me.peer))

    def w_plane_start(b):
        w_plane(0, b).start()
        w_plane(1, b).start()
        w_core(0, b, c).start()

    def w_forward(b):
        w_plane(0, b).wait_recv()
        w_diag(0, b, me.wx).start()
        w_core(1, b, c).start()
        w_plane(1, b).wait_recv()
        w_diag(1, b, me.wy).start()
        w_core(2, b, c).start()

    def w_finish(b):
        for k in range(2):
            w_diag(k, b, me.wd).wait_recv()
        w_core(3, b, c).start()

    def w_hop(h):
        @pl.when(z - 1 - h >= 0)
        def _():
            w_line(True, z - 1 - h, False).wait_recv()

            @pl.when(z < nz - 1)
            def _():
                w_line(True, z - 1 - h, False).start()

        @pl.when(z + 1 + h < nz)
        def _():
            w_line(False, z + 1 + h, False).wait_recv()

            @pl.when(z > 0)
            def _():
                w_line(False, z + 1 + h, False).start()

    def at_hop(h, act):
        @pl.when(z - 1 - h >= 0)
        def _():
            act(z - 1 - h)

        @pl.when(z + 1 + h < nz)
        def _():
            act(z + 1 + h)

    for q in range(nz):
        cols = pl.ds(q * part, part)
        if q + 1 < nz:
            tok_turn(q + 1)
        for k in range(2):
            where = x.at[block_rows(me.wd, k * half, half), cols]
            send(
                where,
                where,
                sem_tok.at[0, 2 + k, q],
                sem_tok.at[1, 2 + k, q],
                (me.wy if k == 0 else me.wx, ta),
            ).wait_recv()
        normed, _ = norm_stats(x[:, cols].astype(F32))
        low = (normed * pfull[:, 0:1] + pfull[:, 1:2]).astype(BF16)
        layer[:, cols] = low
        for t in range(nta):
            layer_pad[t * slot : t * slot + wdepth, :] = low[t * wdepth : (t + 1) * wdepth]
        made = jnp.dot(wvc[...], layer_pad[...], preferred_element_type=F32)
        made = made + pfull[block_rows(wa), :][:, 2:3]
        place = lax.broadcasted_iota(jnp.int32, (width, part), 1) + q * part
        made = jnp.where(place.astype(F32) < ln[0:1, 0:1], made, 0.0)
        value[ta, :, cols] = made.astype(BF16)
        xown[:, pl.ds(q * CHUNK, CHUNK)] = x[:, lanes(q * part + wa * CHUNK)]

        @pl.when(z < nz - 1)
        def _():
            value_copy(0, z, q, c).start()

        @pl.when(z > 0)
        def _():
            value_copy(1, z, q, c).start()

        value_copy(2, z, q, c).start()
        if q < nz - 1:
            w_hop(q)
    out_layer = pltpu.make_async_copy(layer, layer_out, sem_local.at[4])
    out_layer.start()

    def cot_copy(step, q):
        w = (wa + step) % nwa
        return send(
            cot.at[:, lanes(q * part + w * CHUNK)],
            cown.at[block_rows(wa), pl.ds(q * CHUNK, CHUNK)],
            sem_cot.at[0, step, q],
            sem_cot.at[1, step, q],
            (w, ta),
        )

    def cot_own(q):
        return pltpu.make_async_copy(
            cot.at[:, lanes(q * part + wa * CHUNK)],
            cown.at[block_rows(wa), pl.ds(q * CHUNK, CHUNK)],
            sem_cot.at[0, 0, q],
        )

    own_w.wait()

    w_plane_start(z)
    for h in range(nz - 1):
        at_hop(h, w_plane_start)
    for q in range(nz):
        cot_own(q).start()
        for step in range(1, nwa):
            cot_copy(step, q).start()

    def att_copy(s, j):
        return send(
            attsend.at[s, :, pl.ds(j * CHUNK, CHUNK)],
            attended.at[block_rows(wa), lanes(z * CHUNK)],
            sem_att.at[0, s, j],
            sem_att.at[1, wa, z],
            (2 * c + j, s),
        )

    def att_local(s, j):
        return pltpu.make_async_copy(
            attsend.at[s, :, pl.ds(j * CHUNK, CHUNK)],
            attended.at[block_rows(wa), lanes(z * CHUNK)],
            sem_att.at[0, s, j],
        )

    def is_self(s, j):
        return jnp.logical_and(s == ta, 2 * c + j == wa)

    def mix(b):
        for core in range(2):
            s = 2 * b + core
            pltpu.make_async_copy(value.at[s], value_out.at[s], sem_out.at[s]).start()
        length = [lens[rows_at((2 * b + core) * 8, 8, 8), :][0:1, 0:1] for core in range(2)]
        place = lax.broadcasted_iota(jnp.int32, (hdim, query), 1) + ta * query
        place = place.astype(F32)
        for h in range(heads):
            group = slice(h * hdim, (h + 1) * hdim)
            pair = jnp.concatenate([value[2 * b, group, :], value[2 * b + 1, group, :]], axis=0)
            both = lax.dot_general(pair, terms[h], ROWS_NT, preferred_element_type=F32)
            for core in range(2):
                s = 2 * b + core
                inverse = zinv[h, rows_at(s * 8, 8, 8), :][0:1]
                one = both[core * hdim : (core + 1) * hdim] * inverse
                mixed[s, group, :] = one
                one = jnp.where(place < length[core], one, 0.0)
                attsend[s, group, :] = one.astype(BF16)
        for core in range(2):
            s = 2 * b + core
            for j in range(2):

                @pl.when(is_self(s, j))
                def _():
                    att_local(s, j).start()

                @pl.when(jnp.logical_not(is_self(s, j)))
                def _():
                    att_copy(s, j).start()

    def core_ready(b):
        for q in range(nz):
            value_copy(2, b, q, 1 - c).wait_recv()

    for h in range(nz - 1):
        below, above = z - 1 - h, z + 1 + h
        for q in range(nz):

            @pl.when(below >= 0)
            def _():
                value_copy(0, below, q, c).wait_recv()

                @pl.when(z < nz - 1)
                def _():
                    value_copy(0, below, q, c).start()

                value_copy(2, below, q, c).start()

            @pl.when(above < nz)
            def _():
                value_copy(1, above, q, c).wait_recv()

                @pl.when(z > 0)
                def _():
                    value_copy(1, above, q, c).start()

                value_copy(2, above, q, c).start()

        if h == 0:
            core_ready(z)
            mix(z)

        @pl.when(below >= 0)
        def _():
            core_ready(below)
            mix(below)

        @pl.when(above < nz)
        def _():
            core_ready(above)
            mix(above)

        if h == 0:
            w_forward(z)
        else:
            at_hop(h - 1, w_forward)
    at_hop(nz - 2, w_forward)
    for b in range(nz):
        w_finish(b)

    for step in range(1, nta):
        ta_copy(step).wait_send()
    for step in range(nz):
        wv_core(step, c).wait_send()
        if step:
            wv_z(step).wait_send()
    for step in range(1, nwa):
        par_copy(step).wait_send()
        for q in range(nz):
            cot_copy(step, q).wait_send()
    for q in range(nz):
        cot_own(q).wait()
        for k in range(2):
            tok_copy(k, q).wait_send()
            tok_fwd(k, q).wait_send()
    for step in range(1, nwa):
        for q in range(nz):
            cot_copy(step, q).wait_recv()

    def line_sends(b, carry):
        reach_up = jnp.logical_and(b <= z, z < nz - 1)
        reach_down = jnp.logical_and(b >= z, z > 0)

        @pl.when(reach_up)
        def _():
            w_line(True, b, False).wait_send()
            for q in range(nz):
                value_copy(0, b, q, c).wait_send()

        @pl.when(reach_down)
        def _():
            w_line(False, b, False).wait_send()
            for q in range(nz):
                value_copy(1, b, q, c).wait_send()

        for q in range(nz):
            value_copy(2, b, q, c).wait_send()
        for k in range(2):
            w_plane(k, b).wait_send()
        w_diag(0, b, me.wx).wait_send()
        w_diag(1, b, me.wy).wait_send()
        for r in range(4):
            w_core(r, b, c).wait_send()
            w_core(r, b, 1 - c).wait_recv()
        return carry

    lax.fori_loop(0, nz, line_sends, 0)

    def att_sends(s, carry):
        pltpu.make_async_copy(value.at[s], value_out.at[s], sem_out.at[s]).wait()
        for j in range(2):

            @pl.when(is_self(s, j))
            def _():
                att_local(s, j).wait()

            @pl.when(jnp.logical_not(is_self(s, j)))
            def _():
                att_copy(s, j).wait_send()

        return carry

    lax.fori_loop(0, nta, att_sends, 0)
    mine = wa // 2

    def att_arrivals(k, carry):
        w, b = k // nz, k % nz

        @pl.when(jnp.logical_not(jnp.logical_and(w == wa, 2 * b + mine == ta)))
        def _():
            where = attended.at[block_rows(w), lanes(b * CHUNK)]
            send(where, where, sem_att.at[0, 0, 0], sem_att.at[1, w, b], (w, 2 * b + mine)).wait_recv()

        return carry

    lax.fori_loop(0, nwa * nz, att_arrivals, 0)
    out_terms.wait()
    out_layer.wait()


def run_forward(dims, tok, cot, wp, prow, ln, logits):
    nwa, nta = dims
    nz = nta // 2
    width, seq = tok.shape
    depth = width * nwa
    own = seq // nwa
    heads, query, _ = logits.shape
    slot = PAD
    dma = pltpu.SemaphoreType.DMA
    return pl.pallas_call(
        functools.partial(forward_kernel, dims),
        out_shape=(
            shape_of((depth, own), BF16),
            shape_of((depth, own), BF16),
            shape_of((depth, own), BF16),
            shape_of((nwa, nta) + wp.shape, BF16),
            shape_of((depth, seq), BF16),
            shape_of((nta, width, seq), BF16),
            shape_of((heads, query, seq), BF16),
            shape_of((nta, width, query), F32),
            shape_of((heads, nta * 8, query), F32),
            shape_of((nta * 8, CHUNK), F32),
            shape_of((depth, PAD), F32),
            shape_of((8, (prow.shape[1] - 2 * CHUNK) * nwa), F32),
        ),
        in_specs=anywhere(3) + whole(3),
        out_specs=tuple(whole(3) + anywhere(4) + whole(5)),
        scratch_shapes=[
            pltpu.VMEM((depth, seq), BF16),
            pltpu.VMEM((width, nta * slot), BF16),
            pltpu.VMEM((nta * slot, seq // nz), BF16),
            pltpu.VMEM((depth, seq), BF16),
            pltpu.VMEM((nta, width, seq), BF16),
            pltpu.VMEM((heads, query, seq), BF16),
            pltpu.VMEM((nta, width, query), BF16),
            pltpu.VMEM((nwa,) + prow.shape, F32),
            dma((2, 4, nz)),
            dma((2, nwa)),
            dma((2, nta)),
            dma((2, 3, nz, nz)),
            dma((2, 10, nz)),
            dma((2, nwa, nz)),
            dma((2, nta, max(nz, 2))),
            dma((8,)),
            dma((nta,)),
            dma((2, 2, nz)),
        ],
        compiler_params=pltpu.CompilerParams(
            collective_id=1, has_side_effects=True, vmem_limit_bytes=VMEM_BYTES
        ),
        cost_estimate=pl.CostEstimate(
            flops=4 * 10**9, bytes_accessed=60 * 10**6, transcendentals=2 * 10**6
        ),
    )(tok, cot, wp, prow, ln, logits)


def gelu_pair(u):
    root = 0.7978845608028654
    square = u * u
    bent = jnp.tanh(root * u * (1.0 + 0.044715 * square))
    low_half = 0.5 * (1.0 + bent)
    slope = low_half + 0.5 * u * (1.0 - bent * bent) * root * (1.0 + 3.0 * 0.044715 * square)
    return (u * low_half, slope)


def middle_kernel(
    dims,
    attended,
    xown,
    cown,
    pfull,
    rfull,
    ln,
    block,
    wo,
    out,
    dattended,
    dresid,
    wgrad,
    vcol,
    vrow,
    resid,
    normed,
    inverse,
    layer,
    layer_t,
    grad_t,
    feed,
    dlayer,
    wide,
    gblock,
    gwo,
    sem_g,
):
    nwa, nta = dims
    step = pl.program_id(0)
    last = pl.num_programs(0) - 1
    wa = lax.axis_index("wa")
    depth, own = xown.shape
    width = depth // nwa
    group, one = block.shape[1], block.shape[3] // 2
    cols = group * one
    wdepth = depth // nta

    def joined(start):
        parts = [block[:, g, :, start : start + one].reshape(depth, one) for g in range(group)]
        return jnp.concatenate(parts, axis=1)

    up, down_t = joined(0), joined(one)

    def wide_wo():
        joined = [
            jnp.concatenate([wo[w, t] for t in range(nta)], axis=1) for w in range(nwa)
        ]
        return jnp.concatenate(joined, axis=0)

    @pl.when(step == 0)
    def _():
        branch = lax.dot_general(wide_wo(), attended[...], ROWS_TN, preferred_element_type=F32)
        branch = jnp.concatenate(
            [branch[t * PAD : t * PAD + wdepth] for t in range(nta)], axis=0
        )
        res = xown[...].astype(F32) + branch + pfull[:, 3:4]
        resid[...] = res
        norm, inv = norm_stats(res)
        normed[...] = norm
        inverse[...] = jnp.broadcast_to(inv, inverse.shape)
        low = (norm * pfull[:, 4:5] + pfull[:, 5:6]).astype(BF16)
        layer[...] = low
        layer_t[...] = low.T
        grad_t[...] = cown[...].T
        feed[...] = jnp.zeros_like(feed)
        dlayer[...] = jnp.zeros_like(dlayer)

    at = lanes(step * cols, cols)
    upper = jnp.dot(layer_t[...], up, preferred_element_type=F32) + rfull[0:1, at]
    hidden, slope = gelu_pair(upper)
    hidden = hidden.astype(BF16)
    dhidden = jnp.dot(grad_t[...], down_t, preferred_element_type=F32)
    dupper = (dhidden * slope).astype(BF16)
    vrow[:, at] = jnp.broadcast_to(
        jnp.sum(dupper.astype(F32), axis=0, keepdims=True), (vrow.shape[0], cols)
    )
    feed[...] += lax.dot_general(down_t, hidden, ROWS_NT, preferred_element_type=F32)
    dlayer[...] += lax.dot_general(up, dupper, ROWS_NT, preferred_element_type=F32)
    gup = jnp.dot(layer[...], dupper, preferred_element_type=F32)
    gdown = jnp.dot(cown[...], hidden, preferred_element_type=F32)

    def put(at_step, slot):
        return pltpu.make_async_copy(
            gblock.at[slot],
            wgrad.at[:, at_step, :, :, pl.ds(0, 2 * one)],
            sem_g.at[slot],
        )

    for slot in range(2):

        @pl.when(step % 2 == slot)
        def _():
            @pl.when(step >= 2)
            def _():
                put(step - 2, slot).wait()

            for g in range(group):
                part = slice(g * one, (g + 1) * one)
                gblock[slot, :, g, :, :one] = gup[:, part].reshape(nwa, width, one).astype(BF16)
                gblock[slot, :, g, :, one:] = gdown[:, part].reshape(nwa, width, one).astype(BF16)
            put(step, slot).start()

    @pl.when(step == last)
    def _():
        grad = cown[...].astype(F32)
        out[...] = (resid[...] + feed[...] + pfull[:, 6:7]).astype(BF16)
        dl = dlayer[...]
        norm = normed[...]
        e = dl * pfull[:, 4:5]
        mean_e = jnp.sum(e, axis=0, keepdims=True) / depth
        mean_n = jnp.sum(e * norm, axis=0, keepdims=True) / depth
        dres = grad + inverse[0:1, :] * (e - mean_e - norm * mean_n)
        dresid[...] = dres
        low = dres.astype(BF16)
        vcol[...] = jnp.zeros_like(vcol)
        vcol[:, 3:4] = jnp.sum(low.astype(F32), axis=1, keepdims=True)
        vcol[:, 4:5] = jnp.sum(dl * norm, axis=1, keepdims=True)
        vcol[:, 5:6] = jnp.sum(dl, axis=1, keepdims=True)
        vcol[:, 6:7] = jnp.sum(grad, axis=1, keepdims=True)
        wide[...] = jnp.zeros_like(wide)
        for t in range(nta):
            wide[t * PAD : t * PAD + wdepth, :] = low[t * wdepth : (t + 1) * wdepth]
        da = jnp.dot(wide_wo(), wide[...], preferred_element_type=F32)
        lane = lax.broadcasted_iota(jnp.int32, (depth, own), 1)
        place = (lane // CHUNK) * (CHUNK * nwa) + lane % CHUNK + wa * CHUNK
        da = jnp.where(place.astype(F32) < ln[0:1, 0:1], da, 0.0)
        dattended[...] = da.astype(BF16)
        made = lax.dot_general(attended[...], wide[...], ROWS_NT, preferred_element_type=F32)
        for t in range(nta):
            piece = made[:, t * PAD : (t + 1) * PAD].reshape(nwa, width, PAD)
            gwo[:, t // 2, t % 2] = piece.astype(BF16)
        rest = pltpu.make_async_copy(
            gwo, wgrad.at[:, :, :, :, pl.ds(2 * one, PAD)], sem_g.at[2]
        )
        rest.start()
        put(last - 1, (nta // group - 2) % 2).wait()
        put(last, (nta // group - 1) % 2).wait()
        rest.wait()


def run_middle(dims, attended, xown, cown, pfull, rfull, ln, weights):
    nwa, nta = dims
    depth, own = xown.shape
    width = weights.shape[2]
    both = weights.shape[3] - 2 * PAD
    hidden = both // 2 * nta

    def full(shape):
        return pl.BlockSpec(shape, lambda i: (0,) * len(shape))

    group = 2
    block = pl.BlockSpec((nwa, group, width, both), lambda i: (0, i, 0, 0))
    wo = pl.BlockSpec((nwa, nta, width, PAD), lambda i: (0, 0, 0, both // PAD))
    return pl.pallas_call(
        functools.partial(middle_kernel, dims),
        grid=(nta // group,),
        out_shape=(
            shape_of((depth, own), BF16),
            shape_of((depth, own), BF16),
            shape_of((depth, own), F32),
            shape_of((nwa, nta // 2, 2, width, both + PAD), BF16),
            shape_of((depth, PAD), F32),
            shape_of((8, hidden), F32),
        ),
        in_specs=[
            full((depth, own)),
            full((depth, own)),
            full((depth, own)),
            full(pfull.shape),
            full(rfull.shape),
            full(ln.shape),
            block,
            wo,
        ],
        out_specs=(
            full((depth, own)),
            full((depth, own)),
            full((depth, own)),
            pl.BlockSpec(memory_space=pl.ANY),
            full((depth, PAD)),
            full((8, hidden)),
        ),
        scratch_shapes=[
            pltpu.VMEM((depth, own), F32),
            pltpu.VMEM((depth, own), F32),
            pltpu.VMEM((8, own), F32),
            pltpu.VMEM((depth, own), BF16),
            pltpu.VMEM((own, depth), BF16),
            pltpu.VMEM((own, depth), BF16),
            pltpu.VMEM((depth, own), F32),
            pltpu.VMEM((depth, own), F32),
            pltpu.VMEM((nta * PAD, own), BF16),
            pltpu.VMEM((2, nwa, group, width, both), BF16),
            pltpu.VMEM((nwa, nta // 2, 2, width, PAD), BF16),
            pltpu.SemaphoreType.DMA((3,)),
        ],
        compiler_params=pltpu.CompilerParams(vmem_limit_bytes=VMEM_BYTES),
        cost_estimate=pl.CostEstimate(
            flops=17 * 10**9, bytes_accessed=40 * 10**6, transcendentals=2 * 10**6
        ),
    )(attended, xown, cown, pfull, rfull, ln, weights, weights)


def backward_kernel(
    dims,
    dattended,
    outown,
    dresid_in,
    xown_in,
    terms_in,
    mixed_in,
    zinv,
    lens,
    ln,
    pfull,
    layer_in,
    weights,
    wgrad,
    vcol,
    vrow,
    scaled,
    shift,
    output,
    tgrad,
    vgrad,
    vectors,
    wsum,
    dresid,
    xown,
    terms,
    mixed,
    layer,
    normed,
    invs,
    wvt,
    gains,
    biases,
    da,
    partial,
    paired,
    up_in,
    down_in,
    gown,
    gpeer,
    first_x,
    first_y,
    second_x,
    second_y,
    gup_in,
    gdown_in,
    dvalue,
    dvown,
    wv,
    vsend,
    vrecv,
    tsend,
    csend,
    crecv,
    csum,
    crecv2,
    sem_da,
    sem_out,
    sem_core,
    sem_line,
    sem_dv,
    sem_tg,
    sem_v,
    sem_c,
    sem_c2,
    sem_local,
    sem_g,
    sem_gline,
):
    nwa, nta = dims
    me = Place(nwa, nta)
    wa, ta, z, c = me.wa, me.ta, me.z, me.c
    nz = me.nz
    depth, own = dresid.shape
    width = depth // nwa
    wdepth = depth // nta
    heads, query, seq = terms.shape
    hdim = width // heads
    part = seq // nz
    pairs = (
        (terms_in, terms),
        (mixed_in, mixed),
        (xown_in, xown),
        (dresid_in, dresid),
        (layer_in, layer),
    )
    fetch = [
        pltpu.make_async_copy(src, dst, sem_local.at[1 + i]) for i, (src, dst) in enumerate(pairs)
    ]
    for copy in fetch:
        copy.start()
    me.enter()

    def block_rows(w):
        return rows_at(w * width, width, 32)

    def da_copy(w, b, local):
        core = wa // 2
        src = dattended.at[block_rows(w), lanes(b * CHUNK)]
        dst = da.at[ta, :, lanes((wa % 2) * CHUNK)]
        if local:
            return pltpu.make_async_copy(src, dst, sem_da.at[0, w, b])
        return send(src, dst, sem_da.at[0, w, b], sem_da.at[1, ta, wa % 2], (w, 2 * b + core))

    def da_self(w, b):
        return jnp.logical_and(w == wa, 2 * b + wa // 2 == ta)

    def far(i):
        low_end = 1 - z // (nz // 2)
        return (nz - 1 - i) * low_end + i * (1 - low_end)

    def da_start(k, carry):
        w, b = (wa + k % nwa) % nwa, far(k // nwa)

        @pl.when(da_self(w, b))
        def _():
            da_copy(w, b, True).start()

        @pl.when(jnp.logical_not(da_self(w, b)))
        def _():
            da_copy(w, b, False).start()

        return carry

    lax.fori_loop(0, nwa * nz, da_start, 0)

    def back_copy(src, dst, sems, step, q):
        w = (wa + step) % nwa
        return send(
            src.at[block_rows(w), pl.ds(q * CHUNK, CHUNK)],
            dst.at[:, lanes(q * part + wa * CHUNK)],
            sems.at[0, step, q],
            sems.at[1, step, q],
            (w, ta),
        )

    def back_own(src, dst, sems, q):
        return pltpu.make_async_copy(
            src.at[block_rows(wa), pl.ds(q * CHUNK, CHUNK)],
            dst.at[:, lanes(q * part + wa * CHUNK)],
            sems.at[0, 0, q],
        )

    get_wv = pltpu.make_async_copy(
        weights.at[:, :, :, pl.ds(weights.shape[3] - PAD, PAD)], wv, sem_local.at[0]
    )
    get_wv.start()

    half = width // 2
    order = []
    for j in range(nz):
        for b in (nz - 1 - j, j):
            if b not in order:
                order.append(b)

    def g_core(b, core):
        return send(
            wgrad.at[:, b, core],
            gpeer.at[b],
            sem_g.at[0, 0, b],
            sem_g.at[1, 0, b],
            (wa, me.peer),
        )

    def g_load(b):
        return pltpu.make_async_copy(wgrad.at[:, b, c], gown.at[b], sem_g.at[0, 7, b])

    def g_first(k, r, b):
        near = me.wx if k == 0 else me.wy
        which = near if r == 0 else me.wd
        return send(
            gown.at[b, which, pl.ds(k * half, half)],
            (first_x if k == 0 else first_y).at[b, r],
            sem_g.at[0, 1 + 2 * k + r, b],
            sem_g.at[1, 1 + 2 * k + r, b],
            (near, ta),
        )

    def g_second(k, b):
        near = me.wy if k == 0 else me.wx
        return send(
            gown.at[b, near, pl.ds(k * half, half)],
            (second_x if k == 0 else second_y).at[b],
            sem_g.at[0, 5 + k, b],
            sem_g.at[1, 5 + k, b],
            (near, ta),
        )

    def g_add(b, which, k, extra):
        rows = pl.ds(k * half, half)
        gown[b, which, rows, :] = (
            gown[b, which, rows, :].astype(F32) + extra.astype(F32)
        ).astype(BF16)

    def g_cores(b):
        g_load(b).wait()
        g_core(b, c).wait_recv()
        for w in range(nwa):
            gown[b, w] = (gown[b, w].astype(F32) + gpeer[b, w].astype(F32)).astype(BF16)
        for k in range(2):
            for r in range(2):
                g_first(k, r, b).start()

    def g_plane(b):
        for k in range(2):
            for r in range(2):
                g_first(k, r, b).wait_recv()
            landed = first_x if k == 0 else first_y
            g_add(b, me.wy if k == 0 else me.wx, k, landed[b, 1])
            g_second(k, b).start()
            g_add(b, wa, k, landed[b, 0])

    def g_end(b):
        for k in range(2):
            g_second(k, b).wait_recv()
            g_add(b, wa, k, (second_x if k == 0 else second_y)[b])

    def g_line(up, j):
        k = 0 if up else 1
        target = nz - 1 - j if up else j
        return send(
            gown.at[target, wa],
            (gup_in if up else gdown_in).at[j],
            sem_gline.at[0, k, j],
            sem_gline.at[1, k, j],
            (wa, ta + 2 if up else ta - 2),
        )

    def g_hop(j):
        target = nz - 1 - j

        @pl.when(z < target)
        def _():
            @pl.when(z > 0)
            def _():
                g_line(True, j).wait_recv()
                gown[target, wa] = (
                    gown[target, wa].astype(F32) + gup_in[j].astype(F32)
                ).astype(BF16)

            g_line(True, j).start()

        @pl.when(z > j)
        def _():
            @pl.when(z < nz - 1)
            def _():
                g_line(False, j).wait_recv()
                gown[j, wa] = (gown[j, wa].astype(F32) + gdown_in[j].astype(F32)).astype(BF16)

            g_line(False, j).start()

    def g_final():
        @pl.when(z == 0)
        def _():
            g_line(False, 0).wait_recv()
            wsum[...] = gown[0, wa].astype(F32) + gdown_in[0].astype(F32)

        @pl.when(z == nz - 1)
        def _():
            g_line(True, 0).wait_recv()
            wsum[...] = gown[nz - 1, wa].astype(F32) + gup_in[0].astype(F32)

        for b in range(1, nz - 1):

            @pl.when(z == b)
            def _():
                g_line(True, nz - 1 - b).wait_recv()
                g_line(False, b).wait_recv()
                both = gup_in[nz - 1 - b].astype(F32) + gdown_in[b].astype(F32)
                wsum[...] = gown[b, wa].astype(F32) + both

    for b in order:
        g_core(b, 1 - c).start()
        g_load(b).start()

    def da_arrive(s, j):
        own_piece = jnp.logical_and(s == ta, 2 * c + j == wa)
        where = da.at[s, :, lanes(j * CHUNK)]

        @pl.when(own_piece)
        def _():
            da_copy(wa, z, True).wait()

        @pl.when(jnp.logical_not(own_piece))
        def _():
            send(where, where, sem_da.at[0, 0, 0], sem_da.at[1, s, j], (2 * c + j, s)).wait_recv()

    def da_sent(k, carry):
        w, b = (wa + k // nz) % nwa, k % nz

        @pl.when(jnp.logical_not(da_self(w, b)))
        def _():
            da_copy(w, b, False).wait_send()

        return carry

    def prepare(b):
        for core in range(2):
            for j in range(2):
                da_arrive(2 * b + core, j)
        for h in range(heads):
            group = slice(h * hdim, (h + 1) * hdim)
            both = []
            for s in (2 * b, 2 * b + 1):
                one = da[s, group, :].astype(F32) * zinv[h, s * 8 : s * 8 + 1, :]
                both.append(one.astype(BF16))
                scaled[s, group, :] = both[-1]
            made = jnp.dot(
                jnp.concatenate(both, axis=0), terms[h], preferred_element_type=F32
            ).astype(BF16)
            partial[2 * b, group, :] = made[:hdim]
            partial[2 * b + 1, group, :] = made[hdim:]
        core_copy(b, 1 - c).start()

    def shifts():
        for h in range(heads):
            group = slice(h * hdim, (h + 1) * hdim)
            for s in range(nta):
                inv = zinv[h, s * 8 : s * 8 + 1, :]
                one = da[s, group, :].astype(F32) * mixed[s, group, :]
                along = jnp.sum(one, axis=0, keepdims=True)
                shift[h, s * 8 : (s + 1) * 8, :] = jnp.broadcast_to(along * inv, (8, query))

    def core_copy(b, core):
        return send(
            partial.at[2 * b + core],
            paired.at[b],
            sem_core.at[0, b],
            sem_core.at[1, b],
            (wa, me.peer),
        )

    def out_start():
        for q in range(nz):
            back_own(outown, output, sem_out, q).start()
            for step in range(1, nwa):
                back_copy(outown, output, sem_out, step, q).start()

    def line_copy(up, j, q):
        k = 0 if up else 1
        cols = pl.ds(q * part, part)
        return send(
            partial.at[2 * (nz - 1 - j if up else j) + c, :, cols],
            (up_in if up else down_in).at[j, :, cols],
            sem_line.at[0, k, j, q],
            sem_line.at[1, k, j, q],
            (wa, ta + 2 if up else ta - 2),
        )

    ready = set()

    def core_ready(b):
        if b not in ready:
            ready.add(b)
            core_copy(b, c).wait_recv()

    def chip_sum(b, q):
        cols = pl.ds(q * part, part)
        return partial[2 * b + c, :, cols].astype(F32) + paired[b, :, cols].astype(F32)

    def line_step(up, j, q):
        target = nz - 1 - j if up else j
        landed = up_in if up else down_in
        cols = pl.ds(q * part, part)

        @pl.when(z < target if up else z > target)
        def _():
            first = z == (0 if up else nz - 1)

            @pl.when(jnp.logical_not(first))
            def _():
                line_copy(up, j, q).wait_recv()
                total = chip_sum(target, q) + landed[j, :, cols].astype(F32)
                partial[2 * target + c, :, cols] = total.astype(BF16)

            @pl.when(first)
            def _():
                partial[2 * target + c, :, cols] = chip_sum(target, q).astype(BF16)

            line_copy(up, j, q).start()

    def line(j):
        core_ready(nz - 1 - j)
        core_ready(j)
        for q in range(nz):
            line_step(True, j, q)
            line_step(False, j, q)

    fetch[0].wait()
    for b in order:
        g_cores(b)
    prepare(order[0])
    prepare(order[1])
    line(0)
    for b in order[2:]:
        prepare(b)
    for j in range(1, nz - 1):
        line(j)
    for b in range(nz):
        core_ready(b)

    fetch[1].wait()
    shifts()
    get_wv.wait()
    for t in range(nta):
        turned = jnp.concatenate([wv[w, t] for w in range(nwa)], axis=0).T
        wvt[t * wdepth : (t + 1) * wdepth, :] = turned[:wdepth]
    fetch[2].wait()
    fetch[3].wait()
    norm, inv = norm_stats(xown[...].astype(F32))
    normed[...] = norm
    invs[...] = jnp.broadcast_to(inv, invs.shape)
    gains[...] = jnp.zeros_like(gains)
    biases[...] = jnp.zeros_like(biases)
    fetch[4].wait()
    for b in order:
        g_plane(b)
    out_start()

    def dv_copy(step, q):
        w = (wa + step) % nwa
        return send(
            dvalue.at[:, lanes(q * part + w * CHUNK)],
            dvown.at[block_rows(wa), pl.ds(q * CHUNK, CHUNK)],
            sem_dv.at[0, step, q],
            sem_dv.at[1, step, q],
            (w, ta),
        )

    place = lax.broadcasted_iota(jnp.int32, (width, part), 1).astype(F32)

    def final(q):
        cols = pl.ds(q * part, part)
        key_valid = place + q * part < ln[0:1, 0:1]
        for b in range(nz):

            @pl.when(z == b)
            def _():
                total = chip_sum(b, q)
                if b > 0:
                    line_copy(True, nz - 1 - b, q).wait_recv()
                    total = total + up_in[nz - 1 - b, :, cols].astype(F32)
                if b < nz - 1:
                    line_copy(False, b, q).wait_recv()
                    total = total + down_in[b, :, cols].astype(F32)
                dvalue[:, cols] = jnp.where(key_valid, total, 0.0).astype(BF16)

        for step in range(1, nwa):
            dv_copy(step, q).start()
        dvown[block_rows(wa), q * CHUNK : (q + 1) * CHUNK] = dvalue[
            :, lanes(q * part + wa * CHUNK)
        ]

    for q in range(nz):
        final(q)

    vmade = lax.dot_general(layer[...], dvalue[...], ROWS_NT, preferred_element_type=F32)
    vsend[...] = vmade.astype(BF16).reshape(nta, wdepth, width)
    vbias = jnp.sum(dvalue[...].astype(F32), axis=1, keepdims=True)

    def v_copy(step):
        t = (ta + step) % nta
        return send(
            vsend.at[t], vrecv.at[step], sem_v.at[0, step], sem_v.at[1, step], (wa, t)
        )

    for step in range(1, nta):
        v_copy(step).start()

    for b in order:
        g_end(b)
    g_hop(0)
    for q in range(nz):
        cols = slice(q * CHUNK, (q + 1) * CHUNK)
        for step in range(1, nwa):
            dv_copy(step, q).wait_recv()
        dl = jnp.dot(wvt[...], dvown[:, cols], preferred_element_type=F32)
        norm = normed[:, cols]
        e = dl * pfull[:, 0:1]
        mean_e = jnp.sum(e, axis=0, keepdims=True) / depth
        mean_n = jnp.sum(e * norm, axis=0, keepdims=True) / depth
        made = dresid[:, cols] + invs[0:1, cols] * (e - mean_e - norm * mean_n)
        tsend[:, cols] = made.astype(BF16)
        back_own(tsend, tgrad, sem_tg, q).start()
        for step in range(1, nwa):
            back_copy(tsend, tgrad, sem_tg, step, q).start()
        gains[...] += dl * norm
        biases[...] += dl

    g_hop(1)
    gain = jnp.sum(gains[...], axis=1, keepdims=True)
    bias = jnp.sum(biases[...], axis=1, keepdims=True)
    column = lax.broadcasted_iota(jnp.int32, (depth, PAD), 1)
    cols = jnp.where(column == 0, gain, jnp.where(column == 1, bias, vcol[...]))
    wide = vrow.shape[1] // nwa
    gap = csend.shape[2] - wide
    for w in range(nwa):
        piece = cols[w * width : (w + 1) * width]
        piece = jnp.concatenate([piece, jnp.zeros((gap - width, PAD), F32)], axis=0)
        csend[w, :, :gap] = piece.T[:8]
        csend[w, :, gap:] = vrow[:, w * wide : (w + 1) * wide]

    def c_copy(step):
        w = (wa + step) % nwa
        return send(csend.at[w], crecv.at[step], sem_c.at[0, step], sem_c.at[1, step], (w, ta))

    for step in range(1, nwa):
        c_copy(step).start()
    crecv[0] = csend[wa]
    piece = jnp.concatenate(
        [jnp.broadcast_to(vbias, (width, PAD)), jnp.zeros((gap - width, PAD), F32)], axis=0
    )
    vb_row = jnp.concatenate([piece.T[:8], jnp.zeros((8, wide), F32)], axis=1)
    row = lax.broadcasted_iota(jnp.int32, vb_row.shape, 0)
    total = jnp.where(row == 2, vb_row, 0.0) + crecv[0]
    for step in range(1, nwa):
        c_copy(step).wait_recv()
        total = total + crecv[step]
    csum[...] = total

    def c2_copy(step):
        t = (ta + step) % nta
        return send(csum, crecv2.at[step], sem_c2.at[0, step], sem_c2.at[1, step], (wa, t))

    for step in range(1, nta):
        c2_copy(step).start()
    for j in range(2, nz - 1):
        g_hop(j)
    value_total = vsend[ta].astype(F32)
    for step in range(1, nta):
        v_copy(step).wait_recv()
        value_total = value_total + vrecv[step].astype(F32)
    vgrad[...] = value_total
    g_final()
    crecv2[0] = csum[...]
    for step in range(1, nta):
        c2_copy(step).wait_recv()
    full = jnp.zeros(csum.shape, F32)
    for t in range(nta):
        full = full + crecv2[(ta - t + nta) % nta]
    vectors[...] = full

    lax.fori_loop(0, nwa * nz, da_sent, 0)
    for step in range(1, nwa):
        for q in range(nz):
            back_copy(tsend, tgrad, sem_tg, step, q).wait()
            back_copy(outown, output, sem_out, step, q).wait()
            dv_copy(step, q).wait_send()
        c_copy(step).wait_send()
    for q in range(nz):
        back_own(outown, output, sem_out, q).wait()
        back_own(tsend, tgrad, sem_tg, q).wait()
    for step in range(1, nta):
        v_copy(step).wait_send()
        c2_copy(step).wait_send()
    for b in range(nz):
        core_copy(b, 1 - c).wait_send()
        g_core(b, 1 - c).wait_send()
        for k in range(2):
            g_first(k, 0, b).wait_send()
            g_first(k, 1, b).wait_send()
            g_second(k, b).wait_send()
    for j in range(nz - 1):

        @pl.when(z < nz - 1 - j)
        def _():
            for q in range(nz):
                line_copy(True, j, q).wait_send()
            g_line(True, j).wait_send()

        @pl.when(z > j)
        def _():
            for q in range(nz):
                line_copy(False, j, q).wait_send()
            g_line(False, j).wait_send()


def run_backward(
    dims, dattended, outown, dresid, xown, terms, mixed, zinv, lens, ln, pfull, layer, weights, wgrad, vcol, vrow
):
    nwa, nta = dims
    nz = nta // 2
    half, both = weights.shape[2] // 2, wgrad.shape[4]
    depth, own = dresid.shape
    width = depth // nwa
    heads, query, seq = terms.shape
    wdepth = depth // nta
    wide = 256 + vrow.shape[1] // nwa
    dma = pltpu.SemaphoreType.DMA
    return pl.pallas_call(
        functools.partial(backward_kernel, dims),
        out_shape=(
            shape_of((nta, width, query), BF16),
            shape_of((heads, nta * 8, query), F32),
            shape_of((width, seq), BF16),
            shape_of((width, seq), BF16),
            shape_of((wdepth, width), F32),
            shape_of((8, wide), F32),
            shape_of((width, both), F32),
        ),
        in_specs=anywhere(6) + whole(4) + anywhere(3) + whole(2),
        out_specs=tuple(whole(7)),
        scratch_shapes=[
            pltpu.VMEM((depth, own), F32),
            pltpu.VMEM((depth, own), BF16),
            pltpu.VMEM((heads, query, seq), BF16),
            pltpu.VMEM((nta, width, query), F32),
            pltpu.VMEM((depth, seq), BF16),
            pltpu.VMEM((depth, own), F32),
            pltpu.VMEM((8, own), F32),
            pltpu.VMEM((depth, depth), BF16),
            pltpu.VMEM((depth, CHUNK), F32),
            pltpu.VMEM((depth, CHUNK), F32),
            pltpu.VMEM((nta, width, query), BF16),
            pltpu.VMEM((nta, width, seq), BF16),
            pltpu.VMEM((nz, width, seq), BF16),
            pltpu.VMEM((nz - 1, width, seq), BF16),
            pltpu.VMEM((nz - 1, width, seq), BF16),
            pltpu.VMEM((nz, nwa, width, both), BF16),
            pltpu.VMEM((nz, nwa, width, both), BF16),
            pltpu.VMEM((nz, 2, half, both), BF16),
            pltpu.VMEM((nz, 2, half, both), BF16),
            pltpu.VMEM((nz, half, both), BF16),
            pltpu.VMEM((nz, half, both), BF16),
            pltpu.VMEM((nz - 1, width, both), BF16),
            pltpu.VMEM((nz - 1, width, both), BF16),
            pltpu.VMEM((width, seq), BF16),
            pltpu.VMEM((depth, own), BF16),
            pltpu.VMEM((nwa, nta, width, PAD), BF16),
            pltpu.VMEM((nta, wdepth, width), BF16),
            pltpu.VMEM((nta, wdepth, width), BF16),
            pltpu.VMEM((depth, own), BF16),
            pltpu.VMEM((nwa, 8, wide), F32),
            pltpu.VMEM((nwa, 8, wide), F32),
            pltpu.VMEM((8, wide), F32),
            pltpu.VMEM((nta, 8, wide), F32),
            dma((2, nta, max(nz, 2))),
            dma((2, nwa, nz)),
            dma((2, nz)),
            dma((2, 2, nz, nz)),
            dma((2, nwa, nz)),
            dma((2, nwa, nz)),
            dma((2, nta)),
            dma((2, nwa)),
            dma((2, nta)),
            dma((6,)),
            dma((2, 8, nz)),
            dma((2, 2, nz)),
        ],
        compiler_params=pltpu.CompilerParams(
            collective_id=2, has_side_effects=True, vmem_limit_bytes=VMEM_BYTES
        ),
        cost_estimate=pl.CostEstimate(
            flops=4 * 10**9, bytes_accessed=80 * 10**6, transcendentals=0
        ),
    )(
        dattended, outown, dresid, xown, terms, mixed, zinv, lens, ln, pfull, layer, weights, wgrad,
        vcol, vrow,
    )


def logits_kernel(terms, scaled, value, shift, lens, out):
    nta = scaled.shape[0]
    cols = terms.shape[2]
    stacked = jnp.concatenate([scaled[s] for s in range(nta)], axis=0)
    values = jnp.concatenate([value[s] for s in range(nta)], axis=0)
    made = lax.dot_general(stacked, values, ROWS_TN, preferred_element_type=F32)
    where = (nta * 8, cols)
    place = lax.broadcasted_iota(jnp.int32, where, 1) + pl.program_id(1) * cols
    first = lax.broadcasted_iota(jnp.int32, where, 0) % 8 == 0
    valid = jnp.logical_and(place.astype(F32) < lens[:, 0:1], first)
    valid = jnp.where(valid, 1.0, 0.0).astype(BF16)
    high = shift[0].astype(BF16)
    rest = (shift[0] - high.astype(F32)).astype(BF16)
    made = made - lax.dot_general(high, valid, ROWS_TN, preferred_element_type=F32)
    made = made - lax.dot_general(rest, valid, ROWS_TN, preferred_element_type=F32)
    out[0] = terms[0].astype(F32) * made


def run_logits(terms, scaled, value, shift, lens):
    heads, query, seq = terms.shape
    nta, width, _ = scaled.shape
    hdim = width // heads
    cols = min(1024, seq)
    return pl.pallas_call(
        logits_kernel,
        grid=(heads, seq // cols),
        out_shape=shape_of((heads, query, seq), F32),
        in_specs=[
            pl.BlockSpec((1, query, cols), lambda h, k: (h, 0, k)),
            pl.BlockSpec((nta, hdim, query), lambda h, k: (0, h, 0)),
            pl.BlockSpec((nta, hdim, cols), lambda h, k: (0, h, k)),
            pl.BlockSpec((1, nta * 8, query), lambda h, k: (h, 0, 0)),
            pl.BlockSpec(lens.shape, lambda h, k: (0, 0)),
        ],
        out_specs=pl.BlockSpec((1, query, cols), lambda h, k: (h, 0, k)),
        compiler_params=pltpu.CompilerParams(vmem_limit_bytes=VMEM_BYTES),
        cost_estimate=pl.CostEstimate(
            flops=2 * 10**9, bytes_accessed=16 * 10**6, transcendentals=0
        ),
    )(terms, scaled, value, shift, lens)


def on_device_fast(
    dims,
    tokens,
    seq_lengths,
    norm1_gain,
    norm1_bias,
    value_weight,
    value_bias,
    synth_logits,
    out_weight,
    out_bias,
    norm2_gain,
    norm2_bias,
    up_weight,
    up_bias,
    down_weight,
    down_bias,
    cotangent,
):
    nwa, nta = dims
    width = tokens.shape[0]
    slim = ((0, 0), (0, PAD - out_weight.shape[1]))
    packed = jnp.concatenate(
        [up_weight, down_weight.T, jnp.pad(out_weight, slim), jnp.pad(value_weight.T, slim)], axis=1
    )
    per_feature = (
        norm1_gain,
        norm1_bias,
        value_bias,
        out_bias,
        norm2_gain,
        norm2_bias,
        down_bias,
    )
    prow = jnp.pad(jnp.stack(per_feature), ((0, 1), (0, 2 * CHUNK - width)))
    prow = jnp.concatenate([prow, jnp.broadcast_to(up_bias, (8, up_bias.shape[0]))], axis=1)
    ln = jnp.broadcast_to(seq_lengths.astype(F32)[:, None], (8, CHUNK))
    logits = synth_logits.transpose(1, 0, 2)
    (
        xown,
        cown,
        attended,
        weights,
        layer,
        value,
        terms,
        mixed,
        zinv,
        lens,
        pfull,
        rfull,
    ) = run_forward(dims, tokens, cotangent, packed, prow, ln, logits)
    outown, dattended, dresid, wgrad, vcol, vrow = run_middle(
        dims, attended, xown, cown, pfull, rfull, ln, weights
    )
    scaled, shift, output, tgrad, vgrad, vectors, wsum = run_backward(
        dims,
        dattended,
        outown,
        dresid,
        xown,
        terms,
        mixed,
        zinv,
        lens,
        ln,
        pfull,
        layer,
        weights,
        wgrad,
        vcol,
        vrow,
    )
    logits_grad = run_logits(terms, scaled, value, shift, lens)
    cols = up_weight.shape[1]
    gap = vectors.shape[1] - up_bias.shape[0]
    return (
        output,
        tgrad.astype(F32),
        vectors[0, :width],
        vectors[1, :width],
        vgrad,
        vectors[2, :width],
        logits_grad.transpose(1, 0, 2),
        wsum[:, 2 * cols : 2 * cols + out_weight.shape[1]],
        vectors[3, :width],
        vectors[4, :width],
        vectors[5, :width],
        wsum[:, :cols],
        vectors[0, gap:],
        wsum[:, cols : 2 * cols].T,
        vectors[6, :width],
    )


def fits(mesh):
    return mesh.shape["wa"] == 4 and mesh.shape["ta"] == 8


def solution(mesh):
    placed = (
        P("wa", "ta"),
        P("ta"),
        P("wa"),
        P("wa"),
        P("ta", "wa"),
        P("wa"),
        P("ta", "wa", None),
        P("wa", "ta"),
        P("wa"),
        P("wa"),
        P("wa"),
        P("wa", "ta"),
        P("wa"),
        P("ta", "wa"),
        P("wa"),
        P("wa", "ta"),
    )
    sizes = (mesh.shape["wa"], mesh.shape["ta"])
    body = functools.partial(on_device_fast, sizes) if fits(mesh) else on_device
    return jax.shard_map(
        body,
        mesh=mesh,
        in_specs=placed,
        out_specs=(
            P("wa", "ta"),
            P("wa", "ta"),
            P("wa"),
            P("wa"),
            P("ta", "wa"),
            P("wa"),
            P("ta", "wa", None),
            P("wa", "ta"),
            P("wa"),
            P("wa"),
            P("wa"),
            P("wa", "ta"),
            P("wa"),
            P("ta", "wa"),
            P("wa"),
        ),
        check_vma=False,
    )
```

```python
import functools

import jax
import jax.numpy as jnp
from jax import lax
from jax.experimental import pallas as pl
from jax.experimental.pallas import tpu as pltpu
from jax.sharding import PartitionSpec as P

D = 768


EPSILON = 1e-05
ALONG_FEATURES = (((1,), (1,)), ((), ()))
ALONG_ROWS = (((0,), (0,)), ((), ()))


def row_statistics(first_term, second_term):
    return lax.psum((jnp.sum(first_term, axis=1), jnp.sum(second_term, axis=1)), "wa")


def all_features(features_part):
    return lax.all_gather(features_part, "wa", axis=1, tiled=True)


def feature_share(partial_sum):
    return lax.psum_scatter(partial_sum, "wa", scatter_dimension=1, tiled=True)


def norm_forward(inputs, norm_gain, norm_bias):
    row_total, row_squares = row_statistics(inputs, inputs * inputs)
    row_mean = row_total / D
    variance = row_squares / D - row_mean * row_mean
    inverse = lax.rsqrt(variance + EPSILON)
    normed = (inputs - row_mean[:, None]) * inverse[:, None]
    return (normed * norm_gain + norm_bias, normed, inverse)


def norm_backward(incoming, normed, inverse, norm_gain):
    scaled = incoming * norm_gain
    row_total, row_along = row_statistics(scaled, scaled * normed)
    return inverse[:, None] * (scaled - row_total[:, None] / D - normed * row_along[:, None] / D)


def weights_of(logit_rows, length_all):
    seq_len = logit_rows.shape[2]
    key_valid = (jnp.arange(seq_len)[None, :] < length_all[:, None]).astype(jnp.bfloat16)
    terms = jnp.exp(logit_rows.astype(jnp.float32)).astype(jnp.bfloat16)
    sums = jnp.einsum("phk,sk->sph", terms, key_valid, preferred_element_type=jnp.float32)
    return (terms, sums, key_valid)


def attend(terms, sums, value_all, query_rows):
    mixed = jnp.einsum("phk,skhd->sphd", terms, value_all, preferred_element_type=jnp.float32)
    mixed = mixed / sums[..., None]
    return (mixed, (mixed * query_rows[:, :, None, None]).astype(jnp.bfloat16))


def attend_back(terms, sums, key_valid, value_all, mixed, grad_rows):
    along = jnp.sum(grad_rows.astype(jnp.float32) * mixed, axis=-1) / sums
    scaled = (grad_rows.astype(jnp.float32) / sums[..., None]).astype(jnp.bfloat16)
    dvalue_part = jnp.einsum("phk,sphd->skhd", terms, scaled, preferred_element_type=jnp.float32)
    dlogits = jnp.einsum("sphd,skhd->phk", scaled, value_all, preferred_element_type=jnp.float32)
    high = along.astype(jnp.bfloat16)
    rest = (along - high.astype(jnp.float32)).astype(jnp.bfloat16)
    shift = sum(
        jnp.einsum("sph,sk->phk", part, key_valid, preferred_element_type=jnp.float32)
        for part in (high, rest)
    )
    return (dvalue_part, terms.astype(jnp.float32) * (dlogits - shift))


def on_device(
    tokens,
    seq_lengths,
    norm1_gain,
    norm1_bias,
    value_weight,
    value_bias,
    synth_logits,
    out_weight,
    out_bias,
    norm2_gain,
    norm2_bias,
    up_weight,
    up_bias,
    down_weight,
    down_bias,
    cotangent,
):
    rows_dev = tokens.shape[1]
    local_width = tokens.shape[0]
    seq_count = seq_lengths.shape[0]
    seq_len = synth_logits.shape[2]
    head_count = synth_logits.shape[1]
    head_dim = local_width // head_count
    value_cols, out_rows, up_rows, down_cols = (
        lax.all_gather(value_weight, "ta", axis=0, tiled=True),
        lax.all_gather(out_weight, "ta", axis=1, tiled=True),
        lax.all_gather(up_weight, "ta", axis=1, tiled=True),
        lax.all_gather(down_weight, "ta", axis=0, tiled=True),
    )
    up_block, down_block = (
        lax.all_to_all(up_rows.T, "wa", split_axis=0, concat_axis=1, tiled=True),
        lax.all_to_all(down_cols, "wa", split_axis=0, concat_axis=1, tiled=True),
    )
    inputs = tokens.T.astype(jnp.float32)
    pre_one, normed_one, inverse_one = norm_forward(inputs, norm1_gain, norm1_bias)
    layer_one = all_features(pre_one.astype(jnp.bfloat16))
    values = (
        jnp.dot(layer_one, value_cols, preferred_element_type=jnp.float32) + value_bias
    ).astype(jnp.bfloat16)
    value_heads = values.reshape(seq_count, seq_len, head_count, head_dim)
    positions = jnp.arange(seq_len)
    key_valid = positions[None, :] < seq_lengths[:, None]
    query_valid = key_valid.astype(jnp.float32)
    length_all = lax.all_gather(seq_lengths, "ta", axis=0, tiled=True)
    block_rows = synth_logits.shape[0]
    value_all = lax.all_gather(
        value_heads * key_valid[:, :, None, None].astype(jnp.bfloat16), "ta", axis=0, tiled=True
    )
    terms, sums, key_valid_all = weights_of(synth_logits, length_all)
    block_positions = lax.axis_index("ta") * block_rows + jnp.arange(block_rows)
    query_rows = (block_positions[None, :] < length_all[:, None]).astype(jnp.float32)
    mixed_rows, mixed_low = attend(terms, sums, value_all, query_rows)
    attended = lax.all_to_all(mixed_low, "ta", split_axis=0, concat_axis=1, tiled=True)
    attended = attended.reshape(rows_dev, local_width)
    branch = (
        feature_share(jnp.dot(attended, out_rows, preferred_element_type=jnp.float32)) + out_bias
    )
    resid = inputs + branch
    pre_two, normed_two, inverse_two = norm_forward(resid, norm2_gain, norm2_bias)
    layer_two = all_features(pre_two.astype(jnp.bfloat16))
    upper = (
        lax.dot_general(layer_two, up_block, ALONG_FEATURES, preferred_element_type=jnp.float32)
        + up_bias
    )
    hidden, gelu_back = jax.vjp(jax.nn.gelu, upper)
    hidden_low = hidden.astype(jnp.bfloat16)
    feed = (
        feature_share(jnp.dot(hidden_low, down_block, preferred_element_type=jnp.float32))
        + down_bias
    )
    output = (resid + feed).astype(jnp.bfloat16)
    cotangent_rows = cotangent.T
    grad_in = cotangent_rows.astype(jnp.float32)
    grad_full = all_features(cotangent_rows)
    dhidden = lax.dot_general(
        grad_full, down_block, ALONG_FEATURES, preferred_element_type=jnp.float32
    )
    dupper = gelu_back(dhidden)[0].astype(jnp.bfloat16)
    down_part = lax.dot_general(
        hidden_low, grad_full, ALONG_ROWS, preferred_element_type=jnp.float32
    )
    up_part = lax.dot_general(dupper, layer_two, ALONG_ROWS, preferred_element_type=jnp.float32)
    up_bias_part = jnp.sum(dupper.astype(jnp.float32), axis=0)
    down_bias_part = jnp.sum(grad_in, axis=0)
    dlayer_two = feature_share(jnp.dot(dupper, up_block, preferred_element_type=jnp.float32))
    gain_two_part = jnp.sum(dlayer_two * normed_two, axis=0)
    bias_two_part = jnp.sum(dlayer_two, axis=0)
    dresid = grad_in + norm_backward(dlayer_two, normed_two, inverse_two, norm2_gain)
    dbranch = dresid.astype(jnp.bfloat16)
    dbranch_full = all_features(dbranch)
    dattended = lax.dot_general(
        dbranch_full, out_rows, ALONG_FEATURES, preferred_element_type=jnp.float32
    ).astype(jnp.bfloat16)
    out_part = lax.dot_general(
        attended, dbranch_full, ALONG_ROWS, preferred_element_type=jnp.float32
    )
    out_bias_part = jnp.sum(dbranch.astype(jnp.float32), axis=0)
    grad_heads = dattended.reshape(seq_count, seq_len, head_count, head_dim)
    grad_heads = grad_heads * query_valid[:, :, None, None].astype(jnp.bfloat16)
    grad_block = lax.all_to_all(grad_heads, "ta", split_axis=1, concat_axis=0, tiled=True)
    dvalue_part, logits_grad = attend_back(
        terms, sums, key_valid_all, value_all, mixed_rows, grad_block
    )
    dvalue_rows = dvalue_part.astype(jnp.bfloat16).reshape(-1, local_width)
    dvalue_rows = lax.psum_scatter(dvalue_rows, "ta", scatter_dimension=0, tiled=True)
    dvalues = dvalue_rows * query_valid.reshape(rows_dev, 1).astype(jnp.bfloat16)
    value_part = lax.dot_general(layer_one, dvalues, ALONG_ROWS, preferred_element_type=jnp.float32)
    value_bias_part = jnp.sum(dvalues.astype(jnp.float32), axis=0)
    dlayer_one = feature_share(
        lax.dot_general(dvalues, value_cols, ALONG_FEATURES, preferred_element_type=jnp.float32)
    )
    gain_one_part = jnp.sum(dlayer_one * normed_one, axis=0)
    bias_one_part = jnp.sum(dlayer_one, axis=0)
    tokens_grad = dresid + norm_backward(dlayer_one, normed_one, inverse_one, norm1_gain)
    up_back, down_back = (
        lax.all_to_all(up_part, "wa", split_axis=1, concat_axis=0, tiled=True),
        lax.all_to_all(down_part, "wa", split_axis=1, concat_axis=0, tiled=True),
    )
    value_grad, out_grad, up_grad, down_grad = (
        lax.psum_scatter(value_part, "ta", scatter_dimension=0, tiled=True),
        lax.psum_scatter(out_part, "ta", scatter_dimension=1, tiled=True),
        lax.psum_scatter(up_back, "ta", scatter_dimension=0, tiled=True),
        lax.psum_scatter(down_back, "ta", scatter_dimension=0, tiled=True),
    )
    vector_grads = lax.psum(
        (
            gain_one_part,
            bias_one_part,
            value_bias_part,
            out_bias_part,
            gain_two_part,
            bias_two_part,
            up_bias_part,
            down_bias_part,
        ),
        "ta",
    )
    return (
        output.T,
        tokens_grad.T,
        vector_grads[0],
        vector_grads[1],
        value_grad,
        vector_grads[2],
        logits_grad,
        out_grad,
        vector_grads[3],
        vector_grads[4],
        vector_grads[5],
        up_grad.T,
        vector_grads[6],
        down_grad,
        vector_grads[7],
    )


MESH = pl.DeviceIdType.MESH
ROWS_NT = (((1,), (1,)), ((), ()))
ROWS_TN = (((0,), (0,)), ((), ()))
F32 = jnp.float32
BF16 = jnp.bfloat16
VMEM_BYTES = 60 * 2**20
CHUNK = 128
PAD = 128
AHEAD = 1


def whole(count):
    return [pl.BlockSpec(memory_space=pltpu.VMEM)] * count


def anywhere(count):
    return [pl.BlockSpec(memory_space=pl.ANY)] * count


def shape_of(shape, dtype):
    return jax.ShapeDtypeStruct(shape, dtype)


def lanes(start, size=CHUNK):
    return pl.ds(pl.multiple_of(start, CHUNK), size)


def rows_at(start, size, unit):
    return pl.ds(pl.multiple_of(start, unit), size)


class Place:
    def __init__(self, nwa, nta):
        self.nwa, self.nta, self.nz = nwa, nta, nta // 2
        self.wa = lax.axis_index("wa")
        self.ta = lax.axis_index("ta")
        self.z = self.ta // 2
        self.c = self.ta % 2
        self.peer = self.ta + 1 - 2 * self.c
        self.wx = self.wa + 1 - 2 * (self.wa % 2)
        self.wy = (self.wa + 2) % 4
        self.wd = 3 - self.wa

    def enter(self):
        barrier = pltpu.get_barrier_semaphore()
        total = self.nwa * self.nta

        def greet(step, carry):
            w = (self.wa + step // self.nta) % self.nwa
            t = (self.ta + step % self.nta) % self.nta
            pl.semaphore_signal(barrier, inc=1, device_id=(w, t), device_id_type=MESH)
            return carry

        lax.fori_loop(1, total, greet, 0)
        pl.semaphore_wait(barrier, total - 1)


def send(src, dst, ssem, rsem, device):
    return pltpu.make_async_remote_copy(
        src_ref=src,
        dst_ref=dst,
        send_sem=ssem,
        recv_sem=rsem,
        device_id=device,
        device_id_type=MESH,
    )


def when(condition):
    return pl.when(condition)


def norm_stats(block):
    width = block.shape[0]
    mean = jnp.sum(block, axis=0, keepdims=True) / width
    centred = block - mean
    variance = jnp.sum(centred * centred, axis=0, keepdims=True) / width
    inverse = lax.rsqrt(variance + EPSILON)
    return (centred * inverse, inverse)


def forward_kernel(
    dims,
    tok,
    cot,
    wsmall,
    wlarge,
    prow,
    ln,
    logits,
    xown,
    small,
    large,
    layer_out,
    value_out,
    term_out,
    mixed,
    zinv,
    lens,
    pfull,
    out,
    dattended,
    dresid,
    wgrad,
    vcol,
    vrow,
    cown,
    attended,
    rfull,
    wo,
    wblock,
    resid,
    normed,
    inverse,
    layer_two,
    layer_t,
    grad_t,
    feed,
    dlayer,
    wide,
    gblock,
    gwo,
    x,
    wvc,
    layer_pad,
    layer,
    value,
    terms,
    attsend,
    rows,
    sem_tok,
    sem_par,
    sem_ta,
    sem_val,
    sem_small,
    sem_large,
    sem_cot,
    sem_att,
    sem_local,
    sem_out,
    sem_wv,
    sem_g,
):
    nwa, nta = dims
    me = Place(nwa, nta)
    wa, ta, z, c = me.wa, me.ta, me.z, me.c
    nz = me.nz
    width = tok.shape[0]
    half = width // 2
    seq = tok.shape[1]
    part = seq // nz
    query = seq // nta
    slot = wvc.shape[1] // nta
    wdepth = wvc.shape[0] * nwa // nta
    heads = terms.shape[0]
    hdim = width // heads
    split = wsmall.shape[1] - PAD
    get_logits = pltpu.make_async_copy(logits, terms, sem_local.at[5])
    get_logits.start()
    me.enter()
    done = []

    def block_rows(w, off=0, size=width):
        return rows_at(w * width + off, size, 32)

    def tok_copy(k, q):
        device = (me.wx if k == 0 else me.wy, ta)
        return send(
            tok.at[:, pl.ds(q * part, part)],
            x.at[block_rows(wa), pl.ds(q * part, part)],
            sem_tok.at[0, k, q],
            sem_tok.at[1, k, q],
            device,
        )

    def tok_fwd(k, q):
        source = me.wx if k == 0 else me.wy
        device = (me.wy if k == 0 else me.wx, ta)
        where = x.at[block_rows(source, k * half, half), pl.ds(q * part, part)]
        return send(where, where, sem_tok.at[0, 2 + k, q], sem_tok.at[1, 2 + k, q], device)

    own_x = pltpu.make_async_copy(tok, x.at[block_rows(wa)], sem_local.at[0])
    own_x.start()

    def tok_start(q):
        for k in range(2):
            tok_copy(k, q).start()

    def tok_turn(q):
        for k in range(2):
            tok_copy(k, q).wait_recv()
            tok_fwd(k, q).start()
        if q + AHEAD < nz:
            tok_start(q + AHEAD)

    for q in range(AHEAD):
        tok_start(q)

    def par_copy(step):
        w = (wa + step) % nwa
        return send(prow, rows.at[wa], sem_par.at[0, step], sem_par.at[1, step], (w, ta))

    def ta_copy(step):
        t = (ta + step) % nta
        return send(
            ln, lens.at[rows_at(ta * 8, 8, 8)], sem_ta.at[0, step], sem_ta.at[1, step], (wa, t)
        )

    def wv_column(b, core):
        return wvc.at[:, lanes((2 * b + core) * slot)]

    def wv_z(step):
        b = (z + step) % nz
        src = wsmall.at[:, pl.ds(split, PAD)]
        return send(
            src, wv_column(z, c), sem_wv.at[0, 0, step], sem_wv.at[1, 0, step], (wa, 2 * b + c)
        )

    def wv_core(step, core):
        where = wv_column((z - step + nz) % nz, core)
        return send(where, where, sem_wv.at[0, 1, step], sem_wv.at[1, 1, step], (wa, me.peer))

    own_wv = pltpu.make_async_copy(wsmall.at[:, pl.ds(split, PAD)], wv_column(z, c), sem_local.at[1])
    own_wv.start()
    for step in range(nz - 1, 0, -1):
        wv_z(step).start()
    for step in range(1, nwa):
        par_copy(step).start()
    for step in range(1, nta):
        ta_copy(step).start()
    rows[wa] = prow[...]
    lens[rows_at(ta * 8, 8, 8), :] = ln[...]
    own_wv.wait()
    wv_core(0, c).start()

    stores = ((wsmall, small, sem_small), (wlarge, large, sem_large))
    own_w = [
        pltpu.make_async_copy(src, dst.at[wa, ta], sem_local.at[2 + 4 * i])
        for i, (src, dst, _) in enumerate(stores)
    ]
    for copy in own_w:
        copy.start()

    def w_line(p, up, b, own):
        src, dst, sem = stores[p]
        where = dst.at[wa, 2 * b + c]
        k = 0 if up else 1
        return send(
            src if own else where,
            where,
            sem.at[0, k, b],
            sem.at[1, k, b],
            (wa, ta + 2 if up else ta - 2),
        )

    for step in range(1, nz):
        wv_z(step).wait_recv()
        wv_core(step, c).start()
    @pl.when(z < nz - 1)
    def _():
        for p in range(2):
            w_line(p, True, z, True).start()

    @pl.when(z > 0)
    def _():
        for p in range(2):
            w_line(p, False, z, True).start()

    layer_pad[...] = jnp.zeros_like(layer_pad)
    get_logits.wait()
    for h in range(heads):
        terms[h] = jnp.exp(terms[h].astype(F32)).astype(BF16)
    out_terms = pltpu.make_async_copy(terms, term_out, sem_local.at[3])
    out_terms.start()

    tok_turn(0)
    for step in range(1, nwa):
        par_copy(step).wait_recv()
    gap = 2 * CHUNK
    for w in range(nwa):
        piece = jnp.concatenate([rows[w, :, :gap], jnp.zeros((PAD - 8, gap), F32)], axis=0)
        pfull[w * width : (w + 1) * width, :] = piece.T[:width]
        span = rows.shape[2] - gap
        rfull[:, w * span : (w + 1) * span] = rows[w, :, gap:]
    for step in range(1, nta):
        ta_copy(step).wait_recv()
    for step in range(nz):
        wv_core(step, 1 - c).wait_recv()
    own_x.wait()

    positions = lax.broadcasted_iota(jnp.int32, (nta * 8, seq), 1).astype(F32)
    key_valid = jnp.where(positions < lens[:, 0:1], 1.0, 0.0).astype(BF16)
    for h in range(heads):
        sums = lax.dot_general(key_valid, terms[h], ROWS_NT, preferred_element_type=F32)
        zinv[h] = 1.0 / sums

    def value_copy(kind, b, q, core):
        where = value.at[2 * b + core, :, pl.ds(q * part, part)]
        t = (ta + 2, ta - 2, me.peer)[kind]
        return send(where, where, sem_val.at[0, kind, b, q], sem_val.at[1, kind, b, q], (wa, t))

    def w_plane(p, k, b):
        device = (me.wx if k == 0 else me.wy, ta)
        where, sem = stores[p][1].at[wa, 2 * b + c], stores[p][2]
        return send(where, where, sem.at[0, 2 + k, b], sem.at[1, 2 + k, b], device)

    def w_diag(p, k, b, source):
        device = (me.wy if k == 0 else me.wx, ta)
        where, sem = stores[p][1].at[source, 2 * b + c, pl.ds(k * half, half)], stores[p][2]
        return send(where, where, sem.at[0, 4 + k, b], sem.at[1, 4 + k, b], device)

    def w_core(p, r, b, core):
        source = (wa, me.wx, me.wy, me.wd)[r]
        where, sem = stores[p][1].at[source, 2 * b + core], stores[p][2]
        return send(where, where, sem.at[0, 6 + r, b], sem.at[1, 6 + r, b], (wa, me.peer))

    def w_start(p, b):
        w_plane(p, 0, b).start()
        w_plane(p, 1, b).start()
        w_core(p, 0, b, c).start()

    def w_forward(p, b):
        w_plane(p, 0, b).wait_recv()
        w_diag(p, 0, b, me.wx).start()
        w_core(p, 1, b, c).start()
        w_plane(p, 1, b).wait_recv()
        w_diag(p, 1, b, me.wy).start()
        w_core(p, 2, b, c).start()

    def w_finish(p, b):
        for k in range(2):
            w_diag(p, k, b, me.wd).wait_recv()
        w_core(p, 3, b, c).start()

    def w_landed(p, h):
        @pl.when(z - 1 - h >= 0)
        def _():
            w_line(p, True, z - 1 - h, False).wait_recv()

        @pl.when(z + 1 + h < nz)
        def _():
            w_line(p, False, z + 1 + h, False).wait_recv()

    def w_onward(p, h):
        @pl.when(jnp.logical_and(z - 1 - h >= 0, z < nz - 1))
        def _():
            w_line(p, True, z - 1 - h, False).start()

        @pl.when(jnp.logical_and(z + 1 + h < nz, z > 0))
        def _():
            w_line(p, False, z + 1 + h, False).start()

    def at_hop(h, act, *args):
        @pl.when(z - 1 - h >= 0)
        def _():
            act(*args, z - 1 - h)

        @pl.when(z + 1 + h < nz)
        def _():
            act(*args, z + 1 + h)

    for q in range(nz):
        cols = pl.ds(q * part, part)
        if q + 1 < nz:
            tok_turn(q + 1)
        for k in range(2):
            where = x.at[block_rows(me.wd, k * half, half), cols]
            send(
                where,
                where,
                sem_tok.at[0, 2 + k, q],
                sem_tok.at[1, 2 + k, q],
                (me.wy if k == 0 else me.wx, ta),
            ).wait_recv()
        centred, _ = norm_stats(x[:, cols].astype(F32))
        low = (centred * pfull[:, 0:1] + pfull[:, 1:2]).astype(BF16)
        layer[:, cols] = low
        for t in range(nta):
            layer_pad[t * slot : t * slot + wdepth, :] = low[t * wdepth : (t + 1) * wdepth]
        made = jnp.dot(wvc[...], layer_pad[...], preferred_element_type=F32)
        made = made + pfull[block_rows(wa), :][:, 2:3]
        place = lax.broadcasted_iota(jnp.int32, (width, part), 1) + q * part
        made = jnp.where(place.astype(F32) < ln[0:1, 0:1], made, 0.0)
        value[ta, :, cols] = made.astype(BF16)
        xown[:, pl.ds(q * CHUNK, CHUNK)] = x[:, lanes(q * part + wa * CHUNK)]

        @pl.when(z < nz - 1)
        def _():
            value_copy(0, z, q, c).start()

        @pl.when(z > 0)
        def _():
            value_copy(1, z, q, c).start()

        value_copy(2, z, q, c).start()
        if q < nz - 1:
            w_landed(0, q)
            w_onward(0, q)
    out_layer = pltpu.make_async_copy(layer, layer_out, sem_local.at[4])
    out_layer.start()

    def cot_copy(step, q):
        w = (wa + step) % nwa
        return send(
            cot.at[:, lanes(q * part + w * CHUNK)],
            cown.at[block_rows(wa), pl.ds(q * CHUNK, CHUNK)],
            sem_cot.at[0, step, q],
            sem_cot.at[1, step, q],
            (w, ta),
        )

    def cot_own(q):
        return pltpu.make_async_copy(
            cot.at[:, lanes(q * part + wa * CHUNK)],
            cown.at[block_rows(wa), pl.ds(q * CHUNK, CHUNK)],
            sem_cot.at[0, 0, q],
        )

    for copy in own_w:
        copy.wait()
    w_start(0, z)
    for h in range(nz - 1):
        at_hop(h, w_start, 0)
    w_start(1, z)
    w_landed(1, 0)
    at_hop(0, w_start, 1)
    for q in range(nz):
        cot_own(q).start()
        for step in range(1, nwa):
            cot_copy(step, q).start()

    def att_copy(s, j):
        return send(
            attsend.at[s, :, pl.ds(j * CHUNK, CHUNK)],
            attended.at[block_rows(wa), lanes(z * CHUNK)],
            sem_att.at[0, s, j],
            sem_att.at[1, wa, z],
            (2 * c + j, s),
        )

    def att_local(s, j):
        return pltpu.make_async_copy(
            attsend.at[s, :, pl.ds(j * CHUNK, CHUNK)],
            attended.at[block_rows(wa), lanes(z * CHUNK)],
            sem_att.at[0, s, j],
        )

    def is_self(s, j):
        return jnp.logical_and(s == ta, 2 * c + j == wa)

    def mix(b):
        for core in range(2):
            s = 2 * b + core
            pltpu.make_async_copy(value.at[s], value_out.at[s], sem_out.at[s]).start()
        length = [lens[rows_at((2 * b + core) * 8, 8, 8), :][0:1, 0:1] for core in range(2)]
        place = lax.broadcasted_iota(jnp.int32, (hdim, query), 1) + ta * query
        place = place.astype(F32)
        for h in range(heads):
            group = slice(h * hdim, (h + 1) * hdim)
            pair = jnp.concatenate([value[2 * b, group, :], value[2 * b + 1, group, :]], axis=0)
            both = lax.dot_general(pair, terms[h], ROWS_NT, preferred_element_type=F32)
            for core in range(2):
                s = 2 * b + core
                inverse = zinv[h, rows_at(s * 8, 8, 8), :][0:1]
                one = both[core * hdim : (core + 1) * hdim] * inverse
                mixed[s, group, :] = one
                one = jnp.where(place < length[core], one, 0.0)
                attsend[s, group, :] = one.astype(BF16)
        for core in range(2):
            s = 2 * b + core
            for j in range(2):

                @pl.when(is_self(s, j))
                def _():
                    att_local(s, j).start()

                @pl.when(jnp.logical_not(is_self(s, j)))
                def _():
                    att_copy(s, j).start()

    def core_ready(b):
        for q in range(nz):
            value_copy(2, b, q, 1 - c).wait_recv()

    for h in range(nz - 1):
        below, above = z - 1 - h, z + 1 + h
        for q in range(nz):

            @pl.when(below >= 0)
            def _():
                value_copy(0, below, q, c).wait_recv()

                @pl.when(z < nz - 1)
                def _():
                    value_copy(0, below, q, c).start()

                value_copy(2, below, q, c).start()

            @pl.when(above < nz)
            def _():
                value_copy(1, above, q, c).wait_recv()

                @pl.when(z > 0)
                def _():
                    value_copy(1, above, q, c).start()

                value_copy(2, above, q, c).start()

        if h == 0:
            core_ready(z)
            mix(z)

        @pl.when(below >= 0)
        def _():
            core_ready(below)
            mix(below)

        @pl.when(above < nz)
        def _():
            core_ready(above)
            mix(above)

        if h == 0:
            w_forward(0, z)
            for other in range(nz - 1):
                at_hop(other, w_forward, 0)
        if h == 1:
            w_onward(1, 0)
            w_forward(1, z)
            w_finish(0, z)
            for other in range(nz - 1):
                at_hop(other, w_finish, 0)
    at_hop(0, w_forward, 1)
    w_finish(1, z)
    at_hop(0, w_finish, 1)

    def w_cores(p, b):
        for r in range(4):
            w_core(p, r, b, 1 - c).wait_recv()

    depth, own = xown.shape
    both = wlarge.shape[1]
    one = both // 2

    def turn(i):
        pair = z + 1 - 2 * (z % 2)
        late = jnp.where(i == 2, nz // 2 - z // 2, (nz - 1) * (1 - z // 2))
        return jnp.where(i == 0, z, jnp.where(i == 1, pair, late))

    def load(i, slot):
        b = turn(i)
        return pltpu.make_async_copy(
            large.at[:, pl.ds(2 * b, 2)], wblock.at[slot], sem_g.at[slot]
        )

    w_cores(1, turn(0))
    load(0, 0).start()
    for b in range(nz):
        w_cores(0, b)
    get_wo = pltpu.make_async_copy(small.at[:, :, :, pl.ds(0, PAD)], wo, sem_g.at[2])
    get_wo.start()
    for q in range(nz):
        cot_own(q).wait()
        for step in range(1, nwa):
            cot_copy(step, q).wait_recv()
    grad_t[...] = cown[...].T
    w_cores(1, turn(1))
    load(1, 1).start()

    def att_sends(s, carry):
        pltpu.make_async_copy(value.at[s], value_out.at[s], sem_out.at[s]).wait()
        for j in range(2):

            @pl.when(is_self(s, j))
            def _():
                att_local(s, j).wait()

            @pl.when(jnp.logical_not(is_self(s, j)))
            def _():
                att_copy(s, j).wait_send()

        return carry

    lax.fori_loop(0, nta, att_sends, 0)
    mine = wa // 2

    def att_arrivals(k, carry):
        w, b = k // nz, k % nz

        @pl.when(jnp.logical_not(jnp.logical_and(w == wa, 2 * b + mine == ta)))
        def _():
            where = attended.at[block_rows(w), lanes(b * CHUNK)]
            send(where, where, sem_att.at[0, 0, 0], sem_att.at[1, w, b], (w, 2 * b + mine)).wait_recv()

        return carry

    w_landed(1, 1)
    w_onward(1, 1)
    at_hop(1, w_start, 1)
    lax.fori_loop(0, nwa * nz, att_arrivals, 0)
    get_wo.wait()

    def wide_wo():
        joined = [
            jnp.concatenate([wo[w, t] for t in range(nta)], axis=1) for w in range(nwa)
        ]
        return jnp.concatenate(joined, axis=0)

    branch = lax.dot_general(wide_wo(), attended[...], ROWS_TN, preferred_element_type=F32)
    branch = jnp.concatenate([branch[t * PAD : t * PAD + wdepth] for t in range(nta)], axis=0)
    res = xown[...].astype(F32) + branch + pfull[:, 3:4]
    resid[...] = res
    norm, inv = norm_stats(res)
    normed[...] = norm
    inverse[...] = jnp.broadcast_to(inv, inverse.shape)
    low = (norm * pfull[:, 4:5] + pfull[:, 5:6]).astype(BF16)
    layer_two[...] = low
    layer_t[...] = low.T
    feed[...] = jnp.zeros_like(feed)
    dlayer[...] = jnp.zeros_like(dlayer)

    def put(i):
        return pltpu.make_async_copy(
            gblock, wgrad.at[:, turn(i), :, :, pl.ds(0, both)], sem_g.at[3]
        )

    def middle(i, carry):
        slot = i % 2

        @pl.when(i == 2)
        def _():
            at_hop(1, w_finish, 1)
            w_landed(1, 2)
            at_hop(2, w_start, 1)
            w_cores(1, turn(2))
            load(2, 0).start()

        @pl.when(i == 3)
        def _():
            at_hop(2, w_forward, 1)
            at_hop(2, w_finish, 1)
            w_cores(1, turn(3))
            load(3, 1).start()

        load(i, slot).wait()
        held = wblock.at[slot]

        def joined(start):
            parts = [held[:, g, :, start : start + one].reshape(depth, one) for g in range(2)]
            return jnp.concatenate(parts, axis=1)

        up, down_t = joined(0), joined(one)
        at = lanes(turn(i) * both, both)
        upper = jnp.dot(layer_t[...], up, preferred_element_type=F32) + rfull[0:1, at]
        hidden, slope = gelu_pair(upper)
        hidden = hidden.astype(BF16)
        dhidden = jnp.dot(grad_t[...], down_t, preferred_element_type=F32)
        dupper = (dhidden * slope).astype(BF16)
        vrow[:, at] = jnp.broadcast_to(
            jnp.sum(dupper.astype(F32), axis=0, keepdims=True), (vrow.shape[0], both)
        )
        feed[...] += lax.dot_general(down_t, hidden, ROWS_NT, preferred_element_type=F32)
        dlayer[...] += lax.dot_general(up, dupper, ROWS_NT, preferred_element_type=F32)
        gup = jnp.dot(layer_two[...], dupper, preferred_element_type=F32)
        gdown = jnp.dot(cown[...], hidden, preferred_element_type=F32)

        @pl.when(i > 0)
        def _():
            put(i - 1).wait()

        for g in range(2):
            piece = slice(g * one, (g + 1) * one)
            gblock[:, g, :, :one] = gup[:, piece].reshape(nwa, width, one).astype(BF16)
            gblock[:, g, :, one:] = gdown[:, piece].reshape(nwa, width, one).astype(BF16)
        put(i).start()

        @pl.when(i == 0)
        def _():
            at_hop(1, w_forward, 1)

        return carry

    lax.fori_loop(0, nz, middle, 0)

    grad = cown[...].astype(F32)
    out[...] = (resid[...] + feed[...] + pfull[:, 6:7]).astype(BF16)
    dl = dlayer[...]
    norm = normed[...]
    e = dl * pfull[:, 4:5]
    mean_e = jnp.sum(e, axis=0, keepdims=True) / depth
    mean_n = jnp.sum(e * norm, axis=0, keepdims=True) / depth
    dres = grad + inverse[0:1, :] * (e - mean_e - norm * mean_n)
    dresid[...] = dres
    low = dres.astype(BF16)
    vcol[...] = jnp.zeros_like(vcol)
    vcol[:, 3:4] = jnp.sum(low.astype(F32), axis=1, keepdims=True)
    vcol[:, 4:5] = jnp.sum(dl * norm, axis=1, keepdims=True)
    vcol[:, 5:6] = jnp.sum(dl, axis=1, keepdims=True)
    vcol[:, 6:7] = jnp.sum(grad, axis=1, keepdims=True)
    wide[...] = jnp.zeros_like(wide)
    for t in range(nta):
        wide[t * PAD : t * PAD + wdepth, :] = low[t * wdepth : (t + 1) * wdepth]
    da = jnp.dot(wide_wo(), wide[...], preferred_element_type=F32)
    lane = lax.broadcasted_iota(jnp.int32, (depth, own), 1)
    place = (lane // CHUNK) * (CHUNK * nwa) + lane % CHUNK + wa * CHUNK
    da = jnp.where(place.astype(F32) < ln[0:1, 0:1], da, 0.0)
    dattended[...] = da.astype(BF16)
    made = lax.dot_general(attended[...], wide[...], ROWS_NT, preferred_element_type=F32)
    for t in range(nta):
        piece = made[:, t * PAD : (t + 1) * PAD].reshape(nwa, width, PAD)
        gwo[:, t // 2, t % 2] = piece.astype(BF16)
    rest = pltpu.make_async_copy(gwo, wgrad.at[:, :, :, :, pl.ds(both, PAD)], sem_g.at[4])
    rest.start()
    put(nz - 1).wait()
    rest.wait()

    for step in range(1, nta):
        ta_copy(step).wait_send()
    for step in range(nz):
        wv_core(step, c).wait_send()
        if step:
            wv_z(step).wait_send()
    for step in range(1, nwa):
        par_copy(step).wait_send()
        for q in range(nz):
            cot_copy(step, q).wait_send()
    for q in range(nz):
        for k in range(2):
            tok_copy(k, q).wait_send()
            tok_fwd(k, q).wait_send()

    def line_sends(b, carry):
        reach_up = jnp.logical_and(b <= z, z < nz - 1)
        reach_down = jnp.logical_and(b >= z, z > 0)

        @pl.when(reach_up)
        def _():
            for p in range(2):
                w_line(p, True, b, False).wait_send()
            for q in range(nz):
                value_copy(0, b, q, c).wait_send()

        @pl.when(reach_down)
        def _():
            for p in range(2):
                w_line(p, False, b, False).wait_send()
            for q in range(nz):
                value_copy(1, b, q, c).wait_send()

        for q in range(nz):
            value_copy(2, b, q, c).wait_send()
        for p in range(2):
            for k in range(2):
                w_plane(p, k, b).wait_send()
            w_diag(p, 0, b, me.wx).wait_send()
            w_diag(p, 1, b, me.wy).wait_send()
            for r in range(4):
                w_core(p, r, b, c).wait_send()
        return carry

    lax.fori_loop(0, nz, line_sends, 0)

    out_terms.wait()
    out_layer.wait()


def run_forward(dims, tok, cot, wsmall, wlarge, prow, ln, logits):
    nwa, nta = dims
    nz = nta // 2
    width, seq = tok.shape
    depth = width * nwa
    own = seq // nwa
    heads, query, _ = logits.shape
    slot = PAD
    both = wlarge.shape[1]
    hidden = both // 2 * nta
    dma = pltpu.SemaphoreType.DMA
    return pl.pallas_call(
        functools.partial(forward_kernel, dims),
        out_shape=(
            shape_of((depth, own), BF16),
            shape_of((nwa, nta) + wsmall.shape, BF16),
            shape_of((nwa, nta) + wlarge.shape, BF16),
            shape_of((depth, seq), BF16),
            shape_of((nta, width, seq), BF16),
            shape_of((heads, query, seq), BF16),
            shape_of((nta, width, query), F32),
            shape_of((heads, nta * 8, query), F32),
            shape_of((nta * 8, CHUNK), F32),
            shape_of((depth, PAD), F32),
            shape_of((depth, own), BF16),
            shape_of((depth, own), BF16),
            shape_of((depth, own), F32),
            shape_of((nwa, nz, 2, width, both + PAD), BF16),
            shape_of((depth, PAD), F32),
            shape_of((8, hidden), F32),
        ),
        in_specs=anywhere(4) + whole(2) + anywhere(1),
        out_specs=tuple(whole(1) + anywhere(5) + whole(7) + anywhere(1) + whole(2)),
        scratch_shapes=[
            pltpu.VMEM((depth, own), BF16),
            pltpu.VMEM((depth, own), BF16),
            pltpu.VMEM((8, hidden), F32),
            pltpu.VMEM((nwa, nta, width, PAD), BF16),
            pltpu.VMEM((2, nwa, 2, width, both), BF16),
            pltpu.VMEM((depth, own), F32),
            pltpu.VMEM((depth, own), F32),
            pltpu.VMEM((8, own), F32),
            pltpu.VMEM((depth, own), BF16),
            pltpu.VMEM((own, depth), BF16),
            pltpu.VMEM((own, depth), BF16),
            pltpu.VMEM((depth, own), F32),
            pltpu.VMEM((depth, own), F32),
            pltpu.VMEM((nta * PAD, own), BF16),
            pltpu.VMEM((nwa, 2, width, both), BF16),
            pltpu.VMEM((nwa, nz, 2, width, PAD), BF16),
            pltpu.VMEM((depth, seq), BF16),
            pltpu.VMEM((width, nta * slot), BF16),
            pltpu.VMEM((nta * slot, seq // nz), BF16),
            pltpu.VMEM((depth, seq), BF16),
            pltpu.VMEM((nta, width, seq), BF16),
            pltpu.VMEM((heads, query, seq), BF16),
            pltpu.VMEM((nta, width, query), BF16),
            pltpu.VMEM((nwa,) + prow.shape, F32),
            dma((2, 4, nz)),
            dma((2, nwa)),
            dma((2, nta)),
            dma((2, 3, nz, nz)),
            dma((2, 10, nz)),
            dma((2, 10, nz)),
            dma((2, nwa, nz)),
            dma((2, nta, max(nz, 2))),
            dma((8,)),
            dma((nta,)),
            dma((2, 2, nz)),
            dma((5,)),
        ],
        compiler_params=pltpu.CompilerParams(
            collective_id=1, has_side_effects=True, vmem_limit_bytes=VMEM_BYTES
        ),
        cost_estimate=pl.CostEstimate(
            flops=20 * 10**9, bytes_accessed=80 * 10**6, transcendentals=4 * 10**6
        ),
    )(tok, cot, wsmall, wlarge, prow, ln, logits)


def gelu_pair(u):
    root = 0.7978845608028654
    square = u * u
    bent = jnp.tanh(root * u * (1.0 + 0.044715 * square))
    low_half = 0.5 * (1.0 + bent)
    slope = low_half + 0.5 * u * (1.0 - bent * bent) * root * (1.0 + 3.0 * 0.044715 * square)
    return (u * low_half, slope)


def backward_kernel(
    dims,
    dattended,
    outown,
    dresid_in,
    xown_in,
    terms_in,
    mixed_in,
    zinv,
    lens,
    ln,
    pfull,
    layer_in,
    weights,
    wgrad,
    vcol,
    vrow,
    scaled,
    shift,
    output,
    tgrad,
    vgrad,
    vectors,
    wsum,
    dresid,
    xown,
    terms,
    mixed,
    layer,
    normed,
    invs,
    wvt,
    gains,
    biases,
    da,
    partial,
    paired,
    up_in,
    down_in,
    gown,
    gpeer,
    first_x,
    first_y,
    second_x,
    second_y,
    gup_in,
    gdown_in,
    dvalue,
    dvown,
    wv,
    vsend,
    vrecv,
    tsend,
    csend,
    crecv,
    csum,
    crecv2,
    sem_da,
    sem_out,
    sem_core,
    sem_line,
    sem_dv,
    sem_tg,
    sem_v,
    sem_c,
    sem_c2,
    sem_local,
    sem_g,
    sem_gline,
):
    nwa, nta = dims
    me = Place(nwa, nta)
    wa, ta, z, c = me.wa, me.ta, me.z, me.c
    nz = me.nz
    depth, own = dresid.shape
    width = depth // nwa
    wdepth = depth // nta
    heads, query, seq = terms.shape
    hdim = width // heads
    part = seq // nz
    pairs = (
        (terms_in, terms),
        (mixed_in, mixed),
        (xown_in, xown),
        (dresid_in, dresid),
        (layer_in, layer),
    )
    fetch = [
        pltpu.make_async_copy(src, dst, sem_local.at[1 + i]) for i, (src, dst) in enumerate(pairs)
    ]
    for copy in fetch:
        copy.start()
    me.enter()

    def block_rows(w):
        return rows_at(w * width, width, 32)

    def da_copy(w, b, local):
        core = wa // 2
        src = dattended.at[block_rows(w), lanes(b * CHUNK)]
        dst = da.at[ta, :, lanes((wa % 2) * CHUNK)]
        if local:
            return pltpu.make_async_copy(src, dst, sem_da.at[0, w, b])
        return send(src, dst, sem_da.at[0, w, b], sem_da.at[1, ta, wa % 2], (w, 2 * b + core))

    def da_self(w, b):
        return jnp.logical_and(w == wa, 2 * b + wa // 2 == ta)

    def far(i):
        low_end = 1 - z // (nz // 2)
        return (nz - 1 - i) * low_end + i * (1 - low_end)

    def da_start(k, carry):
        w, b = (wa + k % nwa) % nwa, far(k // nwa)

        @pl.when(da_self(w, b))
        def _():
            da_copy(w, b, True).start()

        @pl.when(jnp.logical_not(da_self(w, b)))
        def _():
            da_copy(w, b, False).start()

        return carry

    lax.fori_loop(0, nwa * nz, da_start, 0)

    def back_copy(src, dst, sems, step, q):
        w = (wa + step) % nwa
        return send(
            src.at[block_rows(w), pl.ds(q * CHUNK, CHUNK)],
            dst.at[:, lanes(q * part + wa * CHUNK)],
            sems.at[0, step, q],
            sems.at[1, step, q],
            (w, ta),
        )

    def back_own(src, dst, sems, q):
        return pltpu.make_async_copy(
            src.at[block_rows(wa), pl.ds(q * CHUNK, CHUNK)],
            dst.at[:, lanes(q * part + wa * CHUNK)],
            sems.at[0, 0, q],
        )

    get_wv = pltpu.make_async_copy(
        weights.at[:, :, :, pl.ds(weights.shape[3] - PAD, PAD)], wv, sem_local.at[0]
    )
    get_wv.start()

    half = width // 2
    order = []
    for j in range(nz):
        for b in (nz - 1 - j, j):
            if b not in order:
                order.append(b)

    def g_core(b, core):
        return send(
            wgrad.at[:, b, core],
            gpeer.at[b],
            sem_g.at[0, 0, b],
            sem_g.at[1, 0, b],
            (wa, me.peer),
        )

    def g_load(b):
        return pltpu.make_async_copy(wgrad.at[:, b, c], gown.at[b], sem_g.at[0, 7, b])

    def g_first(k, r, b):
        near = me.wx if k == 0 else me.wy
        which = near if r == 0 else me.wd
        return send(
            gown.at[b, which, pl.ds(k * half, half)],
            (first_x if k == 0 else first_y).at[b, r],
            sem_g.at[0, 1 + 2 * k + r, b],
            sem_g.at[1, 1 + 2 * k + r, b],
            (near, ta),
        )

    def g_second(k, b):
        near = me.wy if k == 0 else me.wx
        return send(
            gown.at[b, near, pl.ds(k * half, half)],
            (second_x if k == 0 else second_y).at[b],
            sem_g.at[0, 5 + k, b],
            sem_g.at[1, 5 + k, b],
            (near, ta),
        )

    def g_add(b, which, k, extra):
        rows = pl.ds(k * half, half)
        gown[b, which, rows, :] = (
            gown[b, which, rows, :].astype(F32) + extra.astype(F32)
        ).astype(BF16)

    def g_cores(b):
        g_load(b).wait()
        g_core(b, c).wait_recv()
        for w in range(nwa):
            gown[b, w] = (gown[b, w].astype(F32) + gpeer[b, w].astype(F32)).astype(BF16)
        for k in range(2):
            for r in range(2):
                g_first(k, r, b).start()

    def g_plane(b):
        for k in range(2):
            for r in range(2):
                g_first(k, r, b).wait_recv()
            landed = first_x if k == 0 else first_y
            g_add(b, me.wy if k == 0 else me.wx, k, landed[b, 1])
            g_second(k, b).start()
            g_add(b, wa, k, landed[b, 0])

    def g_end(b):
        for k in range(2):
            g_second(k, b).wait_recv()
            g_add(b, wa, k, (second_x if k == 0 else second_y)[b])

    def g_line(up, j):
        k = 0 if up else 1
        target = nz - 1 - j if up else j
        return send(
            gown.at[target, wa],
            (gup_in if up else gdown_in).at[j],
            sem_gline.at[0, k, j],
            sem_gline.at[1, k, j],
            (wa, ta + 2 if up else ta - 2),
        )

    def g_origin():
        @pl.when(z == 0)
        def _():
            for j in range(nz - 1):
                g_line(True, j).start()

        @pl.when(z == nz - 1)
        def _():
            for j in range(nz - 1):
                g_line(False, j).start()

    def g_hop(j):
        target = nz - 1 - j

        @pl.when(jnp.logical_and(z < target, z > 0))
        def _():
            g_line(True, j).wait_recv()
            gown[target, wa] = (gown[target, wa].astype(F32) + gup_in[j].astype(F32)).astype(BF16)
            g_line(True, j).start()

        @pl.when(jnp.logical_and(z > j, z < nz - 1))
        def _():
            g_line(False, j).wait_recv()
            gown[j, wa] = (gown[j, wa].astype(F32) + gdown_in[j].astype(F32)).astype(BF16)
            g_line(False, j).start()

    def g_final():
        @pl.when(z == 0)
        def _():
            g_line(False, 0).wait_recv()
            wsum[...] = gown[0, wa].astype(F32) + gdown_in[0].astype(F32)

        @pl.when(z == nz - 1)
        def _():
            g_line(True, 0).wait_recv()
            wsum[...] = gown[nz - 1, wa].astype(F32) + gup_in[0].astype(F32)

        for b in range(1, nz - 1):

            @pl.when(z == b)
            def _():
                g_line(True, nz - 1 - b).wait_recv()
                g_line(False, b).wait_recv()
                both = gup_in[nz - 1 - b].astype(F32) + gdown_in[b].astype(F32)
                wsum[...] = gown[b, wa].astype(F32) + both

    for b in order:
        g_core(b, 1 - c).start()
        g_load(b).start()

    def da_arrive(s, j):
        own_piece = jnp.logical_and(s == ta, 2 * c + j == wa)
        where = da.at[s, :, lanes(j * CHUNK)]

        @pl.when(own_piece)
        def _():
            da_copy(wa, z, True).wait()

        @pl.when(jnp.logical_not(own_piece))
        def _():
            send(where, where, sem_da.at[0, 0, 0], sem_da.at[1, s, j], (2 * c + j, s)).wait_recv()

    def da_sent(k, carry):
        w, b = (wa + k // nz) % nwa, k % nz

        @pl.when(jnp.logical_not(da_self(w, b)))
        def _():
            da_copy(w, b, False).wait_send()

        return carry

    def prepare(b):
        for core in range(2):
            for j in range(2):
                da_arrive(2 * b + core, j)
        for h in range(heads):
            group = slice(h * hdim, (h + 1) * hdim)
            both = []
            for s in (2 * b, 2 * b + 1):
                one = da[s, group, :].astype(F32) * zinv[h, s * 8 : s * 8 + 1, :]
                both.append(one.astype(BF16))
                scaled[s, group, :] = both[-1]
            made = jnp.dot(
                jnp.concatenate(both, axis=0), terms[h], preferred_element_type=F32
            ).astype(BF16)
            partial[2 * b, group, :] = made[:hdim]
            partial[2 * b + 1, group, :] = made[hdim:]
        core_copy(b, 1 - c).start()

    def shifts():
        for h in range(heads):
            group = slice(h * hdim, (h + 1) * hdim)
            for s in range(nta):
                inv = zinv[h, s * 8 : s * 8 + 1, :]
                one = da[s, group, :].astype(F32) * mixed[s, group, :]
                along = jnp.sum(one, axis=0, keepdims=True)
                shift[h, s * 8 : (s + 1) * 8, :] = jnp.broadcast_to(along * inv, (8, query))

    def core_copy(b, core):
        return send(
            partial.at[2 * b + core],
            paired.at[b],
            sem_core.at[0, b],
            sem_core.at[1, b],
            (wa, me.peer),
        )

    def out_start():
        for q in range(nz):
            back_own(outown, output, sem_out, q).start()
            for step in range(1, nwa):
                back_copy(outown, output, sem_out, step, q).start()

    def line_copy(up, j, q):
        k = 0 if up else 1
        cols = pl.ds(q * part, part)
        return send(
            partial.at[2 * (nz - 1 - j if up else j) + c, :, cols],
            (up_in if up else down_in).at[j, :, cols],
            sem_line.at[0, k, j, q],
            sem_line.at[1, k, j, q],
            (wa, ta + 2 if up else ta - 2),
        )

    ready = set()

    def core_ready(b):
        if b not in ready:
            ready.add(b)
            core_copy(b, c).wait_recv()

    def chip_sum(b, q):
        cols = pl.ds(q * part, part)
        return partial[2 * b + c, :, cols].astype(F32) + paired[b, :, cols].astype(F32)

    def line_step(up, j, q):
        target = nz - 1 - j if up else j
        landed = up_in if up else down_in
        cols = pl.ds(q * part, part)

        @pl.when(z < target if up else z > target)
        def _():
            first = z == (0 if up else nz - 1)

            @pl.when(jnp.logical_not(first))
            def _():
                line_copy(up, j, q).wait_recv()
                total = chip_sum(target, q) + landed[j, :, cols].astype(F32)
                partial[2 * target + c, :, cols] = total.astype(BF16)

            @pl.when(first)
            def _():
                partial[2 * target + c, :, cols] = chip_sum(target, q).astype(BF16)

            line_copy(up, j, q).start()

    def line(j):
        core_ready(nz - 1 - j)
        core_ready(j)
        for q in range(nz):
            line_step(True, j, q)
            line_step(False, j, q)

    fetch[0].wait()
    for b in order:
        g_cores(b)
    prepare(order[0])
    prepare(order[1])
    line(0)
    for b in order[2:]:
        prepare(b)
    for j in range(1, nz - 1):
        line(j)
    for b in range(nz):
        core_ready(b)

    fetch[1].wait()
    shifts()
    get_wv.wait()
    for t in range(nta):
        turned = jnp.concatenate([wv[w, t] for w in range(nwa)], axis=0).T
        wvt[t * wdepth : (t + 1) * wdepth, :] = turned[:wdepth]
    fetch[2].wait()
    fetch[3].wait()
    norm, inv = norm_stats(xown[...].astype(F32))
    normed[...] = norm
    invs[...] = jnp.broadcast_to(inv, invs.shape)
    gains[...] = jnp.zeros_like(gains)
    biases[...] = jnp.zeros_like(biases)
    fetch[4].wait()
    for b in order:
        g_plane(b)
    out_start()

    def dv_copy(step, q):
        w = (wa + step) % nwa
        return send(
            dvalue.at[:, lanes(q * part + w * CHUNK)],
            dvown.at[block_rows(wa), pl.ds(q * CHUNK, CHUNK)],
            sem_dv.at[0, step, q],
            sem_dv.at[1, step, q],
            (w, ta),
        )

    place = lax.broadcasted_iota(jnp.int32, (width, part), 1).astype(F32)

    def final(q):
        cols = pl.ds(q * part, part)
        key_valid = place + q * part < ln[0:1, 0:1]
        for b in range(nz):

            @pl.when(z == b)
            def _():
                total = chip_sum(b, q)
                if b > 0:
                    line_copy(True, nz - 1 - b, q).wait_recv()
                    total = total + up_in[nz - 1 - b, :, cols].astype(F32)
                if b < nz - 1:
                    line_copy(False, b, q).wait_recv()
                    total = total + down_in[b, :, cols].astype(F32)
                dvalue[:, cols] = jnp.where(key_valid, total, 0.0).astype(BF16)

        for step in range(1, nwa):
            dv_copy(step, q).start()
        dvown[block_rows(wa), q * CHUNK : (q + 1) * CHUNK] = dvalue[
            :, lanes(q * part + wa * CHUNK)
        ]

    for b in order:
        g_end(b)
    g_origin()
    for q in range(nz):
        final(q)

    g_hop(0)
    vmade = lax.dot_general(layer[...], dvalue[...], ROWS_NT, preferred_element_type=F32)
    vsend[...] = vmade.astype(BF16).reshape(nta, wdepth, width)
    vbias = jnp.sum(dvalue[...].astype(F32), axis=1, keepdims=True)

    def v_copy(step):
        t = (ta + step) % nta
        return send(
            vsend.at[t], vrecv.at[step], sem_v.at[0, step], sem_v.at[1, step], (wa, t)
        )

    for step in range(1, nta):
        v_copy(step).start()

    for q in range(nz):
        cols = slice(q * CHUNK, (q + 1) * CHUNK)
        for step in range(1, nwa):
            dv_copy(step, q).wait_recv()
        dl = jnp.dot(wvt[...], dvown[:, cols], preferred_element_type=F32)
        norm = normed[:, cols]
        e = dl * pfull[:, 0:1]
        mean_e = jnp.sum(e, axis=0, keepdims=True) / depth
        mean_n = jnp.sum(e * norm, axis=0, keepdims=True) / depth
        made = dresid[:, cols] + invs[0:1, cols] * (e - mean_e - norm * mean_n)
        tsend[:, cols] = made.astype(BF16)
        back_own(tsend, tgrad, sem_tg, q).start()
        for step in range(1, nwa):
            back_copy(tsend, tgrad, sem_tg, step, q).start()
        gains[...] += dl * norm
        biases[...] += dl

    gain = jnp.sum(gains[...], axis=1, keepdims=True)
    bias = jnp.sum(biases[...], axis=1, keepdims=True)
    column = lax.broadcasted_iota(jnp.int32, (depth, PAD), 1)
    cols = jnp.where(column == 0, gain, jnp.where(column == 1, bias, vcol[...]))
    wide = vrow.shape[1] // nwa
    gap = csend.shape[2] - wide
    for w in range(nwa):
        piece = cols[w * width : (w + 1) * width]
        piece = jnp.concatenate([piece, jnp.zeros((gap - width, PAD), F32)], axis=0)
        csend[w, :, :gap] = piece.T[:8]
        csend[w, :, gap:] = vrow[:, w * wide : (w + 1) * wide]

    def c_copy(step):
        w = (wa + step) % nwa
        return send(csend.at[w], crecv.at[step], sem_c.at[0, step], sem_c.at[1, step], (w, ta))

    for step in range(1, nwa):
        c_copy(step).start()
    g_hop(1)
    crecv[0] = csend[wa]
    piece = jnp.concatenate(
        [jnp.broadcast_to(vbias, (width, PAD)), jnp.zeros((gap - width, PAD), F32)], axis=0
    )
    vb_row = jnp.concatenate([piece.T[:8], jnp.zeros((8, wide), F32)], axis=1)
    row = lax.broadcasted_iota(jnp.int32, vb_row.shape, 0)
    total = jnp.where(row == 2, vb_row, 0.0) + crecv[0]
    for step in range(1, nwa):
        c_copy(step).wait_recv()
        total = total + crecv[step]
    csum[...] = total

    def c2_copy(step):
        t = (ta + step) % nta
        return send(csum, crecv2.at[step], sem_c2.at[0, step], sem_c2.at[1, step], (wa, t))

    for step in range(1, nta):
        c2_copy(step).start()
    for j in range(2, nz - 1):
        g_hop(j)
    value_total = vsend[ta].astype(F32)
    for step in range(1, nta):
        v_copy(step).wait_recv()
        value_total = value_total + vrecv[step].astype(F32)
    vgrad[...] = value_total
    g_final()
    crecv2[0] = csum[...]
    for step in range(1, nta):
        c2_copy(step).wait_recv()
    full = jnp.zeros(csum.shape, F32)
    for t in range(nta):
        full = full + crecv2[(ta - t + nta) % nta]
    vectors[...] = full

    lax.fori_loop(0, nwa * nz, da_sent, 0)
    for step in range(1, nwa):
        for q in range(nz):
            back_copy(tsend, tgrad, sem_tg, step, q).wait()
            back_copy(outown, output, sem_out, step, q).wait()
            dv_copy(step, q).wait_send()
        c_copy(step).wait_send()
    for q in range(nz):
        back_own(outown, output, sem_out, q).wait()
        back_own(tsend, tgrad, sem_tg, q).wait()
    for step in range(1, nta):
        v_copy(step).wait_send()
        c2_copy(step).wait_send()
    for b in range(nz):
        core_copy(b, 1 - c).wait_send()
        g_core(b, 1 - c).wait_send()
        for k in range(2):
            g_first(k, 0, b).wait_send()
            g_first(k, 1, b).wait_send()
            g_second(k, b).wait_send()
    for j in range(nz - 1):

        @pl.when(z < nz - 1 - j)
        def _():
            for q in range(nz):
                line_copy(True, j, q).wait_send()
            g_line(True, j).wait_send()

        @pl.when(z > j)
        def _():
            for q in range(nz):
                line_copy(False, j, q).wait_send()
            g_line(False, j).wait_send()


def run_backward(
    dims, dattended, outown, dresid, xown, terms, mixed, zinv, lens, ln, pfull, layer, weights, wgrad, vcol, vrow
):
    nwa, nta = dims
    nz = nta // 2
    half, both = weights.shape[2] // 2, wgrad.shape[4]
    depth, own = dresid.shape
    width = depth // nwa
    heads, query, seq = terms.shape
    wdepth = depth // nta
    wide = 256 + vrow.shape[1] // nwa
    dma = pltpu.SemaphoreType.DMA
    return pl.pallas_call(
        functools.partial(backward_kernel, dims),
        out_shape=(
            shape_of((nta, width, query), BF16),
            shape_of((heads, nta * 8, query), F32),
            shape_of((width, seq), BF16),
            shape_of((width, seq), BF16),
            shape_of((wdepth, width), F32),
            shape_of((8, wide), F32),
            shape_of((width, both), F32),
        ),
        in_specs=anywhere(6) + whole(4) + anywhere(3) + whole(2),
        out_specs=tuple(whole(7)),
        scratch_shapes=[
            pltpu.VMEM((depth, own), F32),
            pltpu.VMEM((depth, own), BF16),
            pltpu.VMEM((heads, query, seq), BF16),
            pltpu.VMEM((nta, width, query), F32),
            pltpu.VMEM((depth, seq), BF16),
            pltpu.VMEM((depth, own), F32),
            pltpu.VMEM((8, own), F32),
            pltpu.VMEM((depth, depth), BF16),
            pltpu.VMEM((depth, CHUNK), F32),
            pltpu.VMEM((depth, CHUNK), F32),
            pltpu.VMEM((nta, width, query), BF16),
            pltpu.VMEM((nta, width, seq), BF16),
            pltpu.VMEM((nz, width, seq), BF16),
            pltpu.VMEM((nz - 1, width, seq), BF16),
            pltpu.VMEM((nz - 1, width, seq), BF16),
            pltpu.VMEM((nz, nwa, width, both), BF16),
            pltpu.VMEM((nz, nwa, width, both), BF16),
            pltpu.VMEM((nz, 2, half, both), BF16),
            pltpu.VMEM((nz, 2, half, both), BF16),
            pltpu.VMEM((nz, half, both), BF16),
            pltpu.VMEM((nz, half, both), BF16),
            pltpu.VMEM((nz - 1, width, both), BF16),
            pltpu.VMEM((nz - 1, width, both), BF16),
            pltpu.VMEM((width, seq), BF16),
            pltpu.VMEM((depth, own), BF16),
            pltpu.VMEM((nwa, nta, width, PAD), BF16),
            pltpu.VMEM((nta, wdepth, width), BF16),
            pltpu.VMEM((nta, wdepth, width), BF16),
            pltpu.VMEM((depth, own), BF16),
            pltpu.VMEM((nwa, 8, wide), F32),
            pltpu.VMEM((nwa, 8, wide), F32),
            pltpu.VMEM((8, wide), F32),
            pltpu.VMEM((nta, 8, wide), F32),
            dma((2, nta, max(nz, 2))),
            dma((2, nwa, nz)),
            dma((2, nz)),
            dma((2, 2, nz, nz)),
            dma((2, nwa, nz)),
            dma((2, nwa, nz)),
            dma((2, nta)),
            dma((2, nwa)),
            dma((2, nta)),
            dma((6,)),
            dma((2, 8, nz)),
            dma((2, 2, nz)),
        ],
        compiler_params=pltpu.CompilerParams(
            collective_id=2, has_side_effects=True, vmem_limit_bytes=VMEM_BYTES
        ),
        cost_estimate=pl.CostEstimate(
            flops=4 * 10**9, bytes_accessed=80 * 10**6, transcendentals=0
        ),
    )(
        dattended, outown, dresid, xown, terms, mixed, zinv, lens, ln, pfull, layer, weights, wgrad,
        vcol, vrow,
    )


def logits_kernel(
    terms,
    scaled,
    value,
    shift,
    lens,
    output,
    tgrad,
    wsum,
    vgrad,
    out,
    output_out,
    tgrad_out,
    up_out,
    down_out,
    wo_out,
    vgrad_out,
):
    nta = scaled.shape[0]
    output_out[...] = output[...]
    tgrad_out[...] = tgrad[...].astype(F32)
    vgrad_out[...] = vgrad[...]
    hidden = up_out.shape[1]
    up_out[...] = wsum[:, :hidden]
    down_out[...] = wsum[:, hidden : 2 * hidden]
    wo_out[...] = wsum[:, 2 * hidden : 2 * hidden + wo_out.shape[1]]
    cols = terms.shape[2]
    stacked = jnp.concatenate([scaled[s] for s in range(nta)], axis=0)
    values = jnp.concatenate([value[s] for s in range(nta)], axis=0)
    made = lax.dot_general(stacked, values, ROWS_TN, preferred_element_type=F32)
    where = (nta * 8, cols)
    place = lax.broadcasted_iota(jnp.int32, where, 1) + pl.program_id(1) * cols
    first = lax.broadcasted_iota(jnp.int32, where, 0) % 8 == 0
    valid = jnp.logical_and(place.astype(F32) < lens[:, 0:1], first)
    valid = jnp.where(valid, 1.0, 0.0).astype(BF16)
    high = shift[0].astype(BF16)
    rest = (shift[0] - high.astype(F32)).astype(BF16)
    made = made - lax.dot_general(high, valid, ROWS_TN, preferred_element_type=F32)
    made = made - lax.dot_general(rest, valid, ROWS_TN, preferred_element_type=F32)
    out[0] = terms[0].astype(F32) * made


def run_logits(terms, scaled, value, shift, lens, output, tgrad, wsum, vgrad):
    heads, query, seq = terms.shape
    nta, width, _ = scaled.shape
    hdim = width // heads
    cols = min(1024, seq)
    steps = seq // cols
    wdepth = vgrad.shape[0]
    hidden = (wsum.shape[1] - PAD) // 2
    total = heads * steps

    def rows_of(array, lanes_in=None):
        shape = (array[0] // total, lanes_in or array[1])
        return pl.BlockSpec(shape, lambda h, k: (h * steps + k, 0))

    return pl.pallas_call(
        logits_kernel,
        grid=(heads, steps),
        out_shape=(
            shape_of((heads, query, seq), F32),
            shape_of((width, seq), BF16),
            shape_of((width, seq), F32),
            shape_of((width, hidden), F32),
            shape_of((width, hidden), F32),
            shape_of((width, wdepth), F32),
            shape_of(vgrad.shape, F32),
        ),
        in_specs=[
            pl.BlockSpec((1, query, cols), lambda h, k: (h, 0, k)),
            pl.BlockSpec((nta, hdim, query), lambda h, k: (0, h, 0)),
            pl.BlockSpec((nta, hdim, cols), lambda h, k: (0, h, k)),
            pl.BlockSpec((1, nta * 8, query), lambda h, k: (h, 0, 0)),
            pl.BlockSpec(lens.shape, lambda h, k: (0, 0)),
            rows_of(output.shape),
            rows_of(tgrad.shape),
            rows_of(wsum.shape),
            rows_of(vgrad.shape),
        ],
        out_specs=(
            pl.BlockSpec((1, query, cols), lambda h, k: (h, 0, k)),
            rows_of(output.shape),
            rows_of(tgrad.shape),
            rows_of((width, hidden)),
            rows_of((width, hidden)),
            rows_of((width, wdepth)),
            rows_of(vgrad.shape),
        ),
        compiler_params=pltpu.CompilerParams(vmem_limit_bytes=VMEM_BYTES),
        cost_estimate=pl.CostEstimate(
            flops=2 * 10**9, bytes_accessed=20 * 10**6, transcendentals=0
        ),
    )(terms, scaled, value, shift, lens, output, tgrad, wsum, vgrad)


def on_device_fast(
    dims,
    tokens,
    seq_lengths,
    norm1_gain,
    norm1_bias,
    value_weight,
    value_bias,
    synth_logits,
    out_weight,
    out_bias,
    norm2_gain,
    norm2_bias,
    up_weight,
    up_bias,
    down_weight,
    down_bias,
    cotangent,
):
    nwa, nta = dims
    width = tokens.shape[0]
    slim = ((0, 0), (0, PAD - out_weight.shape[1]))
    wlarge = jnp.concatenate([up_weight, down_weight.T], axis=1)
    wsmall = jnp.concatenate([jnp.pad(out_weight, slim), jnp.pad(value_weight.T, slim)], axis=1)
    per_feature = (
        norm1_gain,
        norm1_bias,
        value_bias,
        out_bias,
        norm2_gain,
        norm2_bias,
        down_bias,
    )
    prow = jnp.pad(jnp.stack(per_feature), ((0, 1), (0, 2 * CHUNK - width)))
    prow = jnp.concatenate([prow, jnp.broadcast_to(up_bias, (8, up_bias.shape[0]))], axis=1)
    ln = jnp.broadcast_to(seq_lengths.astype(F32)[:, None], (8, CHUNK))
    logits = synth_logits.transpose(1, 0, 2)
    (
        xown,
        weights,
        _,
        layer,
        value,
        terms,
        mixed,
        zinv,
        lens,
        pfull,
        outown,
        dattended,
        dresid,
        wgrad,
        vcol,
        vrow,
    ) = run_forward(dims, tokens, cotangent, wsmall, wlarge, prow, ln, logits)
    scaled, shift, output, tgrad, vgrad, vectors, wsum = run_backward(
        dims,
        dattended,
        outown,
        dresid,
        xown,
        terms,
        mixed,
        zinv,
        lens,
        ln,
        pfull,
        layer,
        weights,
        wgrad,
        vcol,
        vrow,
    )
    logits_grad, output, tgrad, up_grad, down_grad, out_grad, vgrad = run_logits(
        terms, scaled, value, shift, lens, output, tgrad, wsum, vgrad
    )
    gap = vectors.shape[1] - up_bias.shape[0]
    return (
        output,
        tgrad,
        vectors[0, :width],
        vectors[1, :width],
        vgrad,
        vectors[2, :width],
        logits_grad.transpose(1, 0, 2),
        out_grad,
        vectors[3, :width],
        vectors[4, :width],
        vectors[5, :width],
        up_grad,
        vectors[0, gap:],
        down_grad.T,
        vectors[6, :width],
    )


def fits(mesh):
    return mesh.shape["wa"] == 4 and mesh.shape["ta"] == 8


def solution(mesh):
    placed = (
        P("wa", "ta"),
        P("ta"),
        P("wa"),
        P("wa"),
        P("ta", "wa"),
        P("wa"),
        P("ta", "wa", None),
        P("wa", "ta"),
        P("wa"),
        P("wa"),
        P("wa"),
        P("wa", "ta"),
        P("wa"),
        P("ta", "wa"),
        P("wa"),
        P("wa", "ta"),
    )
    sizes = (mesh.shape["wa"], mesh.shape["ta"])
    body = functools.partial(on_device_fast, sizes) if fits(mesh) else on_device
    return jax.shard_map(
        body,
        mesh=mesh,
        in_specs=placed,
        out_specs=(
            P("wa", "ta"),
            P("wa", "ta"),
            P("wa"),
            P("wa"),
            P("ta", "wa"),
            P("wa"),
            P("ta", "wa", None),
            P("wa", "ta"),
            P("wa"),
            P("wa"),
            P("wa"),
            P("wa", "ta"),
            P("wa"),
            P("ta", "wa"),
            P("wa"),
        ),
        check_vma=False,
    )
```

```python
import functools

import jax
import jax.numpy as jnp
from jax import lax
from jax.experimental import pallas as pl
from jax.experimental.pallas import tpu as pltpu
from jax.sharding import PartitionSpec as P

D = 768


EPSILON = 1e-05
ALONG_FEATURES = (((1,), (1,)), ((), ()))
ALONG_ROWS = (((0,), (0,)), ((), ()))


def row_statistics(first_term, second_term):
    return lax.psum((jnp.sum(first_term, axis=1), jnp.sum(second_term, axis=1)), "wa")


def all_features(features_part):
    return lax.all_gather(features_part, "wa", axis=1, tiled=True)


def feature_share(partial_sum):
    return lax.psum_scatter(partial_sum, "wa", scatter_dimension=1, tiled=True)


def norm_forward(inputs, norm_gain, norm_bias):
    row_total, row_squares = row_statistics(inputs, inputs * inputs)
    row_mean = row_total / D
    variance = row_squares / D - row_mean * row_mean
    inverse = lax.rsqrt(variance + EPSILON)
    normed = (inputs - row_mean[:, None]) * inverse[:, None]
    return (normed * norm_gain + norm_bias, normed, inverse)


def norm_backward(incoming, normed, inverse, norm_gain):
    scaled = incoming * norm_gain
    row_total, row_along = row_statistics(scaled, scaled * normed)
    return inverse[:, None] * (scaled - row_total[:, None] / D - normed * row_along[:, None] / D)


def weights_of(logit_rows, length_all):
    seq_len = logit_rows.shape[2]
    key_valid = (jnp.arange(seq_len)[None, :] < length_all[:, None]).astype(jnp.bfloat16)
    terms = jnp.exp(logit_rows.astype(jnp.float32)).astype(jnp.bfloat16)
    sums = jnp.einsum("phk,sk->sph", terms, key_valid, preferred_element_type=jnp.float32)
    return (terms, sums, key_valid)


def attend(terms, sums, value_all, query_rows):
    mixed = jnp.einsum("phk,skhd->sphd", terms, value_all, preferred_element_type=jnp.float32)
    mixed = mixed / sums[..., None]
    return (mixed, (mixed * query_rows[:, :, None, None]).astype(jnp.bfloat16))


def attend_back(terms, sums, key_valid, value_all, mixed, grad_rows):
    along = jnp.sum(grad_rows.astype(jnp.float32) * mixed, axis=-1) / sums
    scaled = (grad_rows.astype(jnp.float32) / sums[..., None]).astype(jnp.bfloat16)
    dvalue_part = jnp.einsum("phk,sphd->skhd", terms, scaled, preferred_element_type=jnp.float32)
    dlogits = jnp.einsum("sphd,skhd->phk", scaled, value_all, preferred_element_type=jnp.float32)
    high = along.astype(jnp.bfloat16)
    rest = (along - high.astype(jnp.float32)).astype(jnp.bfloat16)
    shift = sum(
        jnp.einsum("sph,sk->phk", part, key_valid, preferred_element_type=jnp.float32)
        for part in (high, rest)
    )
    return (dvalue_part, terms.astype(jnp.float32) * (dlogits - shift))


def on_device(
    tokens,
    seq_lengths,
    norm1_gain,
    norm1_bias,
    value_weight,
    value_bias,
    synth_logits,
    out_weight,
    out_bias,
    norm2_gain,
    norm2_bias,
    up_weight,
    up_bias,
    down_weight,
    down_bias,
    cotangent,
):
    rows_dev = tokens.shape[1]
    local_width = tokens.shape[0]
    seq_count = seq_lengths.shape[0]
    seq_len = synth_logits.shape[2]
    head_count = synth_logits.shape[1]
    head_dim = local_width // head_count
    value_cols, out_rows, up_rows, down_cols = (
        lax.all_gather(value_weight, "ta", axis=0, tiled=True),
        lax.all_gather(out_weight, "ta", axis=1, tiled=True),
        lax.all_gather(up_weight, "ta", axis=1, tiled=True),
        lax.all_gather(down_weight, "ta", axis=0, tiled=True),
    )
    up_block, down_block = (
        lax.all_to_all(up_rows.T, "wa", split_axis=0, concat_axis=1, tiled=True),
        lax.all_to_all(down_cols, "wa", split_axis=0, concat_axis=1, tiled=True),
    )
    inputs = tokens.T.astype(jnp.float32)
    pre_one, normed_one, inverse_one = norm_forward(inputs, norm1_gain, norm1_bias)
    layer_one = all_features(pre_one.astype(jnp.bfloat16))
    values = (
        jnp.dot(layer_one, value_cols, preferred_element_type=jnp.float32) + value_bias
    ).astype(jnp.bfloat16)
    value_heads = values.reshape(seq_count, seq_len, head_count, head_dim)
    positions = jnp.arange(seq_len)
    key_valid = positions[None, :] < seq_lengths[:, None]
    query_valid = key_valid.astype(jnp.float32)
    length_all = lax.all_gather(seq_lengths, "ta", axis=0, tiled=True)
    block_rows = synth_logits.shape[0]
    value_all = lax.all_gather(
        value_heads * key_valid[:, :, None, None].astype(jnp.bfloat16), "ta", axis=0, tiled=True
    )
    terms, sums, key_valid_all = weights_of(synth_logits, length_all)
    block_positions = lax.axis_index("ta") * block_rows + jnp.arange(block_rows)
    query_rows = (block_positions[None, :] < length_all[:, None]).astype(jnp.float32)
    mixed_rows, mixed_low = attend(terms, sums, value_all, query_rows)
    attended = lax.all_to_all(mixed_low, "ta", split_axis=0, concat_axis=1, tiled=True)
    attended = attended.reshape(rows_dev, local_width)
    branch = (
        feature_share(jnp.dot(attended, out_rows, preferred_element_type=jnp.float32)) + out_bias
    )
    resid = inputs + branch
    pre_two, normed_two, inverse_two = norm_forward(resid, norm2_gain, norm2_bias)
    layer_two = all_features(pre_two.astype(jnp.bfloat16))
    upper = (
        lax.dot_general(layer_two, up_block, ALONG_FEATURES, preferred_element_type=jnp.float32)
        + up_bias
    )
    hidden, gelu_back = jax.vjp(jax.nn.gelu, upper)
    hidden_low = hidden.astype(jnp.bfloat16)
    feed = (
        feature_share(jnp.dot(hidden_low, down_block, preferred_element_type=jnp.float32))
        + down_bias
    )
    output = (resid + feed).astype(jnp.bfloat16)
    cotangent_rows = cotangent.T
    grad_in = cotangent_rows.astype(jnp.float32)
    grad_full = all_features(cotangent_rows)
    dhidden = lax.dot_general(
        grad_full, down_block, ALONG_FEATURES, preferred_element_type=jnp.float32
    )
    dupper = gelu_back(dhidden)[0].astype(jnp.bfloat16)
    down_part = lax.dot_general(
        hidden_low, grad_full, ALONG_ROWS, preferred_element_type=jnp.float32
    )
    up_part = lax.dot_general(dupper, layer_two, ALONG_ROWS, preferred_element_type=jnp.float32)
    up_bias_part = jnp.sum(dupper.astype(jnp.float32), axis=0)
    down_bias_part = jnp.sum(grad_in, axis=0)
    dlayer_two = feature_share(jnp.dot(dupper, up_block, preferred_element_type=jnp.float32))
    gain_two_part = jnp.sum(dlayer_two * normed_two, axis=0)
    bias_two_part = jnp.sum(dlayer_two, axis=0)
    dresid = grad_in + norm_backward(dlayer_two, normed_two, inverse_two, norm2_gain)
    dbranch = dresid.astype(jnp.bfloat16)
    dbranch_full = all_features(dbranch)
    dattended = lax.dot_general(
        dbranch_full, out_rows, ALONG_FEATURES, preferred_element_type=jnp.float32
    ).astype(jnp.bfloat16)
    out_part = lax.dot_general(
        attended, dbranch_full, ALONG_ROWS, preferred_element_type=jnp.float32
    )
    out_bias_part = jnp.sum(dbranch.astype(jnp.float32), axis=0)
    grad_heads = dattended.reshape(seq_count, seq_len, head_count, head_dim)
    grad_heads = grad_heads * query_valid[:, :, None, None].astype(jnp.bfloat16)
    grad_block = lax.all_to_all(grad_heads, "ta", split_axis=1, concat_axis=0, tiled=True)
    dvalue_part, logits_grad = attend_back(
        terms, sums, key_valid_all, value_all, mixed_rows, grad_block
    )
    dvalue_rows = dvalue_part.astype(jnp.bfloat16).reshape(-1, local_width)
    dvalue_rows = lax.psum_scatter(dvalue_rows, "ta", scatter_dimension=0, tiled=True)
    dvalues = dvalue_rows * query_valid.reshape(rows_dev, 1).astype(jnp.bfloat16)
    value_part = lax.dot_general(layer_one, dvalues, ALONG_ROWS, preferred_element_type=jnp.float32)
    value_bias_part = jnp.sum(dvalues.astype(jnp.float32), axis=0)
    dlayer_one = feature_share(
        lax.dot_general(dvalues, value_cols, ALONG_FEATURES, preferred_element_type=jnp.float32)
    )
    gain_one_part = jnp.sum(dlayer_one * normed_one, axis=0)
    bias_one_part = jnp.sum(dlayer_one, axis=0)
    tokens_grad = dresid + norm_backward(dlayer_one, normed_one, inverse_one, norm1_gain)
    up_back, down_back = (
        lax.all_to_all(up_part, "wa", split_axis=1, concat_axis=0, tiled=True),
        lax.all_to_all(down_part, "wa", split_axis=1, concat_axis=0, tiled=True),
    )
    value_grad, out_grad, up_grad, down_grad = (
        lax.psum_scatter(value_part, "ta", scatter_dimension=0, tiled=True),
        lax.psum_scatter(out_part, "ta", scatter_dimension=1, tiled=True),
        lax.psum_scatter(up_back, "ta", scatter_dimension=0, tiled=True),
        lax.psum_scatter(down_back, "ta", scatter_dimension=0, tiled=True),
    )
    vector_grads = lax.psum(
        (
            gain_one_part,
            bias_one_part,
            value_bias_part,
            out_bias_part,
            gain_two_part,
            bias_two_part,
            up_bias_part,
            down_bias_part,
        ),
        "ta",
    )
    return (
        output.T,
        tokens_grad.T,
        vector_grads[0],
        vector_grads[1],
        value_grad,
        vector_grads[2],
        logits_grad,
        out_grad,
        vector_grads[3],
        vector_grads[4],
        vector_grads[5],
        up_grad.T,
        vector_grads[6],
        down_grad,
        vector_grads[7],
    )


MESH = pl.DeviceIdType.MESH
ROWS_NT = (((1,), (1,)), ((), ()))
ROWS_TN = (((0,), (0,)), ((), ()))
F32 = jnp.float32
BF16 = jnp.bfloat16
VMEM_BYTES = 60 * 2**20
CHUNK = 128
PAD = 128
AHEAD = 1


def whole(count):
    return [pl.BlockSpec(memory_space=pltpu.VMEM)] * count


def anywhere(count):
    return [pl.BlockSpec(memory_space=pl.ANY)] * count


def shape_of(shape, dtype):
    return jax.ShapeDtypeStruct(shape, dtype)


def lanes(start, size=CHUNK):
    return pl.ds(pl.multiple_of(start, CHUNK), size)


def rows_at(start, size, unit):
    return pl.ds(pl.multiple_of(start, unit), size)


class Place:
    def __init__(self, nwa, nta):
        self.nwa, self.nta, self.nz = nwa, nta, nta // 2
        self.wa = lax.axis_index("wa")
        self.ta = lax.axis_index("ta")
        self.z = self.ta // 2
        self.c = self.ta % 2
        self.peer = self.ta + 1 - 2 * self.c
        self.wx = self.wa + 1 - 2 * (self.wa % 2)
        self.wy = (self.wa + 2) % 4
        self.wd = 3 - self.wa

    def enter(self):
        barrier = pltpu.get_barrier_semaphore()
        total = self.nwa * self.nta

        def greet(step, carry):
            w = (self.wa + step // self.nta) % self.nwa
            t = (self.ta + step % self.nta) % self.nta
            pl.semaphore_signal(barrier, inc=1, device_id=(w, t), device_id_type=MESH)
            return carry

        lax.fori_loop(1, total, greet, 0)
        pl.semaphore_wait(barrier, total - 1)


def send(src, dst, ssem, rsem, device):
    return pltpu.make_async_remote_copy(
        src_ref=src,
        dst_ref=dst,
        send_sem=ssem,
        recv_sem=rsem,
        device_id=device,
        device_id_type=MESH,
    )


def when(condition):
    return pl.when(condition)


def norm_stats(block):
    width = block.shape[0]
    mean = jnp.sum(block, axis=0, keepdims=True) / width
    centred = block - mean
    variance = jnp.sum(centred * centred, axis=0, keepdims=True) / width
    inverse = lax.rsqrt(variance + EPSILON)
    return (centred * inverse, inverse)


def forward_kernel(
    dims,
    tok,
    cot,
    wout,
    wval,
    wup,
    wdown,
    prow,
    ln,
    logits,
    xown,
    small,
    large,
    layer_out,
    value_out,
    term_out,
    mixed,
    zinv,
    lens,
    pfull,
    out,
    dattended,
    dresid,
    wgrad,
    vcol,
    vrow,
    cown,
    attended,
    rfull,
    wo,
    wblock,
    resid,
    normed,
    inverse,
    layer_two,
    layer_t,
    grad_t,
    feed,
    dlayer,
    wide,
    gblock,
    gwo,
    x,
    wvc,
    layer_pad,
    layer,
    value,
    terms,
    attsend,
    rows,
    turned,
    wsmall,
    sem_tok,
    sem_par,
    sem_ta,
    sem_val,
    sem_small,
    sem_large,
    sem_cot,
    sem_att,
    sem_local,
    sem_out,
    sem_wv,
    sem_g,
):
    nwa, nta = dims
    me = Place(nwa, nta)
    wa, ta, z, c = me.wa, me.ta, me.z, me.c
    nz = me.nz
    width = tok.shape[0]
    half = width // 2
    seq = tok.shape[1]
    part = seq // nz
    query = seq // nta
    slot = wvc.shape[1] // nta
    wdepth = wvc.shape[0] * nwa // nta
    heads = terms.shape[0]
    hdim = width // heads
    split = PAD
    get_logits = pltpu.make_async_copy(logits, terms, sem_local.at[5])
    get_logits.start()
    stores = ((small, sem_small), (large, sem_large))
    one = wup.shape[1]
    own_w = (
        pltpu.make_async_copy(wsmall, small.at[wa, ta], sem_local.at[2]),
        pltpu.make_async_copy(wup, large.at[wa, ta, :, pl.ds(0, one)], sem_local.at[6]),
        pltpu.make_async_copy(wdown, large.at[wa, ta, :, pl.ds(one, one)], sem_local.at[7]),
    )
    own_w[1].start()
    own_w[2].start()
    turned[...] = jnp.zeros_like(turned)
    turned[:wdepth, :width] = wval[...]
    wsmall[...] = jnp.zeros_like(wsmall)
    wsmall[:, :wdepth] = wout[...]
    wsmall[:, split:] = turned[...].T[:width]
    own_w[0].start()
    me.enter()


    def block_rows(w, off=0, size=width):
        return rows_at(w * width + off, size, 32)

    def tok_copy(k, q):
        device = (me.wx if k == 0 else me.wy, ta)
        return send(
            tok.at[:, pl.ds(q * part, part)],
            x.at[block_rows(wa), pl.ds(q * part, part)],
            sem_tok.at[0, k, q],
            sem_tok.at[1, k, q],
            device,
        )

    def tok_fwd(k, q):
        source = me.wx if k == 0 else me.wy
        device = (me.wy if k == 0 else me.wx, ta)
        where = x.at[block_rows(source, k * half, half), pl.ds(q * part, part)]
        return send(where, where, sem_tok.at[0, 2 + k, q], sem_tok.at[1, 2 + k, q], device)

    own_x = pltpu.make_async_copy(tok, x.at[block_rows(wa)], sem_local.at[0])
    own_x.start()

    def tok_start(q):
        for k in range(2):
            tok_copy(k, q).start()

    def tok_turn(q):
        for k in range(2):
            tok_copy(k, q).wait_recv()
            tok_fwd(k, q).start()
        if q + AHEAD < nz:
            tok_start(q + AHEAD)

    for q in range(AHEAD):
        tok_start(q)

    def par_copy(step):
        w = (wa + step) % nwa
        return send(prow, rows.at[wa], sem_par.at[0, step], sem_par.at[1, step], (w, ta))

    def ta_copy(step):
        t = (ta + step) % nta
        return send(
            ln, lens.at[rows_at(ta * 8, 8, 8)], sem_ta.at[0, step], sem_ta.at[1, step], (wa, t)
        )

    def wv_column(b, core):
        return wvc.at[:, lanes((2 * b + core) * slot)]

    def wv_z(step):
        b = (z + step) % nz
        src = wsmall.at[:, pl.ds(split, PAD)]
        return send(
            src, wv_column(z, c), sem_wv.at[0, 0, step], sem_wv.at[1, 0, step], (wa, 2 * b + c)
        )

    def wv_core(step, core):
        where = wv_column((z - step + nz) % nz, core)
        return send(where, where, sem_wv.at[0, 1, step], sem_wv.at[1, 1, step], (wa, me.peer))

    own_wv = pltpu.make_async_copy(wsmall.at[:, pl.ds(split, PAD)], wv_column(z, c), sem_local.at[1])
    own_wv.start()
    for step in range(nz - 1, 0, -1):
        wv_z(step).start()
    for step in range(1, nwa):
        par_copy(step).start()
    for step in range(1, nta):
        ta_copy(step).start()
    rows[wa] = prow[...]
    lens[rows_at(ta * 8, 8, 8), :] = ln[...]
    own_wv.wait()
    wv_core(0, c).start()

    def w_line(p, up, b):
        where, sem = stores[p][0].at[wa, 2 * b + c], stores[p][1]
        k = 0 if up else 1
        return send(
            where, where, sem.at[0, k, b], sem.at[1, k, b], (wa, ta + 2 if up else ta - 2)
        )

    for step in range(1, nz):
        wv_z(step).wait_recv()
        wv_core(step, c).start()
    for copy in own_w:
        copy.wait()

    @pl.when(z < nz - 1)
    def _():
        for p in range(2):
            w_line(p, True, z).start()

    @pl.when(z > 0)
    def _():
        for p in range(2):
            w_line(p, False, z).start()

    layer_pad[...] = jnp.zeros_like(layer_pad)
    get_logits.wait()
    for h in range(heads):
        terms[h] = jnp.exp(terms[h].astype(F32)).astype(BF16)
    out_terms = pltpu.make_async_copy(terms, term_out, sem_local.at[3])
    out_terms.start()

    tok_turn(0)
    for step in range(1, nwa):
        par_copy(step).wait_recv()
    gap = 2 * CHUNK
    for w in range(nwa):
        piece = jnp.concatenate([rows[w, :, :gap], jnp.zeros((PAD - 8, gap), F32)], axis=0)
        pfull[w * width : (w + 1) * width, :] = piece.T[:width]
        span = rows.shape[2] - gap
        rfull[:, w * span : (w + 1) * span] = rows[w, :, gap:]
    for step in range(1, nta):
        ta_copy(step).wait_recv()
    for step in range(nz):
        wv_core(step, 1 - c).wait_recv()
    own_x.wait()

    positions = lax.broadcasted_iota(jnp.int32, (nta * 8, seq), 1).astype(F32)
    key_valid = jnp.where(positions < lens[:, 0:1], 1.0, 0.0).astype(BF16)
    for h in range(heads):
        sums = lax.dot_general(key_valid, terms[h], ROWS_NT, preferred_element_type=F32)
        zinv[h] = 1.0 / sums

    def value_copy(kind, b, q, core):
        where = value.at[2 * b + core, :, pl.ds(q * part, part)]
        t = (ta + 2, ta - 2, me.peer)[kind]
        return send(where, where, sem_val.at[0, kind, b, q], sem_val.at[1, kind, b, q], (wa, t))

    def w_plane(p, k, b):
        device = (me.wx if k == 0 else me.wy, ta)
        where, sem = stores[p][0].at[wa, 2 * b + c], stores[p][1]
        return send(where, where, sem.at[0, 2 + k, b], sem.at[1, 2 + k, b], device)

    def w_diag(p, k, b, source):
        device = (me.wy if k == 0 else me.wx, ta)
        where, sem = stores[p][0].at[source, 2 * b + c, pl.ds(k * half, half)], stores[p][1]
        return send(where, where, sem.at[0, 4 + k, b], sem.at[1, 4 + k, b], device)

    def w_core(p, r, b, core):
        source = (wa, me.wx, me.wy, me.wd)[r]
        where, sem = stores[p][0].at[source, 2 * b + core], stores[p][1]
        return send(where, where, sem.at[0, 6 + r, b], sem.at[1, 6 + r, b], (wa, me.peer))

    def w_start(p, b):
        w_plane(p, 0, b).start()
        w_plane(p, 1, b).start()
        w_core(p, 0, b, c).start()

    def w_forward(p, b):
        w_plane(p, 0, b).wait_recv()
        w_diag(p, 0, b, me.wx).start()
        w_core(p, 1, b, c).start()
        w_plane(p, 1, b).wait_recv()
        w_diag(p, 1, b, me.wy).start()
        w_core(p, 2, b, c).start()

    def w_finish(p, b):
        for k in range(2):
            w_diag(p, k, b, me.wd).wait_recv()
        w_core(p, 3, b, c).start()

    def w_landed(p, h):
        @pl.when(z - 1 - h >= 0)
        def _():
            w_line(p, True, z - 1 - h).wait_recv()

        @pl.when(z + 1 + h < nz)
        def _():
            w_line(p, False, z + 1 + h).wait_recv()

    def w_onward(p, h):
        @pl.when(jnp.logical_and(z - 1 - h >= 0, z < nz - 1))
        def _():
            w_line(p, True, z - 1 - h).start()

        @pl.when(jnp.logical_and(z + 1 + h < nz, z > 0))
        def _():
            w_line(p, False, z + 1 + h).start()

    def at_hop(h, act, *args):
        @pl.when(z - 1 - h >= 0)
        def _():
            act(*args, z - 1 - h)

        @pl.when(z + 1 + h < nz)
        def _():
            act(*args, z + 1 + h)

    for q in range(nz):
        cols = pl.ds(q * part, part)
        if q + 1 < nz:
            tok_turn(q + 1)
        for k in range(2):
            where = x.at[block_rows(me.wd, k * half, half), cols]
            send(
                where,
                where,
                sem_tok.at[0, 2 + k, q],
                sem_tok.at[1, 2 + k, q],
                (me.wy if k == 0 else me.wx, ta),
            ).wait_recv()
        centred, _ = norm_stats(x[:, cols].astype(F32))
        low = (centred * pfull[:, 0:1] + pfull[:, 1:2]).astype(BF16)
        layer[:, cols] = low
        for t in range(nta):
            layer_pad[t * slot : t * slot + wdepth, :] = low[t * wdepth : (t + 1) * wdepth]
        made = jnp.dot(wvc[...], layer_pad[...], preferred_element_type=F32)
        made = made + pfull[block_rows(wa), :][:, 2:3]
        place = lax.broadcasted_iota(jnp.int32, (width, part), 1) + q * part
        made = jnp.where(place.astype(F32) < ln[0:1, 0:1], made, 0.0)
        value[ta, :, cols] = made.astype(BF16)
        xown[:, pl.ds(q * CHUNK, CHUNK)] = x[:, lanes(q * part + wa * CHUNK)]

        @pl.when(z < nz - 1)
        def _():
            value_copy(0, z, q, c).start()

        @pl.when(z > 0)
        def _():
            value_copy(1, z, q, c).start()

        value_copy(2, z, q, c).start()
        if q < nz - 1:
            w_landed(0, q)
            w_onward(0, q)
    out_layer = pltpu.make_async_copy(layer, layer_out, sem_local.at[4])
    out_layer.start()

    def cot_copy(step, q):
        w = (wa + step) % nwa
        return send(
            cot.at[:, lanes(q * part + w * CHUNK)],
            cown.at[block_rows(wa), pl.ds(q * CHUNK, CHUNK)],
            sem_cot.at[0, step, q],
            sem_cot.at[1, step, q],
            (w, ta),
        )

    def cot_own(q):
        return pltpu.make_async_copy(
            cot.at[:, lanes(q * part + wa * CHUNK)],
            cown.at[block_rows(wa), pl.ds(q * CHUNK, CHUNK)],
            sem_cot.at[0, 0, q],
        )

    w_start(0, z)
    for h in range(nz - 1):
        at_hop(h, w_start, 0)
    w_start(1, z)
    w_landed(1, 0)
    at_hop(0, w_start, 1)
    for q in range(nz):
        cot_own(q).start()
        for step in range(1, nwa):
            cot_copy(step, q).start()

    def att_copy(s, j):
        return send(
            attsend.at[s, :, pl.ds(j * CHUNK, CHUNK)],
            attended.at[block_rows(wa), lanes(z * CHUNK)],
            sem_att.at[0, s, j],
            sem_att.at[1, wa, z],
            (2 * c + j, s),
        )

    def att_local(s, j):
        return pltpu.make_async_copy(
            attsend.at[s, :, pl.ds(j * CHUNK, CHUNK)],
            attended.at[block_rows(wa), lanes(z * CHUNK)],
            sem_att.at[0, s, j],
        )

    def is_self(s, j):
        return jnp.logical_and(s == ta, 2 * c + j == wa)

    def mix(b):
        for core in range(2):
            s = 2 * b + core
            pltpu.make_async_copy(value.at[s], value_out.at[s], sem_out.at[s]).start()
        length = [lens[rows_at((2 * b + core) * 8, 8, 8), :][0:1, 0:1] for core in range(2)]
        place = lax.broadcasted_iota(jnp.int32, (hdim, query), 1) + ta * query
        place = place.astype(F32)
        for h in range(heads):
            group = slice(h * hdim, (h + 1) * hdim)
            pair = jnp.concatenate([value[2 * b, group, :], value[2 * b + 1, group, :]], axis=0)
            both = lax.dot_general(pair, terms[h], ROWS_NT, preferred_element_type=F32)
            for core in range(2):
                s = 2 * b + core
                inverse = zinv[h, rows_at(s * 8, 8, 8), :][0:1]
                one = both[core * hdim : (core + 1) * hdim] * inverse
                mixed[s, group, :] = one
                one = jnp.where(place < length[core], one, 0.0)
                attsend[s, group, :] = one.astype(BF16)
        for core in range(2):
            s = 2 * b + core
            for j in range(2):

                @pl.when(is_self(s, j))
                def _():
                    att_local(s, j).start()

                @pl.when(jnp.logical_not(is_self(s, j)))
                def _():
                    att_copy(s, j).start()

    def core_ready(b):
        for q in range(nz):
            value_copy(2, b, q, 1 - c).wait_recv()

    for h in range(nz - 1):
        below, above = z - 1 - h, z + 1 + h
        for q in range(nz):

            @pl.when(below >= 0)
            def _():
                value_copy(0, below, q, c).wait_recv()

                @pl.when(z < nz - 1)
                def _():
                    value_copy(0, below, q, c).start()

                value_copy(2, below, q, c).start()

            @pl.when(above < nz)
            def _():
                value_copy(1, above, q, c).wait_recv()

                @pl.when(z > 0)
                def _():
                    value_copy(1, above, q, c).start()

                value_copy(2, above, q, c).start()

        if h == 0:
            core_ready(z)
            mix(z)

        @pl.when(below >= 0)
        def _():
            core_ready(below)
            mix(below)

        @pl.when(above < nz)
        def _():
            core_ready(above)
            mix(above)

        if h == 0:
            w_forward(0, z)
            for other in range(nz - 1):
                at_hop(other, w_forward, 0)
        if h == 1:
            w_onward(1, 0)
            w_forward(1, z)
            w_finish(0, z)
            for other in range(nz - 1):
                at_hop(other, w_finish, 0)
    at_hop(0, w_forward, 1)
    w_finish(1, z)
    at_hop(0, w_finish, 1)

    def w_cores(p, b):
        for r in range(4):
            w_core(p, r, b, 1 - c).wait_recv()

    depth, own = xown.shape
    both = 2 * one

    def turn(i):
        pair = z + 1 - 2 * (z % 2)
        late = jnp.where(i == 2, nz // 2 - z // 2, (nz - 1) * (1 - z // 2))
        return jnp.where(i == 0, z, jnp.where(i == 1, pair, late))

    def load(i, slot):
        b = turn(i)
        return pltpu.make_async_copy(
            large.at[:, pl.ds(2 * b, 2)], wblock.at[slot], sem_g.at[slot]
        )

    w_cores(1, turn(0))
    load(0, 0).start()
    for b in range(nz):
        w_cores(0, b)
    get_wo = pltpu.make_async_copy(small.at[:, :, :, pl.ds(0, PAD)], wo, sem_g.at[2])
    get_wo.start()
    for q in range(nz):
        cot_own(q).wait()
        for step in range(1, nwa):
            cot_copy(step, q).wait_recv()
    grad_t[...] = cown[...].T
    w_cores(1, turn(1))
    load(1, 1).start()

    def att_sends(s, carry):
        pltpu.make_async_copy(value.at[s], value_out.at[s], sem_out.at[s]).wait()
        for j in range(2):

            @pl.when(is_self(s, j))
            def _():
                att_local(s, j).wait()

            @pl.when(jnp.logical_not(is_self(s, j)))
            def _():
                att_copy(s, j).wait_send()

        return carry

    lax.fori_loop(0, nta, att_sends, 0)
    mine = wa // 2

    def att_arrivals(k, carry):
        w, b = k // nz, k % nz

        @pl.when(jnp.logical_not(jnp.logical_and(w == wa, 2 * b + mine == ta)))
        def _():
            where = attended.at[block_rows(w), lanes(b * CHUNK)]
            send(where, where, sem_att.at[0, 0, 0], sem_att.at[1, w, b], (w, 2 * b + mine)).wait_recv()

        return carry

    w_landed(1, 1)
    w_onward(1, 1)
    at_hop(1, w_start, 1)
    lax.fori_loop(0, nwa * nz, att_arrivals, 0)
    get_wo.wait()

    def wide_wo():
        joined = [
            jnp.concatenate([wo[w, t] for t in range(nta)], axis=1) for w in range(nwa)
        ]
        return jnp.concatenate(joined, axis=0)

    branch = lax.dot_general(wide_wo(), attended[...], ROWS_TN, preferred_element_type=F32)
    branch = jnp.concatenate([branch[t * PAD : t * PAD + wdepth] for t in range(nta)], axis=0)
    res = xown[...].astype(F32) + branch + pfull[:, 3:4]
    resid[...] = res
    norm, inv = norm_stats(res)
    normed[...] = norm
    inverse[...] = jnp.broadcast_to(inv, inverse.shape)
    low = (norm * pfull[:, 4:5] + pfull[:, 5:6]).astype(BF16)
    layer_two[...] = low
    layer_t[...] = low.T
    feed[...] = jnp.zeros_like(feed)
    dlayer[...] = jnp.zeros_like(dlayer)

    def put(i):
        return pltpu.make_async_copy(
            gblock, wgrad.at[:, turn(i), :, :, pl.ds(0, both)], sem_g.at[3]
        )

    def middle(i, carry):
        slot = i % 2

        @pl.when(i == 2)
        def _():
            at_hop(1, w_finish, 1)
            w_landed(1, 2)
            at_hop(2, w_start, 1)
            w_cores(1, turn(2))
            load(2, 0).start()

        @pl.when(i == 3)
        def _():
            at_hop(2, w_forward, 1)
            at_hop(2, w_finish, 1)
            w_cores(1, turn(3))
            load(3, 1).start()

        load(i, slot).wait()
        held = wblock.at[slot]

        def joined(start):
            parts = [held[:, g, :, start : start + one].reshape(depth, one) for g in range(2)]
            return jnp.concatenate(parts, axis=1)

        up, down_t = joined(0), joined(one)
        at = lanes(turn(i) * both, both)
        upper = jnp.dot(layer_t[...], up, preferred_element_type=F32) + rfull[0:1, at]
        hidden, slope = gelu_pair(upper)
        hidden = hidden.astype(BF16)
        dhidden = jnp.dot(grad_t[...], down_t, preferred_element_type=F32)
        dupper = (dhidden * slope).astype(BF16)
        vrow[:, at] = jnp.broadcast_to(
            jnp.sum(dupper.astype(F32), axis=0, keepdims=True), (vrow.shape[0], both)
        )
        feed[...] += lax.dot_general(down_t, hidden, ROWS_NT, preferred_element_type=F32)
        dlayer[...] += lax.dot_general(up, dupper, ROWS_NT, preferred_element_type=F32)
        gup = jnp.dot(layer_two[...], dupper, preferred_element_type=F32)
        gdown = jnp.dot(cown[...], hidden, preferred_element_type=F32)

        @pl.when(i > 0)
        def _():
            put(i - 1).wait()

        for g in range(2):
            piece = slice(g * one, (g + 1) * one)
            gblock[:, g, :, :one] = gup[:, piece].reshape(nwa, width, one).astype(BF16)
            gblock[:, g, :, one:] = gdown[:, piece].reshape(nwa, width, one).astype(BF16)
        put(i).start()

        @pl.when(i == 0)
        def _():
            at_hop(1, w_forward, 1)

        return carry

    lax.fori_loop(0, nz, middle, 0)

    grad = cown[...].astype(F32)
    out[...] = (resid[...] + feed[...] + pfull[:, 6:7]).astype(BF16)
    dl = dlayer[...]
    norm = normed[...]
    e = dl * pfull[:, 4:5]
    mean_e = jnp.sum(e, axis=0, keepdims=True) / depth
    mean_n = jnp.sum(e * norm, axis=0, keepdims=True) / depth
    dres = grad + inverse[0:1, :] * (e - mean_e - norm * mean_n)
    dresid[...] = dres
    low = dres.astype(BF16)
    vcol[...] = jnp.zeros_like(vcol)
    vcol[:, 3:4] = jnp.sum(low.astype(F32), axis=1, keepdims=True)
    vcol[:, 4:5] = jnp.sum(dl * norm, axis=1, keepdims=True)
    vcol[:, 5:6] = jnp.sum(dl, axis=1, keepdims=True)
    vcol[:, 6:7] = jnp.sum(grad, axis=1, keepdims=True)
    wide[...] = jnp.zeros_like(wide)
    for t in range(nta):
        wide[t * PAD : t * PAD + wdepth, :] = low[t * wdepth : (t + 1) * wdepth]
    da = jnp.dot(wide_wo(), wide[...], preferred_element_type=F32)
    lane = lax.broadcasted_iota(jnp.int32, (depth, own), 1)
    place = (lane // CHUNK) * (CHUNK * nwa) + lane % CHUNK + wa * CHUNK
    da = jnp.where(place.astype(F32) < ln[0:1, 0:1], da, 0.0)
    dattended[...] = da.astype(BF16)
    made = lax.dot_general(attended[...], wide[...], ROWS_NT, preferred_element_type=F32)
    for t in range(nta):
        piece = made[:, t * PAD : (t + 1) * PAD].reshape(nwa, width, PAD)
        gwo[:, t // 2, t % 2] = piece.astype(BF16)
    rest = pltpu.make_async_copy(gwo, wgrad.at[:, :, :, :, pl.ds(both, PAD)], sem_g.at[4])
    rest.start()
    put(nz - 1).wait()
    rest.wait()

    for step in range(1, nta):
        ta_copy(step).wait_send()
    for step in range(nz):
        wv_core(step, c).wait_send()
        if step:
            wv_z(step).wait_send()
    for step in range(1, nwa):
        par_copy(step).wait_send()
        for q in range(nz):
            cot_copy(step, q).wait_send()
    for q in range(nz):
        for k in range(2):
            tok_copy(k, q).wait_send()
            tok_fwd(k, q).wait_send()

    def line_sends(b, carry):
        reach_up = jnp.logical_and(b <= z, z < nz - 1)
        reach_down = jnp.logical_and(b >= z, z > 0)

        @pl.when(reach_up)
        def _():
            for p in range(2):
                w_line(p, True, b).wait_send()
            for q in range(nz):
                value_copy(0, b, q, c).wait_send()

        @pl.when(reach_down)
        def _():
            for p in range(2):
                w_line(p, False, b).wait_send()
            for q in range(nz):
                value_copy(1, b, q, c).wait_send()

        for q in range(nz):
            value_copy(2, b, q, c).wait_send()
        for p in range(2):
            for k in range(2):
                w_plane(p, k, b).wait_send()
            w_diag(p, 0, b, me.wx).wait_send()
            w_diag(p, 1, b, me.wy).wait_send()
            for r in range(4):
                w_core(p, r, b, c).wait_send()
        return carry

    lax.fori_loop(0, nz, line_sends, 0)

    out_terms.wait()
    out_layer.wait()


def run_forward(dims, tok, cot, wout, wval, wup, wdown, prow, ln, logits):
    nwa, nta = dims
    nz = nta // 2
    width, seq = tok.shape
    depth = width * nwa
    own = seq // nwa
    heads, query, _ = logits.shape
    slot = PAD
    both = 2 * wup.shape[1]
    hidden = both // 2 * nta
    dma = pltpu.SemaphoreType.DMA
    return pl.pallas_call(
        functools.partial(forward_kernel, dims),
        out_shape=(
            shape_of((depth, own), BF16),
            shape_of((nwa, nta, width, 2 * PAD), BF16),
            shape_of((nwa, nta, width, both), BF16),
            shape_of((depth, seq), BF16),
            shape_of((nta, width, seq), BF16),
            shape_of((heads, query, seq), BF16),
            shape_of((nta, width, query), F32),
            shape_of((heads, nta * 8, query), F32),
            shape_of((nta * 8, CHUNK), F32),
            shape_of((depth, PAD), F32),
            shape_of((depth, own), BF16),
            shape_of((depth, own), BF16),
            shape_of((depth, own), F32),
            shape_of((nwa, nz, 2, width, both + PAD), BF16),
            shape_of((depth, PAD), F32),
            shape_of((8, hidden), F32),
        ),
        in_specs=anywhere(2) + whole(2) + anywhere(2) + whole(2) + anywhere(1),
        out_specs=tuple(whole(1) + anywhere(5) + whole(7) + anywhere(1) + whole(2)),
        scratch_shapes=[
            pltpu.VMEM((depth, own), BF16),
            pltpu.VMEM((depth, own), BF16),
            pltpu.VMEM((8, hidden), F32),
            pltpu.VMEM((nwa, nta, width, PAD), BF16),
            pltpu.VMEM((2, nwa, 2, width, both), BF16),
            pltpu.VMEM((depth, own), F32),
            pltpu.VMEM((depth, own), F32),
            pltpu.VMEM((8, own), F32),
            pltpu.VMEM((depth, own), BF16),
            pltpu.VMEM((own, depth), BF16),
            pltpu.VMEM((own, depth), BF16),
            pltpu.VMEM((depth, own), F32),
            pltpu.VMEM((depth, own), F32),
            pltpu.VMEM((nta * PAD, own), BF16),
            pltpu.VMEM((nwa, 2, width, both), BF16),
            pltpu.VMEM((nwa, nz, 2, width, PAD), BF16),
            pltpu.VMEM((depth, seq), BF16),
            pltpu.VMEM((width, nta * slot), BF16),
            pltpu.VMEM((nta * slot, seq // nz), BF16),
            pltpu.VMEM((depth, seq), BF16),
            pltpu.VMEM((nta, width, seq), BF16),
            pltpu.VMEM((heads, query, seq), BF16),
            pltpu.VMEM((nta, width, query), BF16),
            pltpu.VMEM((nwa,) + prow.shape, F32),
            pltpu.VMEM((PAD, 2 * CHUNK), BF16),
            pltpu.VMEM((width, 2 * PAD), BF16),
            dma((2, 4, nz)),
            dma((2, nwa)),
            dma((2, nta)),
            dma((2, 3, nz, nz)),
            dma((2, 10, nz)),
            dma((2, 10, nz)),
            dma((2, nwa, nz)),
            dma((2, nta, max(nz, 2))),
            dma((8,)),
            dma((nta,)),
            dma((2, 2, nz)),
            dma((5,)),
        ],
        compiler_params=pltpu.CompilerParams(
            collective_id=1, has_side_effects=True, vmem_limit_bytes=VMEM_BYTES
        ),
        cost_estimate=pl.CostEstimate(
            flops=20 * 10**9, bytes_accessed=80 * 10**6, transcendentals=4 * 10**6
        ),
    )(tok, cot, wout, wval, wup, wdown, prow, ln, logits)


def gelu_pair(u):
    root = 0.7978845608028654
    square = u * u
    bent = jnp.tanh(root * u * (1.0 + 0.044715 * square))
    low_half = 0.5 * (1.0 + bent)
    slope = low_half + 0.5 * u * (1.0 - bent * bent) * root * (1.0 + 3.0 * 0.044715 * square)
    return (u * low_half, slope)


def backward_kernel(
    dims,
    dattended,
    outown,
    dresid_in,
    xown_in,
    terms_in,
    mixed_in,
    zinv,
    lens,
    ln,
    pfull,
    layer_in,
    weights,
    wgrad,
    vcol,
    vrow,
    scaled,
    shift,
    output,
    tgrad,
    vgrad,
    vectors,
    wsum,
    dresid,
    xown,
    terms,
    mixed,
    layer,
    normed,
    invs,
    wvt,
    gains,
    biases,
    da,
    partial,
    paired,
    up_in,
    down_in,
    gown,
    gpeer,
    first_x,
    first_y,
    second_x,
    second_y,
    gup_in,
    gdown_in,
    dvalue,
    dvown,
    wv,
    vsend,
    vrecv,
    tsend,
    csend,
    crecv,
    csum,
    crecv2,
    sem_da,
    sem_out,
    sem_core,
    sem_line,
    sem_dv,
    sem_tg,
    sem_v,
    sem_c,
    sem_c2,
    sem_local,
    sem_g,
    sem_gline,
):
    nwa, nta = dims
    me = Place(nwa, nta)
    wa, ta, z, c = me.wa, me.ta, me.z, me.c
    nz = me.nz
    depth, own = dresid.shape
    width = depth // nwa
    wdepth = depth // nta
    heads, query, seq = terms.shape
    hdim = width // heads
    part = seq // nz
    pairs = (
        (terms_in, terms),
        (mixed_in, mixed),
        (xown_in, xown),
        (dresid_in, dresid),
        (layer_in, layer),
    )
    fetch = [
        pltpu.make_async_copy(src, dst, sem_local.at[1 + i]) for i, (src, dst) in enumerate(pairs)
    ]
    for copy in fetch:
        copy.start()
    me.enter()

    def block_rows(w):
        return rows_at(w * width, width, 32)

    def da_copy(w, b, local):
        core = wa // 2
        src = dattended.at[block_rows(w), lanes(b * CHUNK)]
        dst = da.at[ta, :, lanes((wa % 2) * CHUNK)]
        if local:
            return pltpu.make_async_copy(src, dst, sem_da.at[0, w, b])
        return send(src, dst, sem_da.at[0, w, b], sem_da.at[1, ta, wa % 2], (w, 2 * b + core))

    def da_self(w, b):
        return jnp.logical_and(w == wa, 2 * b + wa // 2 == ta)

    def far(i):
        low_end = 1 - z // (nz // 2)
        return (nz - 1 - i) * low_end + i * (1 - low_end)

    def da_start(k, carry):
        w, b = (wa + k % nwa) % nwa, far(k // nwa)

        @pl.when(da_self(w, b))
        def _():
            da_copy(w, b, True).start()

        @pl.when(jnp.logical_not(da_self(w, b)))
        def _():
            da_copy(w, b, False).start()

        return carry

    lax.fori_loop(0, nwa * nz, da_start, 0)

    def back_copy(src, dst, sems, step, q):
        w = (wa + step) % nwa
        return send(
            src.at[block_rows(w), pl.ds(q * CHUNK, CHUNK)],
            dst.at[:, lanes(q * part + wa * CHUNK)],
            sems.at[0, step, q],
            sems.at[1, step, q],
            (w, ta),
        )

    def back_own(src, dst, sems, q):
        return pltpu.make_async_copy(
            src.at[block_rows(wa), pl.ds(q * CHUNK, CHUNK)],
            dst.at[:, lanes(q * part + wa * CHUNK)],
            sems.at[0, 0, q],
        )

    get_wv = pltpu.make_async_copy(
        weights.at[:, :, :, pl.ds(weights.shape[3] - PAD, PAD)], wv, sem_local.at[0]
    )
    get_wv.start()

    half = width // 2
    order = []
    for j in range(nz):
        for b in (nz - 1 - j, j):
            if b not in order:
                order.append(b)

    def g_core(b, core):
        return send(
            wgrad.at[:, b, core],
            gpeer.at[b],
            sem_g.at[0, 0, b],
            sem_g.at[1, 0, b],
            (wa, me.peer),
        )

    def g_load(b):
        return pltpu.make_async_copy(wgrad.at[:, b, c], gown.at[b], sem_g.at[0, 7, b])

    def g_first(k, r, b):
        near = me.wx if k == 0 else me.wy
        which = near if r == 0 else me.wd
        return send(
            gown.at[b, which, pl.ds(k * half, half)],
            (first_x if k == 0 else first_y).at[b, r],
            sem_g.at[0, 1 + 2 * k + r, b],
            sem_g.at[1, 1 + 2 * k + r, b],
            (near, ta),
        )

    def g_second(k, b):
        near = me.wy if k == 0 else me.wx
        return send(
            gown.at[b, near, pl.ds(k * half, half)],
            (second_x if k == 0 else second_y).at[b],
            sem_g.at[0, 5 + k, b],
            sem_g.at[1, 5 + k, b],
            (near, ta),
        )

    def g_add(b, which, k, extra):
        rows = pl.ds(k * half, half)
        gown[b, which, rows, :] = (
            gown[b, which, rows, :].astype(F32) + extra.astype(F32)
        ).astype(BF16)

    def g_cores(b):
        g_load(b).wait()
        g_core(b, c).wait_recv()
        for w in range(nwa):
            gown[b, w] = (gown[b, w].astype(F32) + gpeer[b, w].astype(F32)).astype(BF16)
        for k in range(2):
            for r in range(2):
                g_first(k, r, b).start()

    def g_plane(b):
        for k in range(2):
            for r in range(2):
                g_first(k, r, b).wait_recv()
            landed = first_x if k == 0 else first_y
            g_add(b, me.wy if k == 0 else me.wx, k, landed[b, 1])
            g_second(k, b).start()
            g_add(b, wa, k, landed[b, 0])

    def g_end(b):
        for k in range(2):
            g_second(k, b).wait_recv()
            g_add(b, wa, k, (second_x if k == 0 else second_y)[b])

    def g_line(up, j):
        k = 0 if up else 1
        target = nz - 1 - j if up else j
        return send(
            gown.at[target, wa],
            (gup_in if up else gdown_in).at[j],
            sem_gline.at[0, k, j],
            sem_gline.at[1, k, j],
            (wa, ta + 2 if up else ta - 2),
        )

    def g_origin():
        @pl.when(z == 0)
        def _():
            for j in range(nz - 1):
                g_line(True, j).start()

        @pl.when(z == nz - 1)
        def _():
            for j in range(nz - 1):
                g_line(False, j).start()

    def g_hop(j):
        target = nz - 1 - j

        @pl.when(jnp.logical_and(z < target, z > 0))
        def _():
            g_line(True, j).wait_recv()
            gown[target, wa] = (gown[target, wa].astype(F32) + gup_in[j].astype(F32)).astype(BF16)
            g_line(True, j).start()

        @pl.when(jnp.logical_and(z > j, z < nz - 1))
        def _():
            g_line(False, j).wait_recv()
            gown[j, wa] = (gown[j, wa].astype(F32) + gdown_in[j].astype(F32)).astype(BF16)
            g_line(False, j).start()

    def g_final():
        @pl.when(z == 0)
        def _():
            g_line(False, 0).wait_recv()
            wsum[...] = gown[0, wa].astype(F32) + gdown_in[0].astype(F32)

        @pl.when(z == nz - 1)
        def _():
            g_line(True, 0).wait_recv()
            wsum[...] = gown[nz - 1, wa].astype(F32) + gup_in[0].astype(F32)

        for b in range(1, nz - 1):

            @pl.when(z == b)
            def _():
                g_line(True, nz - 1 - b).wait_recv()
                g_line(False, b).wait_recv()
                both = gup_in[nz - 1 - b].astype(F32) + gdown_in[b].astype(F32)
                wsum[...] = gown[b, wa].astype(F32) + both

    for b in order:
        g_core(b, 1 - c).start()
        g_load(b).start()

    def da_arrive(s, j):
        own_piece = jnp.logical_and(s == ta, 2 * c + j == wa)
        where = da.at[s, :, lanes(j * CHUNK)]

        @pl.when(own_piece)
        def _():
            da_copy(wa, z, True).wait()

        @pl.when(jnp.logical_not(own_piece))
        def _():
            send(where, where, sem_da.at[0, 0, 0], sem_da.at[1, s, j], (2 * c + j, s)).wait_recv()

    def da_sent(k, carry):
        w, b = (wa + k // nz) % nwa, k % nz

        @pl.when(jnp.logical_not(da_self(w, b)))
        def _():
            da_copy(w, b, False).wait_send()

        return carry

    def prepare(b):
        for core in range(2):
            for j in range(2):
                da_arrive(2 * b + core, j)
        for h in range(heads):
            group = slice(h * hdim, (h + 1) * hdim)
            both = []
            for s in (2 * b, 2 * b + 1):
                one = da[s, group, :].astype(F32) * zinv[h, s * 8 : s * 8 + 1, :]
                both.append(one.astype(BF16))
                scaled[s, group, :] = both[-1]
            made = jnp.dot(
                jnp.concatenate(both, axis=0), terms[h], preferred_element_type=F32
            ).astype(BF16)
            partial[2 * b, group, :] = made[:hdim]
            partial[2 * b + 1, group, :] = made[hdim:]
        core_copy(b, 1 - c).start()

    def shifts():
        for h in range(heads):
            group = slice(h * hdim, (h + 1) * hdim)
            for s in range(nta):
                inv = zinv[h, s * 8 : s * 8 + 1, :]
                one = da[s, group, :].astype(F32) * mixed[s, group, :]
                along = jnp.sum(one, axis=0, keepdims=True)
                shift[h, s * 8 : (s + 1) * 8, :] = jnp.broadcast_to(along * inv, (8, query))

    def core_copy(b, core):
        return send(
            partial.at[2 * b + core],
            paired.at[b],
            sem_core.at[0, b],
            sem_core.at[1, b],
            (wa, me.peer),
        )

    def out_start():
        for q in range(nz):
            back_own(outown, output, sem_out, q).start()
            for step in range(1, nwa):
                back_copy(outown, output, sem_out, step, q).start()

    def line_copy(up, j, q):
        k = 0 if up else 1
        cols = pl.ds(q * part, part)
        return send(
            partial.at[2 * (nz - 1 - j if up else j) + c, :, cols],
            (up_in if up else down_in).at[j, :, cols],
            sem_line.at[0, k, j, q],
            sem_line.at[1, k, j, q],
            (wa, ta + 2 if up else ta - 2),
        )

    ready = set()

    def core_ready(b):
        if b not in ready:
            ready.add(b)
            core_copy(b, c).wait_recv()

    def chip_sum(b, q):
        cols = pl.ds(q * part, part)
        return partial[2 * b + c, :, cols].astype(F32) + paired[b, :, cols].astype(F32)

    def line_step(up, j, q):
        target = nz - 1 - j if up else j
        landed = up_in if up else down_in
        cols = pl.ds(q * part, part)

        @pl.when(z < target if up else z > target)
        def _():
            first = z == (0 if up else nz - 1)

            @pl.when(jnp.logical_not(first))
            def _():
                line_copy(up, j, q).wait_recv()
                total = chip_sum(target, q) + landed[j, :, cols].astype(F32)
                partial[2 * target + c, :, cols] = total.astype(BF16)

            @pl.when(first)
            def _():
                partial[2 * target + c, :, cols] = chip_sum(target, q).astype(BF16)

            line_copy(up, j, q).start()

    def line(j):
        core_ready(nz - 1 - j)
        core_ready(j)
        for q in range(nz):
            line_step(True, j, q)
            line_step(False, j, q)

    fetch[0].wait()
    for b in order:
        g_cores(b)
    prepare(order[0])
    prepare(order[1])
    line(0)
    for b in order[2:]:
        prepare(b)
    for j in range(1, nz - 1):
        line(j)
    for b in range(nz):
        core_ready(b)

    fetch[1].wait()
    shifts()
    get_wv.wait()
    for t in range(nta):
        turned = jnp.concatenate([wv[w, t] for w in range(nwa)], axis=0).T
        wvt[t * wdepth : (t + 1) * wdepth, :] = turned[:wdepth]
    fetch[2].wait()
    fetch[3].wait()
    norm, inv = norm_stats(xown[...].astype(F32))
    normed[...] = norm
    invs[...] = jnp.broadcast_to(inv, invs.shape)
    gains[...] = jnp.zeros_like(gains)
    biases[...] = jnp.zeros_like(biases)
    fetch[4].wait()
    for b in order:
        g_plane(b)
    out_start()

    def dv_copy(step, q):
        w = (wa + step) % nwa
        return send(
            dvalue.at[:, lanes(q * part + w * CHUNK)],
            dvown.at[block_rows(wa), pl.ds(q * CHUNK, CHUNK)],
            sem_dv.at[0, step, q],
            sem_dv.at[1, step, q],
            (w, ta),
        )

    place = lax.broadcasted_iota(jnp.int32, (width, part), 1).astype(F32)

    def final(q):
        cols = pl.ds(q * part, part)
        key_valid = place + q * part < ln[0:1, 0:1]
        for b in range(nz):

            @pl.when(z == b)
            def _():
                total = chip_sum(b, q)
                if b > 0:
                    line_copy(True, nz - 1 - b, q).wait_recv()
                    total = total + up_in[nz - 1 - b, :, cols].astype(F32)
                if b < nz - 1:
                    line_copy(False, b, q).wait_recv()
                    total = total + down_in[b, :, cols].astype(F32)
                dvalue[:, cols] = jnp.where(key_valid, total, 0.0).astype(BF16)

        for step in range(1, nwa):
            dv_copy(step, q).start()
        dvown[block_rows(wa), q * CHUNK : (q + 1) * CHUNK] = dvalue[
            :, lanes(q * part + wa * CHUNK)
        ]

    for b in order:
        g_end(b)
    g_origin()
    for q in range(nz):
        final(q)

    g_hop(0)
    vmade = lax.dot_general(layer[...], dvalue[...], ROWS_NT, preferred_element_type=F32)
    vsend[...] = vmade.astype(BF16).reshape(nta, wdepth, width)
    vbias = jnp.sum(dvalue[...].astype(F32), axis=1, keepdims=True)

    def v_copy(step):
        t = (ta + step) % nta
        return send(
            vsend.at[t], vrecv.at[step], sem_v.at[0, step], sem_v.at[1, step], (wa, t)
        )

    for step in range(1, nta):
        v_copy(step).start()

    for q in range(nz):
        cols = slice(q * CHUNK, (q + 1) * CHUNK)
        for step in range(1, nwa):
            dv_copy(step, q).wait_recv()
        dl = jnp.dot(wvt[...], dvown[:, cols], preferred_element_type=F32)
        norm = normed[:, cols]
        e = dl * pfull[:, 0:1]
        mean_e = jnp.sum(e, axis=0, keepdims=True) / depth
        mean_n = jnp.sum(e * norm, axis=0, keepdims=True) / depth
        made = dresid[:, cols] + invs[0:1, cols] * (e - mean_e - norm * mean_n)
        tsend[:, cols] = made.astype(BF16)
        back_own(tsend, tgrad, sem_tg, q).start()
        for step in range(1, nwa):
            back_copy(tsend, tgrad, sem_tg, step, q).start()
        gains[...] += dl * norm
        biases[...] += dl

    gain = jnp.sum(gains[...], axis=1, keepdims=True)
    bias = jnp.sum(biases[...], axis=1, keepdims=True)
    column = lax.broadcasted_iota(jnp.int32, (depth, PAD), 1)
    cols = jnp.where(column == 0, gain, jnp.where(column == 1, bias, vcol[...]))
    wide = vrow.shape[1] // nwa
    gap = csend.shape[2] - wide
    for w in range(nwa):
        piece = cols[w * width : (w + 1) * width]
        piece = jnp.concatenate([piece, jnp.zeros((gap - width, PAD), F32)], axis=0)
        csend[w, :, :gap] = piece.T[:8]
        csend[w, :, gap:] = vrow[:, w * wide : (w + 1) * wide]

    def c_copy(step):
        w = (wa + step) % nwa
        return send(csend.at[w], crecv.at[step], sem_c.at[0, step], sem_c.at[1, step], (w, ta))

    for step in range(1, nwa):
        c_copy(step).start()
    g_hop(1)
    crecv[0] = csend[wa]
    piece = jnp.concatenate(
        [jnp.broadcast_to(vbias, (width, PAD)), jnp.zeros((gap - width, PAD), F32)], axis=0
    )
    vb_row = jnp.concatenate([piece.T[:8], jnp.zeros((8, wide), F32)], axis=1)
    row = lax.broadcasted_iota(jnp.int32, vb_row.shape, 0)
    total = jnp.where(row == 2, vb_row, 0.0) + crecv[0]
    for step in range(1, nwa):
        c_copy(step).wait_recv()
        total = total + crecv[step]
    csum[...] = total

    def c2_copy(step):
        t = (ta + step) % nta
        return send(csum, crecv2.at[step], sem_c2.at[0, step], sem_c2.at[1, step], (wa, t))

    for step in range(1, nta):
        c2_copy(step).start()
    for j in range(2, nz - 1):
        g_hop(j)
    value_total = vsend[ta].astype(F32)
    for step in range(1, nta):
        v_copy(step).wait_recv()
        value_total = value_total + vrecv[step].astype(F32)
    vgrad[...] = value_total
    g_final()
    crecv2[0] = csum[...]
    for step in range(1, nta):
        c2_copy(step).wait_recv()
    full = jnp.zeros(csum.shape, F32)
    for t in range(nta):
        full = full + crecv2[(ta - t + nta) % nta]
    vectors[...] = full

    lax.fori_loop(0, nwa * nz, da_sent, 0)
    for step in range(1, nwa):
        for q in range(nz):
            back_copy(tsend, tgrad, sem_tg, step, q).wait()
            back_copy(outown, output, sem_out, step, q).wait()
            dv_copy(step, q).wait_send()
        c_copy(step).wait_send()
    for q in range(nz):
        back_own(outown, output, sem_out, q).wait()
        back_own(tsend, tgrad, sem_tg, q).wait()
    for step in range(1, nta):
        v_copy(step).wait_send()
        c2_copy(step).wait_send()
    for b in range(nz):
        core_copy(b, 1 - c).wait_send()
        g_core(b, 1 - c).wait_send()
        for k in range(2):
            g_first(k, 0, b).wait_send()
            g_first(k, 1, b).wait_send()
            g_second(k, b).wait_send()
    for j in range(nz - 1):

        @pl.when(z < nz - 1 - j)
        def _():
            for q in range(nz):
                line_copy(True, j, q).wait_send()
            g_line(True, j).wait_send()

        @pl.when(z > j)
        def _():
            for q in range(nz):
                line_copy(False, j, q).wait_send()
            g_line(False, j).wait_send()


def run_backward(
    dims, dattended, outown, dresid, xown, terms, mixed, zinv, lens, ln, pfull, layer, weights, wgrad, vcol, vrow
):
    nwa, nta = dims
    nz = nta // 2
    half, both = weights.shape[2] // 2, wgrad.shape[4]
    depth, own = dresid.shape
    width = depth // nwa
    heads, query, seq = terms.shape
    wdepth = depth // nta
    wide = 256 + vrow.shape[1] // nwa
    dma = pltpu.SemaphoreType.DMA
    return pl.pallas_call(
        functools.partial(backward_kernel, dims),
        out_shape=(
            shape_of((nta, width, query), BF16),
            shape_of((heads, nta * 8, query), F32),
            shape_of((width, seq), BF16),
            shape_of((width, seq), BF16),
            shape_of((wdepth, width), F32),
            shape_of((8, wide), F32),
            shape_of((width, both), F32),
        ),
        in_specs=anywhere(6) + whole(4) + anywhere(3) + whole(2),
        out_specs=tuple(whole(7)),
        scratch_shapes=[
            pltpu.VMEM((depth, own), F32),
            pltpu.VMEM((depth, own), BF16),
            pltpu.VMEM((heads, query, seq), BF16),
            pltpu.VMEM((nta, width, query), F32),
            pltpu.VMEM((depth, seq), BF16),
            pltpu.VMEM((depth, own), F32),
            pltpu.VMEM((8, own), F32),
            pltpu.VMEM((depth, depth), BF16),
            pltpu.VMEM((depth, CHUNK), F32),
            pltpu.VMEM((depth, CHUNK), F32),
            pltpu.VMEM((nta, width, query), BF16),
            pltpu.VMEM((nta, width, seq), BF16),
            pltpu.VMEM((nz, width, seq), BF16),
            pltpu.VMEM((nz - 1, width, seq), BF16),
            pltpu.VMEM((nz - 1, width, seq), BF16),
            pltpu.VMEM((nz, nwa, width, both), BF16),
            pltpu.VMEM((nz, nwa, width, both), BF16),
            pltpu.VMEM((nz, 2, half, both), BF16),
            pltpu.VMEM((nz, 2, half, both), BF16),
            pltpu.VMEM((nz, half, both), BF16),
            pltpu.VMEM((nz, half, both), BF16),
            pltpu.VMEM((nz - 1, width, both), BF16),
            pltpu.VMEM((nz - 1, width, both), BF16),
            pltpu.VMEM((width, seq), BF16),
            pltpu.VMEM((depth, own), BF16),
            pltpu.VMEM((nwa, nta, width, PAD), BF16),
            pltpu.VMEM((nta, wdepth, width), BF16),
            pltpu.VMEM((nta, wdepth, width), BF16),
            pltpu.VMEM((depth, own), BF16),
            pltpu.VMEM((nwa, 8, wide), F32),
            pltpu.VMEM((nwa, 8, wide), F32),
            pltpu.VMEM((8, wide), F32),
            pltpu.VMEM((nta, 8, wide), F32),
            dma((2, nta, max(nz, 2))),
            dma((2, nwa, nz)),
            dma((2, nz)),
            dma((2, 2, nz, nz)),
            dma((2, nwa, nz)),
            dma((2, nwa, nz)),
            dma((2, nta)),
            dma((2, nwa)),
            dma((2, nta)),
            dma((6,)),
            dma((2, 8, nz)),
            dma((2, 2, nz)),
        ],
        compiler_params=pltpu.CompilerParams(
            collective_id=2, has_side_effects=True, vmem_limit_bytes=VMEM_BYTES
        ),
        cost_estimate=pl.CostEstimate(
            flops=4 * 10**9, bytes_accessed=80 * 10**6, transcendentals=0
        ),
    )(
        dattended, outown, dresid, xown, terms, mixed, zinv, lens, ln, pfull, layer, weights, wgrad,
        vcol, vrow,
    )


def logits_kernel(
    terms,
    scaled,
    value,
    shift,
    lens,
    output,
    tgrad,
    wsum,
    vgrad,
    vectors,
    out,
    output_out,
    tgrad_out,
    up_out,
    down_out,
    wo_out,
    vgrad_out,
    *vector_out,
):
    nta = scaled.shape[0]
    for row, ref in enumerate(vector_out[:-1]):
        ref[...] = vectors[row, : ref.shape[0]]
    bias_out = vector_out[-1]
    bias_out[...] = vectors[0, vectors.shape[1] - bias_out.shape[0] :]
    output_out[...] = output[...]
    tgrad_out[...] = tgrad[...].astype(F32)
    vgrad_out[...] = vgrad[...]
    hidden = up_out.shape[1]
    up_out[...] = wsum[:, :hidden]
    down_out[...] = wsum[:, hidden : 2 * hidden]
    wo_out[...] = wsum[:, 2 * hidden : 2 * hidden + wo_out.shape[1]]
    cols = terms.shape[2]
    stacked = jnp.concatenate([scaled[s] for s in range(nta)], axis=0)
    values = jnp.concatenate([value[s] for s in range(nta)], axis=0)
    made = lax.dot_general(stacked, values, ROWS_TN, preferred_element_type=F32)
    where = (nta * 8, cols)
    place = lax.broadcasted_iota(jnp.int32, where, 1) + pl.program_id(1) * cols
    first = lax.broadcasted_iota(jnp.int32, where, 0) % 8 == 0
    valid = jnp.logical_and(place.astype(F32) < lens[:, 0:1], first)
    valid = jnp.where(valid, 1.0, 0.0).astype(BF16)
    high = shift[0].astype(BF16)
    rest = (shift[0] - high.astype(F32)).astype(BF16)
    made = made - lax.dot_general(high, valid, ROWS_TN, preferred_element_type=F32)
    made = made - lax.dot_general(rest, valid, ROWS_TN, preferred_element_type=F32)
    out[0] = terms[0].astype(F32) * made


def run_logits(terms, scaled, value, shift, lens, output, tgrad, wsum, vgrad, vectors):
    heads, query, seq = terms.shape
    nta, width, _ = scaled.shape
    hdim = width // heads
    cols = min(1024, seq)
    steps = seq // cols
    wdepth = vgrad.shape[0]
    hidden = (wsum.shape[1] - PAD) // 2
    nwa = hidden * nta // (vectors.shape[1] - 2 * CHUNK)
    total = heads * steps
    flat = (shape_of((width,), F32),) * 7 + (shape_of((hidden * nta // nwa,), F32),)

    def rows_of(array, lanes_in=None):
        shape = (array[0] // total, lanes_in or array[1])
        return pl.BlockSpec(shape, lambda h, k: (h * steps + k, 0))

    return pl.pallas_call(
        logits_kernel,
        grid=(heads, steps),
        out_shape=(
            shape_of((heads, query, seq), F32),
            shape_of((width, seq), BF16),
            shape_of((width, seq), F32),
            shape_of((width, hidden), F32),
            shape_of((width, hidden), F32),
            shape_of((width, wdepth), F32),
            shape_of(vgrad.shape, F32),
        )
        + flat,
        in_specs=[
            pl.BlockSpec((1, query, cols), lambda h, k: (h, 0, k)),
            pl.BlockSpec((nta, hdim, query), lambda h, k: (0, h, 0)),
            pl.BlockSpec((nta, hdim, cols), lambda h, k: (0, h, k)),
            pl.BlockSpec((1, nta * 8, query), lambda h, k: (h, 0, 0)),
            pl.BlockSpec(lens.shape, lambda h, k: (0, 0)),
            rows_of(output.shape),
            rows_of(tgrad.shape),
            rows_of(wsum.shape),
            rows_of(vgrad.shape),
            pl.BlockSpec(vectors.shape, lambda h, k: (0, 0)),
        ],
        out_specs=(
            pl.BlockSpec((1, query, cols), lambda h, k: (h, 0, k)),
            rows_of(output.shape),
            rows_of(tgrad.shape),
            rows_of((width, hidden)),
            rows_of((width, hidden)),
            rows_of((width, wdepth)),
            rows_of(vgrad.shape),
        )
        + tuple(pl.BlockSpec(one.shape, lambda h, k: (0,)) for one in flat),
        compiler_params=pltpu.CompilerParams(vmem_limit_bytes=VMEM_BYTES),
        cost_estimate=pl.CostEstimate(
            flops=2 * 10**9, bytes_accessed=20 * 10**6, transcendentals=0
        ),
    )(terms, scaled, value, shift, lens, output, tgrad, wsum, vgrad, vectors)


def on_device_fast(
    dims,
    tokens,
    seq_lengths,
    norm1_gain,
    norm1_bias,
    value_weight,
    value_bias,
    synth_logits,
    out_weight,
    out_bias,
    norm2_gain,
    norm2_bias,
    up_weight,
    up_bias,
    down_weight,
    down_bias,
    cotangent,
):
    nwa, nta = dims
    width = tokens.shape[0]
    per_feature = (
        norm1_gain,
        norm1_bias,
        value_bias,
        out_bias,
        norm2_gain,
        norm2_bias,
        down_bias,
    )
    prow = jnp.pad(jnp.stack(per_feature), ((0, 1), (0, 2 * CHUNK - width)))
    prow = jnp.concatenate([prow, jnp.broadcast_to(up_bias, (8, up_bias.shape[0]))], axis=1)
    ln = jnp.broadcast_to(seq_lengths.astype(F32)[:, None], (8, CHUNK))
    logits = synth_logits.transpose(1, 0, 2)
    (
        xown,
        weights,
        _,
        layer,
        value,
        terms,
        mixed,
        zinv,
        lens,
        pfull,
        outown,
        dattended,
        dresid,
        wgrad,
        vcol,
        vrow,
    ) = run_forward(
        dims,
        tokens,
        cotangent,
        out_weight,
        value_weight,
        up_weight,
        down_weight.T,
        prow,
        ln,
        logits,
    )
    scaled, shift, output, tgrad, vgrad, vectors, wsum = run_backward(
        dims,
        dattended,
        outown,
        dresid,
        xown,
        terms,
        mixed,
        zinv,
        lens,
        ln,
        pfull,
        layer,
        weights,
        wgrad,
        vcol,
        vrow,
    )
    logits_grad, output, tgrad, up_grad, down_grad, out_grad, vgrad, *flat = run_logits(
        terms, scaled, value, shift, lens, output, tgrad, wsum, vgrad, vectors
    )
    return (
        output,
        tgrad,
        flat[0],
        flat[1],
        vgrad,
        flat[2],
        logits_grad.transpose(1, 0, 2),
        out_grad,
        flat[3],
        flat[4],
        flat[5],
        up_grad,
        flat[7],
        down_grad.T,
        flat[6],
    )


def fits(mesh):
    return mesh.shape["wa"] == 4 and mesh.shape["ta"] == 8


def solution(mesh):
    placed = (
        P("wa", "ta"),
        P("ta"),
        P("wa"),
        P("wa"),
        P("ta", "wa"),
        P("wa"),
        P("ta", "wa", None),
        P("wa", "ta"),
        P("wa"),
        P("wa"),
        P("wa"),
        P("wa", "ta"),
        P("wa"),
        P("ta", "wa"),
        P("wa"),
        P("wa", "ta"),
    )
    sizes = (mesh.shape["wa"], mesh.shape["ta"])
    body = functools.partial(on_device_fast, sizes) if fits(mesh) else on_device
    return jax.shard_map(
        body,
        mesh=mesh,
        in_specs=placed,
        out_specs=(
            P("wa", "ta"),
            P("wa", "ta"),
            P("wa"),
            P("wa"),
            P("ta", "wa"),
            P("wa"),
            P("ta", "wa", None),
            P("wa", "ta"),
            P("wa"),
            P("wa"),
            P("wa"),
            P("wa", "ta"),
            P("wa"),
            P("ta", "wa"),
            P("wa"),
        ),
        check_vma=False,
    )
```

```python
import functools

import jax
import jax.numpy as jnp
from jax import lax
from jax.experimental import pallas as pl
from jax.experimental.pallas import tpu as pltpu
from jax.sharding import PartitionSpec as P

D = 768


EPSILON = 1e-05
ALONG_FEATURES = (((1,), (1,)), ((), ()))
ALONG_ROWS = (((0,), (0,)), ((), ()))


def row_statistics(first_term, second_term):
    return lax.psum((jnp.sum(first_term, axis=1), jnp.sum(second_term, axis=1)), "wa")


def all_features(features_part):
    return lax.all_gather(features_part, "wa", axis=1, tiled=True)


def feature_share(partial_sum):
    return lax.psum_scatter(partial_sum, "wa", scatter_dimension=1, tiled=True)


def norm_forward(inputs, norm_gain, norm_bias):
    row_total, row_squares = row_statistics(inputs, inputs * inputs)
    row_mean = row_total / D
    variance = row_squares / D - row_mean * row_mean
    inverse = lax.rsqrt(variance + EPSILON)
    normed = (inputs - row_mean[:, None]) * inverse[:, None]
    return (normed * norm_gain + norm_bias, normed, inverse)


def norm_backward(incoming, normed, inverse, norm_gain):
    scaled = incoming * norm_gain
    row_total, row_along = row_statistics(scaled, scaled * normed)
    return inverse[:, None] * (scaled - row_total[:, None] / D - normed * row_along[:, None] / D)


def weights_of(logit_rows, length_all):
    seq_len = logit_rows.shape[2]
    key_valid = (jnp.arange(seq_len)[None, :] < length_all[:, None]).astype(jnp.bfloat16)
    terms = jnp.exp(logit_rows.astype(jnp.float32)).astype(jnp.bfloat16)
    sums = jnp.einsum("phk,sk->sph", terms, key_valid, preferred_element_type=jnp.float32)
    return (terms, sums, key_valid)


def attend(terms, sums, value_all, query_rows):
    mixed = jnp.einsum("phk,skhd->sphd", terms, value_all, preferred_element_type=jnp.float32)
    mixed = mixed / sums[..., None]
    return (mixed, (mixed * query_rows[:, :, None, None]).astype(jnp.bfloat16))


def attend_back(terms, sums, key_valid, value_all, mixed, grad_rows):
    along = jnp.sum(grad_rows.astype(jnp.float32) * mixed, axis=-1) / sums
    scaled = (grad_rows.astype(jnp.float32) / sums[..., None]).astype(jnp.bfloat16)
    dvalue_part = jnp.einsum("phk,sphd->skhd", terms, scaled, preferred_element_type=jnp.float32)
    dlogits = jnp.einsum("sphd,skhd->phk", scaled, value_all, preferred_element_type=jnp.float32)
    high = along.astype(jnp.bfloat16)
    rest = (along - high.astype(jnp.float32)).astype(jnp.bfloat16)
    shift = sum(
        jnp.einsum("sph,sk->phk", part, key_valid, preferred_element_type=jnp.float32)
        for part in (high, rest)
    )
    return (dvalue_part, terms.astype(jnp.float32) * (dlogits - shift))


def on_device(
    tokens,
    seq_lengths,
    norm1_gain,
    norm1_bias,
    value_weight,
    value_bias,
    synth_logits,
    out_weight,
    out_bias,
    norm2_gain,
    norm2_bias,
    up_weight,
    up_bias,
    down_weight,
    down_bias,
    cotangent,
):
    rows_dev = tokens.shape[1]
    local_width = tokens.shape[0]
    seq_count = seq_lengths.shape[0]
    seq_len = synth_logits.shape[2]
    head_count = synth_logits.shape[1]
    head_dim = local_width // head_count
    value_cols, out_rows, up_rows, down_cols = (
        lax.all_gather(value_weight, "ta", axis=0, tiled=True),
        lax.all_gather(out_weight, "ta", axis=1, tiled=True),
        lax.all_gather(up_weight, "ta", axis=1, tiled=True),
        lax.all_gather(down_weight, "ta", axis=0, tiled=True),
    )
    up_block, down_block = (
        lax.all_to_all(up_rows.T, "wa", split_axis=0, concat_axis=1, tiled=True),
        lax.all_to_all(down_cols, "wa", split_axis=0, concat_axis=1, tiled=True),
    )
    inputs = tokens.T.astype(jnp.float32)
    pre_one, normed_one, inverse_one = norm_forward(inputs, norm1_gain, norm1_bias)
    layer_one = all_features(pre_one.astype(jnp.bfloat16))
    values = (
        jnp.dot(layer_one, value_cols, preferred_element_type=jnp.float32) + value_bias
    ).astype(jnp.bfloat16)
    value_heads = values.reshape(seq_count, seq_len, head_count, head_dim)
    positions = jnp.arange(seq_len)
    key_valid = positions[None, :] < seq_lengths[:, None]
    query_valid = key_valid.astype(jnp.float32)
    length_all = lax.all_gather(seq_lengths, "ta", axis=0, tiled=True)
    block_rows = synth_logits.shape[0]
    value_all = lax.all_gather(
        value_heads * key_valid[:, :, None, None].astype(jnp.bfloat16), "ta", axis=0, tiled=True
    )
    terms, sums, key_valid_all = weights_of(synth_logits, length_all)
    block_positions = lax.axis_index("ta") * block_rows + jnp.arange(block_rows)
    query_rows = (block_positions[None, :] < length_all[:, None]).astype(jnp.float32)
    mixed_rows, mixed_low = attend(terms, sums, value_all, query_rows)
    attended = lax.all_to_all(mixed_low, "ta", split_axis=0, concat_axis=1, tiled=True)
    attended = attended.reshape(rows_dev, local_width)
    branch = (
        feature_share(jnp.dot(attended, out_rows, preferred_element_type=jnp.float32)) + out_bias
    )
    resid = inputs + branch
    pre_two, normed_two, inverse_two = norm_forward(resid, norm2_gain, norm2_bias)
    layer_two = all_features(pre_two.astype(jnp.bfloat16))
    upper = (
        lax.dot_general(layer_two, up_block, ALONG_FEATURES, preferred_element_type=jnp.float32)
        + up_bias
    )
    hidden, gelu_back = jax.vjp(jax.nn.gelu, upper)
    hidden_low = hidden.astype(jnp.bfloat16)
    feed = (
        feature_share(jnp.dot(hidden_low, down_block, preferred_element_type=jnp.float32))
        + down_bias
    )
    output = (resid + feed).astype(jnp.bfloat16)
    cotangent_rows = cotangent.T
    grad_in = cotangent_rows.astype(jnp.float32)
    grad_full = all_features(cotangent_rows)
    dhidden = lax.dot_general(
        grad_full, down_block, ALONG_FEATURES, preferred_element_type=jnp.float32
    )
    dupper = gelu_back(dhidden)[0].astype(jnp.bfloat16)
    down_part = lax.dot_general(
        hidden_low, grad_full, ALONG_ROWS, preferred_element_type=jnp.float32
    )
    up_part = lax.dot_general(dupper, layer_two, ALONG_ROWS, preferred_element_type=jnp.float32)
    up_bias_part = jnp.sum(dupper.astype(jnp.float32), axis=0)
    down_bias_part = jnp.sum(grad_in, axis=0)
    dlayer_two = feature_share(jnp.dot(dupper, up_block, preferred_element_type=jnp.float32))
    gain_two_part = jnp.sum(dlayer_two * normed_two, axis=0)
    bias_two_part = jnp.sum(dlayer_two, axis=0)
    dresid = grad_in + norm_backward(dlayer_two, normed_two, inverse_two, norm2_gain)
    dbranch = dresid.astype(jnp.bfloat16)
    dbranch_full = all_features(dbranch)
    dattended = lax.dot_general(
        dbranch_full, out_rows, ALONG_FEATURES, preferred_element_type=jnp.float32
    ).astype(jnp.bfloat16)
    out_part = lax.dot_general(
        attended, dbranch_full, ALONG_ROWS, preferred_element_type=jnp.float32
    )
    out_bias_part = jnp.sum(dbranch.astype(jnp.float32), axis=0)
    grad_heads = dattended.reshape(seq_count, seq_len, head_count, head_dim)
    grad_heads = grad_heads * query_valid[:, :, None, None].astype(jnp.bfloat16)
    grad_block = lax.all_to_all(grad_heads, "ta", split_axis=1, concat_axis=0, tiled=True)
    dvalue_part, logits_grad = attend_back(
        terms, sums, key_valid_all, value_all, mixed_rows, grad_block
    )
    dvalue_rows = dvalue_part.astype(jnp.bfloat16).reshape(-1, local_width)
    dvalue_rows = lax.psum_scatter(dvalue_rows, "ta", scatter_dimension=0, tiled=True)
    dvalues = dvalue_rows * query_valid.reshape(rows_dev, 1).astype(jnp.bfloat16)
    value_part = lax.dot_general(layer_one, dvalues, ALONG_ROWS, preferred_element_type=jnp.float32)
    value_bias_part = jnp.sum(dvalues.astype(jnp.float32), axis=0)
    dlayer_one = feature_share(
        lax.dot_general(dvalues, value_cols, ALONG_FEATURES, preferred_element_type=jnp.float32)
    )
    gain_one_part = jnp.sum(dlayer_one * normed_one, axis=0)
    bias_one_part = jnp.sum(dlayer_one, axis=0)
    tokens_grad = dresid + norm_backward(dlayer_one, normed_one, inverse_one, norm1_gain)
    up_back, down_back = (
        lax.all_to_all(up_part, "wa", split_axis=1, concat_axis=0, tiled=True),
        lax.all_to_all(down_part, "wa", split_axis=1, concat_axis=0, tiled=True),
    )
    value_grad, out_grad, up_grad, down_grad = (
        lax.psum_scatter(value_part, "ta", scatter_dimension=0, tiled=True),
        lax.psum_scatter(out_part, "ta", scatter_dimension=1, tiled=True),
        lax.psum_scatter(up_back, "ta", scatter_dimension=0, tiled=True),
        lax.psum_scatter(down_back, "ta", scatter_dimension=0, tiled=True),
    )
    vector_grads = lax.psum(
        (
            gain_one_part,
            bias_one_part,
            value_bias_part,
            out_bias_part,
            gain_two_part,
            bias_two_part,
            up_bias_part,
            down_bias_part,
        ),
        "ta",
    )
    return (
        output.T,
        tokens_grad.T,
        vector_grads[0],
        vector_grads[1],
        value_grad,
        vector_grads[2],
        logits_grad,
        out_grad,
        vector_grads[3],
        vector_grads[4],
        vector_grads[5],
        up_grad.T,
        vector_grads[6],
        down_grad,
        vector_grads[7],
    )


MESH = pl.DeviceIdType.MESH
ROWS_NT = (((1,), (1,)), ((), ()))
ROWS_TN = (((0,), (0,)), ((), ()))
F32 = jnp.float32
BF16 = jnp.bfloat16
VMEM_BYTES = 60 * 2**20
CHUNK = 128
PAD = 128
AHEAD = 1


def whole(count):
    return [pl.BlockSpec(memory_space=pltpu.VMEM)] * count


def anywhere(count):
    return [pl.BlockSpec(memory_space=pl.ANY)] * count


def shape_of(shape, dtype):
    return jax.ShapeDtypeStruct(shape, dtype)


def lanes(start, size=CHUNK):
    return pl.ds(pl.multiple_of(start, CHUNK), size)


def rows_at(start, size, unit):
    return pl.ds(pl.multiple_of(start, unit), size)


class Place:
    def __init__(self, nwa, nta):
        self.nwa, self.nta, self.nz = nwa, nta, nta // 2
        self.wa = lax.axis_index("wa")
        self.ta = lax.axis_index("ta")
        self.z = self.ta // 2
        self.c = self.ta % 2
        self.peer = self.ta + 1 - 2 * self.c
        self.wx = self.wa + 1 - 2 * (self.wa % 2)
        self.wy = (self.wa + 2) % 4
        self.wd = 3 - self.wa

    def enter(self):
        barrier = pltpu.get_barrier_semaphore()
        total = self.nwa * self.nta

        def greet(step, carry):
            w = (self.wa + step // self.nta) % self.nwa
            t = (self.ta + step % self.nta) % self.nta
            pl.semaphore_signal(barrier, inc=1, device_id=(w, t), device_id_type=MESH)
            return carry

        lax.fori_loop(1, total, greet, 0)
        pl.semaphore_wait(barrier, total - 1)


def send(src, dst, ssem, rsem, device):
    return pltpu.make_async_remote_copy(
        src_ref=src,
        dst_ref=dst,
        send_sem=ssem,
        recv_sem=rsem,
        device_id=device,
        device_id_type=MESH,
    )


def when(condition):
    return pl.when(condition)


def norm_stats(block):
    width = block.shape[0]
    mean = jnp.sum(block, axis=0, keepdims=True) / width
    centred = block - mean
    variance = jnp.sum(centred * centred, axis=0, keepdims=True) / width
    inverse = lax.rsqrt(variance + EPSILON)
    return (centred * inverse, inverse)


def forward_kernel(
    dims,
    tok,
    cot,
    wout,
    wval,
    wup,
    wdown,
    prow,
    ln,
    logits,
    xown,
    small,
    large,
    layer_out,
    value_out,
    term_out,
    mixed,
    zinv,
    lens,
    pfull,
    out,
    dattended,
    dresid,
    wgrad,
    vcol,
    vrow,
    cown,
    attended,
    rfull,
    wo,
    wblock,
    resid,
    normed,
    inverse,
    layer_two,
    layer_t,
    grad_t,
    feed,
    dlayer,
    wide,
    gblock,
    gwo,
    x,
    wvc,
    layer_pad,
    layer,
    value,
    terms,
    attsend,
    rows,
    turned,
    wsmall,
    sem_tok,
    sem_par,
    sem_ta,
    sem_val,
    sem_small,
    sem_large,
    sem_cot,
    sem_att,
    sem_local,
    sem_out,
    sem_wv,
    sem_g,
):
    nwa, nta = dims
    me = Place(nwa, nta)
    wa, ta, z, c = me.wa, me.ta, me.z, me.c
    nz = me.nz
    width = tok.shape[0]
    half = width // 2
    seq = tok.shape[1]
    part = seq // nz
    query = seq // nta
    slot = wvc.shape[1] // nta
    wdepth = wvc.shape[0] * nwa // nta
    heads = terms.shape[0]
    hdim = width // heads
    split = PAD
    get_logits = pltpu.make_async_copy(logits, terms, sem_local.at[5])
    get_logits.start()
    stores = ((small, sem_small), (large, sem_large))
    one = wup.shape[1]
    own_w = (
        pltpu.make_async_copy(wsmall, small.at[wa, ta], sem_local.at[2]),
        pltpu.make_async_copy(wup, large.at[wa, ta, :, pl.ds(0, one)], sem_local.at[6]),
        pltpu.make_async_copy(wdown, large.at[wa, ta, :, pl.ds(one, one)], sem_local.at[7]),
    )
    own_w[1].start()
    own_w[2].start()
    turned[...] = jnp.zeros_like(turned)
    turned[:wdepth, :width] = wval[...]
    wsmall[...] = jnp.zeros_like(wsmall)
    wsmall[:, :wdepth] = wout[...]
    wsmall[:, split:] = turned[...].T[:width]
    own_w[0].start()
    me.enter()


    def block_rows(w, off=0, size=width):
        return rows_at(w * width + off, size, 32)

    def tok_copy(k, q):
        device = (me.wx if k == 0 else me.wy, ta)
        return send(
            tok.at[:, pl.ds(q * part, part)],
            x.at[block_rows(wa), pl.ds(q * part, part)],
            sem_tok.at[0, k, q],
            sem_tok.at[1, k, q],
            device,
        )

    def tok_fwd(k, q):
        source = me.wx if k == 0 else me.wy
        device = (me.wy if k == 0 else me.wx, ta)
        where = x.at[block_rows(source, k * half, half), pl.ds(q * part, part)]
        return send(where, where, sem_tok.at[0, 2 + k, q], sem_tok.at[1, 2 + k, q], device)

    own_x = pltpu.make_async_copy(tok, x.at[block_rows(wa)], sem_local.at[0])
    own_x.start()

    def tok_start(q):
        for k in range(2):
            tok_copy(k, q).start()

    def tok_turn(q):
        for k in range(2):
            tok_copy(k, q).wait_recv()
            tok_fwd(k, q).start()
        if q + AHEAD < nz:
            tok_start(q + AHEAD)

    for q in range(AHEAD):
        tok_start(q)

    def par_copy(step):
        w = (wa + step) % nwa
        return send(prow, rows.at[wa], sem_par.at[0, step], sem_par.at[1, step], (w, ta))

    def ta_copy(step):
        t = (ta + step) % nta
        return send(
            ln, lens.at[rows_at(ta * 8, 8, 8)], sem_ta.at[0, step], sem_ta.at[1, step], (wa, t)
        )

    def wv_column(b, core):
        return wvc.at[:, lanes((2 * b + core) * slot)]

    def wv_z(step):
        b = (z + step) % nz
        src = wsmall.at[:, pl.ds(split, PAD)]
        return send(
            src, wv_column(z, c), sem_wv.at[0, 0, step], sem_wv.at[1, 0, step], (wa, 2 * b + c)
        )

    def wv_core(step, core):
        where = wv_column((z - step + nz) % nz, core)
        return send(where, where, sem_wv.at[0, 1, step], sem_wv.at[1, 1, step], (wa, me.peer))

    own_wv = pltpu.make_async_copy(wsmall.at[:, pl.ds(split, PAD)], wv_column(z, c), sem_local.at[1])
    own_wv.start()
    for step in range(nz - 1, 0, -1):
        wv_z(step).start()
    for step in range(1, nwa):
        par_copy(step).start()
    for step in range(1, nta):
        ta_copy(step).start()
    rows[wa] = prow[...]
    lens[rows_at(ta * 8, 8, 8), :] = ln[...]
    own_wv.wait()
    wv_core(0, c).start()

    def w_line(p, up, b):
        where, sem = stores[p][0].at[wa, 2 * b + c], stores[p][1]
        k = 0 if up else 1
        return send(
            where, where, sem.at[0, k, b], sem.at[1, k, b], (wa, ta + 2 if up else ta - 2)
        )

    for step in range(1, nz):
        wv_z(step).wait_recv()
        wv_core(step, c).start()
    for copy in own_w:
        copy.wait()

    @pl.when(z < nz - 1)
    def _():
        for p in range(2):
            w_line(p, True, z).start()

    @pl.when(z > 0)
    def _():
        for p in range(2):
            w_line(p, False, z).start()

    layer_pad[...] = jnp.zeros_like(layer_pad)
    get_logits.wait()
    for h in range(heads):
        terms[h] = jnp.exp(terms[h].astype(F32)).astype(BF16)
    out_terms = pltpu.make_async_copy(terms, term_out, sem_local.at[3])
    out_terms.start()

    tok_turn(0)
    for step in range(1, nwa):
        par_copy(step).wait_recv()
    gap = 2 * CHUNK
    for w in range(nwa):
        piece = jnp.concatenate([rows[w, :, :gap], jnp.zeros((PAD - 8, gap), F32)], axis=0)
        pfull[w * width : (w + 1) * width, :] = piece.T[:width]
        span = rows.shape[2] - gap
        rfull[:, w * span : (w + 1) * span] = rows[w, :, gap:]
    for step in range(1, nta):
        ta_copy(step).wait_recv()
    for step in range(nz):
        wv_core(step, 1 - c).wait_recv()
    own_x.wait()

    positions = lax.broadcasted_iota(jnp.int32, (nta * 8, seq), 1).astype(F32)
    key_valid = jnp.where(positions < lens[:, 0:1], 1.0, 0.0).astype(BF16)
    for h in range(heads):
        sums = lax.dot_general(key_valid, terms[h], ROWS_NT, preferred_element_type=F32)
        zinv[h] = 1.0 / sums

    def value_copy(kind, b, q, core):
        where = value.at[2 * b + core, :, pl.ds(q * part, part)]
        t = (ta + 2, ta - 2, me.peer)[kind]
        return send(where, where, sem_val.at[0, kind, b, q], sem_val.at[1, kind, b, q], (wa, t))

    def w_plane(p, k, b):
        device = (me.wx if k == 0 else me.wy, ta)
        where, sem = stores[p][0].at[wa, 2 * b + c], stores[p][1]
        return send(where, where, sem.at[0, 2 + k, b], sem.at[1, 2 + k, b], device)

    def w_diag(p, k, b, source):
        device = (me.wy if k == 0 else me.wx, ta)
        where, sem = stores[p][0].at[source, 2 * b + c, pl.ds(k * half, half)], stores[p][1]
        return send(where, where, sem.at[0, 4 + k, b], sem.at[1, 4 + k, b], device)

    def w_core(p, r, b, core):
        source = (wa, me.wx, me.wy, me.wd)[r]
        where, sem = stores[p][0].at[source, 2 * b + core], stores[p][1]
        return send(where, where, sem.at[0, 6 + r, b], sem.at[1, 6 + r, b], (wa, me.peer))

    def w_start(p, b):
        w_plane(p, 0, b).start()
        w_plane(p, 1, b).start()
        w_core(p, 0, b, c).start()

    def w_forward(p, b):
        w_plane(p, 0, b).wait_recv()
        w_diag(p, 0, b, me.wx).start()
        w_core(p, 1, b, c).start()
        w_plane(p, 1, b).wait_recv()
        w_diag(p, 1, b, me.wy).start()
        w_core(p, 2, b, c).start()

    def w_finish(p, b):
        for k in range(2):
            w_diag(p, k, b, me.wd).wait_recv()
        w_core(p, 3, b, c).start()

    def w_landed(p, h):
        @pl.when(z - 1 - h >= 0)
        def _():
            w_line(p, True, z - 1 - h).wait_recv()

        @pl.when(z + 1 + h < nz)
        def _():
            w_line(p, False, z + 1 + h).wait_recv()

    def w_onward(p, h):
        @pl.when(jnp.logical_and(z - 1 - h >= 0, z < nz - 1))
        def _():
            w_line(p, True, z - 1 - h).start()

        @pl.when(jnp.logical_and(z + 1 + h < nz, z > 0))
        def _():
            w_line(p, False, z + 1 + h).start()

    def at_hop(h, act, *args):
        @pl.when(z - 1 - h >= 0)
        def _():
            act(*args, z - 1 - h)

        @pl.when(z + 1 + h < nz)
        def _():
            act(*args, z + 1 + h)

    for q in range(nz):
        cols = pl.ds(q * part, part)
        if q + 1 < nz:
            tok_turn(q + 1)
        for k in range(2):
            where = x.at[block_rows(me.wd, k * half, half), cols]
            send(
                where,
                where,
                sem_tok.at[0, 2 + k, q],
                sem_tok.at[1, 2 + k, q],
                (me.wy if k == 0 else me.wx, ta),
            ).wait_recv()
        centred, _ = norm_stats(x[:, cols].astype(F32))
        low = (centred * pfull[:, 0:1] + pfull[:, 1:2]).astype(BF16)
        layer[:, cols] = low
        for t in range(nta):
            layer_pad[t * slot : t * slot + wdepth, :] = low[t * wdepth : (t + 1) * wdepth]
        made = jnp.dot(wvc[...], layer_pad[...], preferred_element_type=F32)
        made = made + pfull[block_rows(wa), :][:, 2:3]
        place = lax.broadcasted_iota(jnp.int32, (width, part), 1) + q * part
        made = jnp.where(place.astype(F32) < ln[0:1, 0:1], made, 0.0)
        value[ta, :, cols] = made.astype(BF16)
        xown[:, pl.ds(q * CHUNK, CHUNK)] = x[:, lanes(q * part + wa * CHUNK)]

        @pl.when(z < nz - 1)
        def _():
            value_copy(0, z, q, c).start()

        @pl.when(z > 0)
        def _():
            value_copy(1, z, q, c).start()

        value_copy(2, z, q, c).start()
        if q < nz - 1:
            w_landed(0, q)
            w_onward(0, q)
    out_layer = pltpu.make_async_copy(layer, layer_out, sem_local.at[4])
    out_layer.start()

    def cot_copy(step, q):
        w = (wa + step) % nwa
        return send(
            cot.at[:, lanes(q * part + w * CHUNK)],
            cown.at[block_rows(wa), pl.ds(q * CHUNK, CHUNK)],
            sem_cot.at[0, step, q],
            sem_cot.at[1, step, q],
            (w, ta),
        )

    def cot_own(q):
        return pltpu.make_async_copy(
            cot.at[:, lanes(q * part + wa * CHUNK)],
            cown.at[block_rows(wa), pl.ds(q * CHUNK, CHUNK)],
            sem_cot.at[0, 0, q],
        )

    w_start(0, z)
    for h in range(nz - 1):
        at_hop(h, w_start, 0)
    w_start(1, z)
    w_landed(1, 0)
    at_hop(0, w_start, 1)
    for q in range(nz):
        cot_own(q).start()
        for step in range(1, nwa):
            cot_copy(step, q).start()

    def att_copy(s, j):
        return send(
            attsend.at[s, :, pl.ds(j * CHUNK, CHUNK)],
            attended.at[block_rows(wa), lanes(z * CHUNK)],
            sem_att.at[0, s, j],
            sem_att.at[1, wa, z],
            (2 * c + j, s),
        )

    def att_local(s, j):
        return pltpu.make_async_copy(
            attsend.at[s, :, pl.ds(j * CHUNK, CHUNK)],
            attended.at[block_rows(wa), lanes(z * CHUNK)],
            sem_att.at[0, s, j],
        )

    def is_self(s, j):
        return jnp.logical_and(s == ta, 2 * c + j == wa)

    def mix(b):
        for core in range(2):
            s = 2 * b + core
            pltpu.make_async_copy(value.at[s], value_out.at[s], sem_out.at[s]).start()
        length = [lens[rows_at((2 * b + core) * 8, 8, 8), :][0:1, 0:1] for core in range(2)]
        place = lax.broadcasted_iota(jnp.int32, (hdim, query), 1) + ta * query
        place = place.astype(F32)
        for h in range(heads):
            group = slice(h * hdim, (h + 1) * hdim)
            pair = jnp.concatenate([value[2 * b, group, :], value[2 * b + 1, group, :]], axis=0)
            both = lax.dot_general(pair, terms[h], ROWS_NT, preferred_element_type=F32)
            for core in range(2):
                s = 2 * b + core
                inverse = zinv[h, rows_at(s * 8, 8, 8), :][0:1]
                one = both[core * hdim : (core + 1) * hdim] * inverse
                mixed[s, group, :] = one
                one = jnp.where(place < length[core], one, 0.0)
                attsend[s, group, :] = one.astype(BF16)
        for core in range(2):
            s = 2 * b + core
            for j in range(2):

                @pl.when(is_self(s, j))
                def _():
                    att_local(s, j).start()

                @pl.when(jnp.logical_not(is_self(s, j)))
                def _():
                    att_copy(s, j).start()

    def core_ready(b):
        for q in range(nz):
            value_copy(2, b, q, 1 - c).wait_recv()

    for h in range(nz - 1):
        below, above = z - 1 - h, z + 1 + h
        for q in range(nz):

            @pl.when(below >= 0)
            def _():
                value_copy(0, below, q, c).wait_recv()

                @pl.when(z < nz - 1)
                def _():
                    value_copy(0, below, q, c).start()

                value_copy(2, below, q, c).start()

            @pl.when(above < nz)
            def _():
                value_copy(1, above, q, c).wait_recv()

                @pl.when(z > 0)
                def _():
                    value_copy(1, above, q, c).start()

                value_copy(2, above, q, c).start()

        if h == 0:
            core_ready(z)
            mix(z)

        @pl.when(below >= 0)
        def _():
            core_ready(below)
            mix(below)

        @pl.when(above < nz)
        def _():
            core_ready(above)
            mix(above)

        if h == 0:
            w_forward(0, z)
            for other in range(nz - 1):
                at_hop(other, w_forward, 0)
        if h == 1:
            w_onward(1, 0)
            w_forward(1, z)
            w_finish(0, z)
            for other in range(nz - 1):
                at_hop(other, w_finish, 0)
    at_hop(0, w_forward, 1)
    w_finish(1, z)
    at_hop(0, w_finish, 1)

    def w_cores(p, b):
        for r in range(4):
            w_core(p, r, b, 1 - c).wait_recv()

    depth, own = xown.shape
    both = 2 * one

    def turn(i):
        pair = z + 1 - 2 * (z % 2)
        late = jnp.where(i == 2, nz // 2 - z // 2, (nz - 1) * (1 - z // 2))
        return jnp.where(i == 0, z, jnp.where(i == 1, pair, late))

    def load(i, slot):
        b = turn(i)
        return pltpu.make_async_copy(
            large.at[:, pl.ds(2 * b, 2)], wblock.at[slot], sem_g.at[slot]
        )

    w_cores(1, turn(0))
    load(0, 0).start()
    for b in range(nz):
        w_cores(0, b)
    get_wo = pltpu.make_async_copy(small.at[:, :, :, pl.ds(0, PAD)], wo, sem_g.at[2])
    get_wo.start()
    for q in range(nz):
        cot_own(q).wait()
        for step in range(1, nwa):
            cot_copy(step, q).wait_recv()
    grad_t[...] = cown[...].T
    w_cores(1, turn(1))
    load(1, 1).start()

    def att_sends(s, carry):
        pltpu.make_async_copy(value.at[s], value_out.at[s], sem_out.at[s]).wait()
        for j in range(2):

            @pl.when(is_self(s, j))
            def _():
                att_local(s, j).wait()

            @pl.when(jnp.logical_not(is_self(s, j)))
            def _():
                att_copy(s, j).wait_send()

        return carry

    lax.fori_loop(0, nta, att_sends, 0)
    mine = wa // 2

    def att_arrivals(k, carry):
        w, b = k // nz, k % nz

        @pl.when(jnp.logical_not(jnp.logical_and(w == wa, 2 * b + mine == ta)))
        def _():
            where = attended.at[block_rows(w), lanes(b * CHUNK)]
            send(where, where, sem_att.at[0, 0, 0], sem_att.at[1, w, b], (w, 2 * b + mine)).wait_recv()

        return carry

    w_landed(1, 1)
    w_onward(1, 1)
    at_hop(1, w_start, 1)
    lax.fori_loop(0, nwa * nz, att_arrivals, 0)
    get_wo.wait()

    def wide_wo():
        joined = [
            jnp.concatenate([wo[w, t] for t in range(nta)], axis=1) for w in range(nwa)
        ]
        return jnp.concatenate(joined, axis=0)

    branch = lax.dot_general(wide_wo(), attended[...], ROWS_TN, preferred_element_type=F32)
    branch = jnp.concatenate([branch[t * PAD : t * PAD + wdepth] for t in range(nta)], axis=0)
    res = xown[...].astype(F32) + branch + pfull[:, 3:4]
    resid[...] = res
    norm, inv = norm_stats(res)
    normed[...] = norm
    inverse[...] = jnp.broadcast_to(inv, inverse.shape)
    low = (norm * pfull[:, 4:5] + pfull[:, 5:6]).astype(BF16)
    layer_two[...] = low
    layer_t[...] = low.T
    feed[...] = jnp.zeros_like(feed)
    dlayer[...] = jnp.zeros_like(dlayer)

    def put(i):
        return pltpu.make_async_copy(
            gblock, wgrad.at[:, turn(i), :, :, pl.ds(0, both)], sem_g.at[3]
        )

    def middle(i, carry):
        slot = i % 2

        @pl.when(i == 2)
        def _():
            at_hop(1, w_finish, 1)
            w_landed(1, 2)
            at_hop(2, w_start, 1)
            w_cores(1, turn(2))
            load(2, 0).start()

        @pl.when(i == 3)
        def _():
            at_hop(2, w_forward, 1)
            at_hop(2, w_finish, 1)
            w_cores(1, turn(3))
            load(3, 1).start()

        load(i, slot).wait()
        held = wblock.at[slot]

        def joined(start):
            parts = [held[:, g, :, start : start + one].reshape(depth, one) for g in range(2)]
            return jnp.concatenate(parts, axis=1)

        up, down_t = joined(0), joined(one)
        at = lanes(turn(i) * both, both)
        upper = jnp.dot(layer_t[...], up, preferred_element_type=F32) + rfull[0:1, at]
        hidden, slope = gelu_pair(upper)
        hidden = hidden.astype(BF16)
        dhidden = jnp.dot(grad_t[...], down_t, preferred_element_type=F32)
        dupper = (dhidden * slope).astype(BF16)
        vrow[:, at] = jnp.broadcast_to(
            jnp.sum(dupper.astype(F32), axis=0, keepdims=True), (vrow.shape[0], both)
        )
        feed[...] += lax.dot_general(down_t, hidden, ROWS_NT, preferred_element_type=F32)
        dlayer[...] += lax.dot_general(up, dupper, ROWS_NT, preferred_element_type=F32)
        gup = jnp.dot(layer_two[...], dupper, preferred_element_type=F32)
        gdown = jnp.dot(cown[...], hidden, preferred_element_type=F32)

        @pl.when(i > 0)
        def _():
            put(i - 1).wait()

        for g in range(2):
            piece = slice(g * one, (g + 1) * one)
            gblock[:, g, :, :one] = gup[:, piece].reshape(nwa, width, one).astype(BF16)
            gblock[:, g, :, one:] = gdown[:, piece].reshape(nwa, width, one).astype(BF16)
        put(i).start()

        @pl.when(i == 0)
        def _():
            at_hop(1, w_forward, 1)

        return carry

    lax.fori_loop(0, nz, middle, 0)

    grad = cown[...].astype(F32)
    out[...] = (resid[...] + feed[...] + pfull[:, 6:7]).astype(BF16)
    dl = dlayer[...]
    norm = normed[...]
    e = dl * pfull[:, 4:5]
    mean_e = jnp.sum(e, axis=0, keepdims=True) / depth
    mean_n = jnp.sum(e * norm, axis=0, keepdims=True) / depth
    dres = grad + inverse[0:1, :] * (e - mean_e - norm * mean_n)
    dresid[...] = dres
    low = dres.astype(BF16)
    vcol[...] = jnp.zeros_like(vcol)
    vcol[:, 3:4] = jnp.sum(low.astype(F32), axis=1, keepdims=True)
    vcol[:, 4:5] = jnp.sum(dl * norm, axis=1, keepdims=True)
    vcol[:, 5:6] = jnp.sum(dl, axis=1, keepdims=True)
    vcol[:, 6:7] = jnp.sum(grad, axis=1, keepdims=True)
    wide[...] = jnp.zeros_like(wide)
    for t in range(nta):
        wide[t * PAD : t * PAD + wdepth, :] = low[t * wdepth : (t + 1) * wdepth]
    da = jnp.dot(wide_wo(), wide[...], preferred_element_type=F32)
    lane = lax.broadcasted_iota(jnp.int32, (depth, own), 1)
    place = (lane // CHUNK) * (CHUNK * nwa) + lane % CHUNK + wa * CHUNK
    da = jnp.where(place.astype(F32) < ln[0:1, 0:1], da, 0.0)
    dattended[...] = da.astype(BF16)
    made = lax.dot_general(attended[...], wide[...], ROWS_NT, preferred_element_type=F32)
    for t in range(nta):
        piece = made[:, t * PAD : (t + 1) * PAD].reshape(nwa, width, PAD)
        gwo[:, t // 2, t % 2] = piece.astype(BF16)
    rest = pltpu.make_async_copy(gwo, wgrad.at[:, :, :, :, pl.ds(both, PAD)], sem_g.at[4])
    rest.start()
    put(nz - 1).wait()
    rest.wait()

    for step in range(1, nta):
        ta_copy(step).wait_send()
    for step in range(nz):
        wv_core(step, c).wait_send()
        if step:
            wv_z(step).wait_send()
    for step in range(1, nwa):
        par_copy(step).wait_send()
        for q in range(nz):
            cot_copy(step, q).wait_send()
    for q in range(nz):
        for k in range(2):
            tok_copy(k, q).wait_send()
            tok_fwd(k, q).wait_send()

    def line_sends(b, carry):
        reach_up = jnp.logical_and(b <= z, z < nz - 1)
        reach_down = jnp.logical_and(b >= z, z > 0)

        @pl.when(reach_up)
        def _():
            for p in range(2):
                w_line(p, True, b).wait_send()
            for q in range(nz):
                value_copy(0, b, q, c).wait_send()

        @pl.when(reach_down)
        def _():
            for p in range(2):
                w_line(p, False, b).wait_send()
            for q in range(nz):
                value_copy(1, b, q, c).wait_send()

        for q in range(nz):
            value_copy(2, b, q, c).wait_send()
        for p in range(2):
            for k in range(2):
                w_plane(p, k, b).wait_send()
            w_diag(p, 0, b, me.wx).wait_send()
            w_diag(p, 1, b, me.wy).wait_send()
            for r in range(4):
                w_core(p, r, b, c).wait_send()
        return carry

    lax.fori_loop(0, nz, line_sends, 0)

    out_terms.wait()
    out_layer.wait()


def run_forward(dims, tok, cot, wout, wval, wup, wdown, prow, ln, logits):
    nwa, nta = dims
    nz = nta // 2
    width, seq = tok.shape
    depth = width * nwa
    own = seq // nwa
    heads, query, _ = logits.shape
    slot = PAD
    both = 2 * wup.shape[1]
    hidden = both // 2 * nta
    dma = pltpu.SemaphoreType.DMA
    return pl.pallas_call(
        functools.partial(forward_kernel, dims),
        out_shape=(
            shape_of((depth, own), BF16),
            shape_of((nwa, nta, width, 2 * PAD), BF16),
            shape_of((nwa, nta, width, both), BF16),
            shape_of((depth, seq), BF16),
            shape_of((nta, width, seq), BF16),
            shape_of((heads, query, seq), BF16),
            shape_of((nta, width, query), F32),
            shape_of((heads, nta * 8, query), F32),
            shape_of((nta * 8, CHUNK), F32),
            shape_of((depth, PAD), F32),
            shape_of((depth, own), BF16),
            shape_of((depth, own), BF16),
            shape_of((depth, own), F32),
            shape_of((nwa, nz, 2, width, both + PAD), BF16),
            shape_of((depth, PAD), F32),
            shape_of((8, hidden), F32),
        ),
        in_specs=anywhere(2) + whole(2) + anywhere(2) + whole(2) + anywhere(1),
        out_specs=tuple(whole(1) + anywhere(5) + whole(7) + anywhere(1) + whole(2)),
        scratch_shapes=[
            pltpu.VMEM((depth, own), BF16),
            pltpu.VMEM((depth, own), BF16),
            pltpu.VMEM((8, hidden), F32),
            pltpu.VMEM((nwa, nta, width, PAD), BF16),
            pltpu.VMEM((2, nwa, 2, width, both), BF16),
            pltpu.VMEM((depth, own), F32),
            pltpu.VMEM((depth, own), F32),
            pltpu.VMEM((8, own), F32),
            pltpu.VMEM((depth, own), BF16),
            pltpu.VMEM((own, depth), BF16),
            pltpu.VMEM((own, depth), BF16),
            pltpu.VMEM((depth, own), F32),
            pltpu.VMEM((depth, own), F32),
            pltpu.VMEM((nta * PAD, own), BF16),
            pltpu.VMEM((nwa, 2, width, both), BF16),
            pltpu.VMEM((nwa, nz, 2, width, PAD), BF16),
            pltpu.VMEM((depth, seq), BF16),
            pltpu.VMEM((width, nta * slot), BF16),
            pltpu.VMEM((nta * slot, seq // nz), BF16),
            pltpu.VMEM((depth, seq), BF16),
            pltpu.VMEM((nta, width, seq), BF16),
            pltpu.VMEM((heads, query, seq), BF16),
            pltpu.VMEM((nta, width, query), BF16),
            pltpu.VMEM((nwa,) + prow.shape, F32),
            pltpu.VMEM((PAD, 2 * CHUNK), BF16),
            pltpu.VMEM((width, 2 * PAD), BF16),
            dma((2, 4, nz)),
            dma((2, nwa)),
            dma((2, nta)),
            dma((2, 3, nz, nz)),
            dma((2, 10, nz)),
            dma((2, 10, nz)),
            dma((2, nwa, nz)),
            dma((2, nta, max(nz, 2))),
            dma((8,)),
            dma((nta,)),
            dma((2, 2, nz)),
            dma((5,)),
        ],
        compiler_params=pltpu.CompilerParams(
            collective_id=1, has_side_effects=True, vmem_limit_bytes=VMEM_BYTES
        ),
        cost_estimate=pl.CostEstimate(
            flops=20 * 10**9, bytes_accessed=80 * 10**6, transcendentals=4 * 10**6
        ),
    )(tok, cot, wout, wval, wup, wdown, prow, ln, logits)


def gelu_pair(u):
    root = 0.7978845608028654
    square = u * u
    bent = jnp.tanh(root * u * (1.0 + 0.044715 * square))
    low_half = 0.5 * (1.0 + bent)
    slope = low_half + 0.5 * u * (1.0 - bent * bent) * root * (1.0 + 3.0 * 0.044715 * square)
    return (u * low_half, slope)


def backward_kernel(
    dims,
    dattended,
    outown,
    dresid_in,
    xown_in,
    terms_in,
    mixed_in,
    zinv,
    lens,
    ln,
    pfull,
    layer_in,
    weights,
    wgrad,
    vcol,
    vrow,
    scaled,
    shift,
    output,
    tgrad,
    vgrad,
    vectors,
    wsum,
    dresid,
    xown,
    terms,
    mixed,
    layer,
    normed,
    invs,
    wvt,
    gains,
    biases,
    da,
    partial,
    paired,
    up_in,
    down_in,
    gown,
    gpeer,
    first_x,
    first_y,
    second_x,
    second_y,
    gup_in,
    gdown_in,
    dvalue,
    dvown,
    wv,
    vsend,
    vrecv,
    tsend,
    csend,
    crecv,
    csum,
    crecv2,
    sem_da,
    sem_out,
    sem_core,
    sem_line,
    sem_dv,
    sem_tg,
    sem_v,
    sem_c,
    sem_c2,
    sem_local,
    sem_g,
    sem_gline,
):
    nwa, nta = dims
    me = Place(nwa, nta)
    wa, ta, z, c = me.wa, me.ta, me.z, me.c
    nz = me.nz
    depth, own = dresid.shape
    width = depth // nwa
    wdepth = depth // nta
    heads, query, seq = terms.shape
    hdim = width // heads
    part = seq // nz
    pairs = (
        (terms_in, terms),
        (mixed_in, mixed),
        (xown_in, xown),
        (dresid_in, dresid),
        (layer_in, layer),
    )
    fetch = [
        pltpu.make_async_copy(src, dst, sem_local.at[1 + i]) for i, (src, dst) in enumerate(pairs)
    ]
    for copy in fetch:
        copy.start()
    me.enter()

    def block_rows(w):
        return rows_at(w * width, width, 32)

    def da_copy(w, b, local):
        core = wa // 2
        src = dattended.at[block_rows(w), lanes(b * CHUNK)]
        dst = da.at[ta, :, lanes((wa % 2) * CHUNK)]
        if local:
            return pltpu.make_async_copy(src, dst, sem_da.at[0, w, b])
        return send(src, dst, sem_da.at[0, w, b], sem_da.at[1, ta, wa % 2], (w, 2 * b + core))

    def da_self(w, b):
        return jnp.logical_and(w == wa, 2 * b + wa // 2 == ta)

    def far(i):
        low_end = 1 - z // (nz // 2)
        return (nz - 1 - i) * low_end + i * (1 - low_end)

    def da_start(k, carry):
        w, b = (wa + k % nwa) % nwa, far(k // nwa)

        @pl.when(da_self(w, b))
        def _():
            da_copy(w, b, True).start()

        @pl.when(jnp.logical_not(da_self(w, b)))
        def _():
            da_copy(w, b, False).start()

        return carry

    lax.fori_loop(0, nwa * nz, da_start, 0)

    def back_copy(src, dst, sems, step, q):
        w = (wa + step) % nwa
        return send(
            src.at[block_rows(w), pl.ds(q * CHUNK, CHUNK)],
            dst.at[:, lanes(q * part + wa * CHUNK)],
            sems.at[0, step, q],
            sems.at[1, step, q],
            (w, ta),
        )

    def back_own(src, dst, sems, q):
        return pltpu.make_async_copy(
            src.at[block_rows(wa), pl.ds(q * CHUNK, CHUNK)],
            dst.at[:, lanes(q * part + wa * CHUNK)],
            sems.at[0, 0, q],
        )

    get_wv = pltpu.make_async_copy(
        weights.at[:, :, :, pl.ds(weights.shape[3] - PAD, PAD)], wv, sem_local.at[0]
    )
    get_wv.start()

    half = width // 2
    order = []
    for j in range(nz):
        for b in (nz - 1 - j, j):
            if b not in order:
                order.append(b)

    def g_core(b, core):
        return send(
            wgrad.at[:, b, core],
            gpeer.at[b],
            sem_g.at[0, 0, b],
            sem_g.at[1, 0, b],
            (wa, me.peer),
        )

    def g_load(b):
        return pltpu.make_async_copy(wgrad.at[:, b, c], gown.at[b], sem_g.at[0, 7, b])

    def g_first(k, r, b):
        near = me.wx if k == 0 else me.wy
        which = near if r == 0 else me.wd
        return send(
            gown.at[b, which, pl.ds(k * half, half)],
            (first_x if k == 0 else first_y).at[b, r],
            sem_g.at[0, 1 + 2 * k + r, b],
            sem_g.at[1, 1 + 2 * k + r, b],
            (near, ta),
        )

    def g_second(k, b):
        near = me.wy if k == 0 else me.wx
        return send(
            gown.at[b, near, pl.ds(k * half, half)],
            (second_x if k == 0 else second_y).at[b],
            sem_g.at[0, 5 + k, b],
            sem_g.at[1, 5 + k, b],
            (near, ta),
        )

    def g_add(b, which, k, extra):
        rows = pl.ds(k * half, half)
        gown[b, which, rows, :] = (
            gown[b, which, rows, :].astype(F32) + extra.astype(F32)
        ).astype(BF16)

    def g_cores(b):
        g_load(b).wait()
        g_core(b, c).wait_recv()
        for w in range(nwa):
            gown[b, w] = (gown[b, w].astype(F32) + gpeer[b, w].astype(F32)).astype(BF16)
        for k in range(2):
            for r in range(2):
                g_first(k, r, b).start()

    def g_plane(b):
        for k in range(2):
            for r in range(2):
                g_first(k, r, b).wait_recv()
            landed = first_x if k == 0 else first_y
            g_add(b, me.wy if k == 0 else me.wx, k, landed[b, 1])
            g_second(k, b).start()
            g_add(b, wa, k, landed[b, 0])

    def g_end(b):
        for k in range(2):
            g_second(k, b).wait_recv()
            g_add(b, wa, k, (second_x if k == 0 else second_y)[b])

    def g_line(up, j):
        k = 0 if up else 1
        target = nz - 1 - j if up else j
        return send(
            gown.at[target, wa],
            (gup_in if up else gdown_in).at[j],
            sem_gline.at[0, k, j],
            sem_gline.at[1, k, j],
            (wa, ta + 2 if up else ta - 2),
        )

    def g_origin():
        @pl.when(z == 0)
        def _():
            for j in range(nz - 1):
                g_line(True, j).start()

        @pl.when(z == nz - 1)
        def _():
            for j in range(nz - 1):
                g_line(False, j).start()

    def g_hop(j):
        target = nz - 1 - j

        @pl.when(jnp.logical_and(z < target, z > 0))
        def _():
            g_line(True, j).wait_recv()
            gown[target, wa] = (gown[target, wa].astype(F32) + gup_in[j].astype(F32)).astype(BF16)
            g_line(True, j).start()

        @pl.when(jnp.logical_and(z > j, z < nz - 1))
        def _():
            g_line(False, j).wait_recv()
            gown[j, wa] = (gown[j, wa].astype(F32) + gdown_in[j].astype(F32)).astype(BF16)
            g_line(False, j).start()

    def g_final():
        @pl.when(z == 0)
        def _():
            g_line(False, 0).wait_recv()
            wsum[...] = gown[0, wa].astype(F32) + gdown_in[0].astype(F32)

        @pl.when(z == nz - 1)
        def _():
            g_line(True, 0).wait_recv()
            wsum[...] = gown[nz - 1, wa].astype(F32) + gup_in[0].astype(F32)

        for b in range(1, nz - 1):

            @pl.when(z == b)
            def _():
                g_line(True, nz - 1 - b).wait_recv()
                g_line(False, b).wait_recv()
                both = gup_in[nz - 1 - b].astype(F32) + gdown_in[b].astype(F32)
                wsum[...] = gown[b, wa].astype(F32) + both

    for b in order:
        g_core(b, 1 - c).start()
        g_load(b).start()

    def da_arrive(s, j):
        own_piece = jnp.logical_and(s == ta, 2 * c + j == wa)
        where = da.at[s, :, lanes(j * CHUNK)]

        @pl.when(own_piece)
        def _():
            da_copy(wa, z, True).wait()

        @pl.when(jnp.logical_not(own_piece))
        def _():
            send(where, where, sem_da.at[0, 0, 0], sem_da.at[1, s, j], (2 * c + j, s)).wait_recv()

    def da_sent(k, carry):
        w, b = (wa + k // nz) % nwa, k % nz

        @pl.when(jnp.logical_not(da_self(w, b)))
        def _():
            da_copy(w, b, False).wait_send()

        return carry

    def prepare(b):
        for core in range(2):
            for j in range(2):
                da_arrive(2 * b + core, j)
        for h in range(heads):
            group = slice(h * hdim, (h + 1) * hdim)
            both = []
            for s in (2 * b, 2 * b + 1):
                one = da[s, group, :].astype(F32) * zinv[h, s * 8 : s * 8 + 1, :]
                both.append(one.astype(BF16))
                scaled[s, group, :] = both[-1]
            made = jnp.dot(
                jnp.concatenate(both, axis=0), terms[h], preferred_element_type=F32
            ).astype(BF16)
            partial[2 * b, group, :] = made[:hdim]
            partial[2 * b + 1, group, :] = made[hdim:]
        core_copy(b, 1 - c).start()

    def shifts():
        for h in range(heads):
            group = slice(h * hdim, (h + 1) * hdim)
            for s in range(nta):
                inv = zinv[h, s * 8 : s * 8 + 1, :]
                one = da[s, group, :].astype(F32) * mixed[s, group, :]
                along = jnp.sum(one, axis=0, keepdims=True)
                shift[h, s * 8 : (s + 1) * 8, :] = jnp.broadcast_to(along * inv, (8, query))

    def core_copy(b, core):
        return send(
            partial.at[2 * b + core],
            paired.at[b],
            sem_core.at[0, b],
            sem_core.at[1, b],
            (wa, me.peer),
        )

    def out_start():
        for q in range(nz):
            back_own(outown, output, sem_out, q).start()
            for step in range(1, nwa):
                back_copy(outown, output, sem_out, step, q).start()

    def line_copy(up, j, q):
        k = 0 if up else 1
        cols = pl.ds(q * part, part)
        return send(
            partial.at[2 * (nz - 1 - j if up else j) + c, :, cols],
            (up_in if up else down_in).at[j, :, cols],
            sem_line.at[0, k, j, q],
            sem_line.at[1, k, j, q],
            (wa, ta + 2 if up else ta - 2),
        )

    ready = set()

    def core_ready(b):
        if b not in ready:
            ready.add(b)
            core_copy(b, c).wait_recv()

    def chip_sum(b, q):
        cols = pl.ds(q * part, part)
        return partial[2 * b + c, :, cols].astype(F32) + paired[b, :, cols].astype(F32)

    def line_step(up, j, q):
        target = nz - 1 - j if up else j
        landed = up_in if up else down_in
        cols = pl.ds(q * part, part)

        @pl.when(z < target if up else z > target)
        def _():
            first = z == (0 if up else nz - 1)

            @pl.when(jnp.logical_not(first))
            def _():
                line_copy(up, j, q).wait_recv()
                total = chip_sum(target, q) + landed[j, :, cols].astype(F32)
                partial[2 * target + c, :, cols] = total.astype(BF16)

            @pl.when(first)
            def _():
                partial[2 * target + c, :, cols] = chip_sum(target, q).astype(BF16)

            line_copy(up, j, q).start()

    def line(j):
        core_ready(nz - 1 - j)
        core_ready(j)
        for q in range(nz):
            line_step(True, j, q)
            line_step(False, j, q)

    fetch[0].wait()
    for b in order:
        g_cores(b)
    prepare(order[0])
    prepare(order[1])
    line(0)
    for b in order[2:]:
        prepare(b)
    for j in range(1, nz - 1):
        line(j)
    for b in range(nz):
        core_ready(b)

    fetch[1].wait()
    shifts()
    get_wv.wait()
    for t in range(nta):
        turned = jnp.concatenate([wv[w, t] for w in range(nwa)], axis=0).T
        wvt[t * wdepth : (t + 1) * wdepth, :] = turned[:wdepth]
    fetch[2].wait()
    fetch[3].wait()
    norm, inv = norm_stats(xown[...].astype(F32))
    normed[...] = norm
    invs[...] = jnp.broadcast_to(inv, invs.shape)
    gains[...] = jnp.zeros_like(gains)
    biases[...] = jnp.zeros_like(biases)
    fetch[4].wait()
    for b in order:
        g_plane(b)
    out_start()

    def dv_copy(step, q):
        w = (wa + step) % nwa
        return send(
            dvalue.at[:, lanes(q * part + w * CHUNK)],
            dvown.at[block_rows(wa), pl.ds(q * CHUNK, CHUNK)],
            sem_dv.at[0, step, q],
            sem_dv.at[1, step, q],
            (w, ta),
        )

    place = lax.broadcasted_iota(jnp.int32, (width, part), 1).astype(F32)

    def final(q):
        cols = pl.ds(q * part, part)
        key_valid = place + q * part < ln[0:1, 0:1]
        for b in range(nz):

            @pl.when(z == b)
            def _():
                total = chip_sum(b, q)
                if b > 0:
                    line_copy(True, nz - 1 - b, q).wait_recv()
                    total = total + up_in[nz - 1 - b, :, cols].astype(F32)
                if b < nz - 1:
                    line_copy(False, b, q).wait_recv()
                    total = total + down_in[b, :, cols].astype(F32)
                dvalue[:, cols] = jnp.where(key_valid, total, 0.0).astype(BF16)

        for step in range(1, nwa):
            dv_copy(step, q).start()
        dvown[block_rows(wa), q * CHUNK : (q + 1) * CHUNK] = dvalue[
            :, lanes(q * part + wa * CHUNK)
        ]

    for b in order:
        g_end(b)
    g_origin()
    for q in range(nz):
        final(q)

    g_hop(0)
    vmade = lax.dot_general(layer[...], dvalue[...], ROWS_NT, preferred_element_type=F32)
    vsend[...] = vmade.astype(BF16).reshape(nta, wdepth, width)
    vbias = jnp.sum(dvalue[...].astype(F32), axis=1, keepdims=True)

    def v_copy(step):
        t = (ta + step) % nta
        return send(
            vsend.at[t], vrecv.at[step], sem_v.at[0, step], sem_v.at[1, step], (wa, t)
        )

    for step in range(1, nta):
        v_copy(step).start()

    for q in range(nz):
        cols = slice(q * CHUNK, (q + 1) * CHUNK)
        for step in range(1, nwa):
            dv_copy(step, q).wait_recv()
        dl = jnp.dot(wvt[...], dvown[:, cols], preferred_element_type=F32)
        norm = normed[:, cols]
        e = dl * pfull[:, 0:1]
        mean_e = jnp.sum(e, axis=0, keepdims=True) / depth
        mean_n = jnp.sum(e * norm, axis=0, keepdims=True) / depth
        made = dresid[:, cols] + invs[0:1, cols] * (e - mean_e - norm * mean_n)
        tsend[:, cols] = made.astype(BF16)
        back_own(tsend, tgrad, sem_tg, q).start()
        for step in range(1, nwa):
            back_copy(tsend, tgrad, sem_tg, step, q).start()
        gains[...] += dl * norm
        biases[...] += dl

    gain = jnp.sum(gains[...], axis=1, keepdims=True)
    bias = jnp.sum(biases[...], axis=1, keepdims=True)
    column = lax.broadcasted_iota(jnp.int32, (depth, PAD), 1)
    cols = jnp.where(column == 0, gain, jnp.where(column == 1, bias, vcol[...]))
    wide = vrow.shape[1] // nwa
    gap = csend.shape[2] - CHUNK
    used = wide // CHUNK
    for w in range(nwa):
        piece = cols[w * width : (w + 1) * width]
        piece = jnp.concatenate([piece, jnp.zeros((gap - width, PAD), F32)], axis=0)
        csend[w, :, :gap] = piece.T[:8]
        starts = [w * wide + row * CHUNK for row in range(used)]
        packed = [vrow[0:1, start : start + CHUNK] for start in starts]
        csend[w, :, gap:] = jnp.concatenate(packed + [jnp.zeros((8 - used, CHUNK), F32)], axis=0)

    def c_copy(step):
        w = (wa + step) % nwa
        return send(csend.at[w], crecv.at[step], sem_c.at[0, step], sem_c.at[1, step], (w, ta))

    for step in range(1, nwa):
        c_copy(step).start()
    g_hop(1)
    crecv[0] = csend[wa]
    piece = jnp.concatenate(
        [jnp.broadcast_to(vbias, (width, PAD)), jnp.zeros((gap - width, PAD), F32)], axis=0
    )
    vb_row = jnp.concatenate([piece.T[:8], jnp.zeros((8, CHUNK), F32)], axis=1)
    row = lax.broadcasted_iota(jnp.int32, vb_row.shape, 0)
    total = jnp.where(row == 2, vb_row, 0.0) + crecv[0]
    for step in range(1, nwa):
        c_copy(step).wait_recv()
        total = total + crecv[step]
    csum[...] = total

    def c2_copy(step):
        t = (ta + step) % nta
        return send(csum, crecv2.at[step], sem_c2.at[0, step], sem_c2.at[1, step], (wa, t))

    for step in range(1, nta):
        c2_copy(step).start()
    for j in range(2, nz - 1):
        g_hop(j)
    value_total = vsend[ta].astype(F32)
    for step in range(1, nta):
        v_copy(step).wait_recv()
        value_total = value_total + vrecv[step].astype(F32)
    vgrad[...] = value_total
    g_final()
    crecv2[0] = csum[...]
    for step in range(1, nta):
        c2_copy(step).wait_recv()
    full = jnp.zeros(csum.shape, F32)
    for t in range(nta):
        full = full + crecv2[(ta - t + nta) % nta]
    vectors[...] = full

    lax.fori_loop(0, nwa * nz, da_sent, 0)
    for step in range(1, nwa):
        for q in range(nz):
            back_copy(tsend, tgrad, sem_tg, step, q).wait()
            back_copy(outown, output, sem_out, step, q).wait()
            dv_copy(step, q).wait_send()
        c_copy(step).wait_send()
    for q in range(nz):
        back_own(outown, output, sem_out, q).wait()
        back_own(tsend, tgrad, sem_tg, q).wait()
    for step in range(1, nta):
        v_copy(step).wait_send()
        c2_copy(step).wait_send()
    for b in range(nz):
        core_copy(b, 1 - c).wait_send()
        g_core(b, 1 - c).wait_send()
        for k in range(2):
            g_first(k, 0, b).wait_send()
            g_first(k, 1, b).wait_send()
            g_second(k, b).wait_send()
    for j in range(nz - 1):

        @pl.when(z < nz - 1 - j)
        def _():
            for q in range(nz):
                line_copy(True, j, q).wait_send()
            g_line(True, j).wait_send()

        @pl.when(z > j)
        def _():
            for q in range(nz):
                line_copy(False, j, q).wait_send()
            g_line(False, j).wait_send()


def run_backward(
    dims, dattended, outown, dresid, xown, terms, mixed, zinv, lens, ln, pfull, layer, weights, wgrad, vcol, vrow
):
    nwa, nta = dims
    nz = nta // 2
    half, both = weights.shape[2] // 2, wgrad.shape[4]
    depth, own = dresid.shape
    width = depth // nwa
    heads, query, seq = terms.shape
    wdepth = depth // nta
    wide = 3 * CHUNK
    dma = pltpu.SemaphoreType.DMA
    return pl.pallas_call(
        functools.partial(backward_kernel, dims),
        out_shape=(
            shape_of((nta, width, query), BF16),
            shape_of((heads, nta * 8, query), F32),
            shape_of((width, seq), BF16),
            shape_of((width, seq), BF16),
            shape_of((wdepth, width), F32),
            shape_of((8, wide), F32),
            shape_of((width, both), F32),
        ),
        in_specs=anywhere(6) + whole(4) + anywhere(3) + whole(2),
        out_specs=tuple(whole(7)),
        scratch_shapes=[
            pltpu.VMEM((depth, own), F32),
            pltpu.VMEM((depth, own), BF16),
            pltpu.VMEM((heads, query, seq), BF16),
            pltpu.VMEM((nta, width, query), F32),
            pltpu.VMEM((depth, seq), BF16),
            pltpu.VMEM((depth, own), F32),
            pltpu.VMEM((8, own), F32),
            pltpu.VMEM((depth, depth), BF16),
            pltpu.VMEM((depth, CHUNK), F32),
            pltpu.VMEM((depth, CHUNK), F32),
            pltpu.VMEM((nta, width, query), BF16),
            pltpu.VMEM((nta, width, seq), BF16),
            pltpu.VMEM((nz, width, seq), BF16),
            pltpu.VMEM((nz - 1, width, seq), BF16),
            pltpu.VMEM((nz - 1, width, seq), BF16),
            pltpu.VMEM((nz, nwa, width, both), BF16),
            pltpu.VMEM((nz, nwa, width, both), BF16),
            pltpu.VMEM((nz, 2, half, both), BF16),
            pltpu.VMEM((nz, 2, half, both), BF16),
            pltpu.VMEM((nz, half, both), BF16),
            pltpu.VMEM((nz, half, both), BF16),
            pltpu.VMEM((nz - 1, width, both), BF16),
            pltpu.VMEM((nz - 1, width, both), BF16),
            pltpu.VMEM((width, seq), BF16),
            pltpu.VMEM((depth, own), BF16),
            pltpu.VMEM((nwa, nta, width, PAD), BF16),
            pltpu.VMEM((nta, wdepth, width), BF16),
            pltpu.VMEM((nta, wdepth, width), BF16),
            pltpu.VMEM((depth, own), BF16),
            pltpu.VMEM((nwa, 8, wide), F32),
            pltpu.VMEM((nwa, 8, wide), F32),
            pltpu.VMEM((8, wide), F32),
            pltpu.VMEM((nta, 8, wide), F32),
            dma((2, nta, max(nz, 2))),
            dma((2, nwa, nz)),
            dma((2, nz)),
            dma((2, 2, nz, nz)),
            dma((2, nwa, nz)),
            dma((2, nwa, nz)),
            dma((2, nta)),
            dma((2, nwa)),
            dma((2, nta)),
            dma((6,)),
            dma((2, 8, nz)),
            dma((2, 2, nz)),
        ],
        compiler_params=pltpu.CompilerParams(
            collective_id=2, has_side_effects=True, vmem_limit_bytes=VMEM_BYTES
        ),
        cost_estimate=pl.CostEstimate(
            flops=4 * 10**9, bytes_accessed=80 * 10**6, transcendentals=0
        ),
    )(
        dattended, outown, dresid, xown, terms, mixed, zinv, lens, ln, pfull, layer, weights, wgrad,
        vcol, vrow,
    )


def logits_kernel(
    terms,
    scaled,
    value,
    shift,
    lens,
    output,
    tgrad,
    wsum,
    vgrad,
    vectors,
    out,
    output_out,
    tgrad_out,
    up_out,
    down_out,
    wo_out,
    vgrad_out,
    *vector_out,
):
    nta = scaled.shape[0]
    for row, ref in enumerate(vector_out[:-1]):
        ref[...] = vectors[row, : ref.shape[0]]
    bias_out = vector_out[-1]
    gap = vectors.shape[1] - CHUNK
    for row in range(bias_out.shape[0] // CHUNK):
        bias_out[row * CHUNK : (row + 1) * CHUNK] = vectors[row, gap:]
    output_out[...] = output[...]
    tgrad_out[...] = tgrad[...].astype(F32)
    vgrad_out[...] = vgrad[...]
    hidden = up_out.shape[1]
    up_out[...] = wsum[:, :hidden]
    down_out[...] = wsum[:, hidden : 2 * hidden]
    wo_out[...] = wsum[:, 2 * hidden : 2 * hidden + wo_out.shape[1]]
    cols = terms.shape[2]
    stacked = jnp.concatenate([scaled[s] for s in range(nta)], axis=0)
    values = jnp.concatenate([value[s] for s in range(nta)], axis=0)
    made = lax.dot_general(stacked, values, ROWS_TN, preferred_element_type=F32)
    where = (nta * 8, cols)
    place = lax.broadcasted_iota(jnp.int32, where, 1) + pl.program_id(1) * cols
    first = lax.broadcasted_iota(jnp.int32, where, 0) % 8 == 0
    valid = jnp.logical_and(place.astype(F32) < lens[:, 0:1], first)
    valid = jnp.where(valid, 1.0, 0.0).astype(BF16)
    high = shift[0].astype(BF16)
    rest = (shift[0] - high.astype(F32)).astype(BF16)
    made = made - lax.dot_general(high, valid, ROWS_TN, preferred_element_type=F32)
    made = made - lax.dot_general(rest, valid, ROWS_TN, preferred_element_type=F32)
    out[0] = terms[0].astype(F32) * made


def run_logits(terms, scaled, value, shift, lens, output, tgrad, wsum, vgrad, vectors, bias):
    heads, query, seq = terms.shape
    nta, width, _ = scaled.shape
    hdim = width // heads
    cols = min(1024, seq)
    steps = seq // cols
    wdepth = vgrad.shape[0]
    hidden = (wsum.shape[1] - PAD) // 2
    total = heads * steps
    flat = (shape_of((width,), F32),) * 7 + (shape_of((bias,), F32),)

    def rows_of(array, lanes_in=None):
        shape = (array[0] // total, lanes_in or array[1])
        return pl.BlockSpec(shape, lambda h, k: (h * steps + k, 0))

    return pl.pallas_call(
        logits_kernel,
        grid=(heads, steps),
        out_shape=(
            shape_of((heads, query, seq), F32),
            shape_of((width, seq), BF16),
            shape_of((width, seq), F32),
            shape_of((width, hidden), F32),
            shape_of((width, hidden), F32),
            shape_of((width, wdepth), F32),
            shape_of(vgrad.shape, F32),
        )
        + flat,
        in_specs=[
            pl.BlockSpec((1, query, cols), lambda h, k: (h, 0, k)),
            pl.BlockSpec((nta, hdim, query), lambda h, k: (0, h, 0)),
            pl.BlockSpec((nta, hdim, cols), lambda h, k: (0, h, k)),
            pl.BlockSpec((1, nta * 8, query), lambda h, k: (h, 0, 0)),
            pl.BlockSpec(lens.shape, lambda h, k: (0, 0)),
            rows_of(output.shape),
            rows_of(tgrad.shape),
            rows_of(wsum.shape),
            rows_of(vgrad.shape),
            pl.BlockSpec(vectors.shape, lambda h, k: (0, 0)),
        ],
        out_specs=(
            pl.BlockSpec((1, query, cols), lambda h, k: (h, 0, k)),
            rows_of(output.shape),
            rows_of(tgrad.shape),
            rows_of((width, hidden)),
            rows_of((width, hidden)),
            rows_of((width, wdepth)),
            rows_of(vgrad.shape),
        )
        + tuple(pl.BlockSpec(one.shape, lambda h, k: (0,)) for one in flat),
        compiler_params=pltpu.CompilerParams(vmem_limit_bytes=VMEM_BYTES),
        cost_estimate=pl.CostEstimate(
            flops=2 * 10**9, bytes_accessed=20 * 10**6, transcendentals=0
        ),
    )(terms, scaled, value, shift, lens, output, tgrad, wsum, vgrad, vectors)


def on_device_fast(
    dims,
    tokens,
    seq_lengths,
    norm1_gain,
    norm1_bias,
    value_weight,
    value_bias,
    synth_logits,
    out_weight,
    out_bias,
    norm2_gain,
    norm2_bias,
    up_weight,
    up_bias,
    down_weight,
    down_bias,
    cotangent,
):
    nwa, nta = dims
    width = tokens.shape[0]
    per_feature = (
        norm1_gain,
        norm1_bias,
        value_bias,
        out_bias,
        norm2_gain,
        norm2_bias,
        down_bias,
    )
    prow = jnp.pad(jnp.stack(per_feature), ((0, 1), (0, 2 * CHUNK - width)))
    prow = jnp.concatenate([prow, jnp.broadcast_to(up_bias, (8, up_bias.shape[0]))], axis=1)
    ln = jnp.broadcast_to(seq_lengths.astype(F32)[:, None], (8, CHUNK))
    logits = synth_logits.transpose(1, 0, 2)
    (
        xown,
        weights,
        _,
        layer,
        value,
        terms,
        mixed,
        zinv,
        lens,
        pfull,
        outown,
        dattended,
        dresid,
        wgrad,
        vcol,
        vrow,
    ) = run_forward(
        dims,
        tokens,
        cotangent,
        out_weight,
        value_weight,
        up_weight,
        down_weight.T,
        prow,
        ln,
        logits,
    )
    scaled, shift, output, tgrad, vgrad, vectors, wsum = run_backward(
        dims,
        dattended,
        outown,
        dresid,
        xown,
        terms,
        mixed,
        zinv,
        lens,
        ln,
        pfull,
        layer,
        weights,
        wgrad,
        vcol,
        vrow,
    )
    logits_grad, output, tgrad, up_grad, down_grad, out_grad, vgrad, *flat = run_logits(
        terms, scaled, value, shift, lens, output, tgrad, wsum, vgrad, vectors, up_bias.shape[0]
    )
    return (
        output,
        tgrad,
        flat[0],
        flat[1],
        vgrad,
        flat[2],
        logits_grad.transpose(1, 0, 2),
        out_grad,
        flat[3],
        flat[4],
        flat[5],
        up_grad,
        flat[7],
        down_grad.T,
        flat[6],
    )


def fits(mesh):
    return mesh.shape["wa"] == 4 and mesh.shape["ta"] == 8


def solution(mesh):
    placed = (
        P("wa", "ta"),
        P("ta"),
        P("wa"),
        P("wa"),
        P("ta", "wa"),
        P("wa"),
        P("ta", "wa", None),
        P("wa", "ta"),
        P("wa"),
        P("wa"),
        P("wa"),
        P("wa", "ta"),
        P("wa"),
        P("ta", "wa"),
        P("wa"),
        P("wa", "ta"),
    )
    sizes = (mesh.shape["wa"], mesh.shape["ta"])
    body = functools.partial(on_device_fast, sizes) if fits(mesh) else on_device
    return jax.shard_map(
        body,
        mesh=mesh,
        in_specs=placed,
        out_specs=(
            P("wa", "ta"),
            P("wa", "ta"),
            P("wa"),
            P("wa"),
            P("ta", "wa"),
            P("wa"),
            P("ta", "wa", None),
            P("wa", "ta"),
            P("wa"),
            P("wa"),
            P("wa"),
            P("wa", "ta"),
            P("wa"),
            P("ta", "wa"),
            P("wa"),
        ),
        check_vma=False,
    )
```

```python
import functools

import jax
import jax.numpy as jnp
from jax import lax
from jax.experimental import pallas as pl
from jax.experimental.pallas import tpu as pltpu
from jax.sharding import PartitionSpec as P

D = 768


EPSILON = 1e-05
ALONG_FEATURES = (((1,), (1,)), ((), ()))
ALONG_ROWS = (((0,), (0,)), ((), ()))


def row_statistics(first_term, second_term):
    return lax.psum((jnp.sum(first_term, axis=1), jnp.sum(second_term, axis=1)), "wa")


def all_features(features_part):
    return lax.all_gather(features_part, "wa", axis=1, tiled=True)


def feature_share(partial_sum):
    return lax.psum_scatter(partial_sum, "wa", scatter_dimension=1, tiled=True)


def norm_forward(inputs, norm_gain, norm_bias):
    row_total, row_squares = row_statistics(inputs, inputs * inputs)
    row_mean = row_total / D
    variance = row_squares / D - row_mean * row_mean
    inverse = lax.rsqrt(variance + EPSILON)
    normed = (inputs - row_mean[:, None]) * inverse[:, None]
    return (normed * norm_gain + norm_bias, normed, inverse)


def norm_backward(incoming, normed, inverse, norm_gain):
    scaled = incoming * norm_gain
    row_total, row_along = row_statistics(scaled, scaled * normed)
    return inverse[:, None] * (scaled - row_total[:, None] / D - normed * row_along[:, None] / D)


def weights_of(logit_rows, length_all):
    seq_len = logit_rows.shape[2]
    key_valid = (jnp.arange(seq_len)[None, :] < length_all[:, None]).astype(jnp.bfloat16)
    terms = jnp.exp(logit_rows.astype(jnp.float32)).astype(jnp.bfloat16)
    sums = jnp.einsum("phk,sk->sph", terms, key_valid, preferred_element_type=jnp.float32)
    return (terms, sums, key_valid)


def attend(terms, sums, value_all, query_rows):
    mixed = jnp.einsum("phk,skhd->sphd", terms, value_all, preferred_element_type=jnp.float32)
    mixed = mixed / sums[..., None]
    return (mixed, (mixed * query_rows[:, :, None, None]).astype(jnp.bfloat16))


def attend_back(terms, sums, key_valid, value_all, mixed, grad_rows):
    along = jnp.sum(grad_rows.astype(jnp.float32) * mixed, axis=-1) / sums
    scaled = (grad_rows.astype(jnp.float32) / sums[..., None]).astype(jnp.bfloat16)
    dvalue_part = jnp.einsum("phk,sphd->skhd", terms, scaled, preferred_element_type=jnp.float32)
    dlogits = jnp.einsum("sphd,skhd->phk", scaled, value_all, preferred_element_type=jnp.float32)
    high = along.astype(jnp.bfloat16)
    rest = (along - high.astype(jnp.float32)).astype(jnp.bfloat16)
    shift = sum(
        jnp.einsum("sph,sk->phk", part, key_valid, preferred_element_type=jnp.float32)
        for part in (high, rest)
    )
    return (dvalue_part, terms.astype(jnp.float32) * (dlogits - shift))


def on_device(
    tokens,
    seq_lengths,
    norm1_gain,
    norm1_bias,
    value_weight,
    value_bias,
    synth_logits,
    out_weight,
    out_bias,
    norm2_gain,
    norm2_bias,
    up_weight,
    up_bias,
    down_weight,
    down_bias,
    cotangent,
):
    rows_dev = tokens.shape[1]
    local_width = tokens.shape[0]
    seq_count = seq_lengths.shape[0]
    seq_len = synth_logits.shape[2]
    head_count = synth_logits.shape[1]
    head_dim = local_width // head_count
    value_cols, out_rows, up_rows, down_cols = (
        lax.all_gather(value_weight, "ta", axis=0, tiled=True),
        lax.all_gather(out_weight, "ta", axis=1, tiled=True),
        lax.all_gather(up_weight, "ta", axis=1, tiled=True),
        lax.all_gather(down_weight, "ta", axis=0, tiled=True),
    )
    up_block, down_block = (
        lax.all_to_all(up_rows.T, "wa", split_axis=0, concat_axis=1, tiled=True),
        lax.all_to_all(down_cols, "wa", split_axis=0, concat_axis=1, tiled=True),
    )
    inputs = tokens.T.astype(jnp.float32)
    pre_one, normed_one, inverse_one = norm_forward(inputs, norm1_gain, norm1_bias)
    layer_one = all_features(pre_one.astype(jnp.bfloat16))
    values = (
        jnp.dot(layer_one, value_cols, preferred_element_type=jnp.float32) + value_bias
    ).astype(jnp.bfloat16)
    value_heads = values.reshape(seq_count, seq_len, head_count, head_dim)
    positions = jnp.arange(seq_len)
    key_valid = positions[None, :] < seq_lengths[:, None]
    query_valid = key_valid.astype(jnp.float32)
    length_all = lax.all_gather(seq_lengths, "ta", axis=0, tiled=True)
    block_rows = synth_logits.shape[0]
    value_all = lax.all_gather(
        value_heads * key_valid[:, :, None, None].astype(jnp.bfloat16), "ta", axis=0, tiled=True
    )
    terms, sums, key_valid_all = weights_of(synth_logits, length_all)
    block_positions = lax.axis_index("ta") * block_rows + jnp.arange(block_rows)
    query_rows = (block_positions[None, :] < length_all[:, None]).astype(jnp.float32)
    mixed_rows, mixed_low = attend(terms, sums, value_all, query_rows)
    attended = lax.all_to_all(mixed_low, "ta", split_axis=0, concat_axis=1, tiled=True)
    attended = attended.reshape(rows_dev, local_width)
    branch = (
        feature_share(jnp.dot(attended, out_rows, preferred_element_type=jnp.float32)) + out_bias
    )
    resid = inputs + branch
    pre_two, normed_two, inverse_two = norm_forward(resid, norm2_gain, norm2_bias)
    layer_two = all_features(pre_two.astype(jnp.bfloat16))
    upper = (
        lax.dot_general(layer_two, up_block, ALONG_FEATURES, preferred_element_type=jnp.float32)
        + up_bias
    )
    hidden, gelu_back = jax.vjp(jax.nn.gelu, upper)
    hidden_low = hidden.astype(jnp.bfloat16)
    feed = (
        feature_share(jnp.dot(hidden_low, down_block, preferred_element_type=jnp.float32))
        + down_bias
    )
    output = (resid + feed).astype(jnp.bfloat16)
    cotangent_rows = cotangent.T
    grad_in = cotangent_rows.astype(jnp.float32)
    grad_full = all_features(cotangent_rows)
    dhidden = lax.dot_general(
        grad_full, down_block, ALONG_FEATURES, preferred_element_type=jnp.float32
    )
    dupper = gelu_back(dhidden)[0].astype(jnp.bfloat16)
    down_part = lax.dot_general(
        hidden_low, grad_full, ALONG_ROWS, preferred_element_type=jnp.float32
    )
    up_part = lax.dot_general(dupper, layer_two, ALONG_ROWS, preferred_element_type=jnp.float32)
    up_bias_part = jnp.sum(dupper.astype(jnp.float32), axis=0)
    down_bias_part = jnp.sum(grad_in, axis=0)
    dlayer_two = feature_share(jnp.dot(dupper, up_block, preferred_element_type=jnp.float32))
    gain_two_part = jnp.sum(dlayer_two * normed_two, axis=0)
    bias_two_part = jnp.sum(dlayer_two, axis=0)
    dresid = grad_in + norm_backward(dlayer_two, normed_two, inverse_two, norm2_gain)
    dbranch = dresid.astype(jnp.bfloat16)
    dbranch_full = all_features(dbranch)
    dattended = lax.dot_general(
        dbranch_full, out_rows, ALONG_FEATURES, preferred_element_type=jnp.float32
    ).astype(jnp.bfloat16)
    out_part = lax.dot_general(
        attended, dbranch_full, ALONG_ROWS, preferred_element_type=jnp.float32
    )
    out_bias_part = jnp.sum(dbranch.astype(jnp.float32), axis=0)
    grad_heads = dattended.reshape(seq_count, seq_len, head_count, head_dim)
    grad_heads = grad_heads * query_valid[:, :, None, None].astype(jnp.bfloat16)
    grad_block = lax.all_to_all(grad_heads, "ta", split_axis=1, concat_axis=0, tiled=True)
    dvalue_part, logits_grad = attend_back(
        terms, sums, key_valid_all, value_all, mixed_rows, grad_block
    )
    dvalue_rows = dvalue_part.astype(jnp.bfloat16).reshape(-1, local_width)
    dvalue_rows = lax.psum_scatter(dvalue_rows, "ta", scatter_dimension=0, tiled=True)
    dvalues = dvalue_rows * query_valid.reshape(rows_dev, 1).astype(jnp.bfloat16)
    value_part = lax.dot_general(layer_one, dvalues, ALONG_ROWS, preferred_element_type=jnp.float32)
    value_bias_part = jnp.sum(dvalues.astype(jnp.float32), axis=0)
    dlayer_one = feature_share(
        lax.dot_general(dvalues, value_cols, ALONG_FEATURES, preferred_element_type=jnp.float32)
    )
    gain_one_part = jnp.sum(dlayer_one * normed_one, axis=0)
    bias_one_part = jnp.sum(dlayer_one, axis=0)
    tokens_grad = dresid + norm_backward(dlayer_one, normed_one, inverse_one, norm1_gain)
    up_back, down_back = (
        lax.all_to_all(up_part, "wa", split_axis=1, concat_axis=0, tiled=True),
        lax.all_to_all(down_part, "wa", split_axis=1, concat_axis=0, tiled=True),
    )
    value_grad, out_grad, up_grad, down_grad = (
        lax.psum_scatter(value_part, "ta", scatter_dimension=0, tiled=True),
        lax.psum_scatter(out_part, "ta", scatter_dimension=1, tiled=True),
        lax.psum_scatter(up_back, "ta", scatter_dimension=0, tiled=True),
        lax.psum_scatter(down_back, "ta", scatter_dimension=0, tiled=True),
    )
    vector_grads = lax.psum(
        (
            gain_one_part,
            bias_one_part,
            value_bias_part,
            out_bias_part,
            gain_two_part,
            bias_two_part,
            up_bias_part,
            down_bias_part,
        ),
        "ta",
    )
    return (
        output.T,
        tokens_grad.T,
        vector_grads[0],
        vector_grads[1],
        value_grad,
        vector_grads[2],
        logits_grad,
        out_grad,
        vector_grads[3],
        vector_grads[4],
        vector_grads[5],
        up_grad.T,
        vector_grads[6],
        down_grad,
        vector_grads[7],
    )


MESH = pl.DeviceIdType.MESH
ROWS_NT = (((1,), (1,)), ((), ()))
ROWS_TN = (((0,), (0,)), ((), ()))
F32 = jnp.float32
BF16 = jnp.bfloat16
VMEM_BYTES = 60 * 2**20
CHUNK = 128
PAD = 128
AHEAD = 2


def whole(count):
    return [pl.BlockSpec(memory_space=pltpu.VMEM)] * count


def anywhere(count):
    return [pl.BlockSpec(memory_space=pl.ANY)] * count


def shape_of(shape, dtype):
    return jax.ShapeDtypeStruct(shape, dtype)


def lanes(start, size=CHUNK):
    return pl.ds(pl.multiple_of(start, CHUNK), size)


def rows_at(start, size, unit):
    return pl.ds(pl.multiple_of(start, unit), size)


class Place:
    def __init__(self, nwa, nta):
        self.nwa, self.nta, self.nz = nwa, nta, nta // 2
        self.wa = lax.axis_index("wa")
        self.ta = lax.axis_index("ta")
        self.z = self.ta // 2
        self.c = self.ta % 2
        self.peer = self.ta + 1 - 2 * self.c
        self.wx = self.wa + 1 - 2 * (self.wa % 2)
        self.wy = (self.wa + 2) % 4
        self.wd = 3 - self.wa

    def enter(self):
        barrier = pltpu.get_barrier_semaphore()
        total = self.nwa * self.nta

        def greet(step, carry):
            w = (self.wa + step // self.nta) % self.nwa
            t = (self.ta + step % self.nta) % self.nta
            pl.semaphore_signal(barrier, inc=1, device_id=(w, t), device_id_type=MESH)
            return carry

        lax.fori_loop(1, total, greet, 0)
        pl.semaphore_wait(barrier, total - 1)


def send(src, dst, ssem, rsem, device):
    return pltpu.make_async_remote_copy(
        src_ref=src,
        dst_ref=dst,
        send_sem=ssem,
        recv_sem=rsem,
        device_id=device,
        device_id_type=MESH,
    )


def when(condition):
    return pl.when(condition)


def norm_stats(block):
    width = block.shape[0]
    mean = jnp.sum(block, axis=0, keepdims=True) / width
    centred = block - mean
    variance = jnp.sum(centred * centred, axis=0, keepdims=True) / width
    inverse = lax.rsqrt(variance + EPSILON)
    return (centred * inverse, inverse)


def forward_kernel(
    dims,
    tok,
    cot,
    wout,
    wval,
    wup,
    wdown,
    prow,
    ln,
    logits,
    xown,
    small,
    large,
    layer_out,
    value_out,
    term_out,
    mixed,
    zinv,
    lens,
    pfull,
    out,
    dattended,
    dresid,
    wgrad,
    vcol,
    vrow,
    cown,
    attended,
    rfull,
    wo,
    wblock,
    resid,
    normed,
    inverse,
    layer_two,
    layer_t,
    grad_t,
    feed,
    dlayer,
    wide,
    gblock,
    gwo,
    x,
    wvc,
    layer_pad,
    layer,
    value,
    terms,
    attsend,
    rows,
    turned,
    wsmall,
    sem_tok,
    sem_par,
    sem_ta,
    sem_val,
    sem_small,
    sem_large,
    sem_cot,
    sem_att,
    sem_local,
    sem_out,
    sem_wv,
    sem_g,
):
    nwa, nta = dims
    me = Place(nwa, nta)
    wa, ta, z, c = me.wa, me.ta, me.z, me.c
    nz = me.nz
    width = tok.shape[0]
    half = width // 2
    seq = tok.shape[1]
    part = seq // nz
    query = seq // nta
    slot = wvc.shape[1] // nta
    wdepth = wvc.shape[0] * nwa // nta
    heads = terms.shape[0]
    hdim = width // heads
    split = PAD
    get_logits = pltpu.make_async_copy(logits, terms, sem_local.at[5])
    get_logits.start()
    stores = ((small, sem_small), (large, sem_large))
    one = wup.shape[1]
    own_w = (
        pltpu.make_async_copy(wsmall, small.at[wa, ta], sem_local.at[2]),
        pltpu.make_async_copy(wup, large.at[wa, ta, :, pl.ds(0, one)], sem_local.at[6]),
        pltpu.make_async_copy(wdown, large.at[wa, ta, :, pl.ds(one, one)], sem_local.at[7]),
    )
    own_w[1].start()
    own_w[2].start()
    turned[...] = jnp.zeros_like(turned)
    turned[:wdepth, :width] = wval[...]
    wsmall[...] = jnp.zeros_like(wsmall)
    wsmall[:, :wdepth] = wout[...]
    wsmall[:, split:] = turned[...].T[:width]
    own_w[0].start()
    me.enter()


    def block_rows(w, off=0, size=width):
        return rows_at(w * width + off, size, 32)

    def tok_copy(k, q):
        device = (me.wx if k == 0 else me.wy, ta)
        return send(
            tok.at[:, pl.ds(q * part, part)],
            x.at[block_rows(wa), pl.ds(q * part, part)],
            sem_tok.at[0, k, q],
            sem_tok.at[1, k, q],
            device,
        )

    def tok_fwd(k, q):
        source = me.wx if k == 0 else me.wy
        device = (me.wy if k == 0 else me.wx, ta)
        where = x.at[block_rows(source, k * half, half), pl.ds(q * part, part)]
        return send(where, where, sem_tok.at[0, 2 + k, q], sem_tok.at[1, 2 + k, q], device)

    own_x = pltpu.make_async_copy(tok, x.at[block_rows(wa)], sem_local.at[0])
    own_x.start()

    def tok_start(q):
        for k in range(2):
            tok_copy(k, q).start()

    def tok_turn(q):
        for k in range(2):
            tok_copy(k, q).wait_recv()
            tok_fwd(k, q).start()
        if q + AHEAD < nz:
            tok_start(q + AHEAD)

    for q in range(AHEAD):
        tok_start(q)

    def par_copy(step):
        w = (wa + step) % nwa
        return send(prow, rows.at[wa], sem_par.at[0, step], sem_par.at[1, step], (w, ta))

    def ta_copy(step):
        t = (ta + step) % nta
        return send(
            ln, lens.at[rows_at(ta * 8, 8, 8)], sem_ta.at[0, step], sem_ta.at[1, step], (wa, t)
        )

    def wv_column(b, core):
        return wvc.at[:, lanes((2 * b + core) * slot)]

    def wv_z(step):
        b = (z + step) % nz
        src = wsmall.at[:, pl.ds(split, PAD)]
        return send(
            src, wv_column(z, c), sem_wv.at[0, 0, step], sem_wv.at[1, 0, step], (wa, 2 * b + c)
        )

    def wv_core(step, core):
        where = wv_column((z - step + nz) % nz, core)
        return send(where, where, sem_wv.at[0, 1, step], sem_wv.at[1, 1, step], (wa, me.peer))

    own_wv = pltpu.make_async_copy(wsmall.at[:, pl.ds(split, PAD)], wv_column(z, c), sem_local.at[1])
    own_wv.start()
    for step in range(nz - 1, 0, -1):
        wv_z(step).start()
    for step in range(1, nwa):
        par_copy(step).start()
    for step in range(1, nta):
        ta_copy(step).start()
    rows[wa] = prow[...]
    lens[rows_at(ta * 8, 8, 8), :] = ln[...]
    own_wv.wait()
    wv_core(0, c).start()

    def w_line(p, up, b):
        where, sem = stores[p][0].at[wa, 2 * b + c], stores[p][1]
        k = 0 if up else 1
        return send(
            where, where, sem.at[0, k, b], sem.at[1, k, b], (wa, ta + 2 if up else ta - 2)
        )

    for step in range(1, nz):
        wv_z(step).wait_recv()
        wv_core(step, c).start()
    for copy in own_w:
        copy.wait()

    @pl.when(z < nz - 1)
    def _():
        for p in range(2):
            w_line(p, True, z).start()

    @pl.when(z > 0)
    def _():
        for p in range(2):
            w_line(p, False, z).start()

    layer_pad[...] = jnp.zeros_like(layer_pad)
    get_logits.wait()
    for h in range(heads):
        terms[h] = jnp.exp(terms[h].astype(F32)).astype(BF16)
    out_terms = pltpu.make_async_copy(terms, term_out, sem_local.at[3])
    out_terms.start()

    tok_turn(0)
    for step in range(1, nwa):
        par_copy(step).wait_recv()
    gap = 2 * CHUNK
    for w in range(nwa):
        piece = jnp.concatenate([rows[w, :, :gap], jnp.zeros((PAD - 8, gap), F32)], axis=0)
        pfull[w * width : (w + 1) * width, :] = piece.T[:width]
        span = rows.shape[2] - gap
        rfull[:, w * span : (w + 1) * span] = rows[w, :, gap:]
    for step in range(1, nta):
        ta_copy(step).wait_recv()
    for step in range(nz):
        wv_core(step, 1 - c).wait_recv()
    own_x.wait()

    positions = lax.broadcasted_iota(jnp.int32, (nta * 8, seq), 1).astype(F32)
    key_valid = jnp.where(positions < lens[:, 0:1], 1.0, 0.0).astype(BF16)
    for h in range(heads):
        sums = lax.dot_general(key_valid, terms[h], ROWS_NT, preferred_element_type=F32)
        zinv[h] = 1.0 / sums

    def value_copy(kind, b, q, core):
        where = value.at[2 * b + core, :, pl.ds(q * part, part)]
        t = (ta + 2, ta - 2, me.peer)[kind]
        return send(where, where, sem_val.at[0, kind, b, q], sem_val.at[1, kind, b, q], (wa, t))

    def w_plane(p, k, b):
        device = (me.wx if k == 0 else me.wy, ta)
        where, sem = stores[p][0].at[wa, 2 * b + c], stores[p][1]
        return send(where, where, sem.at[0, 2 + k, b], sem.at[1, 2 + k, b], device)

    def w_diag(p, k, b, source):
        device = (me.wy if k == 0 else me.wx, ta)
        where, sem = stores[p][0].at[source, 2 * b + c, pl.ds(k * half, half)], stores[p][1]
        return send(where, where, sem.at[0, 4 + k, b], sem.at[1, 4 + k, b], device)

    def w_core(p, r, b, core):
        source = (wa, me.wx, me.wy, me.wd)[r]
        where, sem = stores[p][0].at[source, 2 * b + core], stores[p][1]
        return send(where, where, sem.at[0, 6 + r, b], sem.at[1, 6 + r, b], (wa, me.peer))

    def w_start(p, b):
        w_plane(p, 0, b).start()
        w_plane(p, 1, b).start()
        w_core(p, 0, b, c).start()

    def w_forward(p, b):
        w_plane(p, 0, b).wait_recv()
        w_diag(p, 0, b, me.wx).start()
        w_core(p, 1, b, c).start()
        w_plane(p, 1, b).wait_recv()
        w_diag(p, 1, b, me.wy).start()
        w_core(p, 2, b, c).start()

    def w_finish(p, b):
        for k in range(2):
            w_diag(p, k, b, me.wd).wait_recv()
        w_core(p, 3, b, c).start()

    def w_landed(p, h):
        @pl.when(z - 1 - h >= 0)
        def _():
            w_line(p, True, z - 1 - h).wait_recv()

        @pl.when(z + 1 + h < nz)
        def _():
            w_line(p, False, z + 1 + h).wait_recv()

    def w_onward(p, h):
        @pl.when(jnp.logical_and(z - 1 - h >= 0, z < nz - 1))
        def _():
            w_line(p, True, z - 1 - h).start()

        @pl.when(jnp.logical_and(z + 1 + h < nz, z > 0))
        def _():
            w_line(p, False, z + 1 + h).start()

    def at_hop(h, act, *args):
        @pl.when(z - 1 - h >= 0)
        def _():
            act(*args, z - 1 - h)

        @pl.when(z + 1 + h < nz)
        def _():
            act(*args, z + 1 + h)

    for q in range(nz):
        cols = pl.ds(q * part, part)
        if q + 1 < nz:
            tok_turn(q + 1)
        for k in range(2):
            where = x.at[block_rows(me.wd, k * half, half), cols]
            send(
                where,
                where,
                sem_tok.at[0, 2 + k, q],
                sem_tok.at[1, 2 + k, q],
                (me.wy if k == 0 else me.wx, ta),
            ).wait_recv()
        centred, _ = norm_stats(x[:, cols].astype(F32))
        low = (centred * pfull[:, 0:1] + pfull[:, 1:2]).astype(BF16)
        layer[:, cols] = low
        for t in range(nta):
            layer_pad[t * slot : t * slot + wdepth, :] = low[t * wdepth : (t + 1) * wdepth]
        made = jnp.dot(wvc[...], layer_pad[...], preferred_element_type=F32)
        made = made + pfull[block_rows(wa), :][:, 2:3]
        place = lax.broadcasted_iota(jnp.int32, (width, part), 1) + q * part
        made = jnp.where(place.astype(F32) < ln[0:1, 0:1], made, 0.0)
        value[ta, :, cols] = made.astype(BF16)
        xown[:, pl.ds(q * CHUNK, CHUNK)] = x[:, lanes(q * part + wa * CHUNK)]

        @pl.when(z < nz - 1)
        def _():
            value_copy(0, z, q, c).start()

        @pl.when(z > 0)
        def _():
            value_copy(1, z, q, c).start()

        value_copy(2, z, q, c).start()
        if q < nz - 1:
            w_landed(0, q)
            w_onward(0, q)
    out_layer = pltpu.make_async_copy(layer, layer_out, sem_local.at[4])
    out_layer.start()

    def cot_copy(step, q):
        w = (wa + step) % nwa
        return send(
            cot.at[:, lanes(q * part + w * CHUNK)],
            cown.at[block_rows(wa), pl.ds(q * CHUNK, CHUNK)],
            sem_cot.at[0, step, q],
            sem_cot.at[1, step, q],
            (w, ta),
        )

    def cot_own(q):
        return pltpu.make_async_copy(
            cot.at[:, lanes(q * part + wa * CHUNK)],
            cown.at[block_rows(wa), pl.ds(q * CHUNK, CHUNK)],
            sem_cot.at[0, 0, q],
        )

    w_start(0, z)
    for h in range(nz - 1):
        at_hop(h, w_start, 0)
    w_start(1, z)
    w_landed(1, 0)
    at_hop(0, w_start, 1)
    for q in range(nz):
        cot_own(q).start()
        for step in range(1, nwa):
            cot_copy(step, q).start()

    def att_copy(s, j):
        return send(
            attsend.at[s, :, pl.ds(j * CHUNK, CHUNK)],
            attended.at[block_rows(wa), lanes(z * CHUNK)],
            sem_att.at[0, s, j],
            sem_att.at[1, wa, z],
            (2 * c + j, s),
        )

    def att_local(s, j):
        return pltpu.make_async_copy(
            attsend.at[s, :, pl.ds(j * CHUNK, CHUNK)],
            attended.at[block_rows(wa), lanes(z * CHUNK)],
            sem_att.at[0, s, j],
        )

    def is_self(s, j):
        return jnp.logical_and(s == ta, 2 * c + j == wa)

    def mix(b):
        for core in range(2):
            s = 2 * b + core
            pltpu.make_async_copy(value.at[s], value_out.at[s], sem_out.at[s]).start()
        length = [lens[rows_at((2 * b + core) * 8, 8, 8), :][0:1, 0:1] for core in range(2)]
        place = lax.broadcasted_iota(jnp.int32, (hdim, query), 1) + ta * query
        place = place.astype(F32)
        for h in range(heads):
            group = slice(h * hdim, (h + 1) * hdim)
            pair = jnp.concatenate([value[2 * b, group, :], value[2 * b + 1, group, :]], axis=0)
            both = lax.dot_general(pair, terms[h], ROWS_NT, preferred_element_type=F32)
            for core in range(2):
                s = 2 * b + core
                inverse = zinv[h, rows_at(s * 8, 8, 8), :][0:1]
                one = both[core * hdim : (core + 1) * hdim] * inverse
                mixed[s, group, :] = one
                one = jnp.where(place < length[core], one, 0.0)
                attsend[s, group, :] = one.astype(BF16)
        for core in range(2):
            s = 2 * b + core
            for j in range(2):

                @pl.when(is_self(s, j))
                def _():
                    att_local(s, j).start()

                @pl.when(jnp.logical_not(is_self(s, j)))
                def _():
                    att_copy(s, j).start()

    def core_ready(b):
        for q in range(nz):
            value_copy(2, b, q, 1 - c).wait_recv()

    def mix_ready(b):
        core_ready(b)
        mix(b)

    def mix_side(h, up):
        b = z - 1 - h if up else z + 1 + h

        @pl.when(b >= 0 if up else b < nz)
        def _():
            mix_ready(b)

    for h in range(nz - 1):
        below, above = z - 1 - h, z + 1 + h
        for q in range(nz):

            @pl.when(below >= 0)
            def _():
                value_copy(0, below, q, c).wait_recv()

                @pl.when(z < nz - 1)
                def _():
                    value_copy(0, below, q, c).start()

                value_copy(2, below, q, c).start()

            @pl.when(above < nz)
            def _():
                value_copy(1, above, q, c).wait_recv()

                @pl.when(z > 0)
                def _():
                    value_copy(1, above, q, c).start()

                value_copy(2, above, q, c).start()

            if h == 0 and q == 1:
                mix_ready(z)
            if h > 0 and q < 2:
                mix_side(h - 1, q == 0)

        if h == 0:
            w_forward(0, z)
            for other in range(nz - 1):
                at_hop(other, w_forward, 0)
        if h == 1:
            w_onward(1, 0)
            w_forward(1, z)
            w_finish(0, z)
            for other in range(nz - 1):
                at_hop(other, w_finish, 0)
    mix_side(nz - 2, True)
    mix_side(nz - 2, False)
    at_hop(0, w_forward, 1)
    w_finish(1, z)
    at_hop(0, w_finish, 1)

    def w_cores(p, b):
        for r in range(4):
            w_core(p, r, b, 1 - c).wait_recv()

    depth, own = xown.shape
    both = 2 * one

    def turn(i):
        pair = z + 1 - 2 * (z % 2)
        late = jnp.where(i == 2, nz // 2 - z // 2, (nz - 1) * (1 - z // 2))
        return jnp.where(i == 0, z, jnp.where(i == 1, pair, late))

    def load(i, slot):
        b = turn(i)
        return pltpu.make_async_copy(
            large.at[:, pl.ds(2 * b, 2)], wblock.at[slot], sem_g.at[slot]
        )

    w_cores(1, turn(0))
    load(0, 0).start()
    for b in range(nz):
        w_cores(0, b)
    get_wo = pltpu.make_async_copy(small.at[:, :, :, pl.ds(0, PAD)], wo, sem_g.at[2])
    get_wo.start()
    for q in range(nz):
        cot_own(q).wait()
        for step in range(1, nwa):
            cot_copy(step, q).wait_recv()
    grad_t[...] = cown[...].T
    w_cores(1, turn(1))
    load(1, 1).start()

    def att_sends(s, carry):
        pltpu.make_async_copy(value.at[s], value_out.at[s], sem_out.at[s]).wait()
        for j in range(2):

            @pl.when(is_self(s, j))
            def _():
                att_local(s, j).wait()

            @pl.when(jnp.logical_not(is_self(s, j)))
            def _():
                att_copy(s, j).wait_send()

        return carry

    lax.fori_loop(0, nta, att_sends, 0)
    mine = wa // 2

    def att_arrivals(k, carry):
        w, b = k // nz, k % nz

        @pl.when(jnp.logical_not(jnp.logical_and(w == wa, 2 * b + mine == ta)))
        def _():
            where = attended.at[block_rows(w), lanes(b * CHUNK)]
            send(where, where, sem_att.at[0, 0, 0], sem_att.at[1, w, b], (w, 2 * b + mine)).wait_recv()

        return carry

    w_landed(1, 1)
    w_onward(1, 1)
    at_hop(1, w_start, 1)
    lax.fori_loop(0, nwa * nz, att_arrivals, 0)
    get_wo.wait()

    def wide_wo():
        joined = [
            jnp.concatenate([wo[w, t] for t in range(nta)], axis=1) for w in range(nwa)
        ]
        return jnp.concatenate(joined, axis=0)

    branch = lax.dot_general(wide_wo(), attended[...], ROWS_TN, preferred_element_type=F32)
    branch = jnp.concatenate([branch[t * PAD : t * PAD + wdepth] for t in range(nta)], axis=0)
    res = xown[...].astype(F32) + branch + pfull[:, 3:4]
    resid[...] = res
    norm, inv = norm_stats(res)
    normed[...] = norm
    inverse[...] = jnp.broadcast_to(inv, inverse.shape)
    low = (norm * pfull[:, 4:5] + pfull[:, 5:6]).astype(BF16)
    layer_two[...] = low
    layer_t[...] = low.T
    feed[...] = jnp.zeros_like(feed)
    dlayer[...] = jnp.zeros_like(dlayer)

    def put(i):
        return pltpu.make_async_copy(
            gblock, wgrad.at[:, turn(i), :, :, pl.ds(0, both)], sem_g.at[3]
        )

    def middle(i, carry):
        slot = i % 2

        @pl.when(i == 2)
        def _():
            at_hop(1, w_finish, 1)
            w_landed(1, 2)
            at_hop(2, w_start, 1)
            w_cores(1, turn(2))
            load(2, 0).start()

        @pl.when(i == 3)
        def _():
            at_hop(2, w_forward, 1)
            at_hop(2, w_finish, 1)
            w_cores(1, turn(3))
            load(3, 1).start()

        load(i, slot).wait()
        held = wblock.at[slot]

        def joined(start):
            parts = [held[:, g, :, start : start + one].reshape(depth, one) for g in range(2)]
            return jnp.concatenate(parts, axis=1)

        up, down_t = joined(0), joined(one)
        at = lanes(turn(i) * both, both)
        upper = jnp.dot(layer_t[...], up, preferred_element_type=F32) + rfull[0:1, at]
        hidden, slope = gelu_pair(upper)
        hidden = hidden.astype(BF16)
        dhidden = jnp.dot(grad_t[...], down_t, preferred_element_type=F32)
        dupper = (dhidden * slope).astype(BF16)
        vrow[:, at] = jnp.broadcast_to(
            jnp.sum(dupper.astype(F32), axis=0, keepdims=True), (vrow.shape[0], both)
        )
        feed[...] += lax.dot_general(down_t, hidden, ROWS_NT, preferred_element_type=F32)
        dlayer[...] += lax.dot_general(up, dupper, ROWS_NT, preferred_element_type=F32)
        gup = jnp.dot(layer_two[...], dupper, preferred_element_type=F32)
        gdown = jnp.dot(cown[...], hidden, preferred_element_type=F32)

        @pl.when(i > 0)
        def _():
            put(i - 1).wait()

        for g in range(2):
            piece = slice(g * one, (g + 1) * one)
            gblock[:, g, :, :one] = gup[:, piece].reshape(nwa, width, one).astype(BF16)
            gblock[:, g, :, one:] = gdown[:, piece].reshape(nwa, width, one).astype(BF16)
        put(i).start()

        @pl.when(i == 0)
        def _():
            at_hop(1, w_forward, 1)

        return carry

    lax.fori_loop(0, nz, middle, 0)

    grad = cown[...].astype(F32)
    out[...] = (resid[...] + feed[...] + pfull[:, 6:7]).astype(BF16)
    dl = dlayer[...]
    norm = normed[...]
    e = dl * pfull[:, 4:5]
    mean_e = jnp.sum(e, axis=0, keepdims=True) / depth
    mean_n = jnp.sum(e * norm, axis=0, keepdims=True) / depth
    dres = grad + inverse[0:1, :] * (e - mean_e - norm * mean_n)
    dresid[...] = dres
    low = dres.astype(BF16)
    vcol[...] = jnp.zeros_like(vcol)
    vcol[:, 3:4] = jnp.sum(low.astype(F32), axis=1, keepdims=True)
    vcol[:, 4:5] = jnp.sum(dl * norm, axis=1, keepdims=True)
    vcol[:, 5:6] = jnp.sum(dl, axis=1, keepdims=True)
    vcol[:, 6:7] = jnp.sum(grad, axis=1, keepdims=True)
    wide[...] = jnp.zeros_like(wide)
    for t in range(nta):
        wide[t * PAD : t * PAD + wdepth, :] = low[t * wdepth : (t + 1) * wdepth]
    da = jnp.dot(wide_wo(), wide[...], preferred_element_type=F32)
    lane = lax.broadcasted_iota(jnp.int32, (depth, own), 1)
    place = (lane // CHUNK) * (CHUNK * nwa) + lane % CHUNK + wa * CHUNK
    da = jnp.where(place.astype(F32) < ln[0:1, 0:1], da, 0.0)
    dattended[...] = da.astype(BF16)
    made = lax.dot_general(attended[...], wide[...], ROWS_NT, preferred_element_type=F32)
    for t in range(nta):
        piece = made[:, t * PAD : (t + 1) * PAD].reshape(nwa, width, PAD)
        gwo[:, t // 2, t % 2] = piece.astype(BF16)
    rest = pltpu.make_async_copy(gwo, wgrad.at[:, :, :, :, pl.ds(both, PAD)], sem_g.at[4])
    rest.start()
    put(nz - 1).wait()
    rest.wait()

    for step in range(1, nta):
        ta_copy(step).wait_send()
    for step in range(nz):
        wv_core(step, c).wait_send()
        if step:
            wv_z(step).wait_send()
    for step in range(1, nwa):
        par_copy(step).wait_send()
        for q in range(nz):
            cot_copy(step, q).wait_send()
    for q in range(nz):
        for k in range(2):
            tok_copy(k, q).wait_send()
            tok_fwd(k, q).wait_send()

    def line_sends(b, carry):
        reach_up = jnp.logical_and(b <= z, z < nz - 1)
        reach_down = jnp.logical_and(b >= z, z > 0)

        @pl.when(reach_up)
        def _():
            for p in range(2):
                w_line(p, True, b).wait_send()
            for q in range(nz):
                value_copy(0, b, q, c).wait_send()

        @pl.when(reach_down)
        def _():
            for p in range(2):
                w_line(p, False, b).wait_send()
            for q in range(nz):
                value_copy(1, b, q, c).wait_send()

        for q in range(nz):
            value_copy(2, b, q, c).wait_send()
        for p in range(2):
            for k in range(2):
                w_plane(p, k, b).wait_send()
            w_diag(p, 0, b, me.wx).wait_send()
            w_diag(p, 1, b, me.wy).wait_send()
            for r in range(4):
                w_core(p, r, b, c).wait_send()
        return carry

    lax.fori_loop(0, nz, line_sends, 0)

    out_terms.wait()
    out_layer.wait()


def run_forward(dims, tok, cot, wout, wval, wup, wdown, prow, ln, logits):
    nwa, nta = dims
    nz = nta // 2
    width, seq = tok.shape
    depth = width * nwa
    own = seq // nwa
    heads, query, _ = logits.shape
    slot = PAD
    both = 2 * wup.shape[1]
    hidden = both // 2 * nta
    dma = pltpu.SemaphoreType.DMA
    return pl.pallas_call(
        functools.partial(forward_kernel, dims),
        out_shape=(
            shape_of((depth, own), BF16),
            shape_of((nwa, nta, width, 2 * PAD), BF16),
            shape_of((nwa, nta, width, both), BF16),
            shape_of((depth, seq), BF16),
            shape_of((nta, width, seq), BF16),
            shape_of((heads, query, seq), BF16),
            shape_of((nta, width, query), F32),
            shape_of((heads, nta * 8, query), F32),
            shape_of((nta * 8, CHUNK), F32),
            shape_of((depth, PAD), F32),
            shape_of((depth, own), BF16),
            shape_of((depth, own), BF16),
            shape_of((depth, own), F32),
            shape_of((nwa, nz, 2, width, both + PAD), BF16),
            shape_of((depth, PAD), F32),
            shape_of((8, hidden), F32),
        ),
        in_specs=anywhere(2) + whole(2) + anywhere(2) + whole(2) + anywhere(1),
        out_specs=tuple(whole(1) + anywhere(5) + whole(7) + anywhere(1) + whole(2)),
        scratch_shapes=[
            pltpu.VMEM((depth, own), BF16),
            pltpu.VMEM((depth, own), BF16),
            pltpu.VMEM((8, hidden), F32),
            pltpu.VMEM((nwa, nta, width, PAD), BF16),
            pltpu.VMEM((2, nwa, 2, width, both), BF16),
            pltpu.VMEM((depth, own), F32),
            pltpu.VMEM((depth, own), F32),
            pltpu.VMEM((8, own), F32),
            pltpu.VMEM((depth, own), BF16),
            pltpu.VMEM((own, depth), BF16),
            pltpu.VMEM((own, depth), BF16),
            pltpu.VMEM((depth, own), F32),
            pltpu.VMEM((depth, own), F32),
            pltpu.VMEM((nta * PAD, own), BF16),
            pltpu.VMEM((nwa, 2, width, both), BF16),
            pltpu.VMEM((nwa, nz, 2, width, PAD), BF16),
            pltpu.VMEM((depth, seq), BF16),
            pltpu.VMEM((width, nta * slot), BF16),
            pltpu.VMEM((nta * slot, seq // nz), BF16),
            pltpu.VMEM((depth, seq), BF16),
            pltpu.VMEM((nta, width, seq), BF16),
            pltpu.VMEM((heads, query, seq), BF16),
            pltpu.VMEM((nta, width, query), BF16),
            pltpu.VMEM((nwa,) + prow.shape, F32),
            pltpu.VMEM((PAD, 2 * CHUNK), BF16),
            pltpu.VMEM((width, 2 * PAD), BF16),
            dma((2, 4, nz)),
            dma((2, nwa)),
            dma((2, nta)),
            dma((2, 3, nz, nz)),
            dma((2, 10, nz)),
            dma((2, 10, nz)),
            dma((2, nwa, nz)),
            dma((2, nta, max(nz, 2))),
            dma((8,)),
            dma((nta,)),
            dma((2, 2, nz)),
            dma((5,)),
        ],
        compiler_params=pltpu.CompilerParams(
            collective_id=1, has_side_effects=True, vmem_limit_bytes=VMEM_BYTES
        ),
        cost_estimate=pl.CostEstimate(
            flops=20 * 10**9, bytes_accessed=80 * 10**6, transcendentals=4 * 10**6
        ),
    )(tok, cot, wout, wval, wup, wdown, prow, ln, logits)


def gelu_pair(u):
    root = 0.7978845608028654
    square = u * u
    bent = jnp.tanh(root * u * (1.0 + 0.044715 * square))
    low_half = 0.5 * (1.0 + bent)
    slope = low_half + 0.5 * u * (1.0 - bent * bent) * root * (1.0 + 3.0 * 0.044715 * square)
    return (u * low_half, slope)


def backward_kernel(
    dims,
    dattended,
    outown,
    dresid_in,
    xown_in,
    terms_in,
    mixed_in,
    zinv,
    lens,
    ln,
    pfull,
    layer_in,
    weights,
    wgrad,
    vcol,
    vrow,
    scaled,
    shift,
    output,
    tgrad,
    vgrad,
    vectors,
    wsum,
    dresid,
    xown,
    terms,
    mixed,
    layer,
    normed,
    invs,
    wvt,
    gains,
    biases,
    da,
    partial,
    paired,
    up_in,
    down_in,
    gown,
    gpeer,
    first_x,
    first_y,
    second_x,
    second_y,
    gup_in,
    gdown_in,
    dvalue,
    dvown,
    wv,
    vsend,
    vrecv,
    tsend,
    csend,
    crecv,
    csum,
    crecv2,
    sem_da,
    sem_out,
    sem_core,
    sem_line,
    sem_dv,
    sem_tg,
    sem_v,
    sem_c,
    sem_c2,
    sem_local,
    sem_g,
    sem_gline,
):
    nwa, nta = dims
    me = Place(nwa, nta)
    wa, ta, z, c = me.wa, me.ta, me.z, me.c
    nz = me.nz
    depth, own = dresid.shape
    width = depth // nwa
    wdepth = depth // nta
    heads, query, seq = terms.shape
    hdim = width // heads
    part = seq // nz
    pairs = (
        (terms_in, terms),
        (mixed_in, mixed),
        (xown_in, xown),
        (dresid_in, dresid),
        (layer_in, layer),
    )
    fetch = [
        pltpu.make_async_copy(src, dst, sem_local.at[1 + i]) for i, (src, dst) in enumerate(pairs)
    ]
    for copy in fetch:
        copy.start()
    me.enter()

    def block_rows(w):
        return rows_at(w * width, width, 32)

    def da_copy(w, b, local):
        core = wa // 2
        src = dattended.at[block_rows(w), lanes(b * CHUNK)]
        dst = da.at[ta, :, lanes((wa % 2) * CHUNK)]
        if local:
            return pltpu.make_async_copy(src, dst, sem_da.at[0, w, b])
        return send(src, dst, sem_da.at[0, w, b], sem_da.at[1, ta, wa % 2], (w, 2 * b + core))

    def da_self(w, b):
        return jnp.logical_and(w == wa, 2 * b + wa // 2 == ta)

    def far(i):
        low_end = 1 - z // (nz // 2)
        return (nz - 1 - i) * low_end + i * (1 - low_end)

    def da_start(k, carry):
        w, b = (wa + k % nwa) % nwa, far(k // nwa)

        @pl.when(da_self(w, b))
        def _():
            da_copy(w, b, True).start()

        @pl.when(jnp.logical_not(da_self(w, b)))
        def _():
            da_copy(w, b, False).start()

        return carry

    lax.fori_loop(0, nwa * nz, da_start, 0)

    def back_copy(src, dst, sems, step, q):
        w = (wa + step) % nwa
        return send(
            src.at[block_rows(w), pl.ds(q * CHUNK, CHUNK)],
            dst.at[:, lanes(q * part + wa * CHUNK)],
            sems.at[0, step, q],
            sems.at[1, step, q],
            (w, ta),
        )

    def back_own(src, dst, sems, q):
        return pltpu.make_async_copy(
            src.at[block_rows(wa), pl.ds(q * CHUNK, CHUNK)],
            dst.at[:, lanes(q * part + wa * CHUNK)],
            sems.at[0, 0, q],
        )

    get_wv = pltpu.make_async_copy(
        weights.at[:, :, :, pl.ds(weights.shape[3] - PAD, PAD)], wv, sem_local.at[0]
    )
    get_wv.start()

    half = width // 2
    order = []
    for j in range(nz):
        for b in (nz - 1 - j, j):
            if b not in order:
                order.append(b)

    def g_core(b, core):
        return send(
            wgrad.at[:, b, core],
            gpeer.at[b],
            sem_g.at[0, 0, b],
            sem_g.at[1, 0, b],
            (wa, me.peer),
        )

    def g_load(b):
        return pltpu.make_async_copy(wgrad.at[:, b, c], gown.at[b], sem_g.at[0, 7, b])

    def g_first(k, r, b):
        near = me.wx if k == 0 else me.wy
        which = near if r == 0 else me.wd
        return send(
            gown.at[b, which, pl.ds(k * half, half)],
            (first_x if k == 0 else first_y).at[b, r],
            sem_g.at[0, 1 + 2 * k + r, b],
            sem_g.at[1, 1 + 2 * k + r, b],
            (near, ta),
        )

    def g_second(k, b):
        near = me.wy if k == 0 else me.wx
        return send(
            gown.at[b, near, pl.ds(k * half, half)],
            (second_x if k == 0 else second_y).at[b],
            sem_g.at[0, 5 + k, b],
            sem_g.at[1, 5 + k, b],
            (near, ta),
        )

    def g_add(b, which, k, extra):
        rows = pl.ds(k * half, half)
        gown[b, which, rows, :] = (
            gown[b, which, rows, :].astype(F32) + extra.astype(F32)
        ).astype(BF16)

    def g_cores(b):
        g_load(b).wait()
        g_core(b, c).wait_recv()
        for w in range(nwa):
            gown[b, w] = (gown[b, w].astype(F32) + gpeer[b, w].astype(F32)).astype(BF16)
        for k in range(2):
            for r in range(2):
                g_first(k, r, b).start()

    def g_plane(b):
        for k in range(2):
            for r in range(2):
                g_first(k, r, b).wait_recv()
            landed = first_x if k == 0 else first_y
            g_add(b, me.wy if k == 0 else me.wx, k, landed[b, 1])
            g_second(k, b).start()
            g_add(b, wa, k, landed[b, 0])

    def g_end(b):
        for k in range(2):
            g_second(k, b).wait_recv()
            g_add(b, wa, k, (second_x if k == 0 else second_y)[b])

    def g_line(up, j):
        k = 0 if up else 1
        target = nz - 1 - j if up else j
        return send(
            gown.at[target, wa],
            (gup_in if up else gdown_in).at[j],
            sem_gline.at[0, k, j],
            sem_gline.at[1, k, j],
            (wa, ta + 2 if up else ta - 2),
        )

    def g_origin():
        @pl.when(z == 0)
        def _():
            for j in range(nz - 1):
                g_line(True, j).start()

        @pl.when(z == nz - 1)
        def _():
            for j in range(nz - 1):
                g_line(False, j).start()

    def g_hop(j):
        target = nz - 1 - j

        @pl.when(jnp.logical_and(z < target, z > 0))
        def _():
            g_line(True, j).wait_recv()
            gown[target, wa] = (gown[target, wa].astype(F32) + gup_in[j].astype(F32)).astype(BF16)
            g_line(True, j).start()

        @pl.when(jnp.logical_and(z > j, z < nz - 1))
        def _():
            g_line(False, j).wait_recv()
            gown[j, wa] = (gown[j, wa].astype(F32) + gdown_in[j].astype(F32)).astype(BF16)
            g_line(False, j).start()

    def g_final():
        @pl.when(z == 0)
        def _():
            g_line(False, 0).wait_recv()
            wsum[...] = gown[0, wa].astype(F32) + gdown_in[0].astype(F32)

        @pl.when(z == nz - 1)
        def _():
            g_line(True, 0).wait_recv()
            wsum[...] = gown[nz - 1, wa].astype(F32) + gup_in[0].astype(F32)

        for b in range(1, nz - 1):

            @pl.when(z == b)
            def _():
                g_line(True, nz - 1 - b).wait_recv()
                g_line(False, b).wait_recv()
                both = gup_in[nz - 1 - b].astype(F32) + gdown_in[b].astype(F32)
                wsum[...] = gown[b, wa].astype(F32) + both

    for b in order:
        g_core(b, 1 - c).start()
        g_load(b).start()

    def da_arrive(s, j):
        own_piece = jnp.logical_and(s == ta, 2 * c + j == wa)
        where = da.at[s, :, lanes(j * CHUNK)]

        @pl.when(own_piece)
        def _():
            da_copy(wa, z, True).wait()

        @pl.when(jnp.logical_not(own_piece))
        def _():
            send(where, where, sem_da.at[0, 0, 0], sem_da.at[1, s, j], (2 * c + j, s)).wait_recv()

    def da_sent(k, carry):
        w, b = (wa + k // nz) % nwa, k % nz

        @pl.when(jnp.logical_not(da_self(w, b)))
        def _():
            da_copy(w, b, False).wait_send()

        return carry

    def prepare(b):
        for core in range(2):
            for j in range(2):
                da_arrive(2 * b + core, j)
        for h in range(heads):
            group = slice(h * hdim, (h + 1) * hdim)
            both = []
            for s in (2 * b, 2 * b + 1):
                one = da[s, group, :].astype(F32) * zinv[h, s * 8 : s * 8 + 1, :]
                both.append(one.astype(BF16))
                scaled[s, group, :] = both[-1]
            made = jnp.dot(
                jnp.concatenate(both, axis=0), terms[h], preferred_element_type=F32
            ).astype(BF16)
            partial[2 * b, group, :] = made[:hdim]
            partial[2 * b + 1, group, :] = made[hdim:]
        core_copy(b, 1 - c).start()

    def shifts():
        for h in range(heads):
            group = slice(h * hdim, (h + 1) * hdim)
            for s in range(nta):
                inv = zinv[h, s * 8 : s * 8 + 1, :]
                one = da[s, group, :].astype(F32) * mixed[s, group, :]
                along = jnp.sum(one, axis=0, keepdims=True)
                shift[h, s * 8 : (s + 1) * 8, :] = jnp.broadcast_to(along * inv, (8, query))

    def core_copy(b, core):
        return send(
            partial.at[2 * b + core],
            paired.at[b],
            sem_core.at[0, b],
            sem_core.at[1, b],
            (wa, me.peer),
        )

    def out_start():
        for q in range(nz):
            back_own(outown, output, sem_out, q).start()
            for step in range(1, nwa):
                back_copy(outown, output, sem_out, step, q).start()

    def line_copy(up, j, q):
        k = 0 if up else 1
        cols = pl.ds(q * part, part)
        return send(
            partial.at[2 * (nz - 1 - j if up else j) + c, :, cols],
            (up_in if up else down_in).at[j, :, cols],
            sem_line.at[0, k, j, q],
            sem_line.at[1, k, j, q],
            (wa, ta + 2 if up else ta - 2),
        )

    ready = set()

    def core_ready(b):
        if b not in ready:
            ready.add(b)
            core_copy(b, c).wait_recv()

    def chip_sum(b, q):
        cols = pl.ds(q * part, part)
        return partial[2 * b + c, :, cols].astype(F32) + paired[b, :, cols].astype(F32)

    def line_step(up, j, q):
        target = nz - 1 - j if up else j
        landed = up_in if up else down_in
        cols = pl.ds(q * part, part)

        @pl.when(z < target if up else z > target)
        def _():
            first = z == (0 if up else nz - 1)

            @pl.when(jnp.logical_not(first))
            def _():
                line_copy(up, j, q).wait_recv()
                total = chip_sum(target, q) + landed[j, :, cols].astype(F32)
                partial[2 * target + c, :, cols] = total.astype(BF16)

            @pl.when(first)
            def _():
                partial[2 * target + c, :, cols] = chip_sum(target, q).astype(BF16)

            line_copy(up, j, q).start()

    def line(j):
        core_ready(nz - 1 - j)
        core_ready(j)
        for q in range(nz):
            line_step(True, j, q)
            line_step(False, j, q)

    fetch[0].wait()
    for b in order:
        g_cores(b)
    prepare(order[0])
    prepare(order[1])
    line(0)
    for b in order[2:]:
        prepare(b)
    for j in range(1, nz - 1):
        line(j)
    for b in range(nz):
        core_ready(b)

    fetch[1].wait()
    shifts()
    get_wv.wait()
    for t in range(nta):
        turned = jnp.concatenate([wv[w, t] for w in range(nwa)], axis=0).T
        wvt[t * wdepth : (t + 1) * wdepth, :] = turned[:wdepth]
    fetch[2].wait()
    fetch[3].wait()
    norm, inv = norm_stats(xown[...].astype(F32))
    normed[...] = norm
    invs[...] = jnp.broadcast_to(inv, invs.shape)
    gains[...] = jnp.zeros_like(gains)
    biases[...] = jnp.zeros_like(biases)
    fetch[4].wait()
    for b in order:
        g_plane(b)
    out_start()

    def dv_copy(step, q):
        w = (wa + step) % nwa
        return send(
            dvalue.at[:, lanes(q * part + w * CHUNK)],
            dvown.at[block_rows(wa), pl.ds(q * CHUNK, CHUNK)],
            sem_dv.at[0, step, q],
            sem_dv.at[1, step, q],
            (w, ta),
        )

    place = lax.broadcasted_iota(jnp.int32, (width, part), 1).astype(F32)

    def final(q):
        cols = pl.ds(q * part, part)
        key_valid = place + q * part < ln[0:1, 0:1]
        for b in range(nz):

            @pl.when(z == b)
            def _():
                total = chip_sum(b, q)
                if b > 0:
                    line_copy(True, nz - 1 - b, q).wait_recv()
                    total = total + up_in[nz - 1 - b, :, cols].astype(F32)
                if b < nz - 1:
                    line_copy(False, b, q).wait_recv()
                    total = total + down_in[b, :, cols].astype(F32)
                dvalue[:, cols] = jnp.where(key_valid, total, 0.0).astype(BF16)

        for step in range(1, nwa):
            dv_copy(step, q).start()
        dvown[block_rows(wa), q * CHUNK : (q + 1) * CHUNK] = dvalue[
            :, lanes(q * part + wa * CHUNK)
        ]

    for b in order:
        g_end(b)
    g_origin()
    for q in range(nz):
        final(q)

    g_hop(0)
    vmade = lax.dot_general(layer[...], dvalue[...], ROWS_NT, preferred_element_type=F32)
    vsend[...] = vmade.astype(BF16).reshape(nta, wdepth, width)
    vbias = jnp.sum(dvalue[...].astype(F32), axis=1, keepdims=True)

    def v_copy(step):
        t = (ta + step) % nta
        return send(
            vsend.at[t], vrecv.at[step], sem_v.at[0, step], sem_v.at[1, step], (wa, t)
        )

    for step in range(1, nta):
        v_copy(step).start()

    for q in range(nz):
        cols = slice(q * CHUNK, (q + 1) * CHUNK)
        for step in range(1, nwa):
            dv_copy(step, q).wait_recv()
        dl = jnp.dot(wvt[...], dvown[:, cols], preferred_element_type=F32)
        norm = normed[:, cols]
        e = dl * pfull[:, 0:1]
        mean_e = jnp.sum(e, axis=0, keepdims=True) / depth
        mean_n = jnp.sum(e * norm, axis=0, keepdims=True) / depth
        made = dresid[:, cols] + invs[0:1, cols] * (e - mean_e - norm * mean_n)
        tsend[:, cols] = made.astype(BF16)
        back_own(tsend, tgrad, sem_tg, q).start()
        for step in range(1, nwa):
            back_copy(tsend, tgrad, sem_tg, step, q).start()
        gains[...] += dl * norm
        biases[...] += dl

    gain = jnp.sum(gains[...], axis=1, keepdims=True)
    bias = jnp.sum(biases[...], axis=1, keepdims=True)
    column = lax.broadcasted_iota(jnp.int32, (depth, PAD), 1)
    cols = jnp.where(column == 0, gain, jnp.where(column == 1, bias, vcol[...]))
    wide = vrow.shape[1] // nwa
    gap = csend.shape[2] - CHUNK
    used = wide // CHUNK
    for w in range(nwa):
        piece = cols[w * width : (w + 1) * width]
        piece = jnp.concatenate([piece, jnp.zeros((gap - width, PAD), F32)], axis=0)
        csend[w, :, :gap] = piece.T[:8]
        starts = [w * wide + row * CHUNK for row in range(used)]
        packed = [vrow[0:1, start : start + CHUNK] for start in starts]
        csend[w, :, gap:] = jnp.concatenate(packed + [jnp.zeros((8 - used, CHUNK), F32)], axis=0)

    def c_copy(step):
        w = (wa + step) % nwa
        return send(csend.at[w], crecv.at[step], sem_c.at[0, step], sem_c.at[1, step], (w, ta))

    for step in range(1, nwa):
        c_copy(step).start()
    g_hop(1)
    crecv[0] = csend[wa]
    piece = jnp.concatenate(
        [jnp.broadcast_to(vbias, (width, PAD)), jnp.zeros((gap - width, PAD), F32)], axis=0
    )
    vb_row = jnp.concatenate([piece.T[:8], jnp.zeros((8, CHUNK), F32)], axis=1)
    row = lax.broadcasted_iota(jnp.int32, vb_row.shape, 0)
    total = jnp.where(row == 2, vb_row, 0.0) + crecv[0]
    for step in range(1, nwa):
        c_copy(step).wait_recv()
        total = total + crecv[step]
    csum[...] = total

    def c2_copy(step):
        t = (ta + step) % nta
        return send(csum, crecv2.at[step], sem_c2.at[0, step], sem_c2.at[1, step], (wa, t))

    for step in range(1, nta):
        c2_copy(step).start()
    for j in range(2, nz - 1):
        g_hop(j)
    value_total = vsend[ta].astype(F32)
    for step in range(1, nta):
        v_copy(step).wait_recv()
        value_total = value_total + vrecv[step].astype(F32)
    vgrad[...] = value_total
    g_final()
    crecv2[0] = csum[...]
    for step in range(1, nta):
        c2_copy(step).wait_recv()
    full = jnp.zeros(csum.shape, F32)
    for t in range(nta):
        full = full + crecv2[(ta - t + nta) % nta]
    vectors[...] = full

    lax.fori_loop(0, nwa * nz, da_sent, 0)
    for step in range(1, nwa):
        for q in range(nz):
            back_copy(tsend, tgrad, sem_tg, step, q).wait()
            back_copy(outown, output, sem_out, step, q).wait()
            dv_copy(step, q).wait_send()
        c_copy(step).wait_send()
    for q in range(nz):
        back_own(outown, output, sem_out, q).wait()
        back_own(tsend, tgrad, sem_tg, q).wait()
    for step in range(1, nta):
        v_copy(step).wait_send()
        c2_copy(step).wait_send()
    for b in range(nz):
        core_copy(b, 1 - c).wait_send()
        g_core(b, 1 - c).wait_send()
        for k in range(2):
            g_first(k, 0, b).wait_send()
            g_first(k, 1, b).wait_send()
            g_second(k, b).wait_send()
    for j in range(nz - 1):

        @pl.when(z < nz - 1 - j)
        def _():
            for q in range(nz):
                line_copy(True, j, q).wait_send()
            g_line(True, j).wait_send()

        @pl.when(z > j)
        def _():
            for q in range(nz):
                line_copy(False, j, q).wait_send()
            g_line(False, j).wait_send()


def run_backward(
    dims, dattended, outown, dresid, xown, terms, mixed, zinv, lens, ln, pfull, layer, weights, wgrad, vcol, vrow
):
    nwa, nta = dims
    nz = nta // 2
    half, both = weights.shape[2] // 2, wgrad.shape[4]
    depth, own = dresid.shape
    width = depth // nwa
    heads, query, seq = terms.shape
    wdepth = depth // nta
    wide = 3 * CHUNK
    dma = pltpu.SemaphoreType.DMA
    return pl.pallas_call(
        functools.partial(backward_kernel, dims),
        out_shape=(
            shape_of((nta, width, query), BF16),
            shape_of((heads, nta * 8, query), F32),
            shape_of((width, seq), BF16),
            shape_of((width, seq), BF16),
            shape_of((wdepth, width), F32),
            shape_of((8, wide), F32),
            shape_of((width, both), F32),
        ),
        in_specs=anywhere(6) + whole(4) + anywhere(3) + whole(2),
        out_specs=tuple(whole(7)),
        scratch_shapes=[
            pltpu.VMEM((depth, own), F32),
            pltpu.VMEM((depth, own), BF16),
            pltpu.VMEM((heads, query, seq), BF16),
            pltpu.VMEM((nta, width, query), F32),
            pltpu.VMEM((depth, seq), BF16),
            pltpu.VMEM((depth, own), F32),
            pltpu.VMEM((8, own), F32),
            pltpu.VMEM((depth, depth), BF16),
            pltpu.VMEM((depth, CHUNK), F32),
            pltpu.VMEM((depth, CHUNK), F32),
            pltpu.VMEM((nta, width, query), BF16),
            pltpu.VMEM((nta, width, seq), BF16),
            pltpu.VMEM((nz, width, seq), BF16),
            pltpu.VMEM((nz - 1, width, seq), BF16),
            pltpu.VMEM((nz - 1, width, seq), BF16),
            pltpu.VMEM((nz, nwa, width, both), BF16),
            pltpu.VMEM((nz, nwa, width, both), BF16),
            pltpu.VMEM((nz, 2, half, both), BF16),
            pltpu.VMEM((nz, 2, half, both), BF16),
            pltpu.VMEM((nz, half, both), BF16),
            pltpu.VMEM((nz, half, both), BF16),
            pltpu.VMEM((nz - 1, width, both), BF16),
            pltpu.VMEM((nz - 1, width, both), BF16),
            pltpu.VMEM((width, seq), BF16),
            pltpu.VMEM((depth, own), BF16),
            pltpu.VMEM((nwa, nta, width, PAD), BF16),
            pltpu.VMEM((nta, wdepth, width), BF16),
            pltpu.VMEM((nta, wdepth, width), BF16),
            pltpu.VMEM((depth, own), BF16),
            pltpu.VMEM((nwa, 8, wide), F32),
            pltpu.VMEM((nwa, 8, wide), F32),
            pltpu.VMEM((8, wide), F32),
            pltpu.VMEM((nta, 8, wide), F32),
            dma((2, nta, max(nz, 2))),
            dma((2, nwa, nz)),
            dma((2, nz)),
            dma((2, 2, nz, nz)),
            dma((2, nwa, nz)),
            dma((2, nwa, nz)),
            dma((2, nta)),
            dma((2, nwa)),
            dma((2, nta)),
            dma((6,)),
            dma((2, 8, nz)),
            dma((2, 2, nz)),
        ],
        compiler_params=pltpu.CompilerParams(
            collective_id=2, has_side_effects=True, vmem_limit_bytes=VMEM_BYTES
        ),
        cost_estimate=pl.CostEstimate(
            flops=4 * 10**9, bytes_accessed=80 * 10**6, transcendentals=0
        ),
    )(
        dattended, outown, dresid, xown, terms, mixed, zinv, lens, ln, pfull, layer, weights, wgrad,
        vcol, vrow,
    )


def logits_kernel(
    terms,
    scaled,
    value,
    shift,
    lens,
    output,
    tgrad,
    wsum,
    vgrad,
    vectors,
    out,
    output_out,
    tgrad_out,
    up_out,
    down_out,
    wo_out,
    vgrad_out,
    *vector_out,
):
    nta = scaled.shape[0]
    for row, ref in enumerate(vector_out[:-1]):
        ref[...] = vectors[row, : ref.shape[0]]
    bias_out = vector_out[-1]
    gap = vectors.shape[1] - CHUNK
    for row in range(bias_out.shape[0] // CHUNK):
        bias_out[row * CHUNK : (row + 1) * CHUNK] = vectors[row, gap:]
    output_out[...] = output[...]
    tgrad_out[...] = tgrad[...].astype(F32)
    vgrad_out[...] = vgrad[...]
    hidden = up_out.shape[1]
    up_out[...] = wsum[:, :hidden]
    down_out[...] = wsum[:, hidden : 2 * hidden]
    wo_out[...] = wsum[:, 2 * hidden : 2 * hidden + wo_out.shape[1]]
    cols = terms.shape[2]
    stacked = jnp.concatenate([scaled[s] for s in range(nta)], axis=0)
    values = jnp.concatenate([value[s] for s in range(nta)], axis=0)
    made = lax.dot_general(stacked, values, ROWS_TN, preferred_element_type=F32)
    where = (nta * 8, cols)
    place = lax.broadcasted_iota(jnp.int32, where, 1) + pl.program_id(1) * cols
    first = lax.broadcasted_iota(jnp.int32, where, 0) % 8 == 0
    valid = jnp.logical_and(place.astype(F32) < lens[:, 0:1], first)
    valid = jnp.where(valid, 1.0, 0.0).astype(BF16)
    high = shift[0].astype(BF16)
    rest = (shift[0] - high.astype(F32)).astype(BF16)
    made = made - lax.dot_general(high, valid, ROWS_TN, preferred_element_type=F32)
    made = made - lax.dot_general(rest, valid, ROWS_TN, preferred_element_type=F32)
    out[0] = terms[0].astype(F32) * made


def run_logits(terms, scaled, value, shift, lens, output, tgrad, wsum, vgrad, vectors, bias):
    heads, query, seq = terms.shape
    nta, width, _ = scaled.shape
    hdim = width // heads
    cols = min(1024, seq)
    steps = seq // cols
    wdepth = vgrad.shape[0]
    hidden = (wsum.shape[1] - PAD) // 2
    total = heads * steps
    flat = (shape_of((width,), F32),) * 7 + (shape_of((bias,), F32),)

    def rows_of(array, lanes_in=None):
        shape = (array[0] // total, lanes_in or array[1])
        return pl.BlockSpec(shape, lambda h, k: (h * steps + k, 0))

    return pl.pallas_call(
        logits_kernel,
        grid=(heads, steps),
        out_shape=(
            shape_of((heads, query, seq), F32),
            shape_of((width, seq), BF16),
            shape_of((width, seq), F32),
            shape_of((width, hidden), F32),
            shape_of((width, hidden), F32),
            shape_of((width, wdepth), F32),
            shape_of(vgrad.shape, F32),
        )
        + flat,
        in_specs=[
            pl.BlockSpec((1, query, cols), lambda h, k: (h, 0, k)),
            pl.BlockSpec((nta, hdim, query), lambda h, k: (0, h, 0)),
            pl.BlockSpec((nta, hdim, cols), lambda h, k: (0, h, k)),
            pl.BlockSpec((1, nta * 8, query), lambda h, k: (h, 0, 0)),
            pl.BlockSpec(lens.shape, lambda h, k: (0, 0)),
            rows_of(output.shape),
            rows_of(tgrad.shape),
            rows_of(wsum.shape),
            rows_of(vgrad.shape),
            pl.BlockSpec(vectors.shape, lambda h, k: (0, 0)),
        ],
        out_specs=(
            pl.BlockSpec((1, query, cols), lambda h, k: (h, 0, k)),
            rows_of(output.shape),
            rows_of(tgrad.shape),
            rows_of((width, hidden)),
            rows_of((width, hidden)),
            rows_of((width, wdepth)),
            rows_of(vgrad.shape),
        )
        + tuple(pl.BlockSpec(one.shape, lambda h, k: (0,)) for one in flat),
        compiler_params=pltpu.CompilerParams(vmem_limit_bytes=VMEM_BYTES),
        cost_estimate=pl.CostEstimate(
            flops=2 * 10**9, bytes_accessed=20 * 10**6, transcendentals=0
        ),
    )(terms, scaled, value, shift, lens, output, tgrad, wsum, vgrad, vectors)


def on_device_fast(
    dims,
    tokens,
    seq_lengths,
    norm1_gain,
    norm1_bias,
    value_weight,
    value_bias,
    synth_logits,
    out_weight,
    out_bias,
    norm2_gain,
    norm2_bias,
    up_weight,
    up_bias,
    down_weight,
    down_bias,
    cotangent,
):
    nwa, nta = dims
    width = tokens.shape[0]
    per_feature = (
        norm1_gain,
        norm1_bias,
        value_bias,
        out_bias,
        norm2_gain,
        norm2_bias,
        down_bias,
    )
    prow = jnp.pad(jnp.stack(per_feature), ((0, 1), (0, 2 * CHUNK - width)))
    prow = jnp.concatenate([prow, jnp.broadcast_to(up_bias, (8, up_bias.shape[0]))], axis=1)
    ln = jnp.broadcast_to(seq_lengths.astype(F32)[:, None], (8, CHUNK))
    logits = synth_logits.transpose(1, 0, 2)
    (
        xown,
        weights,
        _,
        layer,
        value,
        terms,
        mixed,
        zinv,
        lens,
        pfull,
        outown,
        dattended,
        dresid,
        wgrad,
        vcol,
        vrow,
    ) = run_forward(
        dims,
        tokens,
        cotangent,
        out_weight,
        value_weight,
        up_weight,
        down_weight.T,
        prow,
        ln,
        logits,
    )
    scaled, shift, output, tgrad, vgrad, vectors, wsum = run_backward(
        dims,
        dattended,
        outown,
        dresid,
        xown,
        terms,
        mixed,
        zinv,
        lens,
        ln,
        pfull,
        layer,
        weights,
        wgrad,
        vcol,
        vrow,
    )
    logits_grad, output, tgrad, up_grad, down_grad, out_grad, vgrad, *flat = run_logits(
        terms, scaled, value, shift, lens, output, tgrad, wsum, vgrad, vectors, up_bias.shape[0]
    )
    return (
        output,
        tgrad,
        flat[0],
        flat[1],
        vgrad,
        flat[2],
        logits_grad.transpose(1, 0, 2),
        out_grad,
        flat[3],
        flat[4],
        flat[5],
        up_grad,
        flat[7],
        down_grad.T,
        flat[6],
    )


def fits(mesh):
    return mesh.shape["wa"] == 4 and mesh.shape["ta"] == 8


def solution(mesh):
    placed = (
        P("wa", "ta"),
        P("ta"),
        P("wa"),
        P("wa"),
        P("ta", "wa"),
        P("wa"),
        P("ta", "wa", None),
        P("wa", "ta"),
        P("wa"),
        P("wa"),
        P("wa"),
        P("wa", "ta"),
        P("wa"),
        P("ta", "wa"),
        P("wa"),
        P("wa", "ta"),
    )
    sizes = (mesh.shape["wa"], mesh.shape["ta"])
    body = functools.partial(on_device_fast, sizes) if fits(mesh) else on_device
    return jax.shard_map(
        body,
        mesh=mesh,
        in_specs=placed,
        out_specs=(
            P("wa", "ta"),
            P("wa", "ta"),
            P("wa"),
            P("wa"),
            P("ta", "wa"),
            P("wa"),
            P("ta", "wa", None),
            P("wa", "ta"),
            P("wa"),
            P("wa"),
            P("wa"),
            P("wa", "ta"),
            P("wa"),
            P("ta", "wa"),
            P("wa"),
        ),
        check_vma=False,
    )
```

```python
import functools

import jax
import jax.numpy as jnp
from jax import lax
from jax.experimental import pallas as pl
from jax.experimental.pallas import tpu as pltpu
from jax.sharding import PartitionSpec as P

D = 768


EPSILON = 1e-05
ALONG_FEATURES = (((1,), (1,)), ((), ()))
ALONG_ROWS = (((0,), (0,)), ((), ()))


def row_statistics(first_term, second_term):
    return lax.psum((jnp.sum(first_term, axis=1), jnp.sum(second_term, axis=1)), "wa")


def all_features(features_part):
    return lax.all_gather(features_part, "wa", axis=1, tiled=True)


def feature_share(partial_sum):
    return lax.psum_scatter(partial_sum, "wa", scatter_dimension=1, tiled=True)


def norm_forward(inputs, norm_gain, norm_bias):
    row_total, row_squares = row_statistics(inputs, inputs * inputs)
    row_mean = row_total / D
    variance = row_squares / D - row_mean * row_mean
    inverse = lax.rsqrt(variance + EPSILON)
    normed = (inputs - row_mean[:, None]) * inverse[:, None]
    return (normed * norm_gain + norm_bias, normed, inverse)


def norm_backward(incoming, normed, inverse, norm_gain):
    scaled = incoming * norm_gain
    row_total, row_along = row_statistics(scaled, scaled * normed)
    return inverse[:, None] * (scaled - row_total[:, None] / D - normed * row_along[:, None] / D)


def weights_of(logit_rows, length_all):
    seq_len = logit_rows.shape[2]
    key_valid = (jnp.arange(seq_len)[None, :] < length_all[:, None]).astype(jnp.bfloat16)
    terms = jnp.exp(logit_rows.astype(jnp.float32)).astype(jnp.bfloat16)
    sums = jnp.einsum("phk,sk->sph", terms, key_valid, preferred_element_type=jnp.float32)
    return (terms, sums, key_valid)


def attend(terms, sums, value_all, query_rows):
    mixed = jnp.einsum("phk,skhd->sphd", terms, value_all, preferred_element_type=jnp.float32)
    mixed = mixed / sums[..., None]
    return (mixed, (mixed * query_rows[:, :, None, None]).astype(jnp.bfloat16))


def attend_back(terms, sums, key_valid, value_all, mixed, grad_rows):
    along = jnp.sum(grad_rows.astype(jnp.float32) * mixed, axis=-1) / sums
    scaled = (grad_rows.astype(jnp.float32) / sums[..., None]).astype(jnp.bfloat16)
    dvalue_part = jnp.einsum("phk,sphd->skhd", terms, scaled, preferred_element_type=jnp.float32)
    dlogits = jnp.einsum("sphd,skhd->phk", scaled, value_all, preferred_element_type=jnp.float32)
    high = along.astype(jnp.bfloat16)
    rest = (along - high.astype(jnp.float32)).astype(jnp.bfloat16)
    shift = sum(
        jnp.einsum("sph,sk->phk", part, key_valid, preferred_element_type=jnp.float32)
        for part in (high, rest)
    )
    return (dvalue_part, terms.astype(jnp.float32) * (dlogits - shift))


def on_device(
    tokens,
    seq_lengths,
    norm1_gain,
    norm1_bias,
    value_weight,
    value_bias,
    synth_logits,
    out_weight,
    out_bias,
    norm2_gain,
    norm2_bias,
    up_weight,
    up_bias,
    down_weight,
    down_bias,
    cotangent,
):
    rows_dev = tokens.shape[1]
    local_width = tokens.shape[0]
    seq_count = seq_lengths.shape[0]
    seq_len = synth_logits.shape[2]
    head_count = synth_logits.shape[1]
    head_dim = local_width // head_count
    value_cols, out_rows, up_rows, down_cols = (
        lax.all_gather(value_weight, "ta", axis=0, tiled=True),
        lax.all_gather(out_weight, "ta", axis=1, tiled=True),
        lax.all_gather(up_weight, "ta", axis=1, tiled=True),
        lax.all_gather(down_weight, "ta", axis=0, tiled=True),
    )
    up_block, down_block = (
        lax.all_to_all(up_rows.T, "wa", split_axis=0, concat_axis=1, tiled=True),
        lax.all_to_all(down_cols, "wa", split_axis=0, concat_axis=1, tiled=True),
    )
    inputs = tokens.T.astype(jnp.float32)
    pre_one, normed_one, inverse_one = norm_forward(inputs, norm1_gain, norm1_bias)
    layer_one = all_features(pre_one.astype(jnp.bfloat16))
    values = (
        jnp.dot(layer_one, value_cols, preferred_element_type=jnp.float32) + value_bias
    ).astype(jnp.bfloat16)
    value_heads = values.reshape(seq_count, seq_len, head_count, head_dim)
    positions = jnp.arange(seq_len)
    key_valid = positions[None, :] < seq_lengths[:, None]
    query_valid = key_valid.astype(jnp.float32)
    length_all = lax.all_gather(seq_lengths, "ta", axis=0, tiled=True)
    block_rows = synth_logits.shape[0]
    value_all = lax.all_gather(
        value_heads * key_valid[:, :, None, None].astype(jnp.bfloat16), "ta", axis=0, tiled=True
    )
    terms, sums, key_valid_all = weights_of(synth_logits, length_all)
    block_positions = lax.axis_index("ta") * block_rows + jnp.arange(block_rows)
    query_rows = (block_positions[None, :] < length_all[:, None]).astype(jnp.float32)
    mixed_rows, mixed_low = attend(terms, sums, value_all, query_rows)
    attended = lax.all_to_all(mixed_low, "ta", split_axis=0, concat_axis=1, tiled=True)
    attended = attended.reshape(rows_dev, local_width)
    branch = (
        feature_share(jnp.dot(attended, out_rows, preferred_element_type=jnp.float32)) + out_bias
    )
    resid = inputs + branch
    pre_two, normed_two, inverse_two = norm_forward(resid, norm2_gain, norm2_bias)
    layer_two = all_features(pre_two.astype(jnp.bfloat16))
    upper = (
        lax.dot_general(layer_two, up_block, ALONG_FEATURES, preferred_element_type=jnp.float32)
        + up_bias
    )
    hidden, gelu_back = jax.vjp(jax.nn.gelu, upper)
    hidden_low = hidden.astype(jnp.bfloat16)
    feed = (
        feature_share(jnp.dot(hidden_low, down_block, preferred_element_type=jnp.float32))
        + down_bias
    )
    output = (resid + feed).astype(jnp.bfloat16)
    cotangent_rows = cotangent.T
    grad_in = cotangent_rows.astype(jnp.float32)
    grad_full = all_features(cotangent_rows)
    dhidden = lax.dot_general(
        grad_full, down_block, ALONG_FEATURES, preferred_element_type=jnp.float32
    )
    dupper = gelu_back(dhidden)[0].astype(jnp.bfloat16)
    down_part = lax.dot_general(
        hidden_low, grad_full, ALONG_ROWS, preferred_element_type=jnp.float32
    )
    up_part = lax.dot_general(dupper, layer_two, ALONG_ROWS, preferred_element_type=jnp.float32)
    up_bias_part = jnp.sum(dupper.astype(jnp.float32), axis=0)
    down_bias_part = jnp.sum(grad_in, axis=0)
    dlayer_two = feature_share(jnp.dot(dupper, up_block, preferred_element_type=jnp.float32))
    gain_two_part = jnp.sum(dlayer_two * normed_two, axis=0)
    bias_two_part = jnp.sum(dlayer_two, axis=0)
    dresid = grad_in + norm_backward(dlayer_two, normed_two, inverse_two, norm2_gain)
    dbranch = dresid.astype(jnp.bfloat16)
    dbranch_full = all_features(dbranch)
    dattended = lax.dot_general(
        dbranch_full, out_rows, ALONG_FEATURES, preferred_element_type=jnp.float32
    ).astype(jnp.bfloat16)
    out_part = lax.dot_general(
        attended, dbranch_full, ALONG_ROWS, preferred_element_type=jnp.float32
    )
    out_bias_part = jnp.sum(dbranch.astype(jnp.float32), axis=0)
    grad_heads = dattended.reshape(seq_count, seq_len, head_count, head_dim)
    grad_heads = grad_heads * query_valid[:, :, None, None].astype(jnp.bfloat16)
    grad_block = lax.all_to_all(grad_heads, "ta", split_axis=1, concat_axis=0, tiled=True)
    dvalue_part, logits_grad = attend_back(
        terms, sums, key_valid_all, value_all, mixed_rows, grad_block
    )
    dvalue_rows = dvalue_part.astype(jnp.bfloat16).reshape(-1, local_width)
    dvalue_rows = lax.psum_scatter(dvalue_rows, "ta", scatter_dimension=0, tiled=True)
    dvalues = dvalue_rows * query_valid.reshape(rows_dev, 1).astype(jnp.bfloat16)
    value_part = lax.dot_general(layer_one, dvalues, ALONG_ROWS, preferred_element_type=jnp.float32)
    value_bias_part = jnp.sum(dvalues.astype(jnp.float32), axis=0)
    dlayer_one = feature_share(
        lax.dot_general(dvalues, value_cols, ALONG_FEATURES, preferred_element_type=jnp.float32)
    )
    gain_one_part = jnp.sum(dlayer_one * normed_one, axis=0)
    bias_one_part = jnp.sum(dlayer_one, axis=0)
    tokens_grad = dresid + norm_backward(dlayer_one, normed_one, inverse_one, norm1_gain)
    up_back, down_back = (
        lax.all_to_all(up_part, "wa", split_axis=1, concat_axis=0, tiled=True),
        lax.all_to_all(down_part, "wa", split_axis=1, concat_axis=0, tiled=True),
    )
    value_grad, out_grad, up_grad, down_grad = (
        lax.psum_scatter(value_part, "ta", scatter_dimension=0, tiled=True),
        lax.psum_scatter(out_part, "ta", scatter_dimension=1, tiled=True),
        lax.psum_scatter(up_back, "ta", scatter_dimension=0, tiled=True),
        lax.psum_scatter(down_back, "ta", scatter_dimension=0, tiled=True),
    )
    vector_grads = lax.psum(
        (
            gain_one_part,
            bias_one_part,
            value_bias_part,
            out_bias_part,
            gain_two_part,
            bias_two_part,
            up_bias_part,
            down_bias_part,
        ),
        "ta",
    )
    return (
        output.T,
        tokens_grad.T,
        vector_grads[0],
        vector_grads[1],
        value_grad,
        vector_grads[2],
        logits_grad,
        out_grad,
        vector_grads[3],
        vector_grads[4],
        vector_grads[5],
        up_grad.T,
        vector_grads[6],
        down_grad,
        vector_grads[7],
    )


MESH = pl.DeviceIdType.MESH
ROWS_NT = (((1,), (1,)), ((), ()))
ROWS_TN = (((0,), (0,)), ((), ()))
F32 = jnp.float32
BF16 = jnp.bfloat16
VMEM_BYTES = 60 * 2**20
CHUNK = 128
PAD = 128
AHEAD = 2


def whole(count):
    return [pl.BlockSpec(memory_space=pltpu.VMEM)] * count


def anywhere(count):
    return [pl.BlockSpec(memory_space=pl.ANY)] * count


def shape_of(shape, dtype):
    return jax.ShapeDtypeStruct(shape, dtype)


def lanes(start, size=CHUNK):
    return pl.ds(pl.multiple_of(start, CHUNK), size)


def rows_at(start, size, unit):
    return pl.ds(pl.multiple_of(start, unit), size)


class Place:
    def __init__(self, nwa, nta):
        self.nwa, self.nta, self.nz = nwa, nta, nta // 2
        self.wa = lax.axis_index("wa")
        self.ta = lax.axis_index("ta")
        self.z = self.ta // 2
        self.c = self.ta % 2
        self.peer = self.ta + 1 - 2 * self.c
        self.wx = self.wa + 1 - 2 * (self.wa % 2)
        self.wy = (self.wa + 2) % 4
        self.wd = 3 - self.wa

    def enter(self):
        barrier = pltpu.get_barrier_semaphore()
        total = self.nwa * self.nta

        def greet(step, carry):
            w = (self.wa + step // self.nta) % self.nwa
            t = (self.ta + step % self.nta) % self.nta
            pl.semaphore_signal(barrier, inc=1, device_id=(w, t), device_id_type=MESH)
            return carry

        lax.fori_loop(1, total, greet, 0)
        pl.semaphore_wait(barrier, total - 1)


def send(src, dst, ssem, rsem, device):
    return pltpu.make_async_remote_copy(
        src_ref=src,
        dst_ref=dst,
        send_sem=ssem,
        recv_sem=rsem,
        device_id=device,
        device_id_type=MESH,
    )


def when(condition):
    return pl.when(condition)


def norm_stats(block):
    width = block.shape[0]
    mean = jnp.sum(block, axis=0, keepdims=True) / width
    centred = block - mean
    variance = jnp.sum(centred * centred, axis=0, keepdims=True) / width
    inverse = lax.rsqrt(variance + EPSILON)
    return (centred * inverse, inverse)


def forward_kernel(
    dims,
    tok,
    cot,
    wout,
    wval,
    wup,
    wdown,
    prow,
    ln,
    logits,
    xown,
    small,
    large,
    layer_out,
    value_out,
    term_out,
    mixed,
    zinv,
    lens,
    pfull,
    out,
    dattended,
    dresid,
    wgrad,
    vcol,
    vrow,
    cown,
    attended,
    rfull,
    wo,
    wblock,
    resid,
    normed,
    inverse,
    layer_two,
    layer_t,
    grad_t,
    feed,
    dlayer,
    wide,
    gblock,
    gwo,
    x,
    wvc,
    layer_pad,
    layer,
    value,
    terms,
    attsend,
    rows,
    turned,
    wsmall,
    sem_tok,
    sem_par,
    sem_ta,
    sem_val,
    sem_small,
    sem_large,
    sem_cot,
    sem_att,
    sem_local,
    sem_out,
    sem_wv,
    sem_g,
):
    nwa, nta = dims
    me = Place(nwa, nta)
    wa, ta, z, c = me.wa, me.ta, me.z, me.c
    nz = me.nz
    width = tok.shape[0]
    half = width // 2
    seq = tok.shape[1]
    part = seq // nz
    query = seq // nta
    slot = wvc.shape[1] // nta
    wdepth = wvc.shape[0] * nwa // nta
    heads = terms.shape[0]
    hdim = width // heads
    split = PAD
    get_logits = pltpu.make_async_copy(logits, terms, sem_local.at[5])
    get_logits.start()
    stores = ((small, sem_small), (large, sem_large))
    one = wup.shape[1]
    own_w = (
        pltpu.make_async_copy(wsmall, small.at[wa, ta], sem_local.at[2]),
        pltpu.make_async_copy(wup, large.at[wa, ta, :, pl.ds(0, one)], sem_local.at[6]),
        pltpu.make_async_copy(wdown, large.at[wa, ta, :, pl.ds(one, one)], sem_local.at[7]),
    )
    own_w[1].start()
    own_w[2].start()
    turned[...] = jnp.zeros_like(turned)
    turned[:wdepth, :width] = wval[...]
    wsmall[...] = jnp.zeros_like(wsmall)
    wsmall[:, :wdepth] = wout[...]
    wsmall[:, split:] = turned[...].T[:width]
    own_w[0].start()
    me.enter()


    def block_rows(w, off=0, size=width):
        return rows_at(w * width + off, size, 32)

    def tok_copy(k, q):
        device = (me.wx if k == 0 else me.wy, ta)
        return send(
            tok.at[:, pl.ds(q * part, part)],
            x.at[block_rows(wa), pl.ds(q * part, part)],
            sem_tok.at[0, k, q],
            sem_tok.at[1, k, q],
            device,
        )

    def tok_fwd(k, q):
        source = me.wx if k == 0 else me.wy
        device = (me.wy if k == 0 else me.wx, ta)
        where = x.at[block_rows(source, k * half, half), pl.ds(q * part, part)]
        return send(where, where, sem_tok.at[0, 2 + k, q], sem_tok.at[1, 2 + k, q], device)

    own_x = pltpu.make_async_copy(tok, x.at[block_rows(wa)], sem_local.at[0])
    own_x.start()

    def tok_start(q):
        for k in range(2):
            tok_copy(k, q).start()

    def tok_turn(q):
        for k in range(2):
            tok_copy(k, q).wait_recv()
            tok_fwd(k, q).start()
        if q + AHEAD < nz:
            tok_start(q + AHEAD)

    for q in range(AHEAD):
        tok_start(q)

    def par_copy(step):
        w = (wa + step) % nwa
        return send(prow, rows.at[wa], sem_par.at[0, step], sem_par.at[1, step], (w, ta))

    def ta_copy(step):
        t = (ta + step) % nta
        return send(
            ln, lens.at[rows_at(ta * 8, 8, 8)], sem_ta.at[0, step], sem_ta.at[1, step], (wa, t)
        )

    def wv_column(b, core):
        return wvc.at[:, lanes((2 * b + core) * slot)]

    def wv_z(step):
        b = (z + step) % nz
        src = wsmall.at[:, pl.ds(split, PAD)]
        return send(
            src, wv_column(z, c), sem_wv.at[0, 0, step], sem_wv.at[1, 0, step], (wa, 2 * b + c)
        )

    def wv_core(step, core):
        where = wv_column((z - step + nz) % nz, core)
        return send(where, where, sem_wv.at[0, 1, step], sem_wv.at[1, 1, step], (wa, me.peer))

    own_wv = pltpu.make_async_copy(wsmall.at[:, pl.ds(split, PAD)], wv_column(z, c), sem_local.at[1])
    own_wv.start()
    for step in range(nz - 1, 0, -1):
        wv_z(step).start()
    for step in range(1, nwa):
        par_copy(step).start()
    for step in range(1, nta):
        ta_copy(step).start()
    rows[wa] = prow[...]
    lens[rows_at(ta * 8, 8, 8), :] = ln[...]
    own_wv.wait()
    wv_core(0, c).start()

    def w_line(p, up, b):
        where, sem = stores[p][0].at[wa, 2 * b + c], stores[p][1]
        k = 0 if up else 1
        return send(
            where, where, sem.at[0, k, b], sem.at[1, k, b], (wa, ta + 2 if up else ta - 2)
        )

    for step in range(1, nz):
        wv_z(step).wait_recv()
        wv_core(step, c).start()
    for copy in own_w:
        copy.wait()

    @pl.when(z < nz - 1)
    def _():
        for p in range(2):
            w_line(p, True, z).start()

    @pl.when(z > 0)
    def _():
        for p in range(2):
            w_line(p, False, z).start()

    layer_pad[...] = jnp.zeros_like(layer_pad)
    get_logits.wait()
    for h in range(heads):
        terms[h] = jnp.exp(terms[h].astype(F32)).astype(BF16)
    out_terms = pltpu.make_async_copy(terms, term_out, sem_local.at[3])
    out_terms.start()

    tok_turn(0)
    for step in range(1, nwa):
        par_copy(step).wait_recv()
    gap = 2 * CHUNK
    for w in range(nwa):
        piece = jnp.concatenate([rows[w, :, :gap], jnp.zeros((PAD - 8, gap), F32)], axis=0)
        pfull[w * width : (w + 1) * width, :] = piece.T[:width]
        span = rows.shape[2] - gap
        rfull[:, w * span : (w + 1) * span] = rows[w, :, gap:]
    for step in range(1, nta):
        ta_copy(step).wait_recv()
    for step in range(nz):
        wv_core(step, 1 - c).wait_recv()
    own_x.wait()

    positions = lax.broadcasted_iota(jnp.int32, (nta * 8, seq), 1).astype(F32)
    key_valid = jnp.where(positions < lens[:, 0:1], 1.0, 0.0).astype(BF16)
    for h in range(heads):
        sums = lax.dot_general(key_valid, terms[h], ROWS_NT, preferred_element_type=F32)
        zinv[h] = 1.0 / sums

    def value_copy(kind, b, q, core):
        where = value.at[2 * b + core, :, pl.ds(q * part, part)]
        t = (ta + 2, ta - 2, me.peer)[kind]
        return send(where, where, sem_val.at[0, kind, b, q], sem_val.at[1, kind, b, q], (wa, t))

    def w_plane(p, k, b):
        device = (me.wx if k == 0 else me.wy, ta)
        where, sem = stores[p][0].at[wa, 2 * b + c], stores[p][1]
        return send(where, where, sem.at[0, 2 + k, b], sem.at[1, 2 + k, b], device)

    def w_diag(p, k, b, source):
        device = (me.wy if k == 0 else me.wx, ta)
        where, sem = stores[p][0].at[source, 2 * b + c, pl.ds(k * half, half)], stores[p][1]
        return send(where, where, sem.at[0, 4 + k, b], sem.at[1, 4 + k, b], device)

    def w_core(p, r, b, core):
        source = (wa, me.wx, me.wy, me.wd)[r]
        where, sem = stores[p][0].at[source, 2 * b + core], stores[p][1]
        return send(where, where, sem.at[0, 6 + r, b], sem.at[1, 6 + r, b], (wa, me.peer))

    def w_start(p, b):
        w_plane(p, 0, b).start()
        w_plane(p, 1, b).start()
        w_core(p, 0, b, c).start()

    def w_forward(p, b):
        w_plane(p, 0, b).wait_recv()
        w_diag(p, 0, b, me.wx).start()
        w_core(p, 1, b, c).start()
        w_plane(p, 1, b).wait_recv()
        w_diag(p, 1, b, me.wy).start()
        w_core(p, 2, b, c).start()

    def w_finish(p, b):
        for k in range(2):
            w_diag(p, k, b, me.wd).wait_recv()
        w_core(p, 3, b, c).start()

    def w_landed(p, h):
        @pl.when(z - 1 - h >= 0)
        def _():
            w_line(p, True, z - 1 - h).wait_recv()

        @pl.when(z + 1 + h < nz)
        def _():
            w_line(p, False, z + 1 + h).wait_recv()

    def w_onward(p, h):
        @pl.when(jnp.logical_and(z - 1 - h >= 0, z < nz - 1))
        def _():
            w_line(p, True, z - 1 - h).start()

        @pl.when(jnp.logical_and(z + 1 + h < nz, z > 0))
        def _():
            w_line(p, False, z + 1 + h).start()

    def at_hop(h, act, *args):
        @pl.when(z - 1 - h >= 0)
        def _():
            act(*args, z - 1 - h)

        @pl.when(z + 1 + h < nz)
        def _():
            act(*args, z + 1 + h)

    for q in range(nz):
        cols = pl.ds(q * part, part)
        if q + 1 < nz:
            tok_turn(q + 1)
        for k in range(2):
            where = x.at[block_rows(me.wd, k * half, half), cols]
            send(
                where,
                where,
                sem_tok.at[0, 2 + k, q],
                sem_tok.at[1, 2 + k, q],
                (me.wy if k == 0 else me.wx, ta),
            ).wait_recv()
        centred, _ = norm_stats(x[:, cols].astype(F32))
        low = (centred * pfull[:, 0:1] + pfull[:, 1:2]).astype(BF16)
        layer[:, cols] = low
        for t in range(nta):
            layer_pad[t * slot : t * slot + wdepth, :] = low[t * wdepth : (t + 1) * wdepth]
        made = jnp.dot(wvc[...], layer_pad[...], preferred_element_type=F32)
        made = made + pfull[block_rows(wa), :][:, 2:3]
        place = lax.broadcasted_iota(jnp.int32, (width, part), 1) + q * part
        made = jnp.where(place.astype(F32) < ln[0:1, 0:1], made, 0.0)
        value[ta, :, cols] = made.astype(BF16)
        xown[:, pl.ds(q * CHUNK, CHUNK)] = x[:, lanes(q * part + wa * CHUNK)]

        @pl.when(z < nz - 1)
        def _():
            value_copy(0, z, q, c).start()

        @pl.when(z > 0)
        def _():
            value_copy(1, z, q, c).start()

        value_copy(2, z, q, c).start()
        if q < nz - 1:
            w_landed(0, q)
            w_onward(0, q)
    out_layer = pltpu.make_async_copy(layer, layer_out, sem_local.at[4])
    out_layer.start()

    def cot_copy(step, q):
        w = (wa + step) % nwa
        return send(
            cot.at[:, lanes(q * part + w * CHUNK)],
            cown.at[block_rows(wa), pl.ds(q * CHUNK, CHUNK)],
            sem_cot.at[0, step, q],
            sem_cot.at[1, step, q],
            (w, ta),
        )

    def cot_own(q):
        return pltpu.make_async_copy(
            cot.at[:, lanes(q * part + wa * CHUNK)],
            cown.at[block_rows(wa), pl.ds(q * CHUNK, CHUNK)],
            sem_cot.at[0, 0, q],
        )

    w_start(0, z)
    for h in range(nz - 1):
        at_hop(h, w_start, 0)
    w_start(1, z)
    w_landed(1, 0)
    at_hop(0, w_start, 1)
    for q in range(nz):
        cot_own(q).start()
        for step in range(1, nwa):
            cot_copy(step, q).start()

    def att_copy(s, j):
        return send(
            attsend.at[s, :, pl.ds(j * CHUNK, CHUNK)],
            attended.at[block_rows(wa), lanes(z * CHUNK)],
            sem_att.at[0, s, j],
            sem_att.at[1, wa, z],
            (2 * c + j, s),
        )

    def att_local(s, j):
        return pltpu.make_async_copy(
            attsend.at[s, :, pl.ds(j * CHUNK, CHUNK)],
            attended.at[block_rows(wa), lanes(z * CHUNK)],
            sem_att.at[0, s, j],
        )

    def is_self(s, j):
        return jnp.logical_and(s == ta, 2 * c + j == wa)

    def mix(b):
        for core in range(2):
            s = 2 * b + core
            pltpu.make_async_copy(value.at[s], value_out.at[s], sem_out.at[s]).start()
        length = [lens[rows_at((2 * b + core) * 8, 8, 8), :][0:1, 0:1] for core in range(2)]
        place = lax.broadcasted_iota(jnp.int32, (hdim, query), 1) + ta * query
        place = place.astype(F32)
        for h in range(heads):
            group = slice(h * hdim, (h + 1) * hdim)
            pair = jnp.concatenate([value[2 * b, group, :], value[2 * b + 1, group, :]], axis=0)
            both = lax.dot_general(pair, terms[h], ROWS_NT, preferred_element_type=F32)
            for core in range(2):
                s = 2 * b + core
                inverse = zinv[h, rows_at(s * 8, 8, 8), :][0:1]
                one = both[core * hdim : (core + 1) * hdim] * inverse
                mixed[s, group, :] = one
                one = jnp.where(place < length[core], one, 0.0)
                attsend[s, group, :] = one.astype(BF16)
        for core in range(2):
            s = 2 * b + core
            for j in range(2):

                @pl.when(is_self(s, j))
                def _():
                    att_local(s, j).start()

                @pl.when(jnp.logical_not(is_self(s, j)))
                def _():
                    att_copy(s, j).start()

    def core_ready(b):
        for q in range(nz):
            value_copy(2, b, q, 1 - c).wait_recv()

    def mix_ready(b):
        core_ready(b)
        mix(b)

    def mix_side(h, up):
        b = z - 1 - h if up else z + 1 + h

        @pl.when(b >= 0 if up else b < nz)
        def _():
            mix_ready(b)

    for h in range(nz - 1):
        below, above = z - 1 - h, z + 1 + h
        for q in range(nz):

            @pl.when(below >= 0)
            def _():
                value_copy(0, below, q, c).wait_recv()

                @pl.when(z < nz - 1)
                def _():
                    value_copy(0, below, q, c).start()

                value_copy(2, below, q, c).start()

            @pl.when(above < nz)
            def _():
                value_copy(1, above, q, c).wait_recv()

                @pl.when(z > 0)
                def _():
                    value_copy(1, above, q, c).start()

                value_copy(2, above, q, c).start()

            if h == 0 and q == 0:
                mix_ready(z)
            if h > 0 and q < 2:
                mix_side(h - 1, q == 0)

        if h == 0:
            w_forward(0, z)
            for other in range(nz - 1):
                at_hop(other, w_forward, 0)
        if h == 1:
            w_onward(1, 0)
            w_forward(1, z)
            w_finish(0, z)
            for other in range(nz - 1):
                at_hop(other, w_finish, 0)
    mix_side(nz - 2, True)
    mix_side(nz - 2, False)
    at_hop(0, w_forward, 1)
    w_finish(1, z)
    at_hop(0, w_finish, 1)

    def w_cores(p, b):
        for r in range(4):
            w_core(p, r, b, 1 - c).wait_recv()

    depth, own = xown.shape
    both = 2 * one

    def turn(i):
        pair = z + 1 - 2 * (z % 2)
        late = jnp.where(i == 2, nz // 2 - z // 2, (nz - 1) * (1 - z // 2))
        return jnp.where(i == 0, z, jnp.where(i == 1, pair, late))

    def load(i, slot):
        b = turn(i)
        return pltpu.make_async_copy(
            large.at[:, pl.ds(2 * b, 2)], wblock.at[slot], sem_g.at[slot]
        )

    w_cores(1, turn(0))
    load(0, 0).start()
    for b in range(nz):
        w_cores(0, b)
    get_wo = pltpu.make_async_copy(small.at[:, :, :, pl.ds(0, PAD)], wo, sem_g.at[2])
    get_wo.start()
    for q in range(nz):
        cot_own(q).wait()
        for step in range(1, nwa):
            cot_copy(step, q).wait_recv()
    grad_t[...] = cown[...].T
    w_cores(1, turn(1))
    load(1, 1).start()

    def att_sends(s, carry):
        pltpu.make_async_copy(value.at[s], value_out.at[s], sem_out.at[s]).wait()
        for j in range(2):

            @pl.when(is_self(s, j))
            def _():
                att_local(s, j).wait()

            @pl.when(jnp.logical_not(is_self(s, j)))
            def _():
                att_copy(s, j).wait_send()

        return carry

    lax.fori_loop(0, nta, att_sends, 0)
    mine = wa // 2

    def att_arrivals(k, carry):
        w, b = k // nz, k % nz

        @pl.when(jnp.logical_not(jnp.logical_and(w == wa, 2 * b + mine == ta)))
        def _():
            where = attended.at[block_rows(w), lanes(b * CHUNK)]
            send(where, where, sem_att.at[0, 0, 0], sem_att.at[1, w, b], (w, 2 * b + mine)).wait_recv()

        return carry

    w_landed(1, 1)
    w_onward(1, 1)
    at_hop(1, w_start, 1)
    lax.fori_loop(0, nwa * nz, att_arrivals, 0)
    get_wo.wait()

    def wide_wo():
        joined = [
            jnp.concatenate([wo[w, t] for t in range(nta)], axis=1) for w in range(nwa)
        ]
        return jnp.concatenate(joined, axis=0)

    branch = lax.dot_general(wide_wo(), attended[...], ROWS_TN, preferred_element_type=F32)
    branch = jnp.concatenate([branch[t * PAD : t * PAD + wdepth] for t in range(nta)], axis=0)
    res = xown[...].astype(F32) + branch + pfull[:, 3:4]
    resid[...] = res
    norm, inv = norm_stats(res)
    normed[...] = norm
    inverse[...] = jnp.broadcast_to(inv, inverse.shape)
    low = (norm * pfull[:, 4:5] + pfull[:, 5:6]).astype(BF16)
    layer_two[...] = low
    layer_t[...] = low.T
    feed[...] = jnp.zeros_like(feed)
    dlayer[...] = jnp.zeros_like(dlayer)

    def put(i):
        return pltpu.make_async_copy(
            gblock, wgrad.at[:, turn(i), :, :, pl.ds(0, both)], sem_g.at[3]
        )

    def middle(i, carry):
        slot = i % 2

        @pl.when(i == 2)
        def _():
            at_hop(1, w_finish, 1)
            w_landed(1, 2)
            at_hop(2, w_start, 1)
            w_cores(1, turn(2))
            load(2, 0).start()

        @pl.when(i == 3)
        def _():
            at_hop(2, w_forward, 1)
            at_hop(2, w_finish, 1)
            w_cores(1, turn(3))
            load(3, 1).start()

        load(i, slot).wait()
        held = wblock.at[slot]

        def joined(start):
            parts = [held[:, g, :, start : start + one].reshape(depth, one) for g in range(2)]
            return jnp.concatenate(parts, axis=1)

        up, down_t = joined(0), joined(one)
        at = lanes(turn(i) * both, both)
        upper = jnp.dot(layer_t[...], up, preferred_element_type=F32) + rfull[0:1, at]
        hidden, slope = gelu_pair(upper)
        hidden = hidden.astype(BF16)
        dhidden = jnp.dot(grad_t[...], down_t, preferred_element_type=F32)
        dupper = (dhidden * slope).astype(BF16)
        vrow[:, at] = jnp.broadcast_to(
            jnp.sum(dupper.astype(F32), axis=0, keepdims=True), (vrow.shape[0], both)
        )
        feed[...] += lax.dot_general(down_t, hidden, ROWS_NT, preferred_element_type=F32)
        dlayer[...] += lax.dot_general(up, dupper, ROWS_NT, preferred_element_type=F32)
        gup = jnp.dot(layer_two[...], dupper, preferred_element_type=F32)
        gdown = jnp.dot(cown[...], hidden, preferred_element_type=F32)

        @pl.when(i > 0)
        def _():
            put(i - 1).wait()

        for g in range(2):
            piece = slice(g * one, (g + 1) * one)
            gblock[:, g, :, :one] = gup[:, piece].reshape(nwa, width, one).astype(BF16)
            gblock[:, g, :, one:] = gdown[:, piece].reshape(nwa, width, one).astype(BF16)
        put(i).start()

        @pl.when(i == 0)
        def _():
            at_hop(1, w_forward, 1)

        return carry

    lax.fori_loop(0, nz, middle, 0)

    grad = cown[...].astype(F32)
    out[...] = (resid[...] + feed[...] + pfull[:, 6:7]).astype(BF16)
    dl = dlayer[...]
    norm = normed[...]
    e = dl * pfull[:, 4:5]
    mean_e = jnp.sum(e, axis=0, keepdims=True) / depth
    mean_n = jnp.sum(e * norm, axis=0, keepdims=True) / depth
    dres = grad + inverse[0:1, :] * (e - mean_e - norm * mean_n)
    dresid[...] = dres
    low = dres.astype(BF16)
    vcol[...] = jnp.zeros_like(vcol)
    vcol[:, 3:4] = jnp.sum(low.astype(F32), axis=1, keepdims=True)
    vcol[:, 4:5] = jnp.sum(dl * norm, axis=1, keepdims=True)
    vcol[:, 5:6] = jnp.sum(dl, axis=1, keepdims=True)
    vcol[:, 6:7] = jnp.sum(grad, axis=1, keepdims=True)
    wide[...] = jnp.zeros_like(wide)
    for t in range(nta):
        wide[t * PAD : t * PAD + wdepth, :] = low[t * wdepth : (t + 1) * wdepth]
    da = jnp.dot(wide_wo(), wide[...], preferred_element_type=F32)
    lane = lax.broadcasted_iota(jnp.int32, (depth, own), 1)
    place = (lane // CHUNK) * (CHUNK * nwa) + lane % CHUNK + wa * CHUNK
    da = jnp.where(place.astype(F32) < ln[0:1, 0:1], da, 0.0)
    dattended[...] = da.astype(BF16)
    made = lax.dot_general(attended[...], wide[...], ROWS_NT, preferred_element_type=F32)
    for t in range(nta):
        piece = made[:, t * PAD : (t + 1) * PAD].reshape(nwa, width, PAD)
        gwo[:, t // 2, t % 2] = piece.astype(BF16)
    rest = pltpu.make_async_copy(gwo, wgrad.at[:, :, :, :, pl.ds(both, PAD)], sem_g.at[4])
    rest.start()
    put(nz - 1).wait()
    rest.wait()

    for step in range(1, nta):
        ta_copy(step).wait_send()
    for step in range(nz):
        wv_core(step, c).wait_send()
        if step:
            wv_z(step).wait_send()
    for step in range(1, nwa):
        par_copy(step).wait_send()
        for q in range(nz):
            cot_copy(step, q).wait_send()
    for q in range(nz):
        for k in range(2):
            tok_copy(k, q).wait_send()
            tok_fwd(k, q).wait_send()

    def line_sends(b, carry):
        reach_up = jnp.logical_and(b <= z, z < nz - 1)
        reach_down = jnp.logical_and(b >= z, z > 0)

        @pl.when(reach_up)
        def _():
            for p in range(2):
                w_line(p, True, b).wait_send()
            for q in range(nz):
                value_copy(0, b, q, c).wait_send()

        @pl.when(reach_down)
        def _():
            for p in range(2):
                w_line(p, False, b).wait_send()
            for q in range(nz):
                value_copy(1, b, q, c).wait_send()

        for q in range(nz):
            value_copy(2, b, q, c).wait_send()
        for p in range(2):
            for k in range(2):
                w_plane(p, k, b).wait_send()
            w_diag(p, 0, b, me.wx).wait_send()
            w_diag(p, 1, b, me.wy).wait_send()
            for r in range(4):
                w_core(p, r, b, c).wait_send()
        return carry

    lax.fori_loop(0, nz, line_sends, 0)

    out_terms.wait()
    out_layer.wait()


def run_forward(dims, tok, cot, wout, wval, wup, wdown, prow, ln, logits):
    nwa, nta = dims
    nz = nta // 2
    width, seq = tok.shape
    depth = width * nwa
    own = seq // nwa
    heads, query, _ = logits.shape
    slot = PAD
    both = 2 * wup.shape[1]
    hidden = both // 2 * nta
    dma = pltpu.SemaphoreType.DMA
    return pl.pallas_call(
        functools.partial(forward_kernel, dims),
        out_shape=(
            shape_of((depth, own), BF16),
            shape_of((nwa, nta, width, 2 * PAD), BF16),
            shape_of((nwa, nta, width, both), BF16),
            shape_of((depth, seq), BF16),
            shape_of((nta, width, seq), BF16),
            shape_of((heads, query, seq), BF16),
            shape_of((nta, width, query), F32),
            shape_of((heads, nta * 8, query), F32),
            shape_of((nta * 8, CHUNK), F32),
            shape_of((depth, PAD), F32),
            shape_of((depth, own), BF16),
            shape_of((depth, own), BF16),
            shape_of((depth, own), F32),
            shape_of((nwa, nz, 2, width, both + PAD), BF16),
            shape_of((depth, PAD), F32),
            shape_of((8, hidden), F32),
        ),
        in_specs=anywhere(2) + whole(2) + anywhere(2) + whole(2) + anywhere(1),
        out_specs=tuple(whole(1) + anywhere(5) + whole(7) + anywhere(1) + whole(2)),
        scratch_shapes=[
            pltpu.VMEM((depth, own), BF16),
            pltpu.VMEM((depth, own), BF16),
            pltpu.VMEM((8, hidden), F32),
            pltpu.VMEM((nwa, nta, width, PAD), BF16),
            pltpu.VMEM((2, nwa, 2, width, both), BF16),
            pltpu.VMEM((depth, own), F32),
            pltpu.VMEM((depth, own), F32),
            pltpu.VMEM((8, own), F32),
            pltpu.VMEM((depth, own), BF16),
            pltpu.VMEM((own, depth), BF16),
            pltpu.VMEM((own, depth), BF16),
            pltpu.VMEM((depth, own), F32),
            pltpu.VMEM((depth, own), F32),
            pltpu.VMEM((nta * PAD, own), BF16),
            pltpu.VMEM((nwa, 2, width, both), BF16),
            pltpu.VMEM((nwa, nz, 2, width, PAD), BF16),
            pltpu.VMEM((depth, seq), BF16),
            pltpu.VMEM((width, nta * slot), BF16),
            pltpu.VMEM((nta * slot, seq // nz), BF16),
            pltpu.VMEM((depth, seq), BF16),
            pltpu.VMEM((nta, width, seq), BF16),
            pltpu.VMEM((heads, query, seq), BF16),
            pltpu.VMEM((nta, width, query), BF16),
            pltpu.VMEM((nwa,) + prow.shape, F32),
            pltpu.VMEM((PAD, 2 * CHUNK), BF16),
            pltpu.VMEM((width, 2 * PAD), BF16),
            dma((2, 4, nz)),
            dma((2, nwa)),
            dma((2, nta)),
            dma((2, 3, nz, nz)),
            dma((2, 10, nz)),
            dma((2, 10, nz)),
            dma((2, nwa, nz)),
            dma((2, nta, max(nz, 2))),
            dma((8,)),
            dma((nta,)),
            dma((2, 2, nz)),
            dma((5,)),
        ],
        compiler_params=pltpu.CompilerParams(
            collective_id=1, has_side_effects=True, vmem_limit_bytes=VMEM_BYTES
        ),
        cost_estimate=pl.CostEstimate(
            flops=20 * 10**9, bytes_accessed=80 * 10**6, transcendentals=4 * 10**6
        ),
    )(tok, cot, wout, wval, wup, wdown, prow, ln, logits)


def gelu_pair(u):
    root = 0.7978845608028654
    square = u * u
    bent = jnp.tanh(root * u * (1.0 + 0.044715 * square))
    low_half = 0.5 * (1.0 + bent)
    slope = low_half + 0.5 * u * (1.0 - bent * bent) * root * (1.0 + 3.0 * 0.044715 * square)
    return (u * low_half, slope)


def backward_kernel(
    dims,
    dattended,
    outown,
    dresid_in,
    xown_in,
    terms_in,
    mixed_in,
    zinv,
    lens,
    ln,
    pfull,
    layer_in,
    weights,
    wgrad,
    vcol,
    vrow,
    scaled,
    shift,
    output,
    tgrad,
    vgrad,
    vectors,
    wsum,
    dresid,
    xown,
    terms,
    mixed,
    layer,
    normed,
    invs,
    wvt,
    gains,
    biases,
    da,
    partial,
    paired,
    up_in,
    down_in,
    gown,
    gpeer,
    first_x,
    first_y,
    second_x,
    second_y,
    gup_in,
    gdown_in,
    dvalue,
    dvown,
    wv,
    vsend,
    vrecv,
    tsend,
    csend,
    crecv,
    csum,
    crecv2,
    sem_da,
    sem_out,
    sem_core,
    sem_line,
    sem_dv,
    sem_tg,
    sem_v,
    sem_c,
    sem_c2,
    sem_local,
    sem_g,
    sem_gline,
):
    nwa, nta = dims
    me = Place(nwa, nta)
    wa, ta, z, c = me.wa, me.ta, me.z, me.c
    nz = me.nz
    depth, own = dresid.shape
    width = depth // nwa
    wdepth = depth // nta
    heads, query, seq = terms.shape
    hdim = width // heads
    part = seq // nz
    pairs = (
        (terms_in, terms),
        (mixed_in, mixed),
        (xown_in, xown),
        (dresid_in, dresid),
        (layer_in, layer),
    )
    fetch = [
        pltpu.make_async_copy(src, dst, sem_local.at[1 + i]) for i, (src, dst) in enumerate(pairs)
    ]
    for copy in fetch:
        copy.start()
    me.enter()

    def block_rows(w):
        return rows_at(w * width, width, 32)

    def da_copy(w, b, local):
        core = wa // 2
        src = dattended.at[block_rows(w), lanes(b * CHUNK)]
        dst = da.at[ta, :, lanes((wa % 2) * CHUNK)]
        if local:
            return pltpu.make_async_copy(src, dst, sem_da.at[0, w, b])
        return send(src, dst, sem_da.at[0, w, b], sem_da.at[1, ta, wa % 2], (w, 2 * b + core))

    def da_self(w, b):
        return jnp.logical_and(w == wa, 2 * b + wa // 2 == ta)

    def far(i):
        low_end = 1 - z // (nz // 2)
        return (nz - 1 - i) * low_end + i * (1 - low_end)

    def da_start(k, carry):
        w, b = (wa + k % nwa) % nwa, far(k // nwa)

        @pl.when(da_self(w, b))
        def _():
            da_copy(w, b, True).start()

        @pl.when(jnp.logical_not(da_self(w, b)))
        def _():
            da_copy(w, b, False).start()

        return carry

    lax.fori_loop(0, nwa * nz, da_start, 0)

    def back_copy(src, dst, sems, step, q):
        w = (wa + step) % nwa
        return send(
            src.at[block_rows(w), pl.ds(q * CHUNK, CHUNK)],
            dst.at[:, lanes(q * part + wa * CHUNK)],
            sems.at[0, step, q],
            sems.at[1, step, q],
            (w, ta),
        )

    def back_own(src, dst, sems, q):
        return pltpu.make_async_copy(
            src.at[block_rows(wa), pl.ds(q * CHUNK, CHUNK)],
            dst.at[:, lanes(q * part + wa * CHUNK)],
            sems.at[0, 0, q],
        )

    get_wv = pltpu.make_async_copy(
        weights.at[:, :, :, pl.ds(weights.shape[3] - PAD, PAD)], wv, sem_local.at[0]
    )
    get_wv.start()

    half = width // 2
    order = []
    for j in range(nz):
        for b in (nz - 1 - j, j):
            if b not in order:
                order.append(b)

    def g_core(b, core):
        return send(
            wgrad.at[:, b, core],
            gpeer.at[b],
            sem_g.at[0, 0, b],
            sem_g.at[1, 0, b],
            (wa, me.peer),
        )

    def g_load(b):
        return pltpu.make_async_copy(wgrad.at[:, b, c], gown.at[b], sem_g.at[0, 7, b])

    def g_first(k, r, b):
        near = me.wx if k == 0 else me.wy
        which = near if r == 0 else me.wd
        return send(
            gown.at[b, which, pl.ds(k * half, half)],
            (first_x if k == 0 else first_y).at[b, r],
            sem_g.at[0, 1 + 2 * k + r, b],
            sem_g.at[1, 1 + 2 * k + r, b],
            (near, ta),
        )

    def g_second(k, b):
        near = me.wy if k == 0 else me.wx
        return send(
            gown.at[b, near, pl.ds(k * half, half)],
            (second_x if k == 0 else second_y).at[b],
            sem_g.at[0, 5 + k, b],
            sem_g.at[1, 5 + k, b],
            (near, ta),
        )

    def g_add(b, which, k, extra):
        rows = pl.ds(k * half, half)
        gown[b, which, rows, :] = (
            gown[b, which, rows, :].astype(F32) + extra.astype(F32)
        ).astype(BF16)

    def g_cores(b):
        g_load(b).wait()
        g_core(b, c).wait_recv()
        for w in range(nwa):
            gown[b, w] = (gown[b, w].astype(F32) + gpeer[b, w].astype(F32)).astype(BF16)
        for k in range(2):
            for r in range(2):
                g_first(k, r, b).start()

    def g_plane(b):
        for k in range(2):
            for r in range(2):
                g_first(k, r, b).wait_recv()
            landed = first_x if k == 0 else first_y
            g_add(b, me.wy if k == 0 else me.wx, k, landed[b, 1])
            g_second(k, b).start()
            g_add(b, wa, k, landed[b, 0])

    def g_end(b):
        for k in range(2):
            g_second(k, b).wait_recv()
            g_add(b, wa, k, (second_x if k == 0 else second_y)[b])

    def g_line(up, j):
        k = 0 if up else 1
        target = nz - 1 - j if up else j
        return send(
            gown.at[target, wa],
            (gup_in if up else gdown_in).at[j],
            sem_gline.at[0, k, j],
            sem_gline.at[1, k, j],
            (wa, ta + 2 if up else ta - 2),
        )

    def g_origin():
        @pl.when(z == 0)
        def _():
            for j in range(nz - 1):
                g_line(True, j).start()

        @pl.when(z == nz - 1)
        def _():
            for j in range(nz - 1):
                g_line(False, j).start()

    def g_hop(j):
        target = nz - 1 - j

        @pl.when(jnp.logical_and(z < target, z > 0))
        def _():
            g_line(True, j).wait_recv()
            gown[target, wa] = (gown[target, wa].astype(F32) + gup_in[j].astype(F32)).astype(BF16)
            g_line(True, j).start()

        @pl.when(jnp.logical_and(z > j, z < nz - 1))
        def _():
            g_line(False, j).wait_recv()
            gown[j, wa] = (gown[j, wa].astype(F32) + gdown_in[j].astype(F32)).astype(BF16)
            g_line(False, j).start()

    def g_final():
        @pl.when(z == 0)
        def _():
            g_line(False, 0).wait_recv()
            wsum[...] = gown[0, wa].astype(F32) + gdown_in[0].astype(F32)

        @pl.when(z == nz - 1)
        def _():
            g_line(True, 0).wait_recv()
            wsum[...] = gown[nz - 1, wa].astype(F32) + gup_in[0].astype(F32)

        for b in range(1, nz - 1):

            @pl.when(z == b)
            def _():
                g_line(True, nz - 1 - b).wait_recv()
                g_line(False, b).wait_recv()
                both = gup_in[nz - 1 - b].astype(F32) + gdown_in[b].astype(F32)
                wsum[...] = gown[b, wa].astype(F32) + both

    for b in order:
        g_core(b, 1 - c).start()
        g_load(b).start()

    def da_arrive(s, j):
        own_piece = jnp.logical_and(s == ta, 2 * c + j == wa)
        where = da.at[s, :, lanes(j * CHUNK)]

        @pl.when(own_piece)
        def _():
            da_copy(wa, z, True).wait()

        @pl.when(jnp.logical_not(own_piece))
        def _():
            send(where, where, sem_da.at[0, 0, 0], sem_da.at[1, s, j], (2 * c + j, s)).wait_recv()

    def da_sent(k, carry):
        w, b = (wa + k // nz) % nwa, k % nz

        @pl.when(jnp.logical_not(da_self(w, b)))
        def _():
            da_copy(w, b, False).wait_send()

        return carry

    def prepare(b):
        for core in range(2):
            for j in range(2):
                da_arrive(2 * b + core, j)
        for h in range(heads):
            group = slice(h * hdim, (h + 1) * hdim)
            both = []
            for s in (2 * b, 2 * b + 1):
                one = da[s, group, :].astype(F32) * zinv[h, s * 8 : s * 8 + 1, :]
                both.append(one.astype(BF16))
                scaled[s, group, :] = both[-1]
            made = jnp.dot(
                jnp.concatenate(both, axis=0), terms[h], preferred_element_type=F32
            ).astype(BF16)
            partial[2 * b, group, :] = made[:hdim]
            partial[2 * b + 1, group, :] = made[hdim:]
        core_copy(b, 1 - c).start()

    def shifts():
        for h in range(heads):
            group = slice(h * hdim, (h + 1) * hdim)
            for s in range(nta):
                inv = zinv[h, s * 8 : s * 8 + 1, :]
                one = da[s, group, :].astype(F32) * mixed[s, group, :]
                along = jnp.sum(one, axis=0, keepdims=True)
                shift[h, s * 8 : (s + 1) * 8, :] = jnp.broadcast_to(along * inv, (8, query))

    def core_copy(b, core):
        return send(
            partial.at[2 * b + core],
            paired.at[b],
            sem_core.at[0, b],
            sem_core.at[1, b],
            (wa, me.peer),
        )

    def out_start():
        for q in range(nz):
            back_own(outown, output, sem_out, q).start()
            for step in range(1, nwa):
                back_copy(outown, output, sem_out, step, q).start()

    def line_copy(up, j, q):
        k = 0 if up else 1
        cols = pl.ds(q * part, part)
        return send(
            partial.at[2 * (nz - 1 - j if up else j) + c, :, cols],
            (up_in if up else down_in).at[j, :, cols],
            sem_line.at[0, k, j, q],
            sem_line.at[1, k, j, q],
            (wa, ta + 2 if up else ta - 2),
        )

    ready = set()

    def core_ready(b):
        if b not in ready:
            ready.add(b)
            core_copy(b, c).wait_recv()

    def chip_sum(b, q):
        cols = pl.ds(q * part, part)
        return partial[2 * b + c, :, cols].astype(F32) + paired[b, :, cols].astype(F32)

    def line_step(up, j, q):
        target = nz - 1 - j if up else j
        landed = up_in if up else down_in
        cols = pl.ds(q * part, part)

        @pl.when(z < target if up else z > target)
        def _():
            first = z == (0 if up else nz - 1)

            @pl.when(jnp.logical_not(first))
            def _():
                line_copy(up, j, q).wait_recv()
                total = chip_sum(target, q) + landed[j, :, cols].astype(F32)
                partial[2 * target + c, :, cols] = total.astype(BF16)

            @pl.when(first)
            def _():
                partial[2 * target + c, :, cols] = chip_sum(target, q).astype(BF16)

            line_copy(up, j, q).start()

    def line(j):
        core_ready(nz - 1 - j)
        core_ready(j)
        for q in range(nz):
            line_step(True, j, q)
            line_step(False, j, q)

    fetch[0].wait()
    for b in order:
        g_cores(b)
    prepare(order[0])
    prepare(order[1])
    line(0)
    for b in order[2:]:
        prepare(b)
    for j in range(1, nz - 1):
        line(j)
    for b in range(nz):
        core_ready(b)

    fetch[1].wait()
    shifts()
    get_wv.wait()
    for t in range(nta):
        turned = jnp.concatenate([wv[w, t] for w in range(nwa)], axis=0).T
        wvt[t * wdepth : (t + 1) * wdepth, :] = turned[:wdepth]
    fetch[2].wait()
    fetch[3].wait()
    norm, inv = norm_stats(xown[...].astype(F32))
    normed[...] = norm
    invs[...] = jnp.broadcast_to(inv, invs.shape)
    gains[...] = jnp.zeros_like(gains)
    biases[...] = jnp.zeros_like(biases)
    fetch[4].wait()
    for b in order:
        g_plane(b)
    out_start()

    def dv_copy(step, q):
        w = (wa + step) % nwa
        return send(
            dvalue.at[:, lanes(q * part + w * CHUNK)],
            dvown.at[block_rows(wa), pl.ds(q * CHUNK, CHUNK)],
            sem_dv.at[0, step, q],
            sem_dv.at[1, step, q],
            (w, ta),
        )

    place = lax.broadcasted_iota(jnp.int32, (width, part), 1).astype(F32)

    def final(q):
        cols = pl.ds(q * part, part)
        key_valid = place + q * part < ln[0:1, 0:1]
        for b in range(nz):

            @pl.when(z == b)
            def _():
                total = chip_sum(b, q)
                if b > 0:
                    line_copy(True, nz - 1 - b, q).wait_recv()
                    total = total + up_in[nz - 1 - b, :, cols].astype(F32)
                if b < nz - 1:
                    line_copy(False, b, q).wait_recv()
                    total = total + down_in[b, :, cols].astype(F32)
                dvalue[:, cols] = jnp.where(key_valid, total, 0.0).astype(BF16)

        for step in range(1, nwa):
            dv_copy(step, q).start()
        dvown[block_rows(wa), q * CHUNK : (q + 1) * CHUNK] = dvalue[
            :, lanes(q * part + wa * CHUNK)
        ]

    for b in order:
        g_end(b)
    g_origin()
    for q in range(nz):
        final(q)

    g_hop(0)
    vmade = lax.dot_general(layer[...], dvalue[...], ROWS_NT, preferred_element_type=F32)
    vsend[...] = vmade.astype(BF16).reshape(nta, wdepth, width)
    vbias = jnp.sum(dvalue[...].astype(F32), axis=1, keepdims=True)

    def v_copy(step):
        t = (ta + step) % nta
        return send(
            vsend.at[t], vrecv.at[step], sem_v.at[0, step], sem_v.at[1, step], (wa, t)
        )

    for step in range(1, nta):
        v_copy(step).start()

    for q in range(nz):
        cols = slice(q * CHUNK, (q + 1) * CHUNK)
        for step in range(1, nwa):
            dv_copy(step, q).wait_recv()
        dl = jnp.dot(wvt[...], dvown[:, cols], preferred_element_type=F32)
        norm = normed[:, cols]
        e = dl * pfull[:, 0:1]
        mean_e = jnp.sum(e, axis=0, keepdims=True) / depth
        mean_n = jnp.sum(e * norm, axis=0, keepdims=True) / depth
        made = dresid[:, cols] + invs[0:1, cols] * (e - mean_e - norm * mean_n)
        tsend[:, cols] = made.astype(BF16)
        back_own(tsend, tgrad, sem_tg, q).start()
        for step in range(1, nwa):
            back_copy(tsend, tgrad, sem_tg, step, q).start()
        gains[...] += dl * norm
        biases[...] += dl

    gain = jnp.sum(gains[...], axis=1, keepdims=True)
    bias = jnp.sum(biases[...], axis=1, keepdims=True)
    column = lax.broadcasted_iota(jnp.int32, (depth, PAD), 1)
    cols = jnp.where(column == 0, gain, jnp.where(column == 1, bias, vcol[...]))
    wide = vrow.shape[1] // nwa
    gap = csend.shape[2] - CHUNK
    used = wide // CHUNK
    for w in range(nwa):
        piece = cols[w * width : (w + 1) * width]
        piece = jnp.concatenate([piece, jnp.zeros((gap - width, PAD), F32)], axis=0)
        csend[w, :, :gap] = piece.T[:8]
        starts = [w * wide + row * CHUNK for row in range(used)]
        packed = [vrow[0:1, start : start + CHUNK] for start in starts]
        csend[w, :, gap:] = jnp.concatenate(packed + [jnp.zeros((8 - used, CHUNK), F32)], axis=0)

    def c_copy(step):
        w = (wa + step) % nwa
        return send(csend.at[w], crecv.at[step], sem_c.at[0, step], sem_c.at[1, step], (w, ta))

    for step in range(1, nwa):
        c_copy(step).start()
    g_hop(1)
    crecv[0] = csend[wa]
    piece = jnp.concatenate(
        [jnp.broadcast_to(vbias, (width, PAD)), jnp.zeros((gap - width, PAD), F32)], axis=0
    )
    vb_row = jnp.concatenate([piece.T[:8], jnp.zeros((8, CHUNK), F32)], axis=1)
    row = lax.broadcasted_iota(jnp.int32, vb_row.shape, 0)
    total = jnp.where(row == 2, vb_row, 0.0) + crecv[0]
    for step in range(1, nwa):
        c_copy(step).wait_recv()
        total = total + crecv[step]
    csum[...] = total

    def c2_copy(step):
        t = (ta + step) % nta
        return send(csum, crecv2.at[step], sem_c2.at[0, step], sem_c2.at[1, step], (wa, t))

    for step in range(1, nta):
        c2_copy(step).start()
    for j in range(2, nz - 1):
        g_hop(j)
    value_total = vsend[ta].astype(F32)
    for step in range(1, nta):
        v_copy(step).wait_recv()
        value_total = value_total + vrecv[step].astype(F32)
    vgrad[...] = value_total
    g_final()
    crecv2[0] = csum[...]
    for step in range(1, nta):
        c2_copy(step).wait_recv()
    full = jnp.zeros(csum.shape, F32)
    for t in range(nta):
        full = full + crecv2[(ta - t + nta) % nta]
    vectors[...] = full

    lax.fori_loop(0, nwa * nz, da_sent, 0)
    for step in range(1, nwa):
        for q in range(nz):
            back_copy(tsend, tgrad, sem_tg, step, q).wait()
            back_copy(outown, output, sem_out, step, q).wait()
            dv_copy(step, q).wait_send()
        c_copy(step).wait_send()
    for q in range(nz):
        back_own(outown, output, sem_out, q).wait()
        back_own(tsend, tgrad, sem_tg, q).wait()
    for step in range(1, nta):
        v_copy(step).wait_send()
        c2_copy(step).wait_send()
    for b in range(nz):
        core_copy(b, 1 - c).wait_send()
        g_core(b, 1 - c).wait_send()
        for k in range(2):
            g_first(k, 0, b).wait_send()
            g_first(k, 1, b).wait_send()
            g_second(k, b).wait_send()
    for j in range(nz - 1):

        @pl.when(z < nz - 1 - j)
        def _():
            for q in range(nz):
                line_copy(True, j, q).wait_send()
            g_line(True, j).wait_send()

        @pl.when(z > j)
        def _():
            for q in range(nz):
                line_copy(False, j, q).wait_send()
            g_line(False, j).wait_send()


def run_backward(
    dims, dattended, outown, dresid, xown, terms, mixed, zinv, lens, ln, pfull, layer, weights, wgrad, vcol, vrow
):
    nwa, nta = dims
    nz = nta // 2
    half, both = weights.shape[2] // 2, wgrad.shape[4]
    depth, own = dresid.shape
    width = depth // nwa
    heads, query, seq = terms.shape
    wdepth = depth // nta
    wide = 3 * CHUNK
    dma = pltpu.SemaphoreType.DMA
    return pl.pallas_call(
        functools.partial(backward_kernel, dims),
        out_shape=(
            shape_of((nta, width, query), BF16),
            shape_of((heads, nta * 8, query), F32),
            shape_of((width, seq), BF16),
            shape_of((width, seq), BF16),
            shape_of((wdepth, width), F32),
            shape_of((8, wide), F32),
            shape_of((width, both), F32),
        ),
        in_specs=anywhere(6) + whole(4) + anywhere(3) + whole(2),
        out_specs=tuple(whole(7)),
        scratch_shapes=[
            pltpu.VMEM((depth, own), F32),
            pltpu.VMEM((depth, own), BF16),
            pltpu.VMEM((heads, query, seq), BF16),
            pltpu.VMEM((nta, width, query), F32),
            pltpu.VMEM((depth, seq), BF16),
            pltpu.VMEM((depth, own), F32),
            pltpu.VMEM((8, own), F32),
            pltpu.VMEM((depth, depth), BF16),
            pltpu.VMEM((depth, CHUNK), F32),
            pltpu.VMEM((depth, CHUNK), F32),
            pltpu.VMEM((nta, width, query), BF16),
            pltpu.VMEM((nta, width, seq), BF16),
            pltpu.VMEM((nz, width, seq), BF16),
            pltpu.VMEM((nz - 1, width, seq), BF16),
            pltpu.VMEM((nz - 1, width, seq), BF16),
            pltpu.VMEM((nz, nwa, width, both), BF16),
            pltpu.VMEM((nz, nwa, width, both), BF16),
            pltpu.VMEM((nz, 2, half, both), BF16),
            pltpu.VMEM((nz, 2, half, both), BF16),
            pltpu.VMEM((nz, half, both), BF16),
            pltpu.VMEM((nz, half, both), BF16),
            pltpu.VMEM((nz - 1, width, both), BF16),
            pltpu.VMEM((nz - 1, width, both), BF16),
            pltpu.VMEM((width, seq), BF16),
            pltpu.VMEM((depth, own), BF16),
            pltpu.VMEM((nwa, nta, width, PAD), BF16),
            pltpu.VMEM((nta, wdepth, width), BF16),
            pltpu.VMEM((nta, wdepth, width), BF16),
            pltpu.VMEM((depth, own), BF16),
            pltpu.VMEM((nwa, 8, wide), F32),
            pltpu.VMEM((nwa, 8, wide), F32),
            pltpu.VMEM((8, wide), F32),
            pltpu.VMEM((nta, 8, wide), F32),
            dma((2, nta, max(nz, 2))),
            dma((2, nwa, nz)),
            dma((2, nz)),
            dma((2, 2, nz, nz)),
            dma((2, nwa, nz)),
            dma((2, nwa, nz)),
            dma((2, nta)),
            dma((2, nwa)),
            dma((2, nta)),
            dma((6,)),
            dma((2, 8, nz)),
            dma((2, 2, nz)),
        ],
        compiler_params=pltpu.CompilerParams(
            collective_id=2, has_side_effects=True, vmem_limit_bytes=VMEM_BYTES
        ),
        cost_estimate=pl.CostEstimate(
            flops=4 * 10**9, bytes_accessed=80 * 10**6, transcendentals=0
        ),
    )(
        dattended, outown, dresid, xown, terms, mixed, zinv, lens, ln, pfull, layer, weights, wgrad,
        vcol, vrow,
    )


def logits_kernel(
    terms,
    scaled,
    value,
    shift,
    lens,
    output,
    tgrad,
    wsum,
    vgrad,
    vectors,
    out,
    output_out,
    tgrad_out,
    up_out,
    down_out,
    wo_out,
    vgrad_out,
    *vector_out,
):
    nta = scaled.shape[0]
    for row, ref in enumerate(vector_out[:-1]):
        ref[...] = vectors[row, : ref.shape[0]]
    bias_out = vector_out[-1]
    gap = vectors.shape[1] - CHUNK
    for row in range(bias_out.shape[0] // CHUNK):
        bias_out[row * CHUNK : (row + 1) * CHUNK] = vectors[row, gap:]
    output_out[...] = output[...]
    tgrad_out[...] = tgrad[...].astype(F32)
    vgrad_out[...] = vgrad[...]
    hidden = up_out.shape[1]
    up_out[...] = wsum[:, :hidden]
    down_out[...] = wsum[:, hidden : 2 * hidden]
    wo_out[...] = wsum[:, 2 * hidden : 2 * hidden + wo_out.shape[1]]
    cols = terms.shape[2]
    stacked = jnp.concatenate([scaled[s] for s in range(nta)], axis=0)
    values = jnp.concatenate([value[s] for s in range(nta)], axis=0)
    made = lax.dot_general(stacked, values, ROWS_TN, preferred_element_type=F32)
    where = (nta * 8, cols)
    place = lax.broadcasted_iota(jnp.int32, where, 1) + pl.program_id(1) * cols
    first = lax.broadcasted_iota(jnp.int32, where, 0) % 8 == 0
    valid = jnp.logical_and(place.astype(F32) < lens[:, 0:1], first)
    valid = jnp.where(valid, 1.0, 0.0).astype(BF16)
    high = shift[0].astype(BF16)
    rest = (shift[0] - high.astype(F32)).astype(BF16)
    made = made - lax.dot_general(high, valid, ROWS_TN, preferred_element_type=F32)
    made = made - lax.dot_general(rest, valid, ROWS_TN, preferred_element_type=F32)
    out[0] = terms[0].astype(F32) * made


def run_logits(terms, scaled, value, shift, lens, output, tgrad, wsum, vgrad, vectors, bias):
    heads, query, seq = terms.shape
    nta, width, _ = scaled.shape
    hdim = width // heads
    cols = min(2048, seq)
    steps = seq // cols
    wdepth = vgrad.shape[0]
    hidden = (wsum.shape[1] - PAD) // 2
    total = heads * steps
    flat = (shape_of((width,), F32),) * 7 + (shape_of((bias,), F32),)

    def rows_of(array, lanes_in=None):
        shape = (array[0] // total, lanes_in or array[1])
        return pl.BlockSpec(shape, lambda h, k: (h * steps + k, 0))

    return pl.pallas_call(
        logits_kernel,
        grid=(heads, steps),
        out_shape=(
            shape_of((heads, query, seq), F32),
            shape_of((width, seq), BF16),
            shape_of((width, seq), F32),
            shape_of((width, hidden), F32),
            shape_of((width, hidden), F32),
            shape_of((width, wdepth), F32),
            shape_of(vgrad.shape, F32),
        )
        + flat,
        in_specs=[
            pl.BlockSpec((1, query, cols), lambda h, k: (h, 0, k)),
            pl.BlockSpec((nta, hdim, query), lambda h, k: (0, h, 0)),
            pl.BlockSpec((nta, hdim, cols), lambda h, k: (0, h, k)),
            pl.BlockSpec((1, nta * 8, query), lambda h, k: (h, 0, 0)),
            pl.BlockSpec(lens.shape, lambda h, k: (0, 0)),
            rows_of(output.shape),
            rows_of(tgrad.shape),
            rows_of(wsum.shape),
            rows_of(vgrad.shape),
            pl.BlockSpec(vectors.shape, lambda h, k: (0, 0)),
        ],
        out_specs=(
            pl.BlockSpec((1, query, cols), lambda h, k: (h, 0, k)),
            rows_of(output.shape),
            rows_of(tgrad.shape),
            rows_of((width, hidden)),
            rows_of((width, hidden)),
            rows_of((width, wdepth)),
            rows_of(vgrad.shape),
        )
        + tuple(pl.BlockSpec(one.shape, lambda h, k: (0,)) for one in flat),
        compiler_params=pltpu.CompilerParams(vmem_limit_bytes=VMEM_BYTES),
        cost_estimate=pl.CostEstimate(
            flops=2 * 10**9, bytes_accessed=20 * 10**6, transcendentals=0
        ),
    )(terms, scaled, value, shift, lens, output, tgrad, wsum, vgrad, vectors)


def on_device_fast(
    dims,
    tokens,
    seq_lengths,
    norm1_gain,
    norm1_bias,
    value_weight,
    value_bias,
    synth_logits,
    out_weight,
    out_bias,
    norm2_gain,
    norm2_bias,
    up_weight,
    up_bias,
    down_weight,
    down_bias,
    cotangent,
):
    nwa, nta = dims
    width = tokens.shape[0]
    per_feature = (
        norm1_gain,
        norm1_bias,
        value_bias,
        out_bias,
        norm2_gain,
        norm2_bias,
        down_bias,
    )
    prow = jnp.pad(jnp.stack(per_feature), ((0, 1), (0, 2 * CHUNK - width)))
    prow = jnp.concatenate([prow, jnp.broadcast_to(up_bias, (8, up_bias.shape[0]))], axis=1)
    ln = jnp.broadcast_to(seq_lengths.astype(F32)[:, None], (8, CHUNK))
    logits = synth_logits.transpose(1, 0, 2)
    (
        xown,
        weights,
        _,
        layer,
        value,
        terms,
        mixed,
        zinv,
        lens,
        pfull,
        outown,
        dattended,
        dresid,
        wgrad,
        vcol,
        vrow,
    ) = run_forward(
        dims,
        tokens,
        cotangent,
        out_weight,
        value_weight,
        up_weight,
        down_weight.T,
        prow,
        ln,
        logits,
    )
    scaled, shift, output, tgrad, vgrad, vectors, wsum = run_backward(
        dims,
        dattended,
        outown,
        dresid,
        xown,
        terms,
        mixed,
        zinv,
        lens,
        ln,
        pfull,
        layer,
        weights,
        wgrad,
        vcol,
        vrow,
    )
    logits_grad, output, tgrad, up_grad, down_grad, out_grad, vgrad, *flat = run_logits(
        terms, scaled, value, shift, lens, output, tgrad, wsum, vgrad, vectors, up_bias.shape[0]
    )
    return (
        output,
        tgrad,
        flat[0],
        flat[1],
        vgrad,
        flat[2],
        logits_grad.transpose(1, 0, 2),
        out_grad,
        flat[3],
        flat[4],
        flat[5],
        up_grad,
        flat[7],
        down_grad.T,
        flat[6],
    )


def fits(mesh):
    return mesh.shape["wa"] == 4 and mesh.shape["ta"] == 8


def solution(mesh):
    placed = (
        P("wa", "ta"),
        P("ta"),
        P("wa"),
        P("wa"),
        P("ta", "wa"),
        P("wa"),
        P("ta", "wa", None),
        P("wa", "ta"),
        P("wa"),
        P("wa"),
        P("wa"),
        P("wa", "ta"),
        P("wa"),
        P("ta", "wa"),
        P("wa"),
        P("wa", "ta"),
    )
    sizes = (mesh.shape["wa"], mesh.shape["ta"])
    body = functools.partial(on_device_fast, sizes) if fits(mesh) else on_device
    return jax.shard_map(
        body,
        mesh=mesh,
        in_specs=placed,
        out_specs=(
            P("wa", "ta"),
            P("wa", "ta"),
            P("wa"),
            P("wa"),
            P("ta", "wa"),
            P("wa"),
            P("ta", "wa", None),
            P("wa", "ta"),
            P("wa"),
            P("wa"),
            P("wa"),
            P("wa", "ta"),
            P("wa"),
            P("ta", "wa"),
            P("wa"),
        ),
        check_vma=False,
    )
```
